32 devices in a mesh: au: 4 (over y, x), vert: 8 (over z, core).
Axes of the slice: x: 2, y: 2, z: 4, core: 2. Of those that a mesh axis runs over, the one named last changes fastest.
Arguments:
- visibilities: bfloat16 [768, 2, 2048], P(('au', 'vert')), may hold values from -6 to 6
- baseline_offsets: float32 [768, 2, 128], P(('au', 'vert')), may hold values from -8 to 8
- channel_scale: float32 [16], replicated, may hold values from 0.8 to 1.25
- screen_depth: float32 [768], P(('au', 'vert')), may hold values from -300 to 300
- stations: int32 [768, 2], P(('au', 'vert')), may hold values from 0 to 511
- corners: int32 [768, 2], P(('au', 'vert')), may hold values from 0 to 8191, as said below
- beam_terms: bfloat16 [512, 2, 1024], P(('au', 'vert')), may hold values from -5 to 5
Outputs:
- gridded: float32 [8192, 2, 8192], P('au', None, 'vert')
- dirty_image: float32 [8192, 2, 8192], P(('au', 'vert'))
The draws below stay inside these ranges and needn't reach their ends.
Inputs may be any that keep to these rules, and one draw needn't show every extreme that they name: Subgrid s belongs to block d = floor(s / 24); with d = r * 8 + c, corners[s, 0] lies in [r * 2048, (r + 1) * 2048) and the columns corners[s, 1] to corners[s, 1] + 31 lie inside one column tile of 1024 columns. At most 6 subgrids of one block lie in one column tile; for every r one column tile holds exactly 6 subgrids of every block of that r.
All inputs are finite; a program needn't handle non-finite values.
Results may differ from the reference program's by a relative error of at most 0.039.
Values may be sent and summed in bfloat16 or wider, within the bound.
No kernel may reach another device: no remote copies, remote signals or barrier semaphores. Data moves between devices by JAX's collectives and lax.ppermute only.
A program may use at most 128 MiB of HBM per device.

```python
import math
import jax
import jax.numpy as jnp
from jax import lax

G = 8192
SUB = 32
TIMES = 128
CHANNELS = 16
STATIONS = 512
SUB_DEV = 24
TILES_U = 4
TILES_V = 8
TILE_U = 2048
TILE_V = 1024
SUBGRIDS = 768
CAP = 6


def draw_corners(key, part):
    device_total = TILES_U * TILES_V
    key_hot, key_devices = jax.random.split(jax.random.fold_in(key, 11))
    hot_columns = jax.random.randint(key_hot, (TILES_U,), 0, TILES_V)
    device_keys = jax.random.split(key_devices, device_total)

    def one_device(device_key, device):
        random_keys = jax.random.split(device_key, 5)
        row_tile = device // TILES_V
        target = hot_columns[row_tile]
        candidate_options = jnp.arange(TILES_V * CAP, dtype=jnp.int32) // CAP
        middle_point = TILES_V // 2
        extra_reward = (middle_point - jnp.abs(candidate_options - middle_point)) * 4096
        placement_score = jax.random.randint(random_keys[0], candidate_options.shape, 0, 65536) + extra_reward
        placement_score = jnp.where(candidate_options == target, -1, placement_score)
        ranked = placement_score * (TILES_V * CAP) + jnp.arange(TILES_V * CAP, dtype=jnp.int32)
        ordering = jnp.argsort(-ranked)
        chosen = candidate_options[ordering[:SUB_DEV - CAP]]
        targets = jnp.concatenate([chosen, jnp.full((CAP,), target, jnp.int32)])
        targets = targets[jax.random.permutation(random_keys[1], SUB_DEV)]
        row_offset = jax.random.randint(random_keys[2], (SUB_DEV,), 0, TILE_U)
        col_offset = jax.random.randint(random_keys[3], (SUB_DEV,), 0, TILE_V - SUB + 1)
        marks = jax.random.permutation(random_keys[4], SUB_DEV)
        row_offset = row_offset.at[marks[0]].set(0).at[marks[1]].set(TILE_U - 1)
        col_offset = col_offset.at[marks[2]].set(0).at[marks[3]].set(TILE_V - SUB)
        grid_rows = row_tile * TILE_U + row_offset
        grid_cols = targets * TILE_V + col_offset
        return jnp.stack([grid_rows, grid_cols], axis=1)
    result = jax.vmap(one_device)(device_keys, jnp.arange(device_total, dtype=jnp.int32))
    return result.reshape(device_total * SUB_DEV, 2).astype(jnp.int32)


def set_ends(values, own_key, low, largest):
    shape = values.shape
    place = [jax.random.randint(jax.random.fold_in(own_key, axis), (), 0, shape[axis]) for axis in range(len(shape))]
    values = values.at[tuple(place)].set(low)
    longest = shape.index(max(shape))
    place[longest] = (place[longest] + 1) % shape[longest]
    return values.at[tuple(place)].set(largest)


def level_of(key, dims, cuts, least, top_value):
    def one(axis_at, shards_of):
        steps = jax.random.uniform(jax.random.fold_in(jax.random.fold_in(key, 6), axis_at), (shards_of,), jnp.float32, least / len(cuts), top_value / len(cuts))
        return jnp.repeat(jnp.exp(steps), dims[axis_at] // shards_of).reshape((-1,) + (1,) * (len(dims) - axis_at - 1))

    level = one(*cuts[0])
    for cut in cuts[1:]:
        level = level * one(*cut)
    return level


def noise(stream_key, dims, width, most, cuts=(), held_as=jnp.bfloat16):
    entries = width * jax.random.normal(stream_key, dims, jnp.float32)
    if cuts:
        entries = entries * level_of(stream_key, dims, cuts, -0.22, 0.18)
    return jnp.clip(entries, -most, most).astype(held_as)


def setup_inputs(seed: int = 0) -> dict:
    key_list = jax.random.split(jax.random.key(seed), 8)
    return {
        "visibilities": noise(key_list[0], (SUBGRIDS, 2, TIMES * CHANNELS), 1.0, 6.0, ((0, 32),)),
        "baseline_offsets": jnp.clip(jax.random.uniform(key_list[1], (SUBGRIDS, 2, TIMES), jnp.float32, -8.0, 8.0) * level_of(key_list[1], (SUBGRIDS, 2, TIMES), ((0, 32),), -0.4, 0.0), -8.0, 8.0),
        "channel_scale": jnp.clip(jnp.exp(jax.random.uniform(key_list[2], (CHANNELS,), jnp.float32, math.log(0.8), math.log(1.25))), 0.8, 1.25),
        "screen_depth": jnp.clip(jax.random.uniform(key_list[3], (SUBGRIDS,), jnp.float32, -300.0, 300.0) * level_of(key_list[3], (SUBGRIDS,), ((0, 32),), -0.4, 0.0), -300.0, 300.0),
        "stations": set_ends(jax.random.randint(key_list[4], (SUBGRIDS, 2), 0, STATIONS), jax.random.fold_in(key_list[4], 1), 0, STATIONS - 1).astype(jnp.int32),
        "corners": draw_corners(jax.random.fold_in(key_list[7], 71), 0),
        "beam_terms": noise(key_list[6], (STATIONS, 2, SUB * SUB), 1.0, 5.0, ((0, 32),)),
    }


field_view = 0.1
highest = lax.Precision.HIGHEST

def complex_einsum(formula, left_operand_pair, right_pair):
    left_re, left_im = left_operand_pair
    right_re, right_im = right_pair
    real_part = jnp.einsum(formula, left_re, right_re, precision=highest) - jnp.einsum(formula, left_im, right_im, precision=highest)
    imag_part = jnp.einsum(formula, left_re, right_im, precision=highest) + jnp.einsum(formula, left_im, right_re, precision=highest)
    return (real_part, imag_part)

def complex_product(left_operand_pair, right_pair):
    return (left_operand_pair[0] * right_pair[0] - left_operand_pair[1] * right_pair[1], left_operand_pair[0] * right_pair[1] + left_operand_pair[1] * right_pair[0])

def subgrid_table():
    centred = jnp.arange(SUB, dtype=jnp.int32) - SUB // 2
    product = centred[:, None] * centred[None, :] % SUB
    angle = -2.0 * math.pi / SUB * product.astype(jnp.float32)
    return (jnp.cos(angle) / SUB, jnp.sin(angle) / SUB)

def grid_subgrids(vis_items, offset_items, depth_items, beam_first, beam_second, channel_scale):
    item_count = vis_items.shape[0]
    vis_count = vis_items.shape[2]
    pixel_pos = jnp.arange(SUB, dtype=jnp.float32) - SUB // 2
    shift_u = (offset_items[:, 0, :, None] * channel_scale[None, None, :]).reshape(item_count, vis_count)
    shift_v = (offset_items[:, 1, :, None] * channel_scale[None, None, :]).reshape(item_count, vis_count)
    angle_u = 2.0 * math.pi / SUB * pixel_pos[None, :, None] * shift_u[:, None, :]
    angle_v = 2.0 * math.pi / SUB * pixel_pos[None, :, None] * shift_v[:, None, :]
    vis_re = vis_items[:, 0, None, :].astype(jnp.float32)
    vis_im = vis_items[:, 1, None, :].astype(jnp.float32)
    cos_u = jnp.cos(angle_u)
    sin_u = jnp.sin(angle_u)
    weighted_re = (vis_re * cos_u - vis_im * sin_u).astype(jnp.bfloat16)
    weighted_im = (vis_re * sin_u + vis_im * cos_u).astype(jnp.bfloat16)
    phasor_re = jnp.cos(angle_v).astype(jnp.bfloat16)
    phasor_im = jnp.sin(angle_v).astype(jnp.bfloat16)
    sky_pair = complex_einsum('npk,nqk->npq', (weighted_re.astype(jnp.float32), weighted_im.astype(jnp.float32)), (phasor_re.astype(jnp.float32), phasor_im.astype(jnp.float32)))
    taper_line = 1.0 - ((2.0 * jnp.arange(SUB, dtype=jnp.float32) + 1.0 - SUB) / SUB) ** 2
    taper_grid = taper_line[:, None] * taper_line[None, :] / math.sqrt(vis_count)
    sky_angle = pixel_pos * field_view / SUB
    radius_sq = sky_angle[:, None] ** 2 + sky_angle[None, :] ** 2
    screen_angle = -math.pi * depth_items[:, None, None] * radius_sq[None, :, :]
    first_beam = beam_first.astype(jnp.float32).reshape(item_count, 2, SUB, SUB)
    second_beam = beam_second.astype(jnp.float32).reshape(item_count, 2, SUB, SUB)
    pair_term = complex_product((first_beam[:, 0], first_beam[:, 1]), (second_beam[:, 0], -second_beam[:, 1]))
    mixed = complex_product(sky_pair, pair_term)
    screened = complex_product(mixed, (jnp.cos(screen_angle), jnp.sin(screen_angle)))
    corrected = (screened[0] * taper_grid, screened[1] * taper_grid)
    dft_pair = subgrid_table()
    partial_pair = complex_einsum('ip,npq->niq', dft_pair, corrected)
    uv_pair = complex_einsum('niq,jq->nij', partial_pair, dft_pair)
    return jnp.stack(uv_pair, axis=1).reshape(item_count, 2 * SUB * SUB)

def reference(visibilities, baseline_offsets, channel_scale, screen_depth, stations, corners, beam_terms):
    subgrid_total = visibilities.shape[0]
    block_size = math.gcd(subgrid_total, 64)
    block_count = subgrid_total // block_size

    def grid_block(pieces):
        vis_block, offset_block, depth_block, station_block = pieces
        first_beam = jnp.take(beam_terms, station_block[:, 0], axis=0)
        second_beam = jnp.take(beam_terms, station_block[:, 1], axis=0)
        return grid_subgrids(vis_block, offset_block, depth_block, first_beam, second_beam, channel_scale).astype(jnp.bfloat16)
    gridded_blocks = lax.map(grid_block, (visibilities.reshape((block_count, block_size) + visibilities.shape[1:]), baseline_offsets.reshape((block_count, block_size) + baseline_offsets.shape[1:]), screen_depth.reshape(block_count, block_size), stations.reshape(block_count, block_size, 2)))
    uv_values = gridded_blocks.reshape(subgrid_total, 2, SUB, SUB).astype(jnp.float32)
    span_index = jnp.arange(SUB, dtype=jnp.int32)
    row_index = (corners[:, 0, None] + span_index[None, :]) % G
    col_index = corners[:, 1, None] + span_index[None, :]
    gridded = jnp.zeros((G, 2, G), jnp.float32)
    gridded = gridded.at[row_index[:, :, None], :, col_index[:, None, :]].add(jnp.transpose(uv_values, (0, 2, 3, 1)))
    uv_field = lax.complex(gridded[:, 0, :], gridded[:, 1, :])
    spectrum = jnp.fft.ifft2(uv_field) * (G * G)
    image_scale = 1.0 / (SUB * math.sqrt(SUBGRIDS))
    dirty_image = jnp.stack([jnp.real(spectrum).T, jnp.imag(spectrum).T], axis=1) * image_scale
    return (gridded, dirty_image)
```

```python
import functools
import math

import jax
import jax.numpy as jnp
from jax import lax
from jax.experimental import pallas as pl
from jax.experimental.pallas import tpu as pltpu
from jax.sharding import PartitionSpec as P

G = 8192
SUB = 32
HALF = SUB // 2
PACK = 4 * SUB
LANES = 128
FINE = G // SUB
CHUNK = 768
field_view = 0.1
bf16 = jnp.bfloat16
f32 = jnp.float32
VMEM_BYTES = 58 * 1024 * 1024


def cmul(a, b):
    return (a[0] * b[0] - a[1] * b[1], a[0] * b[1] + a[1] * b[0])


def conj(a):
    return (a[0], -a[1])


def sky_kernel(vis_ref, trig_ref, factor_ref, out_ref, left_ref, right_ref):
    vis_count = vis_ref.shape[2]
    step = math.gcd(vis_count, 256)
    row = lax.broadcasted_iota(jnp.int32, (8, step), 0)
    bits = [(row >> bit) % 2 == 1 for bit in range(3)]

    def powers(c, s, extra):
        z = (jnp.broadcast_to(c, (8, step)), jnp.broadcast_to(s, (8, step)))
        low = (jnp.where(bits[0], z[0], 1.0), jnp.where(bits[0], z[1], 0.0))
        power = z
        for bit in (1, 2):
            power = (power[0] * power[0] - power[1] * power[1], 2.0 * power[0] * power[1])
            more = cmul(low, power)
            low = (jnp.where(bits[bit], more[0], low[0]), jnp.where(bits[bit], more[1], low[1]))
        eight = (power[0] * power[0] - power[1] * power[1], 2.0 * power[0] * power[1])
        sixteen = (eight[0] * eight[0] - eight[1] * eight[1], 2.0 * eight[0] * eight[1])
        if extra is not None:
            low = cmul(low, extra)
        blocks = [cmul(low, conj(sixteen)), cmul(low, conj(eight)), low, cmul(low, eight)]
        return [
            jnp.concatenate([blocks[2 * h][part], blocks[2 * h + 1][part]], axis=0).astype(bf16)
            for part in range(2)
            for h in range(2)
        ]

    for start in range(0, vis_count, step):
        at = pl.ds(start, step)
        vis = tuple(
            jnp.broadcast_to(vis_ref[0, part : part + 1, at].astype(f32), (8, step))
            for part in range(2)
        )
        for place, piece in enumerate(powers(trig_ref[0, 0:1, at], trig_ref[0, 1:2, at], vis)):
            left_ref[HALF * place : HALF * (place + 1), at] = piece
        for place, piece in enumerate(powers(trig_ref[0, 2:3, at], trig_ref[0, 3:4, at], None)):
            right_ref[HALF * place : HALF * (place + 1), at] = piece
    both = lax.dot_general(
        left_ref[...], right_ref[...], (((1,), (1,)), ((), ())), preferred_element_type=f32
    )
    sky = (
        both[:SUB, :SUB] - both[SUB:, SUB:],
        both[:SUB, SUB:] + both[SUB:, :SUB],
    )
    done = cmul(sky, (factor_ref[0, :, :SUB], factor_ref[0, :, SUB:]))
    out_ref[0] = jnp.concatenate(
        [done[0][:HALF], done[1][:HALF], done[0][HALF:], done[1][HALF:]], axis=1
    )


def sky_sums(visibilities, trig, factor, interpret=False):
    count, _, vis_count = visibilities.shape
    return pl.pallas_call(
        sky_kernel,
        grid=(count,),
        in_specs=[
            pl.BlockSpec((1, 2, vis_count), lambda s: (s, 0, 0)),
            pl.BlockSpec((1, 4, vis_count), lambda s: (s, 0, 0)),
            pl.BlockSpec((1, SUB, 2 * SUB), lambda s: (s, 0, 0)),
        ],
        out_specs=pl.BlockSpec((1, HALF, PACK), lambda s: (s, 0, 0)),
        out_shape=jax.ShapeDtypeStruct((count, HALF, PACK), f32),
        scratch_shapes=[
            pltpu.VMEM((2 * SUB, vis_count), bf16),
            pltpu.VMEM((2 * SUB, vis_count), bf16),
        ],
        compiler_params=pltpu.CompilerParams(vmem_limit_bytes=VMEM_BYTES),
        cost_estimate=pl.CostEstimate(
            flops=count * 2 * 64 * 64 * vis_count, bytes_accessed=count * 40 * vis_count,
            transcendentals=0,
        ),
        name="sky_sums",
        interpret=interpret,
    )(visibilities, trig, factor)


def correct_kernel(stations_ref, table_ref, sky_ref, right_ref, left_ref, out_ref, mid_ref):
    count = sky_ref.shape[0]
    lane = lax.broadcasted_iota(jnp.int32, (HALF, PACK), 1)
    imag = (lane // SUB) % 2 == 1
    sign = jnp.where(imag, 1.0, -1.0)

    def up(x):
        return pltpu.roll(x, SUB, 1)

    def down(x):
        return pltpu.roll(x, PACK - SUB, 1)

    for s in range(count):
        first = table_ref[stations_ref[2 * s]].astype(f32)
        second = table_ref[stations_ref[2 * s + 1]].astype(f32)
        second_up, second_down = up(second), down(second)
        first_swap = jnp.where(imag, up(first), down(first))
        pair = first * jnp.where(imag, second_up, second) - sign * first_swap * jnp.where(
            imag, second, second_down
        )
        pair_up, pair_down = up(pair), down(pair)
        sky = sky_ref[s]
        sky_swap = jnp.where(imag, up(sky), down(sky))
        corrected = sky * jnp.where(imag, pair_up, pair) + sign * sky_swap * jnp.where(
            imag, pair, pair_down
        )
        mid_ref[HALF * s : HALF * (s + 1), :] = corrected.astype(bf16)
    mid = jnp.dot(mid_ref[...], right_ref[...], preferred_element_type=f32).astype(bf16)
    for s in range(count):
        rows = mid[HALF * s : HALF * (s + 1)]
        tall = jnp.concatenate([rows[:, : 2 * SUB], rows[:, 2 * SUB :]], axis=0)
        four = jnp.dot(left_ref[...], tall, preferred_element_type=f32)
        real = four[:SUB, :SUB] - four[SUB:, SUB:]
        image = four[:SUB, SUB:] + four[SUB:, :SUB]
        out_ref[s] = jnp.concatenate(
            [real[:HALF], image[:HALF], real[HALF:], image[HALF:]], axis=1
        ).astype(bf16)


def corrected_subgrids(stations, table, sky, interpret=False):
    count = sky.shape[0]
    centred = jnp.arange(SUB, dtype=jnp.int32) - HALF
    index = jnp.arange(SUB, dtype=jnp.int32)
    angle = 2.0 * math.pi / SUB * (centred[:, None] * centred[None, :] % SUB).astype(f32)
    cols_re, cols_im = jnp.cos(angle) / SUB, -jnp.sin(angle) / SUB
    block = jnp.concatenate(
        [
            jnp.concatenate([cols_re.T, cols_im.T], axis=1),
            jnp.concatenate([-cols_im.T, cols_re.T], axis=1),
        ],
        axis=0,
    )
    right = jnp.kron(jnp.eye(2, dtype=f32), block).astype(bf16)
    angle = 2.0 * math.pi / SUB * ((index - HALF)[:, None] * centred[None, :] % SUB).astype(f32)
    left = jnp.concatenate([jnp.cos(angle) / SUB, -jnp.sin(angle) / SUB], axis=0).astype(bf16)
    return pl.pallas_call(
        correct_kernel,
        grid_spec=pltpu.PrefetchScalarGridSpec(
            num_scalar_prefetch=1,
            grid=(1,),
            in_specs=[
                pl.BlockSpec(table.shape, lambda i, *_: (0, 0, 0)),
                pl.BlockSpec(sky.shape, lambda i, *_: (0, 0, 0)),
                pl.BlockSpec(right.shape, lambda i, *_: (0, 0)),
                pl.BlockSpec(left.shape, lambda i, *_: (0, 0)),
            ],
            out_specs=pl.BlockSpec((count, HALF, PACK), lambda i, *_: (0, 0, 0)),
            scratch_shapes=[pltpu.VMEM((HALF * count, PACK), bf16)],
        ),
        out_shape=jax.ShapeDtypeStruct((count, HALF, PACK), bf16),
        compiler_params=pltpu.CompilerParams(vmem_limit_bytes=VMEM_BYTES),
        name="correct",
        interpret=interpret,
    )(stations.reshape(-1), table, sky, right, left)


def tile_kernel(
    block_ref, place_ref, uv_ref, out_ref, total_ref, sems, *, per_block, tile_rows, tile_cols
):
    del block_ref
    step = pl.program_id(0)
    lanes = 2 * tile_cols // LANES
    rows_all = total_ref.shape[0]
    zero_rows = math.gcd(rows_all, 1024)

    @pl.when(step == 0)
    def _():
        def clear(i, carry):
            total_ref[pl.ds(pl.multiple_of(i * zero_rows, zero_rows), zero_rows), :] = jnp.zeros(
                (zero_rows, LANES), f32
            )
            return carry

        lax.fori_loop(0, rows_all // zero_rows, clear, 0)

    lane = lax.broadcasted_iota(jnp.int32, (8, LANES), 1)
    row = lax.broadcasted_iota(jnp.int32, (8, LANES), 0)

    def one(s, carry):
        first = (step * per_block + s) * 2
        row_at = place_ref[first]
        col_at = place_ref[first + 1]

        @pl.when(jnp.logical_and(row_at >= 0, col_at >= 0))
        def _():
            packed = uv_ref[pl.ds(pl.multiple_of(s * HALF, HALF), HALF), :].astype(f32)
            tile = col_at // LANES
            offset = col_at % LANES
            shift = row_at % SUB
            base = row_at - shift

            def place(over):
                inside = lane < offset + SUB - LANES if over else (lane >= offset) & (lane < offset + SUB)
                for h in range(2):
                    for part in range(2):
                        from_lane = (2 * h + part) * SUB
                        moved = pltpu.roll(packed, lax.rem(offset - from_lane + LANES, LANES), 1)
                        for group in range(2):
                            values = moved[8 * group : 8 * (group + 1)]
                            first_row = HALF * h + 8 * group
                            late = row + first_row >= shift
                            for wrapped in range(2):
                                keep = jnp.logical_and(inside, late if wrapped == 0 else ~late)
                                start = (base + SUB * wrapped + first_row) * lanes
                                start = start + 2 * (tile + over) + part
                                at = pl.ds(start, 8, stride=lanes)
                                total_ref[at, :] = total_ref[at, :] + jnp.where(keep, values, 0.0)

            place(0)

            @pl.when(offset + SUB > LANES)
            def _():
                place(1)

        return carry

    lax.fori_loop(0, per_block, one, 0)

    @pl.when(step == pl.num_programs(0) - 1)
    def _():
        pieces = sems.shape[0]
        size = tile_rows * lanes // pieces
        copies = [
            pltpu.make_async_copy(
                total_ref.at[pl.ds(SUB * lanes + i * size, size), :],
                out_ref.at[pl.ds(i * size, size), :],
                sems.at[i],
            )
            for i in range(pieces)
        ]
        for copy in copies:
            copy.start()
        for copy in copies:
            copy.wait()


def uv_tile(uv_all, corners_all, au_index, vert_index, au_count, vert_count, interpret=False):
    total = uv_all.shape[0]
    tile_rows, tile_cols = G // au_count, G // vert_count
    per_block = total // au_count
    lanes = 2 * tile_cols // LANES
    before = lax.rem(au_index + au_count - 1, au_count)
    blocks = jnp.stack([au_index, before])
    held = corners_all.reshape(au_count, per_block, 2)
    held = jnp.concatenate(
        [lax.dynamic_index_in_dim(held, au_index, 0, False), lax.dynamic_index_in_dim(held, before, 0, False)]
    )
    row_at = (held[:, 0] - au_index * tile_rows + SUB + G) % G
    row_at = jnp.where(row_at < tile_rows + SUB, row_at, -1)
    col_at = held[:, 1] - vert_index * tile_cols
    col_at = jnp.where((col_at >= 0) & (col_at < tile_cols), col_at, -1)
    places = jnp.stack([row_at, col_at], axis=1).reshape(-1)
    rows_all = (tile_rows + 3 * SUB) * lanes
    result = pl.pallas_call(
        functools.partial(
            tile_kernel, per_block=per_block, tile_rows=tile_rows, tile_cols=tile_cols
        ),
        grid_spec=pltpu.PrefetchScalarGridSpec(
            num_scalar_prefetch=2,
            grid=(2,),
            in_specs=[pl.BlockSpec((per_block * HALF, PACK), lambda i, block, place: (block[i], 0))],
            out_specs=pl.BlockSpec(memory_space=pl.ANY),
            scratch_shapes=[pltpu.VMEM((rows_all, LANES), f32), pltpu.SemaphoreType.DMA((4,))],
        ),
        out_shape=jax.ShapeDtypeStruct((tile_rows * lanes, LANES), f32),
        compiler_params=pltpu.CompilerParams(vmem_limit_bytes=VMEM_BYTES),
        name="uv_tile",
        interpret=interpret,
    )(blocks, places, uv_all.reshape(total * HALF, PACK))
    result = result.reshape(tile_rows, tile_cols // LANES, 2, LANES)
    return jnp.transpose(result, (0, 2, 1, 3)).reshape(tile_rows, 2, tile_cols)


def short_transform(values):
    count = len(values)
    if count == 1:
        return values
    even = short_transform(values[0::2])
    odd = short_transform(values[1::2])
    low, high = [], []
    for k in range(count // 2):
        re, im = odd[k]
        if k == 0:
            turned = (re, im)
        elif 4 * k == count:
            turned = (-im, re)
        elif 8 * k == count:
            root = math.sqrt(0.5)
            turned = ((re - im) * root, (re + im) * root)
        elif 8 * k == 3 * count:
            root = math.sqrt(0.5)
            turned = ((re + im) * -root, (re - im) * root)
        else:
            c, s = math.cos(2 * math.pi * k / count), math.sin(2 * math.pi * k / count)
            turned = (re * c - im * s, re * s + im * c)
        low.append((even[k][0] + turned[0], even[k][1] + turned[1]))
        high.append((even[k][0] - turned[0], even[k][1] - turned[1]))
    return low + high


def image_kernel(
    uv_ref, corner_ref, phase_ref, columns_ref, unit_ref, count_ref, twist_ref,
    out_ref, uv_wide, here, after, shifts, total, *, chunks, row_block
):
    step = pl.program_id(0)
    size = uv_ref.shape[0] // HALF
    image_rows = phase_ref.shape[1]

    @pl.when(step < chunks * HALF)
    def _():
        pair = lax.rem(step, HALF)
        chunk = step // HALF

        @pl.when(pair == 0)
        def _():
            uv_wide[...] = uv_ref[...].astype(f32)
            corner = corner_ref[...]
            coarse, shift = corner // SUB, corner % SUB

            def looked_up(index, length, table):
                place = lax.broadcasted_iota(jnp.int32, (length, size), 0)
                one = (place == index).astype(f32).astype(bf16)
                return lax.dot_general(
                    one, table, (((0,), (0,)), ((), ())), preferred_element_type=f32
                )

            here[...] = looked_up(coarse, FINE, unit_ref[...]).astype(bf16)
            after[...] = looked_up(lax.rem(coarse + 1, FINE), FINE, unit_ref[...]).astype(bf16)
            shifts[...] = looked_up(shift, SUB, count_ref[...])

        rows = uv_wide[pl.ds(pair, size, stride=HALF), :].astype(bf16)
        spread = lax.dot_general(
            columns_ref[...], rows, (((1,), (1,)), ((), ())), preferred_element_type=f32
        )
        for h in range(2):
            index = pair + HALF * h
            start = 2 * image_rows * h
            part = (spread[start : start + image_rows], spread[start + image_rows : start + 2 * image_rows])
            turned = cmul(part, (phase_ref[0], phase_ref[1]))
            left = jnp.concatenate([turned[0].astype(bf16), turned[1].astype(bf16)], axis=1)
            late = shifts[:, :1] > index.astype(f32)
            table = jnp.where(late, after[...], here[...])
            right = jnp.concatenate(
                [table, jnp.concatenate([-table[:, FINE:], table[:, :FINE]], axis=1)], axis=0
            )
            sums = jnp.dot(left, right, preferred_element_type=f32)
            twist = twist_ref[pl.ds(index, 1), :]
            done = cmul((sums[:, :FINE], sums[:, FINE:]), (twist[:, :FINE], twist[:, FINE:]))

            if chunks == 1:
                total[index, 0] = done[0]
                total[index, 1] = done[1]
            else:
                @pl.when(chunk == 0)
                def _():
                    total[index, 0] = done[0]
                    total[index, 1] = done[1]

                @pl.when(chunk > 0)
                def _():
                    total[index, 0] += done[0]
                    total[index, 1] += done[1]

    @pl.when(step >= chunks * HALF)
    def _():
        first = (step - chunks * HALF) * row_block
        wide = 2 * G // LANES

        def eight_rows(group, carry):
            at = pl.ds(pl.multiple_of(first + 8 * group, 8), 8)
            for tile in range(FINE // LANES):
                lanes = pl.ds(tile * LANES, LANES)
                values = [(total[n, 0, at, lanes], total[n, 1, at, lanes]) for n in range(SUB)]
                for k, value in enumerate(short_transform(values)):
                    for part in range(2):
                        column = 2 * (k * (FINE // LANES) + tile) + part
                        out_ref[pl.ds(group * 8 * wide + column, 8, stride=wide), :] = value[part]
            return carry

        lax.fori_loop(0, row_block // 8, eight_rows, 0)


def image_rows_of(uv_all, corners_all, first_row, image_rows, interpret=False):
    total = uv_all.shape[0]
    size = math.gcd(total, CHUNK)
    chunks = total // size
    row_block = math.gcd(image_rows, 32)
    outs = image_rows // row_block
    wide = 2 * G // LANES
    rows = first_row + jnp.arange(image_rows, dtype=jnp.int32)
    turn = 2.0 * math.pi / G
    angle = turn * (rows[:, None] * corners_all[None, :, 1] % G).astype(f32)
    phase = jnp.stack([jnp.cos(angle), jnp.sin(angle)])
    angle = turn * (rows[:, None] * jnp.arange(SUB, dtype=jnp.int32)[None, :] % G).astype(f32)
    re, im = jnp.cos(angle), jnp.sin(angle)
    block = jnp.concatenate(
        [jnp.concatenate([re, -im], axis=1), jnp.concatenate([im, re], axis=1)], axis=0
    )
    columns = jnp.kron(jnp.eye(2, dtype=f32), block).astype(bf16)
    fine = jnp.arange(FINE, dtype=jnp.int32)
    angle = 2.0 * math.pi / FINE * (fine[:, None] * fine[None, :] % FINE).astype(f32)
    unit = jnp.concatenate([jnp.cos(angle), jnp.sin(angle)], axis=1).astype(bf16)
    angle = turn * (jnp.arange(SUB, dtype=jnp.int32)[:, None] * fine[None, :]).astype(f32)
    scale = 1.0 / (SUB * math.sqrt(total))
    twist = jnp.concatenate([jnp.cos(angle), jnp.sin(angle)], axis=1) * scale
    counts = jnp.broadcast_to(jnp.arange(SUB, dtype=f32)[:, None], (SUB, LANES)).astype(bf16)
    last = chunks - 1

    def chunk_of(i):
        return jnp.minimum(i // HALF, last)

    result = pl.pallas_call(
        functools.partial(image_kernel, chunks=chunks, row_block=row_block),
        grid=(chunks * HALF + outs,),
        in_specs=[
            pl.BlockSpec((size * HALF, PACK), lambda i: (chunk_of(i), 0)),
            pl.BlockSpec((1, size), lambda i: (0, chunk_of(i))),
            pl.BlockSpec((2, image_rows, size), lambda i: (0, 0, chunk_of(i))),
            pl.BlockSpec(columns.shape, lambda i: (0, 0)),
            pl.BlockSpec(unit.shape, lambda i: (0, 0)),
            pl.BlockSpec(counts.shape, lambda i: (0, 0)),
            pl.BlockSpec(twist.shape, lambda i: (0, 0)),
        ],
        out_specs=pl.BlockSpec(
            (row_block * wide, LANES), lambda i: (jnp.maximum(i - chunks * HALF, 0), 0)
        ),
        out_shape=jax.ShapeDtypeStruct((image_rows * wide, LANES), f32),
        scratch_shapes=[
            pltpu.VMEM((size * HALF, PACK), f32),
            pltpu.VMEM((size, 2 * FINE), bf16),
            pltpu.VMEM((size, 2 * FINE), bf16),
            pltpu.VMEM((size, LANES), f32),
            pltpu.VMEM((SUB, 2, image_rows, FINE), f32),
        ],
        compiler_params=pltpu.CompilerParams(vmem_limit_bytes=VMEM_BYTES),
        name="image",
        interpret=interpret,
    )(
        uv_all.reshape(total * HALF, PACK), corners_all[:, 0].reshape(1, total),
        phase, columns, unit, counts, twist,
    )
    result = result.reshape(image_rows, G // LANES, 2, LANES)
    return jnp.transpose(result, (0, 2, 1, 3)).reshape(image_rows, 2, G)


def packed_beams(beam_terms):
    count = beam_terms.shape[0]
    parts = beam_terms.reshape(count, 2, 2, HALF, SUB)
    return jnp.transpose(parts, (0, 3, 2, 1, 4)).reshape(count, HALF, PACK)


def base_turns(baseline_offsets, channel_scale):
    count, _, times = baseline_offsets.shape
    shifts = (baseline_offsets[:, :, :, None] * channel_scale).reshape(count, 2, -1)
    angle = 2.0 * math.pi / SUB * shifts
    return jnp.stack([jnp.cos(angle), jnp.sin(angle)], axis=2).reshape(count, 4, -1)


def pixel_factor(screen_depth, shift, vis_count):
    pixel = jnp.arange(SUB, dtype=f32) - HALF
    taper_line = 1.0 - ((2.0 * jnp.arange(SUB, dtype=f32) + 1.0 - SUB) / SUB) ** 2
    taper = taper_line[:, None] * taper_line[None, :] / math.sqrt(vis_count)
    sky_angle = pixel * field_view / SUB
    radius_sq = sky_angle[:, None] ** 2 + sky_angle[None, :] ** 2
    turns = shift[:, None] * (jnp.arange(SUB, dtype=jnp.int32) - HALF)[None, :] % SUB
    angle = (
        -math.pi * screen_depth[:, None, None] * radius_sq
        + (2.0 * math.pi / SUB * turns.astype(f32))[:, :, None]
    )
    return jnp.concatenate([jnp.cos(angle) * taper, jnp.sin(angle) * taper], axis=2)


def on_device(
    visibilities, baseline_offsets, channel_scale, screen_depth, stations, corners, beam_terms
):
    au_count = lax.axis_size("au")
    vert_count = lax.axis_size("vert")
    au_index, vert_index = lax.axis_index("au"), lax.axis_index("vert")
    image_rows = G // (au_count * vert_count)
    vis_count = visibilities.shape[2]
    both = ("au", "vert")
    table = lax.all_gather(packed_beams(beam_terms), both, axis=0, tiled=True)
    corners_all = lax.all_gather(corners, both, axis=0, tiled=True)
    factor = pixel_factor(screen_depth, corners[:, 0] % SUB, vis_count)
    sky = sky_sums(visibilities, base_turns(baseline_offsets, channel_scale), factor)
    uv_own = corrected_subgrids(stations, table, sky)
    uv_all = lax.all_gather(uv_own, both, axis=0, tiled=True)
    gridded = uv_tile(uv_all, corners_all, au_index, vert_index, au_count, vert_count)
    first_row = (au_index * vert_count + vert_index) * image_rows
    dirty_image = image_rows_of(uv_all, corners_all, first_row, image_rows)
    return (gridded, dirty_image)


def solution(mesh):
    return jax.shard_map(
        on_device,
        mesh=mesh,
        in_specs=(
            P(("au", "vert"), None, None),
            P(("au", "vert"), None, None),
            P(),
            P(("au", "vert")),
            P(("au", "vert"), None),
            P(("au", "vert"), None),
            P(("au", "vert"), None, None),
        ),
        out_specs=(P("au", None, "vert"), P(("au", "vert"), None, None)),
        check_vma=False,
    )
```

```python
import functools
import math

import jax
import jax.numpy as jnp
from jax import lax
from jax.experimental import pallas as pl
from jax.experimental.pallas import tpu as pltpu
from jax.sharding import PartitionSpec as P

G = 8192
SUB = 32
HALF = SUB // 2
PACK = 4 * SUB
LANES = 128
FINE = G // SUB
CHUNK = 768
MASK_VALUES = 1 << 22
field_view = 0.1
bf16 = jnp.bfloat16
f32 = jnp.float32
VMEM_BYTES = 58 * 1024 * 1024


def cmul(a, b):
    return (a[0] * b[0] - a[1] * b[1], a[0] * b[1] + a[1] * b[0])


def conj(a):
    return (a[0], -a[1])


def sky_kernel(vis_ref, trig_ref, factor_ref, out_ref, left_ref, right_ref):
    vis_count = vis_ref.shape[2]
    step = math.gcd(vis_count, 256)
    row = lax.broadcasted_iota(jnp.int32, (8, step), 0)
    bits = [(row >> bit) % 2 == 1 for bit in range(3)]

    def powers(c, s, extra):
        z = (jnp.broadcast_to(c, (8, step)), jnp.broadcast_to(s, (8, step)))
        low = (jnp.where(bits[0], z[0], 1.0), jnp.where(bits[0], z[1], 0.0))
        power = z
        for bit in (1, 2):
            power = (power[0] * power[0] - power[1] * power[1], 2.0 * power[0] * power[1])
            more = cmul(low, power)
            low = (jnp.where(bits[bit], more[0], low[0]), jnp.where(bits[bit], more[1], low[1]))
        eight = (power[0] * power[0] - power[1] * power[1], 2.0 * power[0] * power[1])
        sixteen = (eight[0] * eight[0] - eight[1] * eight[1], 2.0 * eight[0] * eight[1])
        if extra is not None:
            low = cmul(low, extra)
        blocks = [cmul(low, conj(sixteen)), cmul(low, conj(eight)), low, cmul(low, eight)]
        return [
            jnp.concatenate([blocks[2 * h][part], blocks[2 * h + 1][part]], axis=0).astype(bf16)
            for part in range(2)
            for h in range(2)
        ]

    for start in range(0, vis_count, step):
        at = pl.ds(start, step)
        vis = tuple(
            jnp.broadcast_to(vis_ref[0, part : part + 1, at].astype(f32), (8, step))
            for part in range(2)
        )
        for place, piece in enumerate(powers(trig_ref[0, 0:1, at], trig_ref[0, 1:2, at], vis)):
            left_ref[HALF * place : HALF * (place + 1), at] = piece
        for place, piece in enumerate(powers(trig_ref[0, 2:3, at], trig_ref[0, 3:4, at], None)):
            right_ref[HALF * place : HALF * (place + 1), at] = piece
    both = lax.dot_general(
        left_ref[...], right_ref[...], (((1,), (1,)), ((), ())), preferred_element_type=f32
    )
    sky = (
        both[:SUB, :SUB] - both[SUB:, SUB:],
        both[:SUB, SUB:] + both[SUB:, :SUB],
    )
    done = cmul(sky, (factor_ref[0, :, :SUB], factor_ref[0, :, SUB:]))
    out_ref[0] = jnp.concatenate(
        [done[0][:HALF], done[1][:HALF], done[0][HALF:], done[1][HALF:]], axis=1
    )


def sky_sums(visibilities, trig, factor, interpret=False):
    count, _, vis_count = visibilities.shape
    return pl.pallas_call(
        sky_kernel,
        grid=(count,),
        in_specs=[
            pl.BlockSpec((1, 2, vis_count), lambda s: (s, 0, 0)),
            pl.BlockSpec((1, 4, vis_count), lambda s: (s, 0, 0)),
            pl.BlockSpec((1, SUB, 2 * SUB), lambda s: (s, 0, 0)),
        ],
        out_specs=pl.BlockSpec((1, HALF, PACK), lambda s: (s, 0, 0)),
        out_shape=jax.ShapeDtypeStruct((count, HALF, PACK), f32),
        scratch_shapes=[
            pltpu.VMEM((2 * SUB, vis_count), bf16),
            pltpu.VMEM((2 * SUB, vis_count), bf16),
        ],
        compiler_params=pltpu.CompilerParams(vmem_limit_bytes=VMEM_BYTES),
        cost_estimate=pl.CostEstimate(
            flops=count * 2 * 64 * 64 * vis_count, bytes_accessed=count * 40 * vis_count,
            transcendentals=0,
        ),
        name="sky_sums",
        interpret=interpret,
    )(visibilities, trig, factor)


def correct_kernel(stations_ref, table_ref, sky_ref, right_ref, left_ref, out_ref, mid_ref):
    count = sky_ref.shape[0]
    lane = lax.broadcasted_iota(jnp.int32, (HALF, PACK), 1)
    imag = (lane // SUB) % 2 == 1
    sign = jnp.where(imag, 1.0, -1.0)

    def up(x):
        return pltpu.roll(x, SUB, 1)

    def down(x):
        return pltpu.roll(x, PACK - SUB, 1)

    for s in range(count):
        first = table_ref[stations_ref[2 * s]].astype(f32)
        second = table_ref[stations_ref[2 * s + 1]].astype(f32)
        second_up, second_down = up(second), down(second)
        first_swap = jnp.where(imag, up(first), down(first))
        pair = first * jnp.where(imag, second_up, second) - sign * first_swap * jnp.where(
            imag, second, second_down
        )
        pair_up, pair_down = up(pair), down(pair)
        sky = sky_ref[s]
        sky_swap = jnp.where(imag, up(sky), down(sky))
        corrected = sky * jnp.where(imag, pair_up, pair) + sign * sky_swap * jnp.where(
            imag, pair, pair_down
        )
        mid_ref[HALF * s : HALF * (s + 1), :] = corrected.astype(bf16)
    mid = jnp.dot(mid_ref[...], right_ref[...], preferred_element_type=f32).astype(bf16)
    for s in range(count):
        rows = mid[HALF * s : HALF * (s + 1)]
        tall = jnp.concatenate([rows[:, : 2 * SUB], rows[:, 2 * SUB :]], axis=0)
        four = jnp.dot(left_ref[...], tall, preferred_element_type=f32)
        real = four[:SUB, :SUB] - four[SUB:, SUB:]
        image = four[:SUB, SUB:] + four[SUB:, :SUB]
        out_ref[s] = jnp.concatenate(
            [real[:HALF], image[:HALF], real[HALF:], image[HALF:]], axis=1
        ).astype(bf16)


def corrected_subgrids(stations, table, sky, interpret=False):
    count = sky.shape[0]
    centred = jnp.arange(SUB, dtype=jnp.int32) - HALF
    index = jnp.arange(SUB, dtype=jnp.int32)
    angle = 2.0 * math.pi / SUB * (centred[:, None] * centred[None, :] % SUB).astype(f32)
    cols_re, cols_im = jnp.cos(angle) / SUB, -jnp.sin(angle) / SUB
    block = jnp.concatenate(
        [
            jnp.concatenate([cols_re.T, cols_im.T], axis=1),
            jnp.concatenate([-cols_im.T, cols_re.T], axis=1),
        ],
        axis=0,
    )
    right = jnp.kron(jnp.eye(2, dtype=f32), block).astype(bf16)
    angle = 2.0 * math.pi / SUB * ((index - HALF)[:, None] * centred[None, :] % SUB).astype(f32)
    left = jnp.concatenate([jnp.cos(angle) / SUB, -jnp.sin(angle) / SUB], axis=0).astype(bf16)
    return pl.pallas_call(
        correct_kernel,
        grid_spec=pltpu.PrefetchScalarGridSpec(
            num_scalar_prefetch=1,
            grid=(1,),
            in_specs=[
                pl.BlockSpec(table.shape, lambda i, *_: (0, 0, 0)),
                pl.BlockSpec(sky.shape, lambda i, *_: (0, 0, 0)),
                pl.BlockSpec(right.shape, lambda i, *_: (0, 0)),
                pl.BlockSpec(left.shape, lambda i, *_: (0, 0)),
            ],
            out_specs=pl.BlockSpec((count, HALF, PACK), lambda i, *_: (0, 0, 0)),
            scratch_shapes=[pltpu.VMEM((HALF * count, PACK), bf16)],
        ),
        out_shape=jax.ShapeDtypeStruct((count, HALF, PACK), bf16),
        compiler_params=pltpu.CompilerParams(vmem_limit_bytes=VMEM_BYTES),
        name="correct",
        interpret=interpret,
    )(stations.reshape(-1), table, sky, right, left)


def add_subgrids(uv_ref, row_ref, col_ref, total_ref, count, lanes):
    lane = lax.broadcasted_iota(jnp.int32, (8, LANES), 1)
    row = lax.broadcasted_iota(jnp.int32, (8, LANES), 0)

    def one(s, carry):
        row_at, col_at = row_ref[s], col_ref[s]

        @pl.when(col_at >= 0)
        def _():
            packed = uv_ref[pl.ds(pl.multiple_of(s * HALF, HALF), HALF), :].astype(f32)
            tile = col_at // LANES
            offset = col_at % LANES
            shift = row_at % SUB
            base = row_at - shift

            def place(over):
                inside = lane < offset + SUB - LANES
                if not over:
                    inside = (lane >= offset) & (lane < offset + SUB)
                for h in range(2):
                    for part in range(2):
                        from_lane = (2 * h + part) * SUB
                        moved = pltpu.roll(packed, lax.rem(offset - from_lane + LANES, LANES), 1)
                        for group in range(2):
                            values = moved[8 * group : 8 * (group + 1)]
                            first_row = HALF * h + 8 * group
                            late = row + first_row >= shift
                            for wrapped in range(2):
                                keep = jnp.logical_and(inside, late if wrapped == 0 else ~late)
                                start = (base + SUB * wrapped + first_row) * lanes
                                start = start + 2 * (tile + over) + part
                                at = pl.ds(start, 8, stride=lanes)
                                total_ref[at, :] = total_ref[at, :] + jnp.where(keep, values, 0.0)

            place(0)

            @pl.when(offset + SUB > LANES)
            def _():
                place(1)

        return carry

    lax.fori_loop(0, count, one, 0)


def tile_kernel(block_ref, row_ref, col_ref, uv_ref, out_ref, total_ref, sems, *, count, tile_rows, lanes):
    del block_ref
    rows_all = total_ref.shape[0]
    zero_rows = math.gcd(rows_all, 1024)

    def clear(i, carry):
        at = pl.ds(pl.multiple_of(i * zero_rows, zero_rows), zero_rows)
        total_ref[at, :] = jnp.zeros((zero_rows, LANES), f32)
        return carry

    lax.fori_loop(0, rows_all // zero_rows, clear, 0)
    add_subgrids(uv_ref, row_ref, col_ref, total_ref, count, lanes)
    pieces = sems.shape[0]
    size = tile_rows * lanes // pieces
    copies = [
        pltpu.make_async_copy(
            total_ref.at[pl.ds(i * size, size), :], out_ref.at[pl.ds(i * size, size), :], sems.at[i]
        )
        for i in range(pieces)
    ]
    for copy in copies:
        copy.start()
    for copy in copies:
        copy.wait()


def spill_kernel(block_ref, row_ref, col_ref, uv_ref, tile_ref, out_ref, total_ref, sem, *, count, lanes):
    del block_ref, tile_ref
    size = SUB * lanes
    kept = total_ref.at[pl.ds(size, size), :]
    copy = pltpu.make_async_copy(out_ref.at[pl.ds(0, size), :], kept, sem)
    copy.start()
    copy.wait()
    add_subgrids(uv_ref, row_ref, col_ref, total_ref, count, lanes)
    copy = pltpu.make_async_copy(kept, out_ref.at[pl.ds(0, size), :], sem)
    copy.start()
    copy.wait()


def column_places(columns, vert_index, tile_cols):
    col_at = columns - vert_index * tile_cols
    return jnp.where((col_at >= 0) & (col_at < tile_cols), col_at, -1)


def uv_tile_own(uv, block, corners, au_index, vert_index, au_count, vert_count, interpret=False):
    count = corners[0].shape[0]
    tile_rows, tile_cols = G // au_count, G // vert_count
    lanes = 2 * tile_cols // LANES
    row_at = corners[0] - au_index * tile_rows
    col_at = column_places(corners[1], vert_index, tile_cols)
    return pl.pallas_call(
        functools.partial(tile_kernel, count=count, tile_rows=tile_rows, lanes=lanes),
        grid_spec=pltpu.PrefetchScalarGridSpec(
            num_scalar_prefetch=3,
            grid=(1,),
            in_specs=[pl.BlockSpec((count * HALF, PACK), lambda i, block, *_: (block[0], 0))],
            out_specs=pl.BlockSpec(memory_space=pl.ANY),
            scratch_shapes=[
                pltpu.VMEM(((tile_rows + 2 * SUB) * lanes, LANES), f32),
                pltpu.SemaphoreType.DMA((4,)),
            ],
        ),
        out_shape=jax.ShapeDtypeStruct((tile_rows * lanes, LANES), f32),
        compiler_params=pltpu.CompilerParams(vmem_limit_bytes=VMEM_BYTES),
        cost_estimate=pl.CostEstimate(
            flops=0, bytes_accessed=10 * tile_rows * tile_cols, transcendentals=0
        ),
        name="uv_tile",
        interpret=interpret,
    )(block.reshape(1), row_at, col_at, uv.reshape(-1, PACK))


def uv_tile_spill(tile, uv, block, corners, au_index, vert_index, au_count, vert_count, interpret=False):
    count = corners[0].shape[0]
    tile_rows, tile_cols = G // au_count, G // vert_count
    lanes = 2 * tile_cols // LANES
    row_at = (corners[0] - au_index * tile_rows + SUB + G) % G
    col_at = jnp.where(row_at < SUB, column_places(corners[1], vert_index, tile_cols), -1)
    result = pl.pallas_call(
        functools.partial(spill_kernel, count=count, lanes=lanes),
        grid_spec=pltpu.PrefetchScalarGridSpec(
            num_scalar_prefetch=3,
            grid=(1,),
            in_specs=[
                pl.BlockSpec((count * HALF, PACK), lambda i, block, *_: (block[0], 0)),
                pl.BlockSpec(memory_space=pl.ANY),
            ],
            out_specs=pl.BlockSpec(memory_space=pl.ANY),
            scratch_shapes=[
                pltpu.VMEM((3 * SUB * lanes, LANES), f32),
                pltpu.SemaphoreType.DMA(()),
            ],
        ),
        out_shape=jax.ShapeDtypeStruct(tile.shape, f32),
        input_output_aliases={4: 0},
        compiler_params=pltpu.CompilerParams(vmem_limit_bytes=VMEM_BYTES),
        cost_estimate=pl.CostEstimate(flops=0, bytes_accessed=8_000_000, transcendentals=0),
        name="uv_spill",
        interpret=interpret,
    )(block.reshape(1), row_at, col_at, uv.reshape(-1, PACK), tile)
    result = result.reshape(tile_rows, tile_cols // LANES, 2, LANES)
    return jnp.transpose(result, (0, 2, 1, 3)).reshape(tile_rows, 2, tile_cols)


def short_transform(values):
    count = len(values)
    if count == 1:
        return values
    even = short_transform(values[0::2])
    odd = short_transform(values[1::2])
    low, high = [], []
    for k in range(count // 2):
        re, im = odd[k]
        if k == 0:
            turned = (re, im)
        elif 4 * k == count:
            turned = (-im, re)
        elif 8 * k == count:
            root = math.sqrt(0.5)
            turned = ((re - im) * root, (re + im) * root)
        elif 8 * k == 3 * count:
            root = math.sqrt(0.5)
            turned = ((re + im) * -root, (re - im) * root)
        else:
            c, s = math.cos(2 * math.pi * k / count), math.sin(2 * math.pi * k / count)
            turned = (re * c - im * s, re * s + im * c)
        low.append((even[k][0] + turned[0], even[k][1] + turned[1]))
        high.append((even[k][0] - turned[0], even[k][1] - turned[1]))
    return low + high


def image_kernel(
    uv_ref, corner_ref, phase_ref, columns_ref, unit_ref, count_ref, twist_ref,
    out_ref, uv_wide, here, after, shifts, total, *, chunks, row_block
):
    step = pl.program_id(0)
    size = uv_ref.shape[0] // HALF
    image_rows = phase_ref.shape[1]

    @pl.when(step < chunks * HALF)
    def _():
        pair = lax.rem(step, HALF)
        chunk = step // HALF

        @pl.when(pair == 0)
        def _():
            uv_wide[...] = uv_ref[...].astype(f32)
            corner = corner_ref[...]
            coarse, shift = corner // SUB, corner % SUB

            def looked_up(index, length, table):
                place = lax.broadcasted_iota(jnp.int32, (length, size), 0)
                one = (place == index).astype(f32).astype(bf16)
                return lax.dot_general(
                    one, table, (((0,), (0,)), ((), ())), preferred_element_type=f32
                )

            here[...] = looked_up(coarse, FINE, unit_ref[...]).astype(bf16)
            after[...] = looked_up(lax.rem(coarse + 1, FINE), FINE, unit_ref[...]).astype(bf16)
            shifts[...] = looked_up(shift, SUB, count_ref[...])

        rows = uv_wide[pl.ds(pair, size, stride=HALF), :].astype(bf16)
        spread = lax.dot_general(
            columns_ref[...], rows, (((1,), (1,)), ((), ())), preferred_element_type=f32
        )
        for h in range(2):
            index = pair + HALF * h
            start = 2 * image_rows * h
            part = (spread[start : start + image_rows], spread[start + image_rows : start + 2 * image_rows])
            turned = cmul(part, (phase_ref[0], phase_ref[1]))
            left = jnp.concatenate([turned[0].astype(bf16), turned[1].astype(bf16)], axis=1)
            late = shifts[:, :1] > index.astype(f32)
            table = jnp.where(late, after[...], here[...])
            right = jnp.concatenate(
                [table, jnp.concatenate([-table[:, FINE:], table[:, :FINE]], axis=1)], axis=0
            )
            sums = jnp.dot(left, right, preferred_element_type=f32)
            twist = twist_ref[pl.ds(index, 1), :]
            done = cmul((sums[:, :FINE], sums[:, FINE:]), (twist[:, :FINE], twist[:, FINE:]))

            if chunks == 1:
                total[index, 0] = done[0]
                total[index, 1] = done[1]
            else:
                @pl.when(chunk == 0)
                def _():
                    total[index, 0] = done[0]
                    total[index, 1] = done[1]

                @pl.when(chunk > 0)
                def _():
                    total[index, 0] += done[0]
                    total[index, 1] += done[1]

    @pl.when(step >= chunks * HALF)
    def _():
        first = (step - chunks * HALF) * row_block
        wide = 2 * G // LANES

        def eight_rows(group, carry):
            at = pl.ds(pl.multiple_of(first + 8 * group, 8), 8)
            for tile in range(FINE // LANES):
                lanes = pl.ds(tile * LANES, LANES)
                values = [(total[n, 0, at, lanes], total[n, 1, at, lanes]) for n in range(SUB)]
                for k, value in enumerate(short_transform(values)):
                    for part in range(2):
                        column = 2 * (k * (FINE // LANES) + tile) + part
                        out_ref[pl.ds(group * 8 * wide + column, 8, stride=wide), :] = value[part]
            return carry

        lax.fori_loop(0, row_block // 8, eight_rows, 0)


def image_rows_of(uv_all, corners_all, first_row, image_rows, interpret=False):
    total = uv_all.shape[0]
    size = math.gcd(total, CHUNK)
    chunks = total // size
    row_block = math.gcd(image_rows, 32)
    outs = image_rows // row_block
    wide = 2 * G // LANES
    rows = first_row + jnp.arange(image_rows, dtype=jnp.int32)
    turn = 2.0 * math.pi / G
    angle = turn * (rows[:, None] * corners_all[1][None, :] % G).astype(f32)
    phase = jnp.stack([jnp.cos(angle), jnp.sin(angle)])
    angle = turn * (rows[:, None] * jnp.arange(SUB, dtype=jnp.int32)[None, :] % G).astype(f32)
    re, im = jnp.cos(angle), jnp.sin(angle)
    block = jnp.concatenate(
        [jnp.concatenate([re, -im], axis=1), jnp.concatenate([im, re], axis=1)], axis=0
    )
    columns = jnp.kron(jnp.eye(2, dtype=f32), block).astype(bf16)
    fine = jnp.arange(FINE, dtype=jnp.int32)
    angle = 2.0 * math.pi / FINE * (fine[:, None] * fine[None, :] % FINE).astype(f32)
    unit = jnp.concatenate([jnp.cos(angle), jnp.sin(angle)], axis=1).astype(bf16)
    angle = turn * (jnp.arange(SUB, dtype=jnp.int32)[:, None] * fine[None, :]).astype(f32)
    scale = 1.0 / (SUB * math.sqrt(total))
    twist = jnp.concatenate([jnp.cos(angle), jnp.sin(angle)], axis=1) * scale
    counts = jnp.broadcast_to(jnp.arange(SUB, dtype=f32)[:, None], (SUB, LANES)).astype(bf16)
    last = chunks - 1

    def chunk_of(i):
        return jnp.minimum(i // HALF, last)

    result = pl.pallas_call(
        functools.partial(image_kernel, chunks=chunks, row_block=row_block),
        grid=(chunks * HALF + outs,),
        in_specs=[
            pl.BlockSpec((size * HALF, PACK), lambda i: (chunk_of(i), 0)),
            pl.BlockSpec((1, size), lambda i: (0, chunk_of(i))),
            pl.BlockSpec((2, image_rows, size), lambda i: (0, 0, chunk_of(i))),
            pl.BlockSpec(columns.shape, lambda i: (0, 0)),
            pl.BlockSpec(unit.shape, lambda i: (0, 0)),
            pl.BlockSpec(counts.shape, lambda i: (0, 0)),
            pl.BlockSpec(twist.shape, lambda i: (0, 0)),
        ],
        out_specs=pl.BlockSpec(
            (row_block * wide, LANES), lambda i: (jnp.maximum(i - chunks * HALF, 0), 0)
        ),
        out_shape=jax.ShapeDtypeStruct((image_rows * wide, LANES), f32),
        scratch_shapes=[
            pltpu.VMEM((size * HALF, PACK), f32),
            pltpu.VMEM((size, 2 * FINE), bf16),
            pltpu.VMEM((size, 2 * FINE), bf16),
            pltpu.VMEM((size, LANES), f32),
            pltpu.VMEM((SUB, 2, image_rows, FINE), f32),
        ],
        compiler_params=pltpu.CompilerParams(vmem_limit_bytes=VMEM_BYTES),
        name="image",
        interpret=interpret,
    )(
        uv_all.reshape(total * HALF, PACK), corners_all[0].reshape(1, total),
        phase, columns, unit, counts, twist,
    )
    result = result.reshape(image_rows, G // LANES, 2, LANES)
    return jnp.transpose(result, (0, 2, 1, 3)).reshape(image_rows, 2, G)


def packed_beams(beam_terms):
    count = beam_terms.shape[0]
    parts = beam_terms.reshape(count, 2, 2, HALF, SUB)
    return jnp.transpose(parts, (0, 3, 2, 1, 4)).reshape(count, HALF, PACK)


def base_turns(baseline_offsets, channel_scale):
    count, _, times = baseline_offsets.shape
    shifts = (baseline_offsets[:, :, :, None] * channel_scale).reshape(count, 2, -1)
    angle = 2.0 * math.pi / SUB * shifts
    return jnp.stack([jnp.cos(angle), jnp.sin(angle)], axis=2).reshape(count, 4, -1)


def pixel_factor(screen_depth, shift, vis_count):
    pixel = jnp.arange(SUB, dtype=f32) - HALF
    taper_line = 1.0 - ((2.0 * jnp.arange(SUB, dtype=f32) + 1.0 - SUB) / SUB) ** 2
    taper = taper_line[:, None] * taper_line[None, :] / math.sqrt(vis_count)
    sky_angle = pixel * field_view / SUB
    radius_sq = sky_angle[:, None] ** 2 + sky_angle[None, :] ** 2
    turns = shift[:, None] * (jnp.arange(SUB, dtype=jnp.int32) - HALF)[None, :] % SUB
    angle = (
        -math.pi * screen_depth[:, None, None] * radius_sq
        + (2.0 * math.pi / SUB * turns.astype(f32))[:, :, None]
    )
    return jnp.concatenate([jnp.cos(angle) * taper, jnp.sin(angle) * taper], axis=2)


def from_partner(value, axis, mask):
    count = lax.axis_size(axis)
    return lax.ppermute(value, axis, [(i, i ^ mask) for i in range(count)])


def gathered(own, by_mask):
    if not by_mask:
        return [lax.all_gather(own, ("au", "vert"), axis=0, tiled=True)]
    au_count, vert_count = lax.axis_size("au"), lax.axis_size("vert")
    line = [own] + [from_partner(own, "vert", 2 * mask) for mask in range(1, vert_count // 2)]
    line = jnp.concatenate(line, axis=0)
    lines = [line] + [from_partner(line, "au", mask) for mask in range(1, au_count)]
    return [
        jnp.concatenate([piece, from_partner(piece, "vert", 1)], axis=0) for piece in lines
    ]


def gathered_place(owner, by_mask):
    if not by_mask:
        return owner
    vert_count = lax.axis_size("vert")
    au_mask = (owner // vert_count) ^ lax.axis_index("au")
    vert_mask = (owner % vert_count) ^ lax.axis_index("vert")
    return au_mask * vert_count + vert_mask % 2 * (vert_count // 2) + vert_mask // 2


def coded_corners(corners):
    digits = jnp.stack([corners[:, 0] // 128, corners[:, 0] % 128, corners[:, 1] // 128, corners[:, 1] % 128])
    flat = digits.astype(f32).astype(bf16).reshape(-1)
    return jnp.pad(flat, (0, HALF * PACK - flat.shape[0])).reshape(1, HALF, PACK)


def decoded_corners(blocks, count):
    digits = blocks.reshape(blocks.shape[0], HALF * PACK).astype(jnp.int32)
    high_row, low_row, high_col, low_col = [
        digits[:, i * count : (i + 1) * count].reshape(-1) for i in range(4)
    ]
    return (high_row * 128 + low_row, high_col * 128 + low_col)


def on_device(
    visibilities, baseline_offsets, channel_scale, screen_depth, stations, corners, beam_terms
):
    au_count = lax.axis_size("au")
    vert_count = lax.axis_size("vert")
    au_index, vert_index = lax.axis_index("au"), lax.axis_index("vert")
    image_rows = G // (au_count * vert_count)
    count, _, vis_count = visibilities.shape
    own_stations = beam_terms.shape[0]
    sent = jnp.concatenate([packed_beams(beam_terms), coded_corners(corners)], axis=0)
    held = au_count * vert_count * count * HALF * PACK
    by_mask = held <= MASK_VALUES
    table = jnp.concatenate(gathered(sent, by_mask), axis=0)
    blocks = table.reshape(au_count * vert_count, own_stations + 1, HALF, PACK)
    corners_all = decoded_corners(blocks[:, own_stations], count)
    owners = stations // own_stations
    station_rows = gathered_place(owners, by_mask) * (own_stations + 1) + stations % own_stations

    factor = pixel_factor(screen_depth, corners[:, 0] % SUB, vis_count)
    trig = base_turns(baseline_offsets, channel_scale)
    part = math.gcd(count, 8)
    sky = jnp.concatenate(
        [
            sky_sums(visibilities[s : s + part], trig[s : s + part], factor[s : s + part])
            for s in range(0, count, part)
        ],
        axis=0,
    )
    uv_own = corrected_subgrids(station_rows, table, sky)
    uv_rows = gathered(uv_own, by_mask)
    per_row = vert_count * count
    where = (au_index, vert_index, au_count, vert_count)

    def row_place(index):
        return gathered_place(index * vert_count + vert_index, by_mask) // vert_count

    def corners_of(place):
        return [lax.dynamic_slice_in_dim(x, place * per_row, per_row) for x in corners_all]

    own_place = row_place(au_index)
    tile = uv_tile_own(uv_rows[0], own_place, corners_of(own_place), *where)
    uv_all = jnp.concatenate(uv_rows, axis=0)
    place = row_place(lax.rem(au_index + au_count - 1, au_count))
    gridded = uv_tile_spill(tile, uv_all, place, corners_of(place), *where)
    first_row = (au_index * vert_count + vert_index) * image_rows
    dirty_image = image_rows_of(uv_all, corners_all, first_row, image_rows)
    return (gridded, dirty_image)


def solution(mesh):
    return jax.shard_map(
        on_device,
        mesh=mesh,
        in_specs=(
            P(("au", "vert"), None, None),
            P(("au", "vert"), None, None),
            P(),
            P(("au", "vert")),
            P(("au", "vert"), None),
            P(("au", "vert"), None),
            P(("au", "vert"), None, None),
        ),
        out_specs=(P("au", None, "vert"), P(("au", "vert"), None, None)),
        check_vma=False,
    )
```

```python
import functools
import math

import jax
import jax.numpy as jnp
from jax import lax
from jax.experimental import pallas as pl
from jax.experimental.pallas import tpu as pltpu
from jax.sharding import PartitionSpec as P

G = 8192
SUB = 32
HALF = SUB // 2
PACK = 4 * SUB
LANES = 128
FINE = G // SUB
CHUNK = 768
MASK_VALUES = 1 << 22
field_view = 0.1
bf16 = jnp.bfloat16
f32 = jnp.float32
VMEM_BYTES = 58 * 1024 * 1024


def cmul(a, b):
    return (a[0] * b[0] - a[1] * b[1], a[0] * b[1] + a[1] * b[0])


def conj(a):
    return (a[0], -a[1])


def sky_kernel(vis_ref, offset_ref, scale_ref, out_ref, cos_ref, sin_ref):
    count, _, vis_count = vis_ref.shape
    times = offset_ref.shape[1]
    step = math.gcd(vis_count, 256)
    row = lax.broadcasted_iota(jnp.int32, (8, step), 0)
    bits = [(row >> bit) % 2 == 1 for bit in range(3)]

    offsets = offset_ref[...]
    parts = []
    for _ in range(3):
        parts.append(offsets.astype(bf16))
        offsets = offsets - parts[-1].astype(f32)
    for start in range(0, vis_count, 512):
        width = min(512, vis_count - start)
        at = pl.ds(start, width)
        time = lax.broadcasted_iota(jnp.int32, (times, width), 0)
        place = lax.broadcasted_iota(jnp.int32, (times, width), 1) + start
        one = (place // (vis_count // times) == time).astype(f32).astype(bf16)
        shifts = sum(jnp.dot(part, one, preferred_element_type=f32) for part in parts)
        half = (math.pi / SUB) * (shifts * scale_ref[:, at])
        square = half * half
        sine, cosine = 1.0, 1.0
        for term in (12, 10, 8, 6, 4, 2):
            sine = 1.0 - square * (1.0 / (term * (term + 1))) * sine
            cosine = 1.0 - square * (1.0 / (term * (term - 1))) * cosine
        sine = sine * half
        cos_ref[:, at] = 1.0 - 2.0 * sine * sine
        sin_ref[:, at] = 2.0 * sine * cosine

    def powers(c, s, extra):
        z = (jnp.broadcast_to(c, (8, step)), jnp.broadcast_to(s, (8, step)))
        low = (jnp.where(bits[0], z[0], 1.0), jnp.where(bits[0], z[1], 0.0))
        power = z
        for bit in (1, 2):
            power = (power[0] * power[0] - power[1] * power[1], 2.0 * power[0] * power[1])
            more = cmul(low, power)
            low = (jnp.where(bits[bit], more[0], low[0]), jnp.where(bits[bit], more[1], low[1]))
        eight = (power[0] * power[0] - power[1] * power[1], 2.0 * power[0] * power[1])
        sixteen = (eight[0] * eight[0] - eight[1] * eight[1], 2.0 * eight[0] * eight[1])
        if extra is not None:
            low = cmul(low, extra)
        blocks = [cmul(low, conj(sixteen)), cmul(low, conj(eight)), low, cmul(low, eight)]
        return jnp.concatenate([block[part] for part in range(2) for block in blocks], axis=0).astype(bf16)

    def one_subgrid(s):
        both = jnp.zeros((2 * SUB, 2 * SUB), f32)
        for start in range(0, vis_count, step):
            at = pl.ds(start, step)
            vis = tuple(
                jnp.broadcast_to(vis_ref[s, part : part + 1, at].astype(f32), (8, step))
                for part in range(2)
            )
            u_row, v_row = pl.ds(2 * s, 1), pl.ds(2 * s + 1, 1)
            left = powers(cos_ref[u_row, at], sin_ref[u_row, at], vis)
            right = powers(cos_ref[v_row, at], sin_ref[v_row, at], None)
            both += lax.dot_general(
                left, right, (((1,), (1,)), ((), ())), preferred_element_type=f32
            )
        real = both[:SUB, :SUB] - both[SUB:, SUB:]
        image = both[:SUB, SUB:] + both[SUB:, :SUB]
        out_ref[s] = jnp.concatenate(
            [real[:HALF], image[:HALF], real[HALF:], image[HALF:]], axis=1
        )

    def some(i, carry):
        for k in range(math.gcd(count, 2)):
            one_subgrid(i * math.gcd(count, 2) + k)
        return carry

    lax.fori_loop(0, count // math.gcd(count, 2), some, 0)


def sky_sums(visibilities, offsets, scale_row, first, count, interpret=False):
    vis_count = visibilities.shape[2]
    times = offsets.shape[1]
    at = first // count
    return pl.pallas_call(
        sky_kernel,
        grid=(1,),
        in_specs=[
            pl.BlockSpec((count, 2, vis_count), lambda i: (at, 0, 0)),
            pl.BlockSpec((2 * count, times), lambda i: (at, 0)),
            pl.BlockSpec((1, vis_count), lambda i: (0, 0)),
        ],
        out_specs=pl.BlockSpec((count, HALF, PACK), lambda i: (0, 0, 0)),
        out_shape=jax.ShapeDtypeStruct((count, HALF, PACK), f32),
        scratch_shapes=[pltpu.VMEM((2 * count, vis_count), f32)] * 2,
        compiler_params=pltpu.CompilerParams(vmem_limit_bytes=VMEM_BYTES),
        cost_estimate=pl.CostEstimate(
            flops=0, bytes_accessed=count * 2_500_000, transcendentals=0
        ),
        name="sky_sums",
        interpret=interpret,
    )(visibilities, offsets, scale_row)


def correct_kernel(stations_ref, *refs, pieces, skies):
    table_refs, refs = refs[:pieces], refs[pieces:]
    sky_refs, refs = refs[:skies], refs[skies:]
    factor_ref, right_ref, left_ref, out_ref, table_ref, mid_ref = refs
    count = factor_ref.shape[0]
    lane = lax.broadcasted_iota(jnp.int32, (HALF, PACK), 1)
    imag = (lane // SUB) % 2 == 1
    sign = jnp.where(imag, 1.0, -1.0)

    def up(x):
        return pltpu.roll(x, SUB, 1)

    def down(x):
        return pltpu.roll(x, PACK - SUB, 1)

    def product(a, b):
        swapped = jnp.where(imag, up(a), down(a))
        return a * jnp.where(imag, up(b), b) + sign * swapped * jnp.where(imag, b, down(b))

    held = 0
    for piece in table_refs:
        table_ref[held : held + piece.shape[0]] = piece[...]
        held += piece.shape[0]
    for s in range(count):
        first = table_ref[stations_ref[2 * s]].astype(f32)
        second = table_ref[stations_ref[2 * s + 1]].astype(f32)
        pair = product(first, -sign * second)
        per = count // skies
        sky = product(sky_refs[s // per][s % per], factor_ref[s])
        mid_ref[HALF * s : HALF * (s + 1), :] = product(sky, pair).astype(bf16)
    mid = jnp.dot(mid_ref[...], right_ref[...], preferred_element_type=f32).astype(bf16)
    for s in range(count):
        rows = mid[HALF * s : HALF * (s + 1)]
        tall = jnp.concatenate([rows[:, : 2 * SUB], rows[:, 2 * SUB :]], axis=0)
        four = jnp.dot(left_ref[...], tall, preferred_element_type=f32)
        real = four[:SUB, :SUB] - four[SUB:, SUB:]
        image = four[:SUB, SUB:] + four[SUB:, :SUB]
        out_ref[s] = jnp.concatenate(
            [real[:HALF], image[:HALF], real[HALF:], image[HALF:]], axis=1
        ).astype(bf16)


def corrected_subgrids(stations, tables, skies, factor, interpret=False):
    count = factor.shape[0]
    centred = jnp.arange(SUB, dtype=jnp.int32) - HALF
    index = jnp.arange(SUB, dtype=jnp.int32)
    angle = 2.0 * math.pi / SUB * (centred[:, None] * centred[None, :] % SUB).astype(f32)
    cols_re, cols_im = jnp.cos(angle) / SUB, -jnp.sin(angle) / SUB
    block = jnp.concatenate(
        [
            jnp.concatenate([cols_re.T, cols_im.T], axis=1),
            jnp.concatenate([-cols_im.T, cols_re.T], axis=1),
        ],
        axis=0,
    )
    right = jnp.kron(jnp.eye(2, dtype=f32), block).astype(bf16)
    angle = 2.0 * math.pi / SUB * ((index - HALF)[:, None] * centred[None, :] % SUB).astype(f32)
    left = jnp.concatenate([jnp.cos(angle) / SUB, -jnp.sin(angle) / SUB], axis=0).astype(bf16)
    rows = sum(piece.shape[0] for piece in tables)
    operands = [*tables, *skies, factor, right, left]

    def whole(operand):
        return pl.BlockSpec(operand.shape, lambda i, *_: (0,) * operand.ndim)

    return pl.pallas_call(
        functools.partial(correct_kernel, pieces=len(tables), skies=len(skies)),
        grid_spec=pltpu.PrefetchScalarGridSpec(
            num_scalar_prefetch=1,
            grid=(1,),
            in_specs=[whole(operand) for operand in operands],
            out_specs=pl.BlockSpec((count, HALF, PACK), lambda i, *_: (0, 0, 0)),
            scratch_shapes=[
                pltpu.VMEM((rows, HALF, PACK), bf16),
                pltpu.VMEM((HALF * count, PACK), bf16),
            ],
        ),
        out_shape=jax.ShapeDtypeStruct((count, HALF, PACK), bf16),
        compiler_params=pltpu.CompilerParams(vmem_limit_bytes=VMEM_BYTES),
        cost_estimate=pl.CostEstimate(flops=0, bytes_accessed=16_000_000, transcendentals=0),
        name="correct",
        interpret=interpret,
    )(stations.reshape(-1), *operands)


def add_subgrids(uv_refs, list_ref, row_ref, col_ref, held_ref, total_ref, lanes):
    first = 0
    for piece in uv_refs:
        held_ref[first : first + piece.shape[0]] = piece[...]
        first += piece.shape[0]
    lane = lax.broadcasted_iota(jnp.int32, (8, LANES), 1)
    row = lax.broadcasted_iota(jnp.int32, (8, LANES), 0)

    def one(entry, carry):
        s = list_ref[entry + 1]
        row_at, col_at = row_ref[s], col_ref[s]
        packed = held_ref[pl.ds(pl.multiple_of(s * HALF, HALF), HALF), :].astype(f32)
        tile = col_at // LANES
        offset = col_at % LANES
        shift = row_at % SUB
        base = row_at - shift

        def place(over):
            inside = lane < offset + SUB - LANES
            if not over:
                inside = (lane >= offset) & (lane < offset + SUB)
            for h in range(2):
                for part in range(2):
                    from_lane = (2 * h + part) * SUB
                    moved = pltpu.roll(packed, lax.rem(offset - from_lane + LANES, LANES), 1)
                    for group in range(2):
                        values = moved[8 * group : 8 * (group + 1)]
                        first_row = HALF * h + 8 * group
                        late = row + first_row >= shift
                        for wrapped in range(2):
                            keep = jnp.logical_and(inside, late if wrapped == 0 else ~late)
                            start = (base + SUB * wrapped + first_row) * lanes
                            start = start + 2 * (tile + over) + part
                            at = pl.ds(start, 8, stride=lanes)
                            total_ref[at, :] = total_ref[at, :] + jnp.where(keep, values, 0.0)

        place(0)

        @pl.when(offset + SUB > LANES)
        def _():
            place(1)

        return carry

    lax.fori_loop(0, list_ref[0], one, 0)


def tile_kernel(block_ref, list_ref, row_ref, col_ref, *refs, pieces, tile_rows, lanes):
    del block_ref
    uv_refs = refs[:pieces]
    out_ref, held_ref, total_ref, sems = refs[pieces:]
    rows_all = total_ref.shape[0]
    zero_rows = math.gcd(rows_all, 1024)

    def clear(i, carry):
        at = pl.ds(pl.multiple_of(i * zero_rows, zero_rows), zero_rows)
        total_ref[at, :] = jnp.zeros((zero_rows, LANES), f32)
        return carry

    lax.fori_loop(0, rows_all // zero_rows, clear, 0)
    add_subgrids(uv_refs, list_ref, row_ref, col_ref, held_ref, total_ref, lanes)
    pieces = sems.shape[0]
    size = tile_rows * lanes // pieces
    copies = [
        pltpu.make_async_copy(
            total_ref.at[pl.ds(i * size, size), :], out_ref.at[pl.ds(i * size, size), :], sems.at[i]
        )
        for i in range(pieces)
    ]
    for copy in copies:
        copy.start()
    for copy in copies:
        copy.wait()


def spill_kernel(block_ref, list_ref, row_ref, col_ref, *refs, pieces, lanes):
    del block_ref
    uv_refs = refs[:pieces]
    _, out_ref, held_ref, total_ref, sem = refs[pieces:]
    size = SUB * lanes
    kept = total_ref.at[pl.ds(size, size), :]
    copy = pltpu.make_async_copy(out_ref.at[pl.ds(0, size), :], kept, sem)
    copy.start()
    copy.wait()
    add_subgrids(uv_refs, list_ref, row_ref, col_ref, held_ref, total_ref, lanes)
    copy = pltpu.make_async_copy(kept, out_ref.at[pl.ds(0, size), :], sem)
    copy.start()
    copy.wait()


def listed(valid):
    count = valid.shape[0]
    index = jnp.arange(count, dtype=jnp.int32)
    before = jnp.sum((index[None, :] < index[:, None]) & valid[None, :], axis=1, dtype=jnp.int32)
    rank = jnp.where(valid, before, -1)
    entries = jnp.sum(
        jnp.where(rank[None, :] == index[:, None], index[None, :], 0), axis=1, dtype=jnp.int32
    )
    return jnp.concatenate([jnp.sum(valid, dtype=jnp.int32)[None], entries])


def tile_places(corners, au_index, vert_index, au_count, vert_count, spilled):
    tile_rows, tile_cols = G // au_count, G // vert_count
    col_at = corners[1] - vert_index * tile_cols
    valid = (col_at >= 0) & (col_at < tile_cols)
    row_at = corners[0] - au_index * tile_rows
    if spilled:
        row_at = (row_at + SUB + G) % G
        valid = valid & (row_at < SUB)
    return listed(valid), row_at, col_at


def uv_tile_own(uv, block, places, au_count, vert_count, interpret=False):
    count = places[1].shape[0]
    tile_rows, tile_cols = G // au_count, G // vert_count
    lanes = 2 * tile_cols // LANES
    rows = count * HALF // len(uv)
    return pl.pallas_call(
        functools.partial(tile_kernel, pieces=len(uv), tile_rows=tile_rows, lanes=lanes),
        grid_spec=pltpu.PrefetchScalarGridSpec(
            num_scalar_prefetch=4,
            grid=(1,),
            in_specs=[pl.BlockSpec((rows, PACK), lambda i, block, *_: (block[0], 0))] * len(uv),
            out_specs=pl.BlockSpec(memory_space=pl.ANY),
            scratch_shapes=[
                pltpu.VMEM((count * HALF, PACK), bf16),
                pltpu.VMEM(((tile_rows + 2 * SUB) * lanes, LANES), f32),
                pltpu.SemaphoreType.DMA((4,)),
            ],
        ),
        out_shape=jax.ShapeDtypeStruct((tile_rows * lanes, LANES), f32),
        compiler_params=pltpu.CompilerParams(vmem_limit_bytes=VMEM_BYTES),
        cost_estimate=pl.CostEstimate(
            flops=0, bytes_accessed=20 * tile_rows * tile_cols, transcendentals=0
        ),
        name="uv_tile",
        interpret=interpret,
    )(block.reshape(1), *places, *[piece.reshape(-1, PACK) for piece in uv])


def uv_tile_spill(tile, uv, block, places, au_count, vert_count, interpret=False):
    count = places[1].shape[0]
    tile_rows, tile_cols = G // au_count, G // vert_count
    lanes = 2 * tile_cols // LANES
    rows = count * HALF // len(uv)
    result = pl.pallas_call(
        functools.partial(spill_kernel, pieces=len(uv), lanes=lanes),
        grid_spec=pltpu.PrefetchScalarGridSpec(
            num_scalar_prefetch=4,
            grid=(1,),
            in_specs=[pl.BlockSpec((rows, PACK), lambda i, block, *_: (block[0], 0))] * len(uv)
            + [pl.BlockSpec(memory_space=pl.ANY)],
            out_specs=pl.BlockSpec(memory_space=pl.ANY),
            scratch_shapes=[
                pltpu.VMEM((count * HALF, PACK), bf16),
                pltpu.VMEM((3 * SUB * lanes, LANES), f32),
                pltpu.SemaphoreType.DMA(()),
            ],
        ),
        out_shape=jax.ShapeDtypeStruct(tile.shape, f32),
        input_output_aliases={4 + len(uv): 0},
        compiler_params=pltpu.CompilerParams(vmem_limit_bytes=VMEM_BYTES),
        cost_estimate=pl.CostEstimate(flops=0, bytes_accessed=8_000_000, transcendentals=0),
        name="uv_spill",
        interpret=interpret,
    )(block.reshape(1), *places, *[piece.reshape(-1, PACK) for piece in uv], tile)
    result = result.reshape(tile_rows, tile_cols // LANES, 2, LANES)
    return jnp.transpose(result, (0, 2, 1, 3)).reshape(tile_rows, 2, tile_cols)


def short_transform(values):
    count = len(values)
    if count == 1:
        return values
    even = short_transform(values[0::2])
    odd = short_transform(values[1::2])
    low, high = [], []
    for k in range(count // 2):
        re, im = odd[k]
        if k == 0:
            turned = (re, im)
        elif 4 * k == count:
            turned = (-im, re)
        elif 8 * k == count:
            root = math.sqrt(0.5)
            turned = ((re - im) * root, (re + im) * root)
        elif 8 * k == 3 * count:
            root = math.sqrt(0.5)
            turned = ((re + im) * -root, (re - im) * root)
        else:
            c, s = math.cos(2 * math.pi * k / count), math.sin(2 * math.pi * k / count)
            turned = (re * c - im * s, re * s + im * c)
        low.append((even[k][0] + turned[0], even[k][1] + turned[1]))
        high.append((even[k][0] - turned[0], even[k][1] - turned[1]))
    return low + high


def image_kernel(
    *refs, pieces, chunks, row_block
):
    uv_refs, refs = refs[:pieces], refs[pieces:]
    corner_ref, phase_ref, columns_ref, unit_ref, count_ref, twist_ref = refs[:6]
    out_ref, uv_wide, here, after, shifts, total = refs[6:]
    step = pl.program_id(0)
    size = uv_wide.shape[0] // HALF
    image_rows = phase_ref.shape[1]

    @pl.when(step < chunks * HALF)
    def _():
        pair = lax.rem(step, HALF)
        chunk = step // HALF

        @pl.when(pair == 0)
        def _():
            held = 0
            for piece in uv_refs:
                uv_wide[held : held + piece.shape[0]] = piece[...].astype(f32)
                held += piece.shape[0]
            corner = corner_ref[...]
            coarse, shift = corner // SUB, corner % SUB

            def looked_up(index, length, table):
                place = lax.broadcasted_iota(jnp.int32, (length, size), 0)
                one = (place == index).astype(f32).astype(bf16)
                return lax.dot_general(
                    one, table, (((0,), (0,)), ((), ())), preferred_element_type=f32
                )

            here[...] = looked_up(coarse, FINE, unit_ref[...]).astype(bf16)
            after[...] = looked_up(lax.rem(coarse + 1, FINE), FINE, unit_ref[...]).astype(bf16)
            shifts[...] = looked_up(shift, SUB, count_ref[...])

        rows = uv_wide[pl.ds(pair, size, stride=HALF), :].astype(bf16)
        spread = lax.dot_general(
            columns_ref[...], rows, (((1,), (1,)), ((), ())), preferred_element_type=f32
        )
        for h in range(2):
            index = pair + HALF * h
            start = 2 * image_rows * h
            part = (spread[start : start + image_rows], spread[start + image_rows : start + 2 * image_rows])
            turned = cmul(part, (phase_ref[0], phase_ref[1]))
            left = jnp.concatenate([turned[0].astype(bf16), turned[1].astype(bf16)], axis=1)
            late = shifts[:, :1] > index.astype(f32)
            table = jnp.where(late, after[...], here[...])
            right = jnp.concatenate(
                [table, jnp.concatenate([-table[:, FINE:], table[:, :FINE]], axis=1)], axis=0
            )
            sums = jnp.dot(left, right, preferred_element_type=f32)
            twist = twist_ref[pl.ds(index, 1), :]
            done = cmul((sums[:, :FINE], sums[:, FINE:]), (twist[:, :FINE], twist[:, FINE:]))

            if chunks == 1:
                total[index, 0] = done[0]
                total[index, 1] = done[1]
            else:
                @pl.when(chunk == 0)
                def _():
                    total[index, 0] = done[0]
                    total[index, 1] = done[1]

                @pl.when(chunk > 0)
                def _():
                    total[index, 0] += done[0]
                    total[index, 1] += done[1]

    @pl.when(step >= chunks * HALF)
    def _():
        first = (step - chunks * HALF) * row_block
        wide = 2 * G // LANES

        def eight_rows(group, carry):
            at = pl.ds(pl.multiple_of(first + 8 * group, 8), 8)
            for tile in range(FINE // LANES):
                lanes = pl.ds(tile * LANES, LANES)
                values = [(total[n, 0, at, lanes], total[n, 1, at, lanes]) for n in range(SUB)]
                for k, value in enumerate(short_transform(values)):
                    for part in range(2):
                        column = 2 * (k * (FINE // LANES) + tile) + part
                        out_ref[pl.ds(group * 8 * wide + column, 8, stride=wide), :] = value[part]
            return carry

        lax.fori_loop(0, row_block // 8, eight_rows, 0)


def image_rows_of(uv, corners_all, first_row, image_rows, interpret=False):
    total = corners_all[0].shape[0]
    size = math.gcd(total, CHUNK) if len(uv) == 1 else total
    chunks = total // size
    row_block = math.gcd(image_rows, 32)
    outs = image_rows // row_block
    wide = 2 * G // LANES
    rows = first_row + jnp.arange(image_rows, dtype=jnp.int32)
    turn = 2.0 * math.pi / G
    angle = turn * (rows[:, None] * corners_all[1][None, :] % G).astype(f32)
    phase = jnp.stack([jnp.cos(angle), jnp.sin(angle)])
    angle = turn * (rows[:, None] * jnp.arange(SUB, dtype=jnp.int32)[None, :] % G).astype(f32)
    re, im = jnp.cos(angle), jnp.sin(angle)
    block = jnp.concatenate(
        [jnp.concatenate([re, -im], axis=1), jnp.concatenate([im, re], axis=1)], axis=0
    )
    columns = jnp.kron(jnp.eye(2, dtype=f32), block).astype(bf16)
    fine = jnp.arange(FINE, dtype=jnp.int32)
    angle = 2.0 * math.pi / FINE * (fine[:, None] * fine[None, :] % FINE).astype(f32)
    unit = jnp.concatenate([jnp.cos(angle), jnp.sin(angle)], axis=1).astype(bf16)
    angle = turn * (jnp.arange(SUB, dtype=jnp.int32)[:, None] * fine[None, :]).astype(f32)
    scale = 1.0 / (SUB * math.sqrt(total))
    twist = jnp.concatenate([jnp.cos(angle), jnp.sin(angle)], axis=1) * scale
    counts = jnp.broadcast_to(jnp.arange(SUB, dtype=f32)[:, None], (SUB, LANES)).astype(bf16)
    last = chunks - 1

    def chunk_of(i):
        return jnp.minimum(i // HALF, last)

    result = pl.pallas_call(
        functools.partial(image_kernel, pieces=len(uv), chunks=chunks, row_block=row_block),
        grid=(chunks * HALF + outs,),
        in_specs=[
            *[pl.BlockSpec((size * HALF // len(uv), PACK), lambda i: (chunk_of(i), 0))] * len(uv),
            pl.BlockSpec((1, size), lambda i: (0, chunk_of(i))),
            pl.BlockSpec((2, image_rows, size), lambda i: (0, 0, chunk_of(i))),
            pl.BlockSpec(columns.shape, lambda i: (0, 0)),
            pl.BlockSpec(unit.shape, lambda i: (0, 0)),
            pl.BlockSpec(counts.shape, lambda i: (0, 0)),
            pl.BlockSpec(twist.shape, lambda i: (0, 0)),
        ],
        out_specs=pl.BlockSpec(
            (row_block * wide, LANES), lambda i: (jnp.maximum(i - chunks * HALF, 0), 0)
        ),
        out_shape=jax.ShapeDtypeStruct((image_rows * wide, LANES), f32),
        scratch_shapes=[
            pltpu.VMEM((size * HALF, PACK), f32),
            pltpu.VMEM((size, 2 * FINE), bf16),
            pltpu.VMEM((size, 2 * FINE), bf16),
            pltpu.VMEM((size, LANES), f32),
            pltpu.VMEM((SUB, 2, image_rows, FINE), f32),
        ],
        compiler_params=pltpu.CompilerParams(vmem_limit_bytes=VMEM_BYTES),
        name="image",
        interpret=interpret,
    )(
        *[piece.reshape(-1, PACK) for piece in uv], corners_all[0].reshape(1, total),
        phase, columns, unit, counts, twist,
    )
    result = result.reshape(image_rows, G // LANES, 2, LANES)
    return jnp.transpose(result, (0, 2, 1, 3)).reshape(image_rows, 2, G)


def packed_beams(beam_terms):
    count = beam_terms.shape[0]
    parts = beam_terms.reshape(count, 2, 2, HALF, SUB)
    return jnp.transpose(parts, (0, 3, 2, 1, 4)).reshape(count, HALF, PACK)


def pixel_factor(screen_depth, shift, vis_count):
    lane = jnp.arange(PACK, dtype=jnp.int32)
    col = lane % SUB
    imag = (lane // SUB) % 2
    row = jnp.arange(HALF, dtype=jnp.int32)[:, None] + (lane // (2 * SUB) * HALF)[None, :]

    def taper(x):
        return 1.0 - ((2.0 * x.astype(f32) + 1.0 - SUB) / SUB) ** 2

    def angle_sq(x):
        return ((x - HALF).astype(f32) * (field_view / SUB)) ** 2

    weight = taper(row) * taper(col) / math.sqrt(vis_count)
    turns = shift[:, None, None] * (row - HALF) % SUB
    angle = (
        -math.pi * screen_depth[:, None, None] * (angle_sq(row) + angle_sq(col))
        + 2.0 * math.pi / SUB * turns.astype(f32)
        - 0.5 * math.pi * imag.astype(f32)
    )
    return jnp.cos(angle) * weight


def from_partner(value, axis, mask):
    count = lax.axis_size(axis)
    return lax.ppermute(value, axis, [(i, i ^ mask) for i in range(count)])


def z_line(own):
    vert_count = lax.axis_size("vert")
    line = [own] + [from_partner(own, "vert", 2 * mask) for mask in range(1, vert_count // 2)]
    return jnp.concatenate(line, axis=0)


def au_lines(line):
    return [line] + [from_partner(line, "au", mask) for mask in range(1, lax.axis_size("au"))]


def with_core(lines):
    return [piece for line in lines for piece in (line, from_partner(line, "vert", 1))]


def whole_gather(own):
    return [lax.all_gather(own, ("au", "vert"), axis=0, tiled=True)]


def gathered_place(owner, by_mask):
    if not by_mask:
        return owner
    vert_count = lax.axis_size("vert")
    au_mask = (owner // vert_count) ^ lax.axis_index("au")
    vert_mask = (owner % vert_count) ^ lax.axis_index("vert")
    return au_mask * vert_count + vert_mask % 2 * (vert_count // 2) + vert_mask // 2


def coded_corners(corners):
    digits = jnp.stack([corners[:, 0] // 128, corners[:, 0] % 128, corners[:, 1] // 128, corners[:, 1] % 128])
    flat = digits.astype(f32).astype(bf16).reshape(-1)
    return jnp.pad(flat, (0, HALF * PACK - flat.shape[0])).reshape(1, HALF, PACK)


def decoded_corners(blocks, count):
    digits = blocks.reshape(blocks.shape[0], HALF * PACK).astype(jnp.int32)
    high_row, low_row, high_col, low_col = [
        digits[:, i * count : (i + 1) * count].reshape(-1) for i in range(4)
    ]
    return (high_row * 128 + low_row, high_col * 128 + low_col)


def on_device(
    visibilities, baseline_offsets, channel_scale, screen_depth, stations, corners, beam_terms
):
    au_count = lax.axis_size("au")
    vert_count = lax.axis_size("vert")
    au_index, vert_index = lax.axis_index("au"), lax.axis_index("vert")
    image_rows = G // (au_count * vert_count)
    count, _, vis_count = visibilities.shape
    own_stations = beam_terms.shape[0]
    held = au_count * vert_count * count * HALF * PACK
    by_mask = held <= MASK_VALUES

    sent = jnp.concatenate([packed_beams(beam_terms), coded_corners(corners)], axis=0)
    offsets = baseline_offsets.reshape(2 * count, -1)
    scale_row = jnp.tile(channel_scale, baseline_offsets.shape[2]).reshape(1, vis_count)
    part = math.gcd(count, 8)
    skies = [sky_sums(visibilities, offsets, scale_row, 0, part)]
    if by_mask:
        line = z_line(sent)
        line, offsets, skies[0] = lax.optimization_barrier((line, offsets, skies[0]))
    for s in range(part, count, part):
        skies.append(sky_sums(visibilities, offsets, scale_row, s, part))
    factor = pixel_factor(screen_depth, corners[:, 0] % SUB, vis_count)
    if by_mask:
        lines = au_lines(line)
        lines, skies = lax.optimization_barrier((lines, skies))
        tables = with_core(lines)
    else:
        tables = whole_gather(sent)
    coded = [
        piece.reshape(-1, own_stations + 1, HALF, PACK)[:, own_stations] for piece in tables
    ]
    corners_all = decoded_corners(jnp.concatenate(coded, axis=0), count)
    owners = stations // own_stations
    station_rows = gathered_place(owners, by_mask) * (own_stations + 1) + stations % own_stations
    uv_own = corrected_subgrids(station_rows, tables, skies, factor)

    per_row = vert_count * count

    def row_place(index):
        return gathered_place(index * vert_count + vert_index, by_mask) // vert_count

    def places_of(place, spilled):
        chosen = [lax.dynamic_slice_in_dim(x, place * per_row, per_row) for x in corners_all]
        return tile_places(chosen, au_index, vert_index, au_count, vert_count, spilled)

    own_place = row_place(au_index)
    before_place = row_place(lax.rem(au_index + au_count - 1, au_count))
    own_list, spill_list = places_of(own_place, False), places_of(before_place, True)
    if by_mask:
        lines = au_lines(z_line(uv_own))
        own_row = with_core(lines[:1])
        tile = uv_tile_own(own_row, own_place, own_list, au_count, vert_count)
        lines, own_row, tile = lax.optimization_barrier((lines, own_row, tile))
        uv = own_row + with_core(lines[1:])
        before = [
            lax.select_n(before_place, *uv[core::2]) if au_count > 2 else uv[core + 2]
            for core in range(2)
        ]
        before_block = jnp.zeros((), jnp.int32)
    else:
        uv = before = whole_gather(uv_own)
        tile = uv_tile_own(uv, own_place, own_list, au_count, vert_count)
        before_block = before_place
    gridded = uv_tile_spill(tile, before, before_block, spill_list, au_count, vert_count)
    first_row = (au_index * vert_count + vert_index) * image_rows
    dirty_image = image_rows_of(uv, corners_all, first_row, image_rows)
    return (gridded, dirty_image)


def solution(mesh):
    return jax.shard_map(
        on_device,
        mesh=mesh,
        in_specs=(
            P(("au", "vert"), None, None),
            P(("au", "vert"), None, None),
            P(),
            P(("au", "vert")),
            P(("au", "vert"), None),
            P(("au", "vert"), None),
            P(("au", "vert"), None, None),
        ),
        out_specs=(P("au", None, "vert"), P(("au", "vert"), None, None)),
        check_vma=False,
    )
```

```python
import functools
import math

import jax
import jax.numpy as jnp
from jax import lax
from jax.experimental import pallas as pl
from jax.experimental.pallas import tpu as pltpu
from jax.sharding import PartitionSpec as P

G = 8192
SUB = 32
HALF = SUB // 2
PACK = 4 * SUB
LANES = 128
FINE = G // SUB
CHUNK = 768
MASK_VALUES = 1 << 22
field_view = 0.1
bf16 = jnp.bfloat16
f32 = jnp.float32
VMEM_BYTES = 58 * 1024 * 1024


def cmul(a, b):
    return (a[0] * b[0] - a[1] * b[1], a[0] * b[1] + a[1] * b[0])


def conj(a):
    return (a[0], -a[1])


def sky_kernel(vis_ref, offset_ref, scale_ref, out_ref, cos_ref, sin_ref):
    count, _, vis_count = vis_ref.shape
    times = offset_ref.shape[1]
    step = math.gcd(vis_count, 256)
    row = lax.broadcasted_iota(jnp.int32, (8, step), 0)
    bits = [(row >> bit) % 2 == 1 for bit in range(3)]

    offsets = offset_ref[...]
    parts = []
    for _ in range(3):
        parts.append(offsets.astype(bf16))
        offsets = offsets - parts[-1].astype(f32)
    for start in range(0, vis_count, 512):
        width = min(512, vis_count - start)
        at = pl.ds(start, width)
        time = lax.broadcasted_iota(jnp.int32, (times, width), 0)
        place = lax.broadcasted_iota(jnp.int32, (times, width), 1) + start
        one = (place // (vis_count // times) == time).astype(f32).astype(bf16)
        shifts = sum(jnp.dot(part, one, preferred_element_type=f32) for part in parts)
        half = (math.pi / SUB) * (shifts * scale_ref[:, at])
        square = half * half
        sine, cosine = 1.0, 1.0
        for term in (12, 10, 8, 6, 4, 2):
            sine = 1.0 - square * (1.0 / (term * (term + 1))) * sine
            cosine = 1.0 - square * (1.0 / (term * (term - 1))) * cosine
        sine = sine * half
        cos_ref[:, at] = 1.0 - 2.0 * sine * sine
        sin_ref[:, at] = 2.0 * sine * cosine

    def powers(c, s, extra):
        z = (jnp.broadcast_to(c, (8, step)), jnp.broadcast_to(s, (8, step)))
        low = (jnp.where(bits[0], z[0], 1.0), jnp.where(bits[0], z[1], 0.0))
        power = z
        for bit in (1, 2):
            power = (power[0] * power[0] - power[1] * power[1], 2.0 * power[0] * power[1])
            more = cmul(low, power)
            low = (jnp.where(bits[bit], more[0], low[0]), jnp.where(bits[bit], more[1], low[1]))
        eight = (power[0] * power[0] - power[1] * power[1], 2.0 * power[0] * power[1])
        sixteen = (eight[0] * eight[0] - eight[1] * eight[1], 2.0 * eight[0] * eight[1])
        if extra is not None:
            low = cmul(low, extra)
        blocks = [cmul(low, conj(sixteen)), cmul(low, conj(eight)), low, cmul(low, eight)]
        return jnp.concatenate([block[part] for part in range(2) for block in blocks], axis=0).astype(bf16)

    def one_subgrid(s):
        both = jnp.zeros((2 * SUB, 2 * SUB), f32)
        for start in range(0, vis_count, step):
            at = pl.ds(start, step)
            vis = tuple(
                jnp.broadcast_to(vis_ref[s, part : part + 1, at].astype(f32), (8, step))
                for part in range(2)
            )
            u_row, v_row = pl.ds(2 * s, 1), pl.ds(2 * s + 1, 1)
            left = powers(cos_ref[u_row, at], sin_ref[u_row, at], vis)
            right = powers(cos_ref[v_row, at], sin_ref[v_row, at], None)
            both += lax.dot_general(
                left, right, (((1,), (1,)), ((), ())), preferred_element_type=f32
            )
        real = both[:SUB, :SUB] - both[SUB:, SUB:]
        image = both[:SUB, SUB:] + both[SUB:, :SUB]
        out_ref[s] = jnp.concatenate(
            [real[:HALF], image[:HALF], real[HALF:], image[HALF:]], axis=1
        )

    def some(i, carry):
        for k in range(math.gcd(count, 2)):
            one_subgrid(i * math.gcd(count, 2) + k)
        return carry

    lax.fori_loop(0, count // math.gcd(count, 2), some, 0)


def sky_sums(visibilities, offsets, scale_row, first, count, interpret=False):
    vis_count = visibilities.shape[2]
    times = offsets.shape[1]
    at = first // count
    return pl.pallas_call(
        sky_kernel,
        grid=(1,),
        in_specs=[
            pl.BlockSpec((count, 2, vis_count), lambda i: (at, 0, 0)),
            pl.BlockSpec((2 * count, times), lambda i: (at, 0)),
            pl.BlockSpec((1, vis_count), lambda i: (0, 0)),
        ],
        out_specs=pl.BlockSpec((count, HALF, PACK), lambda i: (0, 0, 0)),
        out_shape=jax.ShapeDtypeStruct((count, HALF, PACK), f32),
        scratch_shapes=[pltpu.VMEM((2 * count, vis_count), f32)] * 2,
        compiler_params=pltpu.CompilerParams(vmem_limit_bytes=VMEM_BYTES),
        cost_estimate=pl.CostEstimate(
            flops=0, bytes_accessed=count * 2_500_000, transcendentals=0
        ),
        name="sky_sums",
        interpret=interpret,
    )(visibilities, offsets, scale_row)


def correct_kernel(stations_ref, *refs, pieces, skies):
    table_refs, refs = refs[:pieces], refs[pieces:]
    sky_refs, refs = refs[:skies], refs[skies:]
    factor_ref, right_ref, left_ref, out_ref, table_ref, mid_ref = refs
    count = factor_ref.shape[0]
    lane = lax.broadcasted_iota(jnp.int32, (HALF, PACK), 1)
    imag = (lane // SUB) % 2 == 1
    sign = jnp.where(imag, 1.0, -1.0)

    def up(x):
        return pltpu.roll(x, SUB, 1)

    def down(x):
        return pltpu.roll(x, PACK - SUB, 1)

    def product(a, b):
        swapped = jnp.where(imag, up(a), down(a))
        return a * jnp.where(imag, up(b), b) + sign * swapped * jnp.where(imag, b, down(b))

    held = 0
    for piece in table_refs:
        table_ref[held : held + piece.shape[0]] = piece[...]
        held += piece.shape[0]
    for s in range(count):
        first = table_ref[stations_ref[2 * s]].astype(f32)
        second = table_ref[stations_ref[2 * s + 1]].astype(f32)
        pair = product(first, -sign * second)
        per = count // skies
        sky = product(sky_refs[s // per][s % per], factor_ref[s])
        mid_ref[HALF * s : HALF * (s + 1), :] = product(sky, pair).astype(bf16)
    mid = jnp.dot(mid_ref[...], right_ref[...], preferred_element_type=f32).astype(bf16)
    for s in range(count):
        rows = mid[HALF * s : HALF * (s + 1)]
        tall = jnp.concatenate([rows[:, : 2 * SUB], rows[:, 2 * SUB :]], axis=0)
        four = jnp.dot(left_ref[...], tall, preferred_element_type=f32)
        real = four[:SUB, :SUB] - four[SUB:, SUB:]
        image = four[:SUB, SUB:] + four[SUB:, :SUB]
        out_ref[s] = jnp.concatenate(
            [real[:HALF], image[:HALF], real[HALF:], image[HALF:]], axis=1
        ).astype(bf16)


def corrected_subgrids(stations, tables, skies, factor, interpret=False):
    count = factor.shape[0]
    centred = jnp.arange(SUB, dtype=jnp.int32) - HALF
    index = jnp.arange(SUB, dtype=jnp.int32)
    angle = 2.0 * math.pi / SUB * (centred[:, None] * centred[None, :] % SUB).astype(f32)
    cols_re, cols_im = jnp.cos(angle) / SUB, -jnp.sin(angle) / SUB
    block = jnp.concatenate(
        [
            jnp.concatenate([cols_re.T, cols_im.T], axis=1),
            jnp.concatenate([-cols_im.T, cols_re.T], axis=1),
        ],
        axis=0,
    )
    right = jnp.kron(jnp.eye(2, dtype=f32), block).astype(bf16)
    angle = 2.0 * math.pi / SUB * ((index - HALF)[:, None] * centred[None, :] % SUB).astype(f32)
    left = jnp.concatenate([jnp.cos(angle) / SUB, -jnp.sin(angle) / SUB], axis=0).astype(bf16)
    rows = sum(piece.shape[0] for piece in tables)
    operands = [*tables, *skies, factor, right, left]

    def whole(operand):
        return pl.BlockSpec(operand.shape, lambda i, *_: (0,) * operand.ndim)

    return pl.pallas_call(
        functools.partial(correct_kernel, pieces=len(tables), skies=len(skies)),
        grid_spec=pltpu.PrefetchScalarGridSpec(
            num_scalar_prefetch=1,
            grid=(1,),
            in_specs=[whole(operand) for operand in operands],
            out_specs=pl.BlockSpec((count, HALF, PACK), lambda i, *_: (0, 0, 0)),
            scratch_shapes=[
                pltpu.VMEM((rows, HALF, PACK), bf16),
                pltpu.VMEM((HALF * count, PACK), bf16),
            ],
        ),
        out_shape=jax.ShapeDtypeStruct((count, HALF, PACK), bf16),
        compiler_params=pltpu.CompilerParams(vmem_limit_bytes=VMEM_BYTES),
        cost_estimate=pl.CostEstimate(flops=0, bytes_accessed=16_000_000, transcendentals=0),
        name="correct",
        interpret=interpret,
    )(stations.reshape(-1), *operands)


def add_subgrids(uv_refs, list_ref, row_ref, col_ref, held_ref, total_ref, lanes):
    first = 0
    for piece in uv_refs:
        held_ref[first : first + piece.shape[0]] = piece[...]
        first += piece.shape[0]
    lane = lax.broadcasted_iota(jnp.int32, (8, LANES), 1)
    row = lax.broadcasted_iota(jnp.int32, (8, LANES), 0)

    def one(entry, carry):
        s = list_ref[entry + 1]
        row_at, col_at = row_ref[s], col_ref[s]
        packed = held_ref[pl.ds(pl.multiple_of(s * HALF, HALF), HALF), :].astype(f32)
        tile = col_at // LANES
        offset = col_at % LANES
        shift = row_at % SUB
        base = row_at - shift

        def place(over):
            inside = lane < offset + SUB - LANES
            if not over:
                inside = (lane >= offset) & (lane < offset + SUB)
            for h in range(2):
                for part in range(2):
                    from_lane = (2 * h + part) * SUB
                    moved = pltpu.roll(packed, lax.rem(offset - from_lane + LANES, LANES), 1)
                    for group in range(2):
                        values = moved[8 * group : 8 * (group + 1)]
                        first_row = HALF * h + 8 * group
                        late = row + first_row >= shift
                        for wrapped in range(2):
                            keep = jnp.logical_and(inside, late if wrapped == 0 else ~late)
                            start = (base + SUB * wrapped + first_row) * lanes
                            start = start + 2 * (tile + over) + part
                            at = pl.ds(start, 8, stride=lanes)
                            total_ref[at, :] = total_ref[at, :] + jnp.where(keep, values, 0.0)

        place(0)

        @pl.when(offset + SUB > LANES)
        def _():
            place(1)

        return carry

    lax.fori_loop(0, list_ref[0], one, 0)


def tile_kernel(block_ref, list_ref, row_ref, col_ref, *refs, pieces, tile_rows, lanes):
    del block_ref
    uv_refs = refs[:pieces]
    out_ref, held_ref, total_ref, sems = refs[pieces:]
    rows_all = total_ref.shape[0]
    zero_rows = math.gcd(rows_all, 1024)

    def clear(i, carry):
        at = pl.ds(pl.multiple_of(i * zero_rows, zero_rows), zero_rows)
        total_ref[at, :] = jnp.zeros((zero_rows, LANES), f32)
        return carry

    lax.fori_loop(0, rows_all // zero_rows, clear, 0)
    add_subgrids(uv_refs, list_ref, row_ref, col_ref, held_ref, total_ref, lanes)
    pieces = sems.shape[0]
    size = tile_rows * lanes // pieces
    copies = [
        pltpu.make_async_copy(
            total_ref.at[pl.ds(i * size, size), :], out_ref.at[pl.ds(i * size, size), :], sems.at[i]
        )
        for i in range(pieces)
    ]
    for copy in copies:
        copy.start()
    for copy in copies:
        copy.wait()


def spill_kernel(block_ref, list_ref, row_ref, col_ref, *refs, pieces, lanes):
    del block_ref
    uv_refs = refs[:pieces]
    _, out_ref, held_ref, total_ref, sem = refs[pieces:]
    size = SUB * lanes
    kept = total_ref.at[pl.ds(size, size), :]
    copy = pltpu.make_async_copy(out_ref.at[pl.ds(0, size), :], kept, sem)
    copy.start()
    copy.wait()
    add_subgrids(uv_refs, list_ref, row_ref, col_ref, held_ref, total_ref, lanes)
    copy = pltpu.make_async_copy(kept, out_ref.at[pl.ds(0, size), :], sem)
    copy.start()
    copy.wait()


def listed(valid):
    count = valid.shape[0]
    index = jnp.arange(count, dtype=jnp.int32)
    before = jnp.sum((index[None, :] < index[:, None]) & valid[None, :], axis=1, dtype=jnp.int32)
    rank = jnp.where(valid, before, -1)
    entries = jnp.sum(
        jnp.where(rank[None, :] == index[:, None], index[None, :], 0), axis=1, dtype=jnp.int32
    )
    return jnp.concatenate([jnp.sum(valid, dtype=jnp.int32)[None], entries])


def tile_places(corners, au_index, vert_index, au_count, vert_count, spilled):
    tile_rows, tile_cols = G // au_count, G // vert_count
    col_at = corners[1] - vert_index * tile_cols
    valid = (col_at >= 0) & (col_at < tile_cols)
    row_at = corners[0] - au_index * tile_rows
    if spilled:
        row_at = (row_at + SUB + G) % G
        valid = valid & (row_at < SUB)
    return listed(valid), row_at, col_at


def uv_tile_own(uv, block, places, au_count, vert_count, interpret=False):
    count = places[1].shape[0]
    tile_rows, tile_cols = G // au_count, G // vert_count
    lanes = 2 * tile_cols // LANES
    rows = count * HALF // len(uv)
    return pl.pallas_call(
        functools.partial(tile_kernel, pieces=len(uv), tile_rows=tile_rows, lanes=lanes),
        grid_spec=pltpu.PrefetchScalarGridSpec(
            num_scalar_prefetch=4,
            grid=(1,),
            in_specs=[pl.BlockSpec((rows, PACK), lambda i, block, *_: (block[0], 0))] * len(uv),
            out_specs=pl.BlockSpec(memory_space=pl.ANY),
            scratch_shapes=[
                pltpu.VMEM((count * HALF, PACK), bf16),
                pltpu.VMEM(((tile_rows + 2 * SUB) * lanes, LANES), f32),
                pltpu.SemaphoreType.DMA((4,)),
            ],
        ),
        out_shape=jax.ShapeDtypeStruct((tile_rows * lanes, LANES), f32),
        compiler_params=pltpu.CompilerParams(vmem_limit_bytes=VMEM_BYTES),
        cost_estimate=pl.CostEstimate(
            flops=0, bytes_accessed=20 * tile_rows * tile_cols, transcendentals=0
        ),
        name="uv_tile",
        interpret=interpret,
    )(block.reshape(1), *places, *[piece.reshape(-1, PACK) for piece in uv])


def uv_tile_spill(tile, uv, block, places, au_count, vert_count, interpret=False):
    count = places[1].shape[0]
    tile_rows, tile_cols = G // au_count, G // vert_count
    lanes = 2 * tile_cols // LANES
    rows = count * HALF // len(uv)
    result = pl.pallas_call(
        functools.partial(spill_kernel, pieces=len(uv), lanes=lanes),
        grid_spec=pltpu.PrefetchScalarGridSpec(
            num_scalar_prefetch=4,
            grid=(1,),
            in_specs=[pl.BlockSpec((rows, PACK), lambda i, block, *_: (block[0], 0))] * len(uv)
            + [pl.BlockSpec(memory_space=pl.ANY)],
            out_specs=pl.BlockSpec(memory_space=pl.ANY),
            scratch_shapes=[
                pltpu.VMEM((count * HALF, PACK), bf16),
                pltpu.VMEM((3 * SUB * lanes, LANES), f32),
                pltpu.SemaphoreType.DMA(()),
            ],
        ),
        out_shape=jax.ShapeDtypeStruct(tile.shape, f32),
        input_output_aliases={4 + len(uv): 0},
        compiler_params=pltpu.CompilerParams(vmem_limit_bytes=VMEM_BYTES),
        cost_estimate=pl.CostEstimate(flops=0, bytes_accessed=8_000_000, transcendentals=0),
        name="uv_spill",
        interpret=interpret,
    )(block.reshape(1), *places, *[piece.reshape(-1, PACK) for piece in uv], tile)
    result = result.reshape(tile_rows, tile_cols // LANES, 2, LANES)
    return jnp.transpose(result, (0, 2, 1, 3)).reshape(tile_rows, 2, tile_cols)


def short_transform(values):
    count = len(values)
    if count == 1:
        return values
    even = short_transform(values[0::2])
    odd = short_transform(values[1::2])
    low, high = [], []
    for k in range(count // 2):
        re, im = odd[k]
        if k == 0:
            turned = (re, im)
        elif 4 * k == count:
            turned = (-im, re)
        elif 8 * k == count:
            root = math.sqrt(0.5)
            turned = ((re - im) * root, (re + im) * root)
        elif 8 * k == 3 * count:
            root = math.sqrt(0.5)
            turned = ((re + im) * -root, (re - im) * root)
        else:
            c, s = math.cos(2 * math.pi * k / count), math.sin(2 * math.pi * k / count)
            turned = (re * c - im * s, re * s + im * c)
        low.append((even[k][0] + turned[0], even[k][1] + turned[1]))
        high.append((even[k][0] - turned[0], even[k][1] - turned[1]))
    return low + high


def image_kernel(*refs, pieces, chunks, row_block):
    uv_refs, refs = refs[:pieces], refs[pieces:]
    corner_ref, phase_ref, columns_ref, unit_ref, count_ref, twist_ref = refs[:6]
    out_ref, uv_wide, here, after, shifts, left_even, left_odd, total = refs[6:]
    step = pl.program_id(0)
    size = uv_wide.shape[0] // HALF
    image_rows = phase_ref.shape[1]

    def products(pair, h, left):
        rows = uv_wide[pl.ds(pair, size, stride=HALF), :].astype(bf16)
        at = pl.ds(2 * image_rows * h, 2 * image_rows)
        spread = lax.dot_general(
            columns_ref[at, :], rows, (((1,), (1,)), ((), ())), preferred_element_type=f32
        ).astype(bf16)
        turned = cmul((spread[:image_rows], spread[image_rows:]), (phase_ref[0], phase_ref[1]))
        left[h, :image_rows] = turned[0]
        left[h, image_rows:] = turned[1]

    def sums(pair, h, left, first):
        index = pair + HALF * h
        late = shifts[...] > index.astype(f32)
        table = jnp.concatenate(
            [
                jnp.where(late, after[:, t : t + LANES], here[:, t : t + LANES])
                for t in range(0, 2 * FINE, LANES)
            ],
            axis=1,
        )
        four = jnp.dot(left[h], table, preferred_element_type=f32)
        got = (
            four[:image_rows, :FINE] - four[image_rows:, FINE:],
            four[:image_rows, FINE:] + four[image_rows:, :FINE],
        )
        twist = twist_ref[pl.ds(index, 1), :]
        done = cmul(got, (twist[:, :FINE], twist[:, FINE:]))
        for part in range(2):
            total[index, part] = done[part] if first else total[index, part] + done[part]

    def chunk(first):
        held = 0
        for piece in uv_refs:
            uv_wide[held : held + piece.shape[0]] = piece[...].astype(f32)
            held += piece.shape[0]
        corner = corner_ref[...]
        coarse, shift = corner // SUB, corner % SUB

        def looked_up(index, length, table):
            place = lax.broadcasted_iota(jnp.int32, (length, size), 0)
            one = (place == index).astype(f32).astype(bf16)
            return lax.dot_general(one, table, (((0,), (0,)), ((), ())), preferred_element_type=f32)

        here[...] = looked_up(coarse, FINE, unit_ref[...]).astype(bf16)
        after[...] = looked_up(lax.rem(coarse + 1, FINE), FINE, unit_ref[...]).astype(bf16)
        shifts[...] = looked_up(shift, SUB, count_ref[...])
        for h in range(2):
            products(0, h, left_even)

        def two_pairs(i, carry):
            for h in range(2):
                products(2 * i + 1, h, left_odd)
                sums(2 * i, h, left_even, first)
            for h in range(2):
                products(jnp.minimum(2 * i + 2, HALF - 1), h, left_even)
                sums(2 * i + 1, h, left_odd, first)
            return carry

        lax.fori_loop(0, HALF // 2, two_pairs, 0)

    @pl.when(step == 0)
    def _():
        chunk(True)

    if chunks > 1:

        @pl.when((step > 0) & (step < chunks))
        def _():
            chunk(False)

    @pl.when(step >= chunks)
    def _():
        first = (step - chunks) * row_block
        wide = 2 * G // LANES

        def eight_rows(group, carry):
            at = pl.ds(pl.multiple_of(first + 8 * group, 8), 8)
            for tile in range(FINE // LANES):
                lanes = pl.ds(tile * LANES, LANES)
                values = [(total[n, 0, at, lanes], total[n, 1, at, lanes]) for n in range(SUB)]
                for k, value in enumerate(short_transform(values)):
                    for part in range(2):
                        column = 2 * (k * (FINE // LANES) + tile) + part
                        out_ref[pl.ds(group * 8 * wide + column, 8, stride=wide), :] = value[part]
            return carry

        lax.fori_loop(0, row_block // 8, eight_rows, 0)


def image_rows_of(uv, corners_all, first_row, image_rows, interpret=False):
    total = corners_all[0].shape[0]
    size = math.gcd(total, CHUNK) if len(uv) == 1 else total
    chunks = total // size
    row_block = math.gcd(image_rows, 32)
    outs = image_rows // row_block
    wide = 2 * G // LANES
    rows = first_row + jnp.arange(image_rows, dtype=jnp.int32)
    turn = 2.0 * math.pi / G
    angle = turn * (rows[:, None] * corners_all[1][None, :] % G).astype(f32)
    phase = jnp.stack([jnp.cos(angle), jnp.sin(angle)]).astype(bf16)
    angle = turn * (rows[:, None] * jnp.arange(SUB, dtype=jnp.int32)[None, :] % G).astype(f32)
    re, im = jnp.cos(angle), jnp.sin(angle)
    block = jnp.concatenate(
        [jnp.concatenate([re, -im], axis=1), jnp.concatenate([im, re], axis=1)], axis=0
    )
    columns = jnp.kron(jnp.eye(2, dtype=f32), block).astype(bf16)
    fine = jnp.arange(FINE, dtype=jnp.int32)
    angle = 2.0 * math.pi / FINE * (fine[:, None] * fine[None, :] % FINE).astype(f32)
    unit = jnp.concatenate([jnp.cos(angle), jnp.sin(angle)], axis=1).astype(bf16)
    angle = turn * (jnp.arange(SUB, dtype=jnp.int32)[:, None] * fine[None, :]).astype(f32)
    scale = 1.0 / (SUB * math.sqrt(total))
    twist = jnp.concatenate([jnp.cos(angle), jnp.sin(angle)], axis=1) * scale
    counts = jnp.broadcast_to(jnp.arange(SUB, dtype=f32)[:, None], (SUB, LANES)).astype(bf16)
    last = chunks - 1

    def chunk_of(i):
        return jnp.minimum(i, last)

    result = pl.pallas_call(
        functools.partial(image_kernel, pieces=len(uv), chunks=chunks, row_block=row_block),
        grid=(chunks + outs,),
        in_specs=[
            *[pl.BlockSpec((size * HALF // len(uv), PACK), lambda i: (chunk_of(i), 0))] * len(uv),
            pl.BlockSpec((1, size), lambda i: (0, chunk_of(i))),
            pl.BlockSpec((2, image_rows, size), lambda i: (0, 0, chunk_of(i))),
            pl.BlockSpec(columns.shape, lambda i: (0, 0)),
            pl.BlockSpec(unit.shape, lambda i: (0, 0)),
            pl.BlockSpec(counts.shape, lambda i: (0, 0)),
            pl.BlockSpec(twist.shape, lambda i: (0, 0)),
        ],
        out_specs=pl.BlockSpec(
            (row_block * wide, LANES), lambda i: (jnp.maximum(i - chunks, 0), 0)
        ),
        out_shape=jax.ShapeDtypeStruct((image_rows * wide, LANES), f32),
        scratch_shapes=[
            pltpu.VMEM((size * HALF, PACK), f32),
            pltpu.VMEM((size, 2 * FINE), bf16),
            pltpu.VMEM((size, 2 * FINE), bf16),
            pltpu.VMEM((size, LANES), f32),
            pltpu.VMEM((2, 2 * image_rows, size), bf16),
            pltpu.VMEM((2, 2 * image_rows, size), bf16),
            pltpu.VMEM((SUB, 2, image_rows, FINE), f32),
        ],
        compiler_params=pltpu.CompilerParams(vmem_limit_bytes=VMEM_BYTES),
        name="image",
        interpret=interpret,
    )(
        *[piece.reshape(-1, PACK) for piece in uv], corners_all[0].reshape(1, total),
        phase, columns, unit, counts, twist,
    )
    result = result.reshape(image_rows, G // LANES, 2, LANES)
    return jnp.transpose(result, (0, 2, 1, 3)).reshape(image_rows, 2, G)


def packed_beams(beam_terms):
    count = beam_terms.shape[0]
    parts = beam_terms.reshape(count, 2, 2, HALF, SUB)
    return jnp.transpose(parts, (0, 3, 2, 1, 4)).reshape(count, HALF, PACK)


def pixel_factor(screen_depth, shift, vis_count):
    lane = jnp.arange(PACK, dtype=jnp.int32)
    col = lane % SUB
    imag = (lane // SUB) % 2
    row = jnp.arange(HALF, dtype=jnp.int32)[:, None] + (lane // (2 * SUB) * HALF)[None, :]

    def taper(x):
        return 1.0 - ((2.0 * x.astype(f32) + 1.0 - SUB) / SUB) ** 2

    def angle_sq(x):
        return ((x - HALF).astype(f32) * (field_view / SUB)) ** 2

    weight = taper(row) * taper(col) / math.sqrt(vis_count)
    turns = shift[:, None, None] * (row - HALF) % SUB
    angle = (
        -math.pi * screen_depth[:, None, None] * (angle_sq(row) + angle_sq(col))
        + 2.0 * math.pi / SUB * turns.astype(f32)
        - 0.5 * math.pi * imag.astype(f32)
    )
    return jnp.cos(angle) * weight


def from_partner(value, axis, mask):
    count = lax.axis_size(axis)
    return lax.ppermute(value, axis, [(i, i ^ mask) for i in range(count)])


def z_line(own):
    vert_count = lax.axis_size("vert")
    line = [own] + [from_partner(own, "vert", 2 * mask) for mask in range(1, vert_count // 2)]
    return jnp.concatenate(line, axis=0)


def au_lines(line):
    return [line] + [from_partner(line, "au", mask) for mask in range(1, lax.axis_size("au"))]


def with_core(lines):
    return [piece for line in lines for piece in (line, from_partner(line, "vert", 1))]


def whole_gather(own):
    return [lax.all_gather(own, ("au", "vert"), axis=0, tiled=True)]


def gathered_place(owner, by_mask):
    if not by_mask:
        return owner
    vert_count = lax.axis_size("vert")
    au_mask = (owner // vert_count) ^ lax.axis_index("au")
    vert_mask = (owner % vert_count) ^ lax.axis_index("vert")
    return au_mask * vert_count + vert_mask % 2 * (vert_count // 2) + vert_mask // 2


def coded_corners(corners):
    digits = jnp.stack([corners[:, 0] // 128, corners[:, 0] % 128, corners[:, 1] // 128, corners[:, 1] % 128])
    flat = digits.astype(f32).astype(bf16).reshape(-1)
    return jnp.pad(flat, (0, HALF * PACK - flat.shape[0])).reshape(1, HALF, PACK)


def decoded_corners(blocks, count):
    digits = blocks.reshape(blocks.shape[0], HALF * PACK).astype(jnp.int32)
    high_row, low_row, high_col, low_col = [
        digits[:, i * count : (i + 1) * count].reshape(-1) for i in range(4)
    ]
    return (high_row * 128 + low_row, high_col * 128 + low_col)


def on_device(
    visibilities, baseline_offsets, channel_scale, screen_depth, stations, corners, beam_terms
):
    au_count = lax.axis_size("au")
    vert_count = lax.axis_size("vert")
    au_index, vert_index = lax.axis_index("au"), lax.axis_index("vert")
    image_rows = G // (au_count * vert_count)
    count, _, vis_count = visibilities.shape
    own_stations = beam_terms.shape[0]
    held = au_count * vert_count * count * HALF * PACK
    by_mask = held <= MASK_VALUES

    sent = jnp.concatenate([packed_beams(beam_terms), coded_corners(corners)], axis=0)
    offsets = baseline_offsets.reshape(2 * count, -1)
    scale_row = jnp.tile(channel_scale, baseline_offsets.shape[2]).reshape(1, vis_count)
    part = math.gcd(count, 8)
    skies = [sky_sums(visibilities, offsets, scale_row, 0, part)]
    if by_mask:
        line = z_line(sent)
        line, offsets, skies[0] = lax.optimization_barrier((line, offsets, skies[0]))
    for s in range(part, count, part):
        skies.append(sky_sums(visibilities, offsets, scale_row, s, part))
    factor = pixel_factor(screen_depth, corners[:, 0] % SUB, vis_count)
    if by_mask:
        lines = au_lines(line)
        lines, skies = lax.optimization_barrier((lines, skies))
        tables = with_core(lines)
    else:
        tables = whole_gather(sent)
    coded = [
        piece.reshape(-1, own_stations + 1, HALF, PACK)[:, own_stations] for piece in tables
    ]
    corners_all = decoded_corners(jnp.concatenate(coded, axis=0), count)
    owners = stations // own_stations
    station_rows = gathered_place(owners, by_mask) * (own_stations + 1) + stations % own_stations
    uv_own = corrected_subgrids(station_rows, tables, skies, factor)

    per_row = vert_count * count

    def row_place(index):
        return gathered_place(index * vert_count + vert_index, by_mask) // vert_count

    def places_of(place, spilled):
        chosen = [lax.dynamic_slice_in_dim(x, place * per_row, per_row) for x in corners_all]
        return tile_places(chosen, au_index, vert_index, au_count, vert_count, spilled)

    own_place = row_place(au_index)
    before_place = row_place(lax.rem(au_index + au_count - 1, au_count))
    own_list, spill_list = places_of(own_place, False), places_of(before_place, True)
    if by_mask:
        lines = au_lines(z_line(uv_own))
        own_row = with_core(lines[:1])
        tile = uv_tile_own(own_row, own_place, own_list, au_count, vert_count)
        lines, own_row, tile = lax.optimization_barrier((lines, own_row, tile))
        uv = own_row + with_core(lines[1:])
        before = [
            lax.select_n(before_place, *uv[core::2]) if au_count > 2 else uv[core + 2]
            for core in range(2)
        ]
        before_block = jnp.zeros((), jnp.int32)
    else:
        uv = before = whole_gather(uv_own)
        tile = uv_tile_own(uv, own_place, own_list, au_count, vert_count)
        before_block = before_place
    gridded = uv_tile_spill(tile, before, before_block, spill_list, au_count, vert_count)
    first_row = (au_index * vert_count + vert_index) * image_rows
    dirty_image = image_rows_of(uv, corners_all, first_row, image_rows)
    return (gridded, dirty_image)


def solution(mesh):
    return jax.shard_map(
        on_device,
        mesh=mesh,
        in_specs=(
            P(("au", "vert"), None, None),
            P(("au", "vert"), None, None),
            P(),
            P(("au", "vert")),
            P(("au", "vert"), None),
            P(("au", "vert"), None),
            P(("au", "vert"), None, None),
        ),
        out_specs=(P("au", None, "vert"), P(("au", "vert"), None, None)),
        check_vma=False,
    )
```

```python
import functools
import math

import jax
import jax.numpy as jnp
from jax import lax
from jax.experimental import pallas as pl
from jax.experimental.pallas import tpu as pltpu
from jax.sharding import PartitionSpec as P

G = 8192
SUB = 32
HALF = SUB // 2
PACK = 4 * SUB
LANES = 128
FINE = G // SUB
CHUNK = 768
MASK_VALUES = 1 << 22
field_view = 0.1
bf16 = jnp.bfloat16
f32 = jnp.float32
VMEM_BYTES = 58 * 1024 * 1024


def cmul(a, b):
    return (a[0] * b[0] - a[1] * b[1], a[0] * b[1] + a[1] * b[0])


def conj(a):
    return (a[0], -a[1])


def sky_kernel(vis_ref, offset_ref, scale_ref, out_ref, cos_ref, sin_ref):
    count, _, vis_count = vis_ref.shape
    times = offset_ref.shape[1]
    step = math.gcd(vis_count, 256)
    row = lax.broadcasted_iota(jnp.int32, (8, step), 0)
    bits = [(row >> bit) % 2 == 1 for bit in range(3)]

    offsets = offset_ref[...]
    parts = []
    for _ in range(3):
        parts.append(offsets.astype(bf16))
        offsets = offsets - parts[-1].astype(f32)
    for start in range(0, vis_count, 512):
        width = min(512, vis_count - start)
        at = pl.ds(start, width)
        time = lax.broadcasted_iota(jnp.int32, (times, width), 0)
        place = lax.broadcasted_iota(jnp.int32, (times, width), 1) + start
        one = (place // (vis_count // times) == time).astype(f32).astype(bf16)
        shifts = sum(jnp.dot(part, one, preferred_element_type=f32) for part in parts)
        half = (math.pi / SUB) * (shifts * scale_ref[:, at])
        square = half * half
        sine, cosine = 1.0, 1.0
        for term in (12, 10, 8, 6, 4, 2):
            sine = 1.0 - square * (1.0 / (term * (term + 1))) * sine
            cosine = 1.0 - square * (1.0 / (term * (term - 1))) * cosine
        sine = sine * half
        cos_ref[:, at] = 1.0 - 2.0 * sine * sine
        sin_ref[:, at] = 2.0 * sine * cosine

    def powers(c, s, extra):
        z = (jnp.broadcast_to(c, (8, step)), jnp.broadcast_to(s, (8, step)))
        low = (jnp.where(bits[0], z[0], 1.0), jnp.where(bits[0], z[1], 0.0))
        power = z
        for bit in (1, 2):
            power = (power[0] * power[0] - power[1] * power[1], 2.0 * power[0] * power[1])
            more = cmul(low, power)
            low = (jnp.where(bits[bit], more[0], low[0]), jnp.where(bits[bit], more[1], low[1]))
        eight = (power[0] * power[0] - power[1] * power[1], 2.0 * power[0] * power[1])
        sixteen = (eight[0] * eight[0] - eight[1] * eight[1], 2.0 * eight[0] * eight[1])
        if extra is not None:
            low = cmul(low, extra)
        blocks = [cmul(low, conj(sixteen)), cmul(low, conj(eight)), low, cmul(low, eight)]
        return jnp.concatenate([block[part] for part in range(2) for block in blocks], axis=0).astype(bf16)

    def one_subgrid(s):
        both = jnp.zeros((2 * SUB, 2 * SUB), f32)
        for start in range(0, vis_count, step):
            at = pl.ds(start, step)
            vis = tuple(
                jnp.broadcast_to(vis_ref[s, part : part + 1, at].astype(f32), (8, step))
                for part in range(2)
            )
            u_row, v_row = pl.ds(2 * s, 1), pl.ds(2 * s + 1, 1)
            left = powers(cos_ref[u_row, at], sin_ref[u_row, at], vis)
            right = powers(cos_ref[v_row, at], sin_ref[v_row, at], None)
            both += lax.dot_general(
                left, right, (((1,), (1,)), ((), ())), preferred_element_type=f32
            )
        real = both[:SUB, :SUB] - both[SUB:, SUB:]
        image = both[:SUB, SUB:] + both[SUB:, :SUB]
        out_ref[s] = jnp.concatenate(
            [real[:HALF], image[:HALF], real[HALF:], image[HALF:]], axis=1
        )

    def some(i, carry):
        for k in range(math.gcd(count, 2)):
            one_subgrid(i * math.gcd(count, 2) + k)
        return carry

    lax.fori_loop(0, count // math.gcd(count, 2), some, 0)


def sky_sums(visibilities, offsets, scale_row, first, count, interpret=False):
    vis_count = visibilities.shape[2]
    times = offsets.shape[1]
    at = first // count
    return pl.pallas_call(
        sky_kernel,
        grid=(1,),
        in_specs=[
            pl.BlockSpec((count, 2, vis_count), lambda i: (at, 0, 0)),
            pl.BlockSpec((2 * count, times), lambda i: (at, 0)),
            pl.BlockSpec((1, vis_count), lambda i: (0, 0)),
        ],
        out_specs=pl.BlockSpec((count, HALF, PACK), lambda i: (0, 0, 0)),
        out_shape=jax.ShapeDtypeStruct((count, HALF, PACK), f32),
        scratch_shapes=[pltpu.VMEM((2 * count, vis_count), f32)] * 2,
        compiler_params=pltpu.CompilerParams(vmem_limit_bytes=VMEM_BYTES),
        cost_estimate=pl.CostEstimate(
            flops=0, bytes_accessed=count * 2_500_000, transcendentals=0
        ),
        name="sky_sums",
        interpret=interpret,
    )(visibilities, offsets, scale_row)


def correct_kernel(stations_ref, *refs, pieces, skies):
    table_refs, refs = refs[:pieces], refs[pieces:]
    sky_refs, refs = refs[:skies], refs[skies:]
    factor_ref, right_ref, left_ref, out_ref, table_ref, mid_ref = refs
    count = factor_ref.shape[0]
    lane = lax.broadcasted_iota(jnp.int32, (HALF, PACK), 1)
    imag = (lane // SUB) % 2 == 1
    sign = jnp.where(imag, 1.0, -1.0)

    def up(x):
        return pltpu.roll(x, SUB, 1)

    def down(x):
        return pltpu.roll(x, PACK - SUB, 1)

    def product(a, b):
        swapped = jnp.where(imag, up(a), down(a))
        return a * jnp.where(imag, up(b), b) + sign * swapped * jnp.where(imag, b, down(b))

    held = 0
    for piece in table_refs:
        table_ref[held : held + piece.shape[0]] = piece[...]
        held += piece.shape[0]
    for s in range(count):
        first = table_ref[stations_ref[2 * s]].astype(f32)
        second = table_ref[stations_ref[2 * s + 1]].astype(f32)
        pair = product(first, -sign * second)
        per = count // skies
        sky = product(sky_refs[s // per][s % per], factor_ref[s])
        mid_ref[HALF * s : HALF * (s + 1), :] = product(sky, pair).astype(bf16)
    mid = jnp.dot(mid_ref[...], right_ref[...], preferred_element_type=f32).astype(bf16)
    for s in range(count):
        rows = mid[HALF * s : HALF * (s + 1)]
        tall = jnp.concatenate([rows[:, : 2 * SUB], rows[:, 2 * SUB :]], axis=0)
        four = jnp.dot(left_ref[...], tall, preferred_element_type=f32)
        real = four[:SUB, :SUB] - four[SUB:, SUB:]
        image = four[:SUB, SUB:] + four[SUB:, :SUB]
        out_ref[s] = jnp.concatenate(
            [real[:HALF], image[:HALF], real[HALF:], image[HALF:]], axis=1
        ).astype(bf16)


def corrected_subgrids(stations, tables, skies, factor, interpret=False):
    count = factor.shape[0]
    centred = jnp.arange(SUB, dtype=jnp.int32) - HALF
    index = jnp.arange(SUB, dtype=jnp.int32)
    angle = 2.0 * math.pi / SUB * (centred[:, None] * centred[None, :] % SUB).astype(f32)
    cols_re, cols_im = jnp.cos(angle) / SUB, -jnp.sin(angle) / SUB
    block = jnp.concatenate(
        [
            jnp.concatenate([cols_re.T, cols_im.T], axis=1),
            jnp.concatenate([-cols_im.T, cols_re.T], axis=1),
        ],
        axis=0,
    )
    right = jnp.kron(jnp.eye(2, dtype=f32), block).astype(bf16)
    angle = 2.0 * math.pi / SUB * ((index - HALF)[:, None] * centred[None, :] % SUB).astype(f32)
    left = jnp.concatenate([jnp.cos(angle) / SUB, -jnp.sin(angle) / SUB], axis=0).astype(bf16)
    rows = sum(piece.shape[0] for piece in tables)
    operands = [*tables, *skies, factor, right, left]

    def whole(operand):
        return pl.BlockSpec(operand.shape, lambda i, *_: (0,) * operand.ndim)

    return pl.pallas_call(
        functools.partial(correct_kernel, pieces=len(tables), skies=len(skies)),
        grid_spec=pltpu.PrefetchScalarGridSpec(
            num_scalar_prefetch=1,
            grid=(1,),
            in_specs=[whole(operand) for operand in operands],
            out_specs=pl.BlockSpec((count, HALF, PACK), lambda i, *_: (0, 0, 0)),
            scratch_shapes=[
                pltpu.VMEM((rows, HALF, PACK), bf16),
                pltpu.VMEM((HALF * count, PACK), bf16),
            ],
        ),
        out_shape=jax.ShapeDtypeStruct((count, HALF, PACK), bf16),
        compiler_params=pltpu.CompilerParams(vmem_limit_bytes=VMEM_BYTES),
        cost_estimate=pl.CostEstimate(flops=0, bytes_accessed=16_000_000, transcendentals=0),
        name="correct",
        interpret=interpret,
    )(stations.reshape(-1), *operands)


def add_subgrids(uv_refs, list_ref, row_ref, col_ref, held_ref, total_ref, lanes):
    first = 0
    for piece in uv_refs:
        held_ref[first : first + piece.shape[0]] = piece[...]
        first += piece.shape[0]
    lane = lax.broadcasted_iota(jnp.int32, (8, LANES), 1)
    row = lax.broadcasted_iota(jnp.int32, (8, LANES), 0)

    def one(entry, carry):
        s = list_ref[entry + 1]
        row_at, col_at = row_ref[s], col_ref[s]
        packed = held_ref[pl.ds(pl.multiple_of(s * HALF, HALF), HALF), :].astype(f32)
        tile = col_at // LANES
        offset = col_at % LANES
        shift = row_at % SUB
        base = row_at - shift

        def place(over):
            inside = lane < offset + SUB - LANES
            if not over:
                inside = (lane >= offset) & (lane < offset + SUB)
            for h in range(2):
                for part in range(2):
                    from_lane = (2 * h + part) * SUB
                    moved = pltpu.roll(packed, lax.rem(offset - from_lane + LANES, LANES), 1)
                    for group in range(2):
                        values = moved[8 * group : 8 * (group + 1)]
                        first_row = HALF * h + 8 * group
                        late = row + first_row >= shift
                        for wrapped in range(2):
                            keep = jnp.logical_and(inside, late if wrapped == 0 else ~late)
                            start = (base + SUB * wrapped + first_row) * lanes
                            start = start + 2 * (tile + over) + part
                            at = pl.ds(start, 8, stride=lanes)
                            total_ref[at, :] = total_ref[at, :] + jnp.where(keep, values, 0.0)

        place(0)

        @pl.when(offset + SUB > LANES)
        def _():
            place(1)

        return carry

    lax.fori_loop(0, list_ref[0], one, 0)


def tile_kernel(block_ref, list_ref, row_ref, col_ref, *refs, pieces, tile_rows, lanes):
    del block_ref
    uv_refs = refs[:pieces]
    out_ref, held_ref, total_ref, sems = refs[pieces:]
    rows_all = total_ref.shape[0]
    zero_rows = math.gcd(rows_all, 1024)

    def clear(i, carry):
        at = pl.ds(pl.multiple_of(i * zero_rows, zero_rows), zero_rows)
        total_ref[at, :] = jnp.zeros((zero_rows, LANES), f32)
        return carry

    lax.fori_loop(0, rows_all // zero_rows, clear, 0)
    add_subgrids(uv_refs, list_ref, row_ref, col_ref, held_ref, total_ref, lanes)
    pieces = sems.shape[0]
    size = tile_rows * lanes // pieces
    copies = [
        pltpu.make_async_copy(
            total_ref.at[pl.ds(i * size, size), :], out_ref.at[pl.ds(i * size, size), :], sems.at[i]
        )
        for i in range(pieces)
    ]
    for copy in copies:
        copy.start()
    for copy in copies:
        copy.wait()


def spill_kernel(block_ref, list_ref, row_ref, col_ref, *refs, pieces, lanes):
    del block_ref
    uv_refs = refs[:pieces]
    _, out_ref, held_ref, total_ref, sem = refs[pieces:]
    size = SUB * lanes
    kept = total_ref.at[pl.ds(size, size), :]
    copy = pltpu.make_async_copy(out_ref.at[pl.ds(0, size), :], kept, sem)
    copy.start()
    copy.wait()
    add_subgrids(uv_refs, list_ref, row_ref, col_ref, held_ref, total_ref, lanes)
    copy = pltpu.make_async_copy(kept, out_ref.at[pl.ds(0, size), :], sem)
    copy.start()
    copy.wait()


def listed(valid):
    count = valid.shape[0]
    index = jnp.arange(count, dtype=jnp.int32)
    before = jnp.sum((index[None, :] < index[:, None]) & valid[None, :], axis=1, dtype=jnp.int32)
    rank = jnp.where(valid, before, -1)
    entries = jnp.sum(
        jnp.where(rank[None, :] == index[:, None], index[None, :], 0), axis=1, dtype=jnp.int32
    )
    return jnp.concatenate([jnp.sum(valid, dtype=jnp.int32)[None], entries])


def tile_places(corners, au_index, vert_index, au_count, vert_count, spilled):
    tile_rows, tile_cols = G // au_count, G // vert_count
    col_at = corners[1] - vert_index * tile_cols
    valid = (col_at >= 0) & (col_at < tile_cols)
    row_at = corners[0] - au_index * tile_rows
    if spilled:
        row_at = (row_at + SUB + G) % G
        valid = valid & (row_at < SUB)
    return listed(valid), row_at, col_at


def uv_tile_own(uv, block, places, au_count, vert_count, interpret=False):
    count = places[1].shape[0]
    tile_rows, tile_cols = G // au_count, G // vert_count
    lanes = 2 * tile_cols // LANES
    rows = count * HALF // len(uv)
    return pl.pallas_call(
        functools.partial(tile_kernel, pieces=len(uv), tile_rows=tile_rows, lanes=lanes),
        grid_spec=pltpu.PrefetchScalarGridSpec(
            num_scalar_prefetch=4,
            grid=(1,),
            in_specs=[pl.BlockSpec((rows, PACK), lambda i, block, *_: (block[0], 0))] * len(uv),
            out_specs=pl.BlockSpec(memory_space=pl.ANY),
            scratch_shapes=[
                pltpu.VMEM((count * HALF, PACK), bf16),
                pltpu.VMEM(((tile_rows + 2 * SUB) * lanes, LANES), f32),
                pltpu.SemaphoreType.DMA((4,)),
            ],
        ),
        out_shape=jax.ShapeDtypeStruct((tile_rows * lanes, LANES), f32),
        compiler_params=pltpu.CompilerParams(vmem_limit_bytes=VMEM_BYTES),
        cost_estimate=pl.CostEstimate(
            flops=0, bytes_accessed=20 * tile_rows * tile_cols, transcendentals=0
        ),
        name="uv_tile",
        interpret=interpret,
    )(block.reshape(1), *places, *[piece.reshape(-1, PACK) for piece in uv])


def uv_tile_spill(tile, uv, block, places, au_count, vert_count, interpret=False):
    count = places[1].shape[0]
    tile_rows, tile_cols = G // au_count, G // vert_count
    lanes = 2 * tile_cols // LANES
    rows = count * HALF // len(uv)
    result = pl.pallas_call(
        functools.partial(spill_kernel, pieces=len(uv), lanes=lanes),
        grid_spec=pltpu.PrefetchScalarGridSpec(
            num_scalar_prefetch=4,
            grid=(1,),
            in_specs=[pl.BlockSpec((rows, PACK), lambda i, block, *_: (block[0], 0))] * len(uv)
            + [pl.BlockSpec(memory_space=pl.ANY)],
            out_specs=pl.BlockSpec(memory_space=pl.ANY),
            scratch_shapes=[
                pltpu.VMEM((count * HALF, PACK), bf16),
                pltpu.VMEM((3 * SUB * lanes, LANES), f32),
                pltpu.SemaphoreType.DMA(()),
            ],
        ),
        out_shape=jax.ShapeDtypeStruct(tile.shape, f32),
        input_output_aliases={4 + len(uv): 0},
        compiler_params=pltpu.CompilerParams(vmem_limit_bytes=VMEM_BYTES),
        cost_estimate=pl.CostEstimate(flops=0, bytes_accessed=8_000_000, transcendentals=0),
        name="uv_spill",
        interpret=interpret,
    )(block.reshape(1), *places, *[piece.reshape(-1, PACK) for piece in uv], tile)
    result = result.reshape(tile_rows, tile_cols // LANES, 2, LANES)
    return jnp.transpose(result, (0, 2, 1, 3)).reshape(tile_rows, 2, tile_cols)


def short_transform(values):
    count = len(values)
    if count == 1:
        return values
    even = short_transform(values[0::2])
    odd = short_transform(values[1::2])
    low, high = [], []
    for k in range(count // 2):
        re, im = odd[k]
        if k == 0:
            turned = (re, im)
        elif 4 * k == count:
            turned = (-im, re)
        elif 8 * k == count:
            root = math.sqrt(0.5)
            turned = ((re - im) * root, (re + im) * root)
        elif 8 * k == 3 * count:
            root = math.sqrt(0.5)
            turned = ((re + im) * -root, (re - im) * root)
        else:
            c, s = math.cos(2 * math.pi * k / count), math.sin(2 * math.pi * k / count)
            turned = (re * c - im * s, re * s + im * c)
        low.append((even[k][0] + turned[0], even[k][1] + turned[1]))
        high.append((even[k][0] - turned[0], even[k][1] - turned[1]))
    return low + high


def image_kernel(*refs, pieces, chunks, row_block):
    uv_refs, refs = refs[:pieces], refs[pieces:]
    corner_ref, phase_ref, columns_ref, unit_ref, count_ref, twist_ref = refs[:6]
    out_ref, uv_wide, uv_rows, here, after, shifts, left_even, left_odd, total, staged = refs[6:]
    step = pl.program_id(0)
    size = uv_rows.shape[1]
    image_rows = phase_ref.shape[1]

    def products(pair, h, left):
        at = pl.ds(2 * image_rows * h, 2 * image_rows)
        spread = lax.dot_general(
            columns_ref[at, :], uv_rows[pair], (((1,), (1,)), ((), ())), preferred_element_type=f32
        ).astype(bf16)
        turned = cmul((spread[:image_rows], spread[image_rows:]), (phase_ref[0], phase_ref[1]))
        left[h, :image_rows] = turned[0]
        left[h, image_rows:] = turned[1]

    def sums(pair, h, left, first):
        index = pair + HALF * h
        late = shifts[...] > index.astype(f32)
        table = jnp.concatenate(
            [
                jnp.where(late, after[:, t : t + LANES], here[:, t : t + LANES])
                for t in range(0, 2 * FINE, LANES)
            ],
            axis=1,
        )
        four = jnp.dot(left[h], table, preferred_element_type=f32)
        got = (
            four[:image_rows, :FINE] - four[image_rows:, FINE:],
            four[:image_rows, FINE:] + four[image_rows:, :FINE],
        )
        twist = twist_ref[pl.ds(index, 1), :]
        done = cmul(got, (twist[:, :FINE], twist[:, FINE:]))
        for part in range(2):
            total[index, part] = done[part] if first else total[index, part] + done[part]

    def chunk(first):
        held = 0
        for piece in uv_refs:

            def spread_out(s, carry, piece=piece, held=held):
                block = piece[pl.ds(pl.multiple_of(s * HALF, HALF), HALF), :]
                uv_wide[pl.ds((held + s) * (HALF + 1), HALF), :] = block.astype(f32)
                return carry

            count = piece.shape[0] // HALF
            lax.fori_loop(0, count, spread_out, 0, unroll=math.gcd(count, 8))
            held += count
        for row in range(HALF):
            uv_rows[row] = uv_wide[pl.ds(row, size, stride=HALF + 1), :].astype(bf16)
        corner = corner_ref[...]
        coarse, shift = corner // SUB, corner % SUB

        def looked_up(index, length, table):
            place = lax.broadcasted_iota(jnp.int32, (length, size), 0)
            one = (place == index).astype(f32).astype(bf16)
            return lax.dot_general(one, table, (((0,), (0,)), ((), ())), preferred_element_type=f32)

        here[...] = looked_up(coarse, FINE, unit_ref[...]).astype(bf16)
        after[...] = looked_up(lax.rem(coarse + 1, FINE), FINE, unit_ref[...]).astype(bf16)
        shifts[...] = looked_up(shift, SUB, count_ref[...])
        for h in range(2):
            products(0, h, left_even)

        def two_pairs(i, carry):
            for h in range(2):
                products(2 * i + 1, h, left_odd)
                sums(2 * i, h, left_even, first)
            for h in range(2):
                products(jnp.minimum(2 * i + 2, HALF - 1), h, left_even)
                sums(2 * i + 1, h, left_odd, first)
            return carry

        lax.fori_loop(0, HALF // 2, two_pairs, 0)

    @pl.when(step == 0)
    def _():
        chunk(True)

    if chunks > 1:

        @pl.when((step > 0) & (step < chunks))
        def _():
            chunk(False)

    @pl.when(step >= chunks)
    def _():
        first = (step - chunks) * row_block
        wide = 2 * G // LANES

        def eight_rows(group, carry):
            at = pl.ds(pl.multiple_of(first + 8 * group, 8), 8)
            for tile in range(FINE // LANES):
                lanes = pl.ds(tile * LANES, LANES)
                values = [(total[n, 0, at, lanes], total[n, 1, at, lanes]) for n in range(SUB)]
                for k, value in enumerate(short_transform(values)):
                    for part in range(2):
                        column = 2 * (k * (FINE // LANES) + tile) + part
                        staged[pl.ds(column, 8, stride=wide + 1), :] = value[part]
            for row in range(8):
                at = pl.ds(pl.multiple_of((8 * group + row) * wide, wide), wide)
                out_ref[at, :] = staged[row * (wide + 1) : row * (wide + 1) + wide, :]
            return carry

        lax.fori_loop(0, row_block // 8, eight_rows, 0)


def image_rows_of(uv, corners_all, first_row, image_rows, interpret=False):
    total = corners_all[0].shape[0]
    size = math.gcd(total, CHUNK) if len(uv) == 1 else total
    chunks = total // size
    row_block = math.gcd(image_rows, 32)
    outs = image_rows // row_block
    wide = 2 * G // LANES
    rows = first_row + jnp.arange(image_rows, dtype=jnp.int32)
    turn = 2.0 * math.pi / G
    angle = turn * (rows[:, None] * corners_all[1][None, :] % G).astype(f32)
    phase = jnp.stack([jnp.cos(angle), jnp.sin(angle)]).astype(bf16)
    angle = turn * (rows[:, None] * jnp.arange(SUB, dtype=jnp.int32)[None, :] % G).astype(f32)
    re, im = jnp.cos(angle), jnp.sin(angle)
    block = jnp.concatenate(
        [jnp.concatenate([re, -im], axis=1), jnp.concatenate([im, re], axis=1)], axis=0
    )
    columns = jnp.kron(jnp.eye(2, dtype=f32), block).astype(bf16)
    fine = jnp.arange(FINE, dtype=jnp.int32)
    angle = 2.0 * math.pi / FINE * (fine[:, None] * fine[None, :] % FINE).astype(f32)
    unit = jnp.concatenate([jnp.cos(angle), jnp.sin(angle)], axis=1).astype(bf16)
    angle = turn * (jnp.arange(SUB, dtype=jnp.int32)[:, None] * fine[None, :]).astype(f32)
    scale = 1.0 / (SUB * math.sqrt(total))
    twist = jnp.concatenate([jnp.cos(angle), jnp.sin(angle)], axis=1) * scale
    counts = jnp.broadcast_to(jnp.arange(SUB, dtype=f32)[:, None], (SUB, LANES)).astype(bf16)
    last = chunks - 1

    def chunk_of(i):
        return jnp.minimum(i, last)

    result = pl.pallas_call(
        functools.partial(image_kernel, pieces=len(uv), chunks=chunks, row_block=row_block),
        grid=(chunks + outs,),
        in_specs=[
            *[pl.BlockSpec((size * HALF // len(uv), PACK), lambda i: (chunk_of(i), 0))] * len(uv),
            pl.BlockSpec((1, size), lambda i: (0, chunk_of(i))),
            pl.BlockSpec((2, image_rows, size), lambda i: (0, 0, chunk_of(i))),
            pl.BlockSpec(columns.shape, lambda i: (0, 0)),
            pl.BlockSpec(unit.shape, lambda i: (0, 0)),
            pl.BlockSpec(counts.shape, lambda i: (0, 0)),
            pl.BlockSpec(twist.shape, lambda i: (0, 0)),
        ],
        out_specs=pl.BlockSpec(
            (row_block * wide, LANES), lambda i: (jnp.maximum(i - chunks, 0), 0)
        ),
        out_shape=jax.ShapeDtypeStruct((image_rows * wide, LANES), f32),
        scratch_shapes=[
            pltpu.VMEM((size * (HALF + 1) + HALF, PACK), f32),
            pltpu.VMEM((HALF, size, PACK), bf16),
            pltpu.VMEM((size, 2 * FINE), bf16),
            pltpu.VMEM((size, 2 * FINE), bf16),
            pltpu.VMEM((size, LANES), f32),
            pltpu.VMEM((2, 2 * image_rows, size), bf16),
            pltpu.VMEM((2, 2 * image_rows, size), bf16),
            pltpu.VMEM((SUB, 2, image_rows, FINE), f32),
            pltpu.VMEM((8 * (wide + 1) + wide, LANES), f32),
        ],
        compiler_params=pltpu.CompilerParams(vmem_limit_bytes=VMEM_BYTES),
        name="image",
        interpret=interpret,
    )(
        *[piece.reshape(-1, PACK) for piece in uv], corners_all[0].reshape(1, total),
        phase, columns, unit, counts, twist,
    )
    result = result.reshape(image_rows, G // LANES, 2, LANES)
    return jnp.transpose(result, (0, 2, 1, 3)).reshape(image_rows, 2, G)


def packed_beams(beam_terms):
    count = beam_terms.shape[0]
    parts = beam_terms.reshape(count, 2, 2, HALF, SUB)
    return jnp.transpose(parts, (0, 3, 2, 1, 4)).reshape(count, HALF, PACK)


def pixel_factor(screen_depth, shift, vis_count):
    lane = jnp.arange(PACK, dtype=jnp.int32)
    col = lane % SUB
    imag = (lane // SUB) % 2
    row = jnp.arange(HALF, dtype=jnp.int32)[:, None] + (lane // (2 * SUB) * HALF)[None, :]

    def taper(x):
        return 1.0 - ((2.0 * x.astype(f32) + 1.0 - SUB) / SUB) ** 2

    def angle_sq(x):
        return ((x - HALF).astype(f32) * (field_view / SUB)) ** 2

    weight = taper(row) * taper(col) / math.sqrt(vis_count)
    turns = shift[:, None, None] * (row - HALF) % SUB
    angle = (
        -math.pi * screen_depth[:, None, None] * (angle_sq(row) + angle_sq(col))
        + 2.0 * math.pi / SUB * turns.astype(f32)
        - 0.5 * math.pi * imag.astype(f32)
    )
    return jnp.cos(angle) * weight


def from_partner(value, axis, mask):
    count = lax.axis_size(axis)
    return lax.ppermute(value, axis, [(i, i ^ mask) for i in range(count)])


def z_line(own):
    vert_count = lax.axis_size("vert")
    line = [own] + [from_partner(own, "vert", 2 * mask) for mask in range(1, vert_count // 2)]
    return jnp.concatenate(line, axis=0)


def au_lines(line):
    return [line] + [from_partner(line, "au", mask) for mask in range(1, lax.axis_size("au"))]


def with_core(lines):
    return [piece for line in lines for piece in (line, from_partner(line, "vert", 1))]


def whole_gather(own):
    return [lax.all_gather(own, ("au", "vert"), axis=0, tiled=True)]


def gathered_place(owner, by_mask):
    if not by_mask:
        return owner
    vert_count = lax.axis_size("vert")
    au_mask = (owner // vert_count) ^ lax.axis_index("au")
    vert_mask = (owner % vert_count) ^ lax.axis_index("vert")
    return au_mask * vert_count + vert_mask % 2 * (vert_count // 2) + vert_mask // 2


def coded_corners(corners):
    digits = jnp.stack([corners[:, 0] // 128, corners[:, 0] % 128, corners[:, 1] // 128, corners[:, 1] % 128])
    flat = digits.astype(f32).astype(bf16).reshape(-1)
    return jnp.pad(flat, (0, HALF * PACK - flat.shape[0])).reshape(1, HALF, PACK)


def decoded_corners(blocks, count):
    digits = blocks.reshape(blocks.shape[0], HALF * PACK).astype(jnp.int32)
    high_row, low_row, high_col, low_col = [
        digits[:, i * count : (i + 1) * count].reshape(-1) for i in range(4)
    ]
    return (high_row * 128 + low_row, high_col * 128 + low_col)


def on_device(
    visibilities, baseline_offsets, channel_scale, screen_depth, stations, corners, beam_terms
):
    au_count = lax.axis_size("au")
    vert_count = lax.axis_size("vert")
    au_index, vert_index = lax.axis_index("au"), lax.axis_index("vert")
    image_rows = G // (au_count * vert_count)
    count, _, vis_count = visibilities.shape
    own_stations = beam_terms.shape[0]
    held = au_count * vert_count * count * HALF * PACK
    by_mask = held <= MASK_VALUES

    sent = jnp.concatenate([packed_beams(beam_terms), coded_corners(corners)], axis=0)
    offsets = baseline_offsets.reshape(2 * count, -1)
    scale_row = jnp.tile(channel_scale, baseline_offsets.shape[2]).reshape(1, vis_count)
    part = math.gcd(count, 8)
    skies = [sky_sums(visibilities, offsets, scale_row, 0, part)]
    if by_mask:
        line = z_line(sent)
        line, offsets, skies[0] = lax.optimization_barrier((line, offsets, skies[0]))
    for s in range(part, count, part):
        skies.append(sky_sums(visibilities, offsets, scale_row, s, part))
    factor = pixel_factor(screen_depth, corners[:, 0] % SUB, vis_count)
    if by_mask:
        lines = au_lines(line)
        lines, skies = lax.optimization_barrier((lines, skies))
        tables = with_core(lines)
    else:
        tables = whole_gather(sent)
    coded = [
        piece.reshape(-1, own_stations + 1, HALF, PACK)[:, own_stations] for piece in tables
    ]
    corners_all = decoded_corners(jnp.concatenate(coded, axis=0), count)
    owners = stations // own_stations
    station_rows = gathered_place(owners, by_mask) * (own_stations + 1) + stations % own_stations
    uv_own = corrected_subgrids(station_rows, tables, skies, factor)

    per_row = vert_count * count

    def row_place(index):
        return gathered_place(index * vert_count + vert_index, by_mask) // vert_count

    def places_of(place, spilled):
        chosen = [lax.dynamic_slice_in_dim(x, place * per_row, per_row) for x in corners_all]
        return tile_places(chosen, au_index, vert_index, au_count, vert_count, spilled)

    own_place = row_place(au_index)
    before_place = row_place(lax.rem(au_index + au_count - 1, au_count))
    own_list, spill_list = places_of(own_place, False), places_of(before_place, True)
    if by_mask:
        lines = au_lines(z_line(uv_own))
        own_row = with_core(lines[:1])
        tile = uv_tile_own(own_row, own_place, own_list, au_count, vert_count)
        lines, own_row, tile = lax.optimization_barrier((lines, own_row, tile))
        uv = own_row + with_core(lines[1:])
        before = [
            lax.select_n(before_place, *uv[core::2]) if au_count > 2 else uv[core + 2]
            for core in range(2)
        ]
        before_block = jnp.zeros((), jnp.int32)
    else:
        uv = before = whole_gather(uv_own)
        tile = uv_tile_own(uv, own_place, own_list, au_count, vert_count)
        before_block = before_place
    gridded = uv_tile_spill(tile, before, before_block, spill_list, au_count, vert_count)
    first_row = (au_index * vert_count + vert_index) * image_rows
    dirty_image = image_rows_of(uv, corners_all, first_row, image_rows)
    return (gridded, dirty_image)


def solution(mesh):
    return jax.shard_map(
        on_device,
        mesh=mesh,
        in_specs=(
            P(("au", "vert"), None, None),
            P(("au", "vert"), None, None),
            P(),
            P(("au", "vert")),
            P(("au", "vert"), None),
            P(("au", "vert"), None),
            P(("au", "vert"), None, None),
        ),
        out_specs=(P("au", None, "vert"), P(("au", "vert"), None, None)),
        check_vma=False,
    )
```

```python
import functools
import math

import jax
import jax.numpy as jnp
import numpy as np
from jax import lax
from jax.experimental import pallas as pl
from jax.experimental.pallas import tpu as pltpu
from jax.sharding import PartitionSpec as P

G = 8192
SUB = 32
HALF = SUB // 2
PACK = 4 * SUB
LANES = 128
FINE = G // SUB
CHUNK = 768
MASK_VALUES = 1 << 22
field_view = 0.1
bf16 = jnp.bfloat16
f32 = jnp.float32
VMEM_BYTES = 58 * 1024 * 1024


def cmul(a, b):
    return (a[0] * b[0] - a[1] * b[1], a[0] * b[1] + a[1] * b[0])


def conj(a):
    return (a[0], -a[1])


def sky_kernel(vis_ref, offset_ref, scale_ref, out_ref, power_ref):
    count, _, vis_count = vis_ref.shape
    times = offset_ref.shape[1]
    step = math.gcd(vis_count, 256)
    row = lax.broadcasted_iota(jnp.int32, (8, step), 0)
    bits = [(row >> bit) % 2 == 1 for bit in range(3)]

    offsets = offset_ref[...]
    parts = []
    for _ in range(3):
        parts.append(offsets.astype(bf16))
        offsets = offsets - parts[-1].astype(f32)
    channels = vis_count // times
    repeats = max(1, LANES // channels)
    scale = jnp.concatenate([scale_ref[...]] * repeats, axis=1)
    width = math.gcd(vis_count, 512)
    scale = jnp.concatenate([scale] * (width // (repeats * channels)), axis=1)
    for start in range(0, vis_count, width):
        at = pl.ds(start, width)
        time = lax.broadcasted_iota(jnp.int32, (times, width), 0)
        place = lax.broadcasted_iota(jnp.int32, (times, width), 1) + start
        one = (place // channels == time).astype(f32).astype(bf16)
        shifts = sum(jnp.dot(part, one, preferred_element_type=f32) for part in parts)
        half = (math.pi / SUB) * (shifts * scale)
        square = half * half
        sine, cosine = 1.0, 1.0
        for term in (12, 10, 8, 6, 4, 2):
            sine = 1.0 - square * (1.0 / (term * (term + 1))) * sine
            cosine = 1.0 - square * (1.0 / (term * (term - 1))) * cosine
        sine = sine * half
        power = (1.0 - 2.0 * sine * sine, 2.0 * sine * cosine)
        for bit in range(5):
            power_ref[bit, 0, :, at] = power[0]
            power_ref[bit, 1, :, at] = power[1]
            power = (power[0] * power[0] - power[1] * power[1], 2.0 * power[0] * power[1])

    def powers(row, at, extra):
        z = [
            tuple(
                jnp.broadcast_to(power_ref[bit, part, pl.ds(row, 1), at], (8, step))
                for part in range(2)
            )
            for bit in range(5)
        ]
        low = (jnp.where(bits[0], z[0][0], 1.0), jnp.where(bits[0], z[0][1], 0.0))
        for bit in (1, 2):
            more = cmul(low, z[bit])
            low = (jnp.where(bits[bit], more[0], low[0]), jnp.where(bits[bit], more[1], low[1]))
        if extra is not None:
            low = cmul(low, extra)
        blocks = [cmul(low, conj(z[4])), cmul(low, conj(z[3])), low, cmul(low, z[3])]
        return jnp.concatenate([block[part] for part in range(2) for block in blocks], axis=0).astype(bf16)

    def one_subgrid(s):
        both = jnp.zeros((2 * SUB, 2 * SUB), f32)
        for start in range(0, vis_count, step):
            at = pl.ds(start, step)
            vis = tuple(
                jnp.broadcast_to(vis_ref[s, part : part + 1, at].astype(f32), (8, step))
                for part in range(2)
            )
            left = powers(2 * s, at, vis)
            right = powers(2 * s + 1, at, None)
            both += lax.dot_general(
                left, right, (((1,), (1,)), ((), ())), preferred_element_type=f32
            )
        real = both[:SUB, :SUB] - both[SUB:, SUB:]
        image = both[:SUB, SUB:] + both[SUB:, :SUB]
        out_ref[s] = jnp.concatenate(
            [real[:HALF], image[:HALF], real[HALF:], image[HALF:]], axis=1
        )

    def some(i, carry):
        for k in range(math.gcd(count, 2)):
            one_subgrid(i * math.gcd(count, 2) + k)
        return carry

    lax.fori_loop(0, count // math.gcd(count, 2), some, 0)


def sky_sums(visibilities, offsets, scale_row, first, count, interpret=False):
    vis_count = visibilities.shape[2]
    times = offsets.shape[1]
    at = first // count
    return pl.pallas_call(
        sky_kernel,
        grid=(1,),
        in_specs=[
            pl.BlockSpec((count, 2, vis_count), lambda i: (at, 0, 0)),
            pl.BlockSpec((2 * count, times), lambda i: (at, 0)),
            pl.BlockSpec(scale_row.shape, lambda i: (0, 0)),
        ],
        out_specs=pl.BlockSpec((count, HALF, PACK), lambda i: (0, 0, 0)),
        out_shape=jax.ShapeDtypeStruct((count, HALF, PACK), f32),
        scratch_shapes=[pltpu.VMEM((5, 2, 2 * count, vis_count), f32)],
        compiler_params=pltpu.CompilerParams(vmem_limit_bytes=VMEM_BYTES),
        cost_estimate=pl.CostEstimate(
            flops=0, bytes_accessed=count * 2_500_000, transcendentals=0
        ),
        name="sky_sums",
        interpret=interpret,
    )(visibilities, offsets, scale_row)


def correct_kernel(stations_ref, *refs, pieces, skies):
    table_refs, refs = refs[:pieces], refs[pieces:]
    sky_refs, refs = refs[:skies], refs[skies:]
    factor_ref, right_ref, left_ref, out_ref, table_ref, mid_ref = refs
    count = factor_ref.shape[0]
    lane = lax.broadcasted_iota(jnp.int32, (HALF, PACK), 1)
    imag = (lane // SUB) % 2 == 1
    sign = jnp.where(imag, 1.0, -1.0)

    def up(x):
        return pltpu.roll(x, SUB, 1)

    def down(x):
        return pltpu.roll(x, PACK - SUB, 1)

    def product(a, b):
        swapped = jnp.where(imag, up(a), down(a))
        return a * jnp.where(imag, up(b), b) + sign * swapped * jnp.where(imag, b, down(b))

    held = 0
    for piece in table_refs:
        table_ref[held : held + piece.shape[0]] = piece[...]
        held += piece.shape[0]
    for s in range(count):
        first = table_ref[stations_ref[2 * s]].astype(f32)
        second = table_ref[stations_ref[2 * s + 1]].astype(f32)
        pair = product(first, -sign * second)
        per = count // skies
        sky = product(sky_refs[s // per][s % per], factor_ref[s])
        mid_ref[HALF * s : HALF * (s + 1), :] = product(sky, pair).astype(bf16)
    mid = jnp.dot(mid_ref[...], right_ref[...], preferred_element_type=f32).astype(bf16)
    for s in range(count):
        rows = mid[HALF * s : HALF * (s + 1)]
        tall = jnp.concatenate([rows[:, : 2 * SUB], rows[:, 2 * SUB :]], axis=0)
        four = jnp.dot(left_ref[...], tall, preferred_element_type=f32)
        real = four[:SUB, :SUB] - four[SUB:, SUB:]
        image = four[:SUB, SUB:] + four[SUB:, :SUB]
        out_ref[s] = jnp.concatenate(
            [real[:HALF], image[:HALF], real[HALF:], image[HALF:]], axis=1
        ).astype(bf16)


def corrected_subgrids(stations, tables, skies, factor, interpret=False):
    count = factor.shape[0]
    centred = np.arange(SUB) - HALF
    angle = 2.0 * math.pi / SUB * (centred[:, None] * centred[None, :] % SUB)
    re, im = np.cos(angle) / SUB, -np.sin(angle) / SUB
    right = jnp.asarray(np.kron(np.eye(2), np.block([[re, im], [-im, re]])), bf16)
    left = jnp.asarray(np.concatenate([re, im], axis=0), bf16)
    rows = sum(piece.shape[0] for piece in tables)
    operands = [*tables, *skies, factor, right, left]

    def whole(operand):
        return pl.BlockSpec(operand.shape, lambda i, *_: (0,) * operand.ndim)

    return pl.pallas_call(
        functools.partial(correct_kernel, pieces=len(tables), skies=len(skies)),
        grid_spec=pltpu.PrefetchScalarGridSpec(
            num_scalar_prefetch=1,
            grid=(1,),
            in_specs=[whole(operand) for operand in operands],
            out_specs=pl.BlockSpec((count, HALF, PACK), lambda i, *_: (0, 0, 0)),
            scratch_shapes=[
                pltpu.VMEM((rows, HALF, PACK), bf16),
                pltpu.VMEM((HALF * count, PACK), bf16),
            ],
        ),
        out_shape=jax.ShapeDtypeStruct((count, HALF, PACK), bf16),
        compiler_params=pltpu.CompilerParams(vmem_limit_bytes=VMEM_BYTES),
        cost_estimate=pl.CostEstimate(flops=0, bytes_accessed=16_000_000, transcendentals=0),
        name="correct",
        interpret=interpret,
    )(stations.reshape(-1), *operands)


def add_subgrids(uv_refs, list_ref, row_ref, col_ref, held_ref, total_ref, lanes):
    first = 0
    for piece in uv_refs:
        held_ref[first : first + piece.shape[0]] = piece[...]
        first += piece.shape[0]
    lane = lax.broadcasted_iota(jnp.int32, (8, LANES), 1)
    row = lax.broadcasted_iota(jnp.int32, (8, LANES), 0)

    def one(entry, carry):
        s = list_ref[entry + 1]
        row_at, col_at = row_ref[s], col_ref[s]
        packed = held_ref[pl.ds(pl.multiple_of(s * HALF, HALF), HALF), :].astype(f32)
        tile = col_at // LANES
        offset = col_at % LANES
        shift = row_at % SUB
        base = row_at - shift

        def place(over):
            inside = lane < offset + SUB - LANES
            if not over:
                inside = (lane >= offset) & (lane < offset + SUB)
            for h in range(2):
                for part in range(2):
                    from_lane = (2 * h + part) * SUB
                    moved = pltpu.roll(packed, lax.rem(offset - from_lane + LANES, LANES), 1)
                    for group in range(2):
                        values = moved[8 * group : 8 * (group + 1)]
                        first_row = HALF * h + 8 * group
                        late = row + first_row >= shift
                        for wrapped in range(2):
                            keep = jnp.logical_and(inside, late if wrapped == 0 else ~late)
                            start = (base + SUB * wrapped + first_row) * lanes
                            start = start + 2 * (tile + over) + part
                            at = pl.ds(start, 8, stride=lanes)
                            total_ref[at, :] = total_ref[at, :] + jnp.where(keep, values, 0.0)

        place(0)

        @pl.when(offset + SUB > LANES)
        def _():
            place(1)

        return carry

    lax.fori_loop(0, list_ref[0], one, 0)


def tile_kernel(block_ref, list_ref, row_ref, col_ref, *refs, pieces, tile_rows, lanes):
    del block_ref
    uv_refs = refs[:pieces]
    out_ref, held_ref, total_ref, sems = refs[pieces:]
    rows_all = total_ref.shape[0]
    zero_rows = math.gcd(rows_all, 1024)

    def clear(i, carry):
        at = pl.ds(pl.multiple_of(i * zero_rows, zero_rows), zero_rows)
        total_ref[at, :] = jnp.zeros((zero_rows, LANES), f32)
        return carry

    lax.fori_loop(0, rows_all // zero_rows, clear, 0)
    add_subgrids(uv_refs, list_ref, row_ref, col_ref, held_ref, total_ref, lanes)
    pieces = sems.shape[0]
    size = tile_rows * lanes // pieces
    copies = [
        pltpu.make_async_copy(
            total_ref.at[pl.ds(i * size, size), :], out_ref.at[pl.ds(i * size, size), :], sems.at[i]
        )
        for i in range(pieces)
    ]
    for copy in copies:
        copy.start()
    for copy in copies:
        copy.wait()


def spill_kernel(block_ref, list_ref, row_ref, col_ref, *refs, pieces, lanes):
    del block_ref
    uv_refs = refs[:pieces]
    _, out_ref, held_ref, total_ref, sem = refs[pieces:]
    size = SUB * lanes
    kept = total_ref.at[pl.ds(size, size), :]
    copy = pltpu.make_async_copy(out_ref.at[pl.ds(0, size), :], kept, sem)
    copy.start()
    copy.wait()
    add_subgrids(uv_refs, list_ref, row_ref, col_ref, held_ref, total_ref, lanes)
    copy = pltpu.make_async_copy(kept, out_ref.at[pl.ds(0, size), :], sem)
    copy.start()
    copy.wait()


def listed(valid):
    count = valid.shape[0]
    index = jnp.arange(count, dtype=jnp.int32)
    before = jnp.sum((index[None, :] < index[:, None]) & valid[None, :], axis=1, dtype=jnp.int32)
    rank = jnp.where(valid, before, -1)
    entries = jnp.sum(
        jnp.where(rank[None, :] == index[:, None], index[None, :], 0), axis=1, dtype=jnp.int32
    )
    return jnp.concatenate([jnp.sum(valid, dtype=jnp.int32)[None], entries])


def tile_places(corners, au_index, vert_index, au_count, vert_count, spilled):
    tile_rows, tile_cols = G // au_count, G // vert_count
    col_at = corners[1] - vert_index * tile_cols
    valid = (col_at >= 0) & (col_at < tile_cols)
    row_at = corners[0] - au_index * tile_rows
    if spilled:
        row_at = (row_at + SUB + G) % G
        valid = valid & (row_at < SUB)
    return listed(valid), row_at, col_at


def uv_tile_own(uv, block, places, au_count, vert_count, interpret=False):
    count = places[1].shape[0]
    tile_rows, tile_cols = G // au_count, G // vert_count
    lanes = 2 * tile_cols // LANES
    rows = count * HALF // len(uv)
    return pl.pallas_call(
        functools.partial(tile_kernel, pieces=len(uv), tile_rows=tile_rows, lanes=lanes),
        grid_spec=pltpu.PrefetchScalarGridSpec(
            num_scalar_prefetch=4,
            grid=(1,),
            in_specs=[pl.BlockSpec((rows, PACK), lambda i, block, *_: (block[0], 0))] * len(uv),
            out_specs=pl.BlockSpec(memory_space=pl.ANY),
            scratch_shapes=[
                pltpu.VMEM((count * HALF, PACK), bf16),
                pltpu.VMEM(((tile_rows + 2 * SUB) * lanes, LANES), f32),
                pltpu.SemaphoreType.DMA((4,)),
            ],
        ),
        out_shape=jax.ShapeDtypeStruct((tile_rows * lanes, LANES), f32),
        compiler_params=pltpu.CompilerParams(vmem_limit_bytes=VMEM_BYTES),
        cost_estimate=pl.CostEstimate(
            flops=0, bytes_accessed=20 * tile_rows * tile_cols, transcendentals=0
        ),
        name="uv_tile",
        interpret=interpret,
    )(block.reshape(1), *places, *[piece.reshape(-1, PACK) for piece in uv])


def uv_tile_spill(tile, uv, block, places, au_count, vert_count, interpret=False):
    count = places[1].shape[0]
    tile_rows, tile_cols = G // au_count, G // vert_count
    lanes = 2 * tile_cols // LANES
    rows = count * HALF // len(uv)
    result = pl.pallas_call(
        functools.partial(spill_kernel, pieces=len(uv), lanes=lanes),
        grid_spec=pltpu.PrefetchScalarGridSpec(
            num_scalar_prefetch=4,
            grid=(1,),
            in_specs=[pl.BlockSpec((rows, PACK), lambda i, block, *_: (block[0], 0))] * len(uv)
            + [pl.BlockSpec(memory_space=pl.ANY)],
            out_specs=pl.BlockSpec(memory_space=pl.ANY),
            scratch_shapes=[
                pltpu.VMEM((count * HALF, PACK), bf16),
                pltpu.VMEM((3 * SUB * lanes, LANES), f32),
                pltpu.SemaphoreType.DMA(()),
            ],
        ),
        out_shape=jax.ShapeDtypeStruct(tile.shape, f32),
        input_output_aliases={4 + len(uv): 0},
        compiler_params=pltpu.CompilerParams(vmem_limit_bytes=VMEM_BYTES),
        cost_estimate=pl.CostEstimate(flops=0, bytes_accessed=8_000_000, transcendentals=0),
        name="uv_spill",
        interpret=interpret,
    )(block.reshape(1), *places, *[piece.reshape(-1, PACK) for piece in uv], tile)
    result = result.reshape(tile_rows, tile_cols // LANES, 2, LANES)
    return jnp.transpose(result, (0, 2, 1, 3)).reshape(tile_rows, 2, tile_cols)


def short_transform(values):
    count = len(values)
    if count == 1:
        return values
    even = short_transform(values[0::2])
    odd = short_transform(values[1::2])
    low, high = [], []
    for k in range(count // 2):
        re, im = odd[k]
        if k == 0:
            turned = (re, im)
        elif 4 * k == count:
            turned = (-im, re)
        elif 8 * k == count:
            root = math.sqrt(0.5)
            turned = ((re - im) * root, (re + im) * root)
        elif 8 * k == 3 * count:
            root = math.sqrt(0.5)
            turned = ((re + im) * -root, (re - im) * root)
        else:
            c, s = math.cos(2 * math.pi * k / count), math.sin(2 * math.pi * k / count)
            turned = (re * c - im * s, re * s + im * c)
        low.append((even[k][0] + turned[0], even[k][1] + turned[1]))
        high.append((even[k][0] - turned[0], even[k][1] - turned[1]))
    return low + high


def image_kernel(*refs, pieces, chunks, row_block):
    uv_refs, refs = refs[:pieces], refs[pieces:]
    corner_ref, phase_ref, columns_ref, unit_ref, count_ref, twist_ref = refs[:6]
    out_ref, uv_wide, uv_rows, here, after, shifts, left_even, left_odd, total, staged = refs[6:]
    step = pl.program_id(0)
    size = uv_rows.shape[1]
    image_rows = phase_ref.shape[1]

    def products(pair, h, left):
        at = pl.ds(2 * image_rows * h, 2 * image_rows)
        spread = lax.dot_general(
            columns_ref[at, :], uv_rows[pair], (((1,), (1,)), ((), ())), preferred_element_type=f32
        ).astype(bf16)
        turned = cmul((spread[:image_rows], spread[image_rows:]), (phase_ref[0], phase_ref[1]))
        left[h, :image_rows] = turned[0]
        left[h, image_rows:] = turned[1]

    def sums_of(index, left):
        late = shifts[...] > index.astype(f32)
        table = jnp.concatenate(
            [
                jnp.where(late, after[:, t : t + LANES], here[:, t : t + LANES])
                for t in range(0, 2 * FINE, LANES)
            ],
            axis=1,
        )
        four = jnp.dot(left, table, preferred_element_type=f32)
        got = (
            four[:image_rows, :FINE] - four[image_rows:, FINE:],
            four[:image_rows, FINE:] + four[image_rows:, :FINE],
        )
        twist = twist_ref[pl.ds(index, 1), :]
        return cmul(got, (twist[:, :FINE], twist[:, FINE:]))

    def sums(pair, left, first):
        low, high = sums_of(pair, left[0]), sums_of(pair + HALF, left[1])
        turn = twist_ref[pl.ds(SUB + pair, 1), :]
        even = (low[0] + high[0], low[1] + high[1])
        odd = cmul((low[0] - high[0], low[1] - high[1]), (turn[:, :FINE], turn[:, FINE:]))
        for half, done in enumerate((even, odd)):
            for part in range(2):
                at = (half * HALF + pair, part)
                total[at] = done[part] if first else total[at] + done[part]

    def chunk(first):
        held = 0
        for piece in uv_refs:

            def spread_out(s, carry, piece=piece, held=held):
                block = piece[pl.ds(pl.multiple_of(s * HALF, HALF), HALF), :]
                uv_wide[pl.ds((held + s) * (HALF + 1), HALF), :] = block.astype(f32)
                return carry

            count = piece.shape[0] // HALF
            lax.fori_loop(0, count, spread_out, 0, unroll=math.gcd(count, 8))
            held += count
        for row in range(HALF):
            uv_rows[row] = uv_wide[pl.ds(row, size, stride=HALF + 1), :].astype(bf16)
        corner = corner_ref[...]
        coarse, shift = corner // SUB, corner % SUB

        def looked_up(index, length, table):
            place = lax.broadcasted_iota(jnp.int32, (length, size), 0)
            one = (place == index).astype(f32).astype(bf16)
            return lax.dot_general(one, table, (((0,), (0,)), ((), ())), preferred_element_type=f32)

        here[...] = looked_up(coarse, FINE, unit_ref[...]).astype(bf16)
        after[...] = looked_up(lax.rem(coarse + 1, FINE), FINE, unit_ref[...]).astype(bf16)
        shifts[...] = looked_up(shift, SUB, count_ref[...])
        for h in range(2):
            products(0, h, left_even)

        def two_pairs(i, carry):
            for h in range(2):
                products(2 * i + 1, h, left_odd)
            sums(2 * i, left_even, first)
            for h in range(2):
                products(jnp.minimum(2 * i + 2, HALF - 1), h, left_even)
            sums(2 * i + 1, left_odd, first)
            return carry

        lax.fori_loop(0, HALF // 2, two_pairs, 0)

    @pl.when(step == 0)
    def _():
        chunk(True)

    if chunks > 1:

        @pl.when((step > 0) & (step < chunks))
        def _():
            chunk(False)

    @pl.when(step >= chunks)
    def _():
        first = (step - chunks) * row_block
        wide = 2 * G // LANES

        def eight_rows(group, carry):
            at = pl.ds(pl.multiple_of(first + 8 * group, 8), 8)
            for tile in range(FINE // LANES):
                lanes = pl.ds(tile * LANES, LANES)
                for half in range(2):
                    values = [
                        (total[half * HALF + n, 0, at, lanes], total[half * HALF + n, 1, at, lanes])
                        for n in range(HALF)
                    ]
                    for k, value in enumerate(short_transform(values)):
                        for part in range(2):
                            column = 2 * ((2 * k + half) * (FINE // LANES) + tile) + part
                            staged[pl.ds(column, 8, stride=wide + 1), :] = value[part]
            for row in range(8):
                at = pl.ds(pl.multiple_of((8 * group + row) * wide, wide), wide)
                out_ref[at, :] = staged[row * (wide + 1) : row * (wide + 1) + wide, :]
            return carry

        lax.fori_loop(0, row_block // 8, eight_rows, 0)


def image_rows_of(uv, corners_all, first_row, image_rows, interpret=False):
    total = corners_all[0].shape[0]
    size = math.gcd(total, CHUNK) if len(uv) == 1 else total
    chunks = total // size
    row_block = math.gcd(image_rows, 32)
    outs = image_rows // row_block
    wide = 2 * G // LANES
    rows = first_row + jnp.arange(image_rows, dtype=jnp.int32)
    turn = 2.0 * math.pi / G
    angle = turn * (rows[:, None] * corners_all[1][None, :] % G).astype(f32)
    phase = jnp.stack([jnp.cos(angle), jnp.sin(angle)]).astype(bf16)
    angle = turn * (rows[:, None] * jnp.arange(SUB, dtype=jnp.int32)[None, :] % G).astype(f32)
    re, im = jnp.cos(angle), jnp.sin(angle)
    block = jnp.concatenate(
        [jnp.concatenate([re, -im], axis=1), jnp.concatenate([im, re], axis=1)], axis=0
    )
    columns = jnp.kron(jnp.eye(2, dtype=f32), block).astype(bf16)
    fine = np.arange(FINE)
    angle = 2.0 * math.pi / FINE * (fine[:, None] * fine[None, :] % FINE)
    unit = jnp.asarray(np.concatenate([np.cos(angle), np.sin(angle)], axis=1), bf16)
    scale = 1.0 / (SUB * math.sqrt(total))
    angle = 2.0 * math.pi / G * (np.arange(SUB)[:, None] * fine[None, :])
    twist = np.concatenate([np.cos(angle), np.sin(angle)], axis=1) * scale
    angle = 2.0 * math.pi / SUB * np.arange(HALF)[:, None] + 0.0 * fine
    turn_half = np.concatenate([np.cos(angle), np.sin(angle)], axis=1)
    twist = jnp.asarray(np.concatenate([twist, turn_half], axis=0), f32)
    counts = jnp.asarray(np.broadcast_to(np.arange(SUB)[:, None], (SUB, LANES)), bf16)
    last = chunks - 1

    def chunk_of(i):
        return jnp.minimum(i, last)

    result = pl.pallas_call(
        functools.partial(image_kernel, pieces=len(uv), chunks=chunks, row_block=row_block),
        grid=(chunks + outs,),
        in_specs=[
            *[pl.BlockSpec((size * HALF // len(uv), PACK), lambda i: (chunk_of(i), 0))] * len(uv),
            pl.BlockSpec((1, size), lambda i: (0, chunk_of(i))),
            pl.BlockSpec((2, image_rows, size), lambda i: (0, 0, chunk_of(i))),
            pl.BlockSpec(columns.shape, lambda i: (0, 0)),
            pl.BlockSpec(unit.shape, lambda i: (0, 0)),
            pl.BlockSpec(counts.shape, lambda i: (0, 0)),
            pl.BlockSpec(twist.shape, lambda i: (0, 0)),
        ],
        out_specs=pl.BlockSpec(
            (row_block * wide, LANES), lambda i: (jnp.maximum(i - chunks, 0), 0)
        ),
        out_shape=jax.ShapeDtypeStruct((image_rows * wide, LANES), f32),
        scratch_shapes=[
            pltpu.VMEM((size * (HALF + 1) + HALF, PACK), f32),
            pltpu.VMEM((HALF, size, PACK), bf16),
            pltpu.VMEM((size, 2 * FINE), bf16),
            pltpu.VMEM((size, 2 * FINE), bf16),
            pltpu.VMEM((size, LANES), f32),
            pltpu.VMEM((2, 2 * image_rows, size), bf16),
            pltpu.VMEM((2, 2 * image_rows, size), bf16),
            pltpu.VMEM((SUB, 2, image_rows, FINE), f32),
            pltpu.VMEM((8 * (wide + 1) + wide, LANES), f32),
        ],
        compiler_params=pltpu.CompilerParams(vmem_limit_bytes=VMEM_BYTES),
        name="image",
        interpret=interpret,
    )(
        *[piece.reshape(-1, PACK) for piece in uv], corners_all[0].reshape(1, total),
        phase, columns, unit, counts, twist,
    )
    result = result.reshape(image_rows, G // LANES, 2, LANES)
    return jnp.transpose(result, (0, 2, 1, 3)).reshape(image_rows, 2, G)


def packed_beams(beam_terms):
    count = beam_terms.shape[0]
    parts = beam_terms.reshape(count, 2, 2, HALF, SUB)
    return jnp.transpose(parts, (0, 3, 2, 1, 4)).reshape(count, HALF, PACK)


def pixel_factor(screen_depth, shift, vis_count):
    lane = jnp.arange(PACK, dtype=jnp.int32)
    col = lane % SUB
    imag = (lane // SUB) % 2
    row = jnp.arange(HALF, dtype=jnp.int32)[:, None] + (lane // (2 * SUB) * HALF)[None, :]

    def taper(x):
        return 1.0 - ((2.0 * x.astype(f32) + 1.0 - SUB) / SUB) ** 2

    def angle_sq(x):
        return ((x - HALF).astype(f32) * (field_view / SUB)) ** 2

    weight = taper(row) * taper(col) / math.sqrt(vis_count)
    turns = shift[:, None, None] * (row - HALF) % SUB
    angle = (
        -math.pi * screen_depth[:, None, None] * (angle_sq(row) + angle_sq(col))
        + 2.0 * math.pi / SUB * turns.astype(f32)
        - 0.5 * math.pi * imag.astype(f32)
    )
    return jnp.cos(angle) * weight


def from_partner(value, axis, mask):
    count = lax.axis_size(axis)
    return lax.ppermute(value, axis, [(i, i ^ mask) for i in range(count)])


def z_line(own):
    vert_count = lax.axis_size("vert")
    line = [own] + [from_partner(own, "vert", 2 * mask) for mask in range(1, vert_count // 2)]
    return jnp.concatenate(line, axis=0)


def au_lines(line):
    return [line] + [from_partner(line, "au", mask) for mask in range(1, lax.axis_size("au"))]


def with_core(lines):
    return [piece for line in lines for piece in (line, from_partner(line, "vert", 1))]


def whole_gather(own):
    return [lax.all_gather(own, ("au", "vert"), axis=0, tiled=True)]


def gathered_place(owner, by_mask):
    if not by_mask:
        return owner
    vert_count = lax.axis_size("vert")
    au_mask = (owner // vert_count) ^ lax.axis_index("au")
    vert_mask = (owner % vert_count) ^ lax.axis_index("vert")
    return au_mask * vert_count + vert_mask % 2 * (vert_count // 2) + vert_mask // 2


def coded_corners(corners):
    digits = jnp.stack([corners[:, 0] // 128, corners[:, 0] % 128, corners[:, 1] // 128, corners[:, 1] % 128])
    flat = digits.astype(f32).astype(bf16).reshape(-1)
    return jnp.pad(flat, (0, HALF * PACK - flat.shape[0])).reshape(1, HALF, PACK)


def decoded_corners(blocks, count):
    digits = blocks.reshape(blocks.shape[0], HALF * PACK).astype(jnp.int32)
    high_row, low_row, high_col, low_col = [
        digits[:, i * count : (i + 1) * count].reshape(-1) for i in range(4)
    ]
    return (high_row * 128 + low_row, high_col * 128 + low_col)


def on_device(
    visibilities, baseline_offsets, channel_scale, screen_depth, stations, corners, beam_terms
):
    au_count = lax.axis_size("au")
    vert_count = lax.axis_size("vert")
    au_index, vert_index = lax.axis_index("au"), lax.axis_index("vert")
    image_rows = G // (au_count * vert_count)
    count, _, vis_count = visibilities.shape
    own_stations = beam_terms.shape[0]
    held = au_count * vert_count * count * HALF * PACK
    by_mask = held <= MASK_VALUES

    sent = jnp.concatenate([packed_beams(beam_terms), coded_corners(corners)], axis=0)
    offsets = baseline_offsets.reshape(2 * count, -1)
    scale_row = channel_scale.reshape(1, -1)
    part = math.gcd(count, 8)
    skies = [sky_sums(visibilities, offsets, scale_row, 0, part)]
    if by_mask:
        line = z_line(sent)
        line, offsets, skies[0] = lax.optimization_barrier((line, offsets, skies[0]))
    for s in range(part, count, part):
        skies.append(sky_sums(visibilities, offsets, scale_row, s, part))
    factor = pixel_factor(screen_depth, corners[:, 0] % SUB, vis_count)
    if by_mask:
        lines = au_lines(line)
        lines, skies = lax.optimization_barrier((lines, skies))
        tables = with_core(lines)
    else:
        tables = whole_gather(sent)
    coded = [
        piece.reshape(-1, own_stations + 1, HALF, PACK)[:, own_stations] for piece in tables
    ]
    corners_all = decoded_corners(jnp.concatenate(coded, axis=0), count)
    owners = stations // own_stations
    station_rows = gathered_place(owners, by_mask) * (own_stations + 1) + stations % own_stations
    uv_own = corrected_subgrids(station_rows, tables, skies, factor)

    per_row = vert_count * count

    def row_place(index):
        return gathered_place(index * vert_count + vert_index, by_mask) // vert_count

    def places_of(place, spilled):
        chosen = [lax.dynamic_slice_in_dim(x, place * per_row, per_row) for x in corners_all]
        return tile_places(chosen, au_index, vert_index, au_count, vert_count, spilled)

    own_place = row_place(au_index)
    before_place = row_place(lax.rem(au_index + au_count - 1, au_count))
    own_list, spill_list = places_of(own_place, False), places_of(before_place, True)
    if by_mask:
        lines = au_lines(z_line(uv_own))
        own_row = with_core(lines[:1])
        tile = uv_tile_own(own_row, own_place, own_list, au_count, vert_count)
        lines, own_row, tile = lax.optimization_barrier((lines, own_row, tile))
        uv = own_row + with_core(lines[1:])
        before = [
            lax.select_n(before_place, *uv[core::2]) if au_count > 2 else uv[core + 2]
            for core in range(2)
        ]
        before_block = jnp.zeros((), jnp.int32)
    else:
        uv = before = whole_gather(uv_own)
        tile = uv_tile_own(uv, own_place, own_list, au_count, vert_count)
        before_block = before_place
    gridded = uv_tile_spill(tile, before, before_block, spill_list, au_count, vert_count)
    first_row = (au_index * vert_count + vert_index) * image_rows
    dirty_image = image_rows_of(uv, corners_all, first_row, image_rows)
    return (gridded, dirty_image)


def solution(mesh):
    return jax.shard_map(
        on_device,
        mesh=mesh,
        in_specs=(
            P(("au", "vert"), None, None),
            P(("au", "vert"), None, None),
            P(),
            P(("au", "vert")),
            P(("au", "vert"), None),
            P(("au", "vert"), None),
            P(("au", "vert"), None, None),
        ),
        out_specs=(P("au", None, "vert"), P(("au", "vert"), None, None)),
        check_vma=False,
    )
```

```python
import functools
import math

import jax
import jax.numpy as jnp
import numpy as np
from jax import lax
from jax.experimental import pallas as pl
from jax.experimental.pallas import tpu as pltpu
from jax.sharding import PartitionSpec as P

G = 8192
SUB = 32
HALF = SUB // 2
PACK = 4 * SUB
LANES = 128
FINE = G // SUB
LOW = FINE // 2
CHUNK = 768
MASK_VALUES = 1 << 22
field_view = 0.1
bf16 = jnp.bfloat16
f32 = jnp.float32
VMEM_BYTES = 58 * 1024 * 1024


def cmul(a, b):
    return (a[0] * b[0] - a[1] * b[1], a[0] * b[1] + a[1] * b[0])


def conj(a):
    return (a[0], -a[1])


def sky_kernel(vis_ref, offset_ref, scale_ref, out_ref, power_ref):
    count, _, vis_count = vis_ref.shape
    times = offset_ref.shape[1]
    step = math.gcd(vis_count, 256)
    row = lax.broadcasted_iota(jnp.int32, (8, step), 0)
    bits = [(row >> bit) % 2 == 1 for bit in range(3)]

    offsets = offset_ref[...]
    parts = []
    for _ in range(3):
        parts.append(offsets.astype(bf16))
        offsets = offsets - parts[-1].astype(f32)
    channels = vis_count // times
    repeats = max(1, LANES // channels)
    scale = jnp.concatenate([scale_ref[...]] * repeats, axis=1)
    width = math.gcd(vis_count, 512)
    scale = jnp.concatenate([scale] * (width // (repeats * channels)), axis=1)
    for start in range(0, vis_count, width):
        at = pl.ds(start, width)
        time = lax.broadcasted_iota(jnp.int32, (times, width), 0)
        place = lax.broadcasted_iota(jnp.int32, (times, width), 1) + start
        one = (place // channels == time).astype(f32).astype(bf16)
        shifts = sum(jnp.dot(part, one, preferred_element_type=f32) for part in parts)
        half = (math.pi / SUB) * (shifts * scale)
        square = half * half
        sine, cosine = 1.0, 1.0
        for term in (12, 10, 8, 6, 4, 2):
            sine = 1.0 - square * (1.0 / (term * (term + 1))) * sine
            cosine = 1.0 - square * (1.0 / (term * (term - 1))) * cosine
        sine = sine * half
        power = (1.0 - 2.0 * sine * sine, 2.0 * sine * cosine)
        for bit in range(5):
            power_ref[bit, 0, :, at] = power[0]
            power_ref[bit, 1, :, at] = power[1]
            power = (power[0] * power[0] - power[1] * power[1], 2.0 * power[0] * power[1])

    def powers(row, at, extra):
        z = [
            tuple(
                jnp.broadcast_to(power_ref[bit, part, pl.ds(row, 1), at], (8, step))
                for part in range(2)
            )
            for bit in range(5)
        ]
        low = (jnp.where(bits[0], z[0][0], 1.0), jnp.where(bits[0], z[0][1], 0.0))
        for bit in (1, 2):
            more = cmul(low, z[bit])
            low = (jnp.where(bits[bit], more[0], low[0]), jnp.where(bits[bit], more[1], low[1]))
        if extra is not None:
            low = cmul(low, extra)
        blocks = [cmul(low, conj(z[4])), cmul(low, conj(z[3])), low, cmul(low, z[3])]
        return jnp.concatenate([block[part] for part in range(2) for block in blocks], axis=0).astype(bf16)

    def one_subgrid(s):
        both = jnp.zeros((2 * SUB, 2 * SUB), f32)
        for start in range(0, vis_count, step):
            at = pl.ds(start, step)
            vis = tuple(
                jnp.broadcast_to(vis_ref[s, part : part + 1, at].astype(f32), (8, step))
                for part in range(2)
            )
            left = powers(2 * s, at, vis)
            right = powers(2 * s + 1, at, None)
            both += lax.dot_general(
                left, right, (((1,), (1,)), ((), ())), preferred_element_type=f32
            )
        real = both[:SUB, :SUB] - both[SUB:, SUB:]
        image = both[:SUB, SUB:] + both[SUB:, :SUB]
        out_ref[s] = jnp.concatenate(
            [real[:HALF], image[:HALF], real[HALF:], image[HALF:]], axis=1
        )

    def some(i, carry):
        for k in range(math.gcd(count, 2)):
            one_subgrid(i * math.gcd(count, 2) + k)
        return carry

    lax.fori_loop(0, count // math.gcd(count, 2), some, 0)


def sky_sums(visibilities, offsets, scale_row, first, count, interpret=False):
    vis_count = visibilities.shape[2]
    times = offsets.shape[1]
    at = first // count
    return pl.pallas_call(
        sky_kernel,
        grid=(1,),
        in_specs=[
            pl.BlockSpec((count, 2, vis_count), lambda i: (at, 0, 0)),
            pl.BlockSpec((2 * count, times), lambda i: (at, 0)),
            pl.BlockSpec(scale_row.shape, lambda i: (0, 0)),
        ],
        out_specs=pl.BlockSpec((count, HALF, PACK), lambda i: (0, 0, 0)),
        out_shape=jax.ShapeDtypeStruct((count, HALF, PACK), f32),
        scratch_shapes=[pltpu.VMEM((5, 2, 2 * count, vis_count), f32)],
        compiler_params=pltpu.CompilerParams(vmem_limit_bytes=VMEM_BYTES),
        cost_estimate=pl.CostEstimate(
            flops=0, bytes_accessed=count * 2_500_000, transcendentals=0
        ),
        name="sky_sums",
        interpret=interpret,
    )(visibilities, offsets, scale_row)


def correct_kernel(stations_ref, *refs, pieces, skies):
    table_refs, refs = refs[:pieces], refs[pieces:]
    sky_refs, refs = refs[:skies], refs[skies:]
    factor_ref, right_ref, left_ref, out_ref, table_ref, mid_ref = refs
    count = factor_ref.shape[0]
    lane = lax.broadcasted_iota(jnp.int32, (HALF, PACK), 1)
    imag = (lane // SUB) % 2 == 1
    sign = jnp.where(imag, 1.0, -1.0)

    def up(x):
        return pltpu.roll(x, SUB, 1)

    def down(x):
        return pltpu.roll(x, PACK - SUB, 1)

    def product(a, b):
        swapped = jnp.where(imag, up(a), down(a))
        return a * jnp.where(imag, up(b), b) + sign * swapped * jnp.where(imag, b, down(b))

    held = 0
    for piece in table_refs:
        table_ref[held : held + piece.shape[0]] = piece[...]
        held += piece.shape[0]
    for s in range(count):
        first = table_ref[stations_ref[2 * s]].astype(f32)
        second = table_ref[stations_ref[2 * s + 1]].astype(f32)
        pair = product(first, -sign * second)
        per = count // skies
        sky = product(sky_refs[s // per][s % per], factor_ref[s])
        mid_ref[HALF * s : HALF * (s + 1), :] = product(sky, pair).astype(bf16)
    mid = jnp.dot(mid_ref[...], right_ref[...], preferred_element_type=f32).astype(bf16)
    for s in range(count):
        rows = mid[HALF * s : HALF * (s + 1)]
        tall = jnp.concatenate([rows[:, : 2 * SUB], rows[:, 2 * SUB :]], axis=0)
        four = jnp.dot(left_ref[...], tall, preferred_element_type=f32)
        real = four[:SUB, :SUB] - four[SUB:, SUB:]
        image = four[:SUB, SUB:] + four[SUB:, :SUB]
        out_ref[s] = jnp.concatenate(
            [real[:HALF], image[:HALF], real[HALF:], image[HALF:]], axis=1
        ).astype(bf16)


def corrected_subgrids(stations, tables, skies, factor, interpret=False):
    count = factor.shape[0]
    centred = np.arange(SUB) - HALF
    angle = 2.0 * math.pi / SUB * (centred[:, None] * centred[None, :] % SUB)
    re, im = np.cos(angle) / SUB, -np.sin(angle) / SUB
    right = jnp.asarray(np.kron(np.eye(2), np.block([[re, im], [-im, re]])), bf16)
    left = jnp.asarray(np.concatenate([re, im], axis=0), bf16)
    rows = sum(piece.shape[0] for piece in tables)
    operands = [*tables, *skies, factor, right, left]

    def whole(operand):
        return pl.BlockSpec(operand.shape, lambda i, *_: (0,) * operand.ndim)

    return pl.pallas_call(
        functools.partial(correct_kernel, pieces=len(tables), skies=len(skies)),
        grid_spec=pltpu.PrefetchScalarGridSpec(
            num_scalar_prefetch=1,
            grid=(1,),
            in_specs=[whole(operand) for operand in operands],
            out_specs=pl.BlockSpec((count, HALF, PACK), lambda i, *_: (0, 0, 0)),
            scratch_shapes=[
                pltpu.VMEM((rows, HALF, PACK), bf16),
                pltpu.VMEM((HALF * count, PACK), bf16),
            ],
        ),
        out_shape=jax.ShapeDtypeStruct((count, HALF, PACK), bf16),
        compiler_params=pltpu.CompilerParams(vmem_limit_bytes=VMEM_BYTES),
        cost_estimate=pl.CostEstimate(flops=0, bytes_accessed=16_000_000, transcendentals=0),
        name="correct",
        interpret=interpret,
    )(stations.reshape(-1), *operands)


def add_subgrids(uv_refs, list_ref, row_ref, col_ref, held_ref, total_ref, lanes):
    first = 0
    for piece in uv_refs:
        held_ref[first : first + piece.shape[0]] = piece[...]
        first += piece.shape[0]
    lane = lax.broadcasted_iota(jnp.int32, (8, LANES), 1)
    row = lax.broadcasted_iota(jnp.int32, (8, LANES), 0)

    def one(entry, carry):
        s = list_ref[entry + 1]
        row_at, col_at = row_ref[s], col_ref[s]
        packed = held_ref[pl.ds(pl.multiple_of(s * HALF, HALF), HALF), :].astype(f32)
        tile = col_at // LANES
        offset = col_at % LANES
        shift = row_at % SUB
        base = row_at - shift

        def place(over):
            inside = lane < offset + SUB - LANES
            if not over:
                inside = (lane >= offset) & (lane < offset + SUB)
            for h in range(2):
                for part in range(2):
                    from_lane = (2 * h + part) * SUB
                    moved = pltpu.roll(packed, lax.rem(offset - from_lane + LANES, LANES), 1)
                    for group in range(2):
                        values = moved[8 * group : 8 * (group + 1)]
                        first_row = HALF * h + 8 * group
                        late = row + first_row >= shift
                        for wrapped in range(2):
                            keep = jnp.logical_and(inside, late if wrapped == 0 else ~late)
                            start = (base + SUB * wrapped + first_row) * lanes
                            start = start + 2 * (tile + over) + part
                            at = pl.ds(start, 8, stride=lanes)
                            total_ref[at, :] = total_ref[at, :] + jnp.where(keep, values, 0.0)

        place(0)

        @pl.when(offset + SUB > LANES)
        def _():
            place(1)

        return carry

    lax.fori_loop(0, list_ref[0], one, 0)


def tile_kernel(block_ref, list_ref, row_ref, col_ref, *refs, pieces, tile_rows, lanes):
    del block_ref
    uv_refs = refs[:pieces]
    out_ref, held_ref, total_ref, sems = refs[pieces:]
    rows_all = total_ref.shape[0]
    zero_rows = math.gcd(rows_all, 1024)

    def clear(i, carry):
        at = pl.ds(pl.multiple_of(i * zero_rows, zero_rows), zero_rows)
        total_ref[at, :] = jnp.zeros((zero_rows, LANES), f32)
        return carry

    lax.fori_loop(0, rows_all // zero_rows, clear, 0)
    add_subgrids(uv_refs, list_ref, row_ref, col_ref, held_ref, total_ref, lanes)
    pieces = sems.shape[0]
    size = tile_rows * lanes // pieces
    copies = [
        pltpu.make_async_copy(
            total_ref.at[pl.ds(i * size, size), :], out_ref.at[pl.ds(i * size, size), :], sems.at[i]
        )
        for i in range(pieces)
    ]
    for copy in copies:
        copy.start()
    for copy in copies:
        copy.wait()


def spill_kernel(block_ref, list_ref, row_ref, col_ref, *refs, pieces, lanes):
    del block_ref
    uv_refs = refs[:pieces]
    _, out_ref, held_ref, total_ref, sem = refs[pieces:]
    size = SUB * lanes
    kept = total_ref.at[pl.ds(size, size), :]
    copy = pltpu.make_async_copy(out_ref.at[pl.ds(0, size), :], kept, sem)
    copy.start()
    copy.wait()
    add_subgrids(uv_refs, list_ref, row_ref, col_ref, held_ref, total_ref, lanes)
    copy = pltpu.make_async_copy(kept, out_ref.at[pl.ds(0, size), :], sem)
    copy.start()
    copy.wait()


def listed(valid):
    count = valid.shape[0]
    index = jnp.arange(count, dtype=jnp.int32)
    before = jnp.sum((index[None, :] < index[:, None]) & valid[None, :], axis=1, dtype=jnp.int32)
    rank = jnp.where(valid, before, -1)
    entries = jnp.sum(
        jnp.where(rank[None, :] == index[:, None], index[None, :], 0), axis=1, dtype=jnp.int32
    )
    return jnp.concatenate([jnp.sum(valid, dtype=jnp.int32)[None], entries])


def tile_places(corners, au_index, vert_index, au_count, vert_count, spilled):
    tile_rows, tile_cols = G // au_count, G // vert_count
    col_at = corners[1] - vert_index * tile_cols
    valid = (col_at >= 0) & (col_at < tile_cols)
    row_at = corners[0] - au_index * tile_rows
    if spilled:
        row_at = (row_at + SUB + G) % G
        valid = valid & (row_at < SUB)
    return listed(valid), row_at, col_at


def uv_tile_own(uv, block, places, au_count, vert_count, interpret=False):
    count = places[1].shape[0]
    tile_rows, tile_cols = G // au_count, G // vert_count
    lanes = 2 * tile_cols // LANES
    rows = count * HALF // len(uv)
    return pl.pallas_call(
        functools.partial(tile_kernel, pieces=len(uv), tile_rows=tile_rows, lanes=lanes),
        grid_spec=pltpu.PrefetchScalarGridSpec(
            num_scalar_prefetch=4,
            grid=(1,),
            in_specs=[pl.BlockSpec((rows, PACK), lambda i, block, *_: (block[0], 0))] * len(uv),
            out_specs=pl.BlockSpec(memory_space=pl.ANY),
            scratch_shapes=[
                pltpu.VMEM((count * HALF, PACK), bf16),
                pltpu.VMEM(((tile_rows + 2 * SUB) * lanes, LANES), f32),
                pltpu.SemaphoreType.DMA((4,)),
            ],
        ),
        out_shape=jax.ShapeDtypeStruct((tile_rows * lanes, LANES), f32),
        compiler_params=pltpu.CompilerParams(vmem_limit_bytes=VMEM_BYTES),
        cost_estimate=pl.CostEstimate(
            flops=0, bytes_accessed=20 * tile_rows * tile_cols, transcendentals=0
        ),
        name="uv_tile",
        interpret=interpret,
    )(block.reshape(1), *places, *[piece.reshape(-1, PACK) for piece in uv])


def uv_tile_spill(tile, uv, block, places, au_count, vert_count, interpret=False):
    count = places[1].shape[0]
    tile_rows, tile_cols = G // au_count, G // vert_count
    lanes = 2 * tile_cols // LANES
    rows = count * HALF // len(uv)
    result = pl.pallas_call(
        functools.partial(spill_kernel, pieces=len(uv), lanes=lanes),
        grid_spec=pltpu.PrefetchScalarGridSpec(
            num_scalar_prefetch=4,
            grid=(1,),
            in_specs=[pl.BlockSpec((rows, PACK), lambda i, block, *_: (block[0], 0))] * len(uv)
            + [pl.BlockSpec(memory_space=pl.ANY)],
            out_specs=pl.BlockSpec(memory_space=pl.ANY),
            scratch_shapes=[
                pltpu.VMEM((count * HALF, PACK), bf16),
                pltpu.VMEM((3 * SUB * lanes, LANES), f32),
                pltpu.SemaphoreType.DMA(()),
            ],
        ),
        out_shape=jax.ShapeDtypeStruct(tile.shape, f32),
        input_output_aliases={4 + len(uv): 0},
        compiler_params=pltpu.CompilerParams(vmem_limit_bytes=VMEM_BYTES),
        cost_estimate=pl.CostEstimate(flops=0, bytes_accessed=8_000_000, transcendentals=0),
        name="uv_spill",
        interpret=interpret,
    )(block.reshape(1), *places, *[piece.reshape(-1, PACK) for piece in uv], tile)
    result = result.reshape(tile_rows, tile_cols // LANES, 2, LANES)
    return jnp.transpose(result, (0, 2, 1, 3)).reshape(tile_rows, 2, tile_cols)


def short_transform(values):
    count = len(values)
    if count == 1:
        return values
    even = short_transform(values[0::2])
    odd = short_transform(values[1::2])
    low, high = [], []
    for k in range(count // 2):
        re, im = odd[k]
        if k == 0:
            turned = (re, im)
        elif 4 * k == count:
            turned = (-im, re)
        elif 8 * k == count:
            root = math.sqrt(0.5)
            turned = ((re - im) * root, (re + im) * root)
        elif 8 * k == 3 * count:
            root = math.sqrt(0.5)
            turned = ((re + im) * -root, (re - im) * root)
        else:
            c, s = math.cos(2 * math.pi * k / count), math.sin(2 * math.pi * k / count)
            turned = (re * c - im * s, re * s + im * c)
        low.append((even[k][0] + turned[0], even[k][1] + turned[1]))
        high.append((even[k][0] - turned[0], even[k][1] - turned[1]))
    return low + high


def image_kernel(*refs, pieces, chunks, row_block):
    uv_refs, refs = refs[:pieces], refs[pieces:]
    corner_ref, phase_ref, columns_ref, unit_ref, count_ref, twist_ref = refs[:6]
    out_ref, uv_wide, uv_rows, here, after, shifts, left_even, left_odd, total, staged = refs[6:]
    step = pl.program_id(0)
    size = uv_rows.shape[1]
    image_rows = phase_ref.shape[1]

    def products(pair, h, left):
        at = pl.ds(2 * image_rows * h, 2 * image_rows)
        spread = lax.dot_general(
            columns_ref[at, :], uv_rows[pair], (((1,), (1,)), ((), ())), preferred_element_type=f32
        ).astype(bf16)
        turned = cmul((spread[:image_rows], spread[image_rows:]), (phase_ref[0], phase_ref[1]))
        left[h, :image_rows] = turned[0]
        left[h, image_rows:] = turned[1]

    def sums(pair, h, left, first):
        index = pair + HALF * h
        late = shifts[...] > index.astype(f32)
        table = jnp.concatenate(
            [
                jnp.where(late, after[:, t : t + LANES], here[:, t : t + LANES])
                for t in range(0, FINE, LANES)
            ],
            axis=1,
        )
        four = jnp.dot(left[h], table, preferred_element_type=f32)
        even_re, odd_re = four[:image_rows, :LOW], four[:image_rows, LOW:]
        even_im, odd_im = four[image_rows:, :LOW], four[image_rows:, LOW:]
        edge = lax.broadcasted_iota(jnp.int32, (image_rows, LOW), 1) == 0
        low = (
            even_re - jnp.where(edge, 0.0, odd_im),
            even_im + jnp.where(edge, 0.0, odd_re),
        )
        high = (
            jnp.where(edge, odd_re, even_re + odd_im),
            jnp.where(edge, odd_im, even_im - odd_re),
        )
        twist = twist_ref[pl.ds(index, 1), :]
        for half, got in enumerate((low, high)):
            start = 2 * LOW * half
            done = cmul(
                got, (twist[:, start : start + LOW], twist[:, start + LOW : start + 2 * LOW])
            )
            for part in range(2):
                at = (index, part, slice(None), pl.ds(LOW * half, LOW))
                total[at] = done[part] if first else total[at] + done[part]

    def chunk(first):
        held = 0
        for piece in uv_refs:

            def spread_out(s, carry, piece=piece, held=held):
                block = piece[pl.ds(pl.multiple_of(s * HALF, HALF), HALF), :]
                uv_wide[pl.ds((held + s) * (HALF + 1), HALF), :] = block.astype(f32)
                return carry

            count = piece.shape[0] // HALF
            lax.fori_loop(0, count, spread_out, 0, unroll=math.gcd(count, 8))
            held += count
        for row in range(HALF):
            uv_rows[row] = uv_wide[pl.ds(row, size, stride=HALF + 1), :].astype(bf16)
        corner = corner_ref[...]
        coarse, shift = corner // SUB, corner % SUB

        def looked_up(index, length, table):
            place = lax.broadcasted_iota(jnp.int32, (length, size), 0)
            one = (place == index).astype(f32).astype(bf16)
            return lax.dot_general(one, table, (((0,), (0,)), ((), ())), preferred_element_type=f32)

        here[...] = looked_up(coarse, FINE, unit_ref[...]).astype(bf16)
        after[...] = looked_up(lax.rem(coarse + 1, FINE), FINE, unit_ref[...]).astype(bf16)
        shifts[...] = looked_up(shift, SUB, count_ref[...])
        for h in range(2):
            products(0, h, left_even)

        def two_pairs(i, carry):
            for h in range(2):
                products(2 * i + 1, h, left_odd)
                sums(2 * i, h, left_even, first)
            for h in range(2):
                products(jnp.minimum(2 * i + 2, HALF - 1), h, left_even)
                sums(2 * i + 1, h, left_odd, first)
            return carry

        lax.fori_loop(0, HALF // 2, two_pairs, 0)

    @pl.when(step == 0)
    def _():
        chunk(True)

    if chunks > 1:

        @pl.when((step > 0) & (step < chunks))
        def _():
            chunk(False)

    @pl.when(step >= chunks)
    def _():
        first = (step - chunks) * row_block
        wide = 2 * G // LANES
        backward = lax.rem(LOW - lax.broadcasted_iota(jnp.int32, (8, LOW), 1), LOW)

        def eight_rows(group, carry):
            at = pl.ds(pl.multiple_of(first + 8 * group, 8), 8)
            for tile in range(FINE // LANES):
                lanes = pl.ds(tile * LANES, LANES)
                values = [(total[n, 0, at, lanes], total[n, 1, at, lanes]) for n in range(SUB)]
                for k, value in enumerate(short_transform(values)):
                    for part in range(2):
                        ordered = value[part]
                        if tile > 0:
                            ordered = jnp.take_along_axis(
                                ordered, backward, axis=1, mode="promise_in_bounds"
                            )
                        column = 2 * (k * (FINE // LANES) + tile) + part
                        staged[pl.ds(column, 8, stride=wide + 1), :] = ordered
            for row in range(8):
                at = pl.ds(pl.multiple_of((8 * group + row) * wide, wide), wide)
                out_ref[at, :] = staged[row * (wide + 1) : row * (wide + 1) + wide, :]
            return carry

        lax.fori_loop(0, row_block // 8, eight_rows, 0)


def image_rows_of(uv, corners_all, first_row, image_rows, interpret=False):
    total = corners_all[0].shape[0]
    size = math.gcd(total, CHUNK) if len(uv) == 1 else total
    chunks = total // size
    row_block = math.gcd(image_rows, 32)
    outs = image_rows // row_block
    wide = 2 * G // LANES
    rows = first_row + jnp.arange(image_rows, dtype=jnp.int32)
    turn = 2.0 * math.pi / G
    angle = turn * (rows[:, None] * corners_all[1][None, :] % G).astype(f32)
    phase = jnp.stack([jnp.cos(angle), jnp.sin(angle)]).astype(bf16)
    angle = turn * (rows[:, None] * jnp.arange(SUB, dtype=jnp.int32)[None, :] % G).astype(f32)
    re, im = jnp.cos(angle), jnp.sin(angle)
    block = jnp.concatenate(
        [jnp.concatenate([re, -im], axis=1), jnp.concatenate([im, re], axis=1)], axis=0
    )
    columns = jnp.kron(jnp.eye(2, dtype=f32), block).astype(bf16)
    fine, low = np.arange(FINE), np.arange(LOW)
    angle = 2.0 * math.pi / FINE * (fine[:, None] * low[None, :] % FINE)
    odd = np.where(low == 0, 1.0 - 2.0 * (fine[:, None] % 2), np.sin(angle))
    unit = jnp.asarray(np.concatenate([np.cos(angle), odd], axis=1), bf16)
    scale = 1.0 / (SUB * math.sqrt(total))
    high = np.where(low == 0, LOW, FINE - low)
    angles = [2.0 * math.pi / G * (np.arange(SUB)[:, None] * k[None, :]) for k in (low, high)]
    twist = [f(angle) * scale for angle in angles for f in (np.cos, np.sin)]
    twist = jnp.asarray(np.concatenate(twist, axis=1), f32)
    counts = jnp.asarray(np.broadcast_to(np.arange(SUB)[:, None], (SUB, LANES)), bf16)
    last = chunks - 1

    def chunk_of(i):
        return jnp.minimum(i, last)

    result = pl.pallas_call(
        functools.partial(image_kernel, pieces=len(uv), chunks=chunks, row_block=row_block),
        grid=(chunks + outs,),
        in_specs=[
            *[pl.BlockSpec((size * HALF // len(uv), PACK), lambda i: (chunk_of(i), 0))] * len(uv),
            pl.BlockSpec((1, size), lambda i: (0, chunk_of(i))),
            pl.BlockSpec((2, image_rows, size), lambda i: (0, 0, chunk_of(i))),
            pl.BlockSpec(columns.shape, lambda i: (0, 0)),
            pl.BlockSpec(unit.shape, lambda i: (0, 0)),
            pl.BlockSpec(counts.shape, lambda i: (0, 0)),
            pl.BlockSpec(twist.shape, lambda i: (0, 0)),
        ],
        out_specs=pl.BlockSpec(
            (row_block * wide, LANES), lambda i: (jnp.maximum(i - chunks, 0), 0)
        ),
        out_shape=jax.ShapeDtypeStruct((image_rows * wide, LANES), f32),
        scratch_shapes=[
            pltpu.VMEM((size * (HALF + 1) + HALF, PACK), f32),
            pltpu.VMEM((HALF, size, PACK), bf16),
            pltpu.VMEM((size, FINE), bf16),
            pltpu.VMEM((size, FINE), bf16),
            pltpu.VMEM((size, LANES), f32),
            pltpu.VMEM((2, 2 * image_rows, size), bf16),
            pltpu.VMEM((2, 2 * image_rows, size), bf16),
            pltpu.VMEM((SUB, 2, image_rows, FINE), f32),
            pltpu.VMEM((8 * (wide + 1) + wide, LANES), f32),
        ],
        compiler_params=pltpu.CompilerParams(vmem_limit_bytes=VMEM_BYTES),
        name="image",
        interpret=interpret,
    )(
        *[piece.reshape(-1, PACK) for piece in uv], corners_all[0].reshape(1, total),
        phase, columns, unit, counts, twist,
    )
    result = result.reshape(image_rows, G // LANES, 2, LANES)
    return jnp.transpose(result, (0, 2, 1, 3)).reshape(image_rows, 2, G)


def packed_beams(beam_terms):
    count = beam_terms.shape[0]
    parts = beam_terms.reshape(count, 2, 2, HALF, SUB)
    return jnp.transpose(parts, (0, 3, 2, 1, 4)).reshape(count, HALF, PACK)


def pixel_factor(screen_depth, shift, vis_count):
    lane = jnp.arange(PACK, dtype=jnp.int32)
    col = lane % SUB
    imag = (lane // SUB) % 2
    row = jnp.arange(HALF, dtype=jnp.int32)[:, None] + (lane // (2 * SUB) * HALF)[None, :]

    def taper(x):
        return 1.0 - ((2.0 * x.astype(f32) + 1.0 - SUB) / SUB) ** 2

    def angle_sq(x):
        return ((x - HALF).astype(f32) * (field_view / SUB)) ** 2

    weight = taper(row) * taper(col) / math.sqrt(vis_count)
    turns = shift[:, None, None] * (row - HALF) % SUB
    angle = (
        -math.pi * screen_depth[:, None, None] * (angle_sq(row) + angle_sq(col))
        + 2.0 * math.pi / SUB * turns.astype(f32)
        - 0.5 * math.pi * imag.astype(f32)
    )
    return jnp.cos(angle) * weight


def from_partner(value, axis, mask):
    count = lax.axis_size(axis)
    return lax.ppermute(value, axis, [(i, i ^ mask) for i in range(count)])


def z_line(own):
    vert_count = lax.axis_size("vert")
    line = [own] + [from_partner(own, "vert", 2 * mask) for mask in range(1, vert_count // 2)]
    return jnp.concatenate(line, axis=0)


def au_lines(line):
    return [line] + [from_partner(line, "au", mask) for mask in range(1, lax.axis_size("au"))]


def with_core(lines):
    return [piece for line in lines for piece in (line, from_partner(line, "vert", 1))]


def whole_gather(own):
    return [lax.all_gather(own, ("au", "vert"), axis=0, tiled=True)]


def gathered_place(owner, by_mask):
    if not by_mask:
        return owner
    vert_count = lax.axis_size("vert")
    au_mask = (owner // vert_count) ^ lax.axis_index("au")
    vert_mask = (owner % vert_count) ^ lax.axis_index("vert")
    return au_mask * vert_count + vert_mask % 2 * (vert_count // 2) + vert_mask // 2


def coded_corners(corners):
    digits = jnp.stack([corners[:, 0] // 128, corners[:, 0] % 128, corners[:, 1] // 128, corners[:, 1] % 128])
    flat = digits.astype(f32).astype(bf16).reshape(-1)
    return jnp.pad(flat, (0, HALF * PACK - flat.shape[0])).reshape(1, HALF, PACK)


def decoded_corners(blocks, count):
    digits = blocks.reshape(blocks.shape[0], HALF * PACK).astype(jnp.int32)
    high_row, low_row, high_col, low_col = [
        digits[:, i * count : (i + 1) * count].reshape(-1) for i in range(4)
    ]
    return (high_row * 128 + low_row, high_col * 128 + low_col)


def on_device(
    visibilities, baseline_offsets, channel_scale, screen_depth, stations, corners, beam_terms
):
    au_count = lax.axis_size("au")
    vert_count = lax.axis_size("vert")
    au_index, vert_index = lax.axis_index("au"), lax.axis_index("vert")
    image_rows = G // (au_count * vert_count)
    count, _, vis_count = visibilities.shape
    own_stations = beam_terms.shape[0]
    held = au_count * vert_count * count * HALF * PACK
    by_mask = held <= MASK_VALUES

    sent = jnp.concatenate([packed_beams(beam_terms), coded_corners(corners)], axis=0)
    offsets = baseline_offsets.reshape(2 * count, -1)
    scale_row = channel_scale.reshape(1, -1)
    part = math.gcd(count, 8)
    skies = [sky_sums(visibilities, offsets, scale_row, 0, part)]
    if by_mask:
        line = z_line(sent)
        line, offsets, skies[0] = lax.optimization_barrier((line, offsets, skies[0]))
    for s in range(part, count, part):
        skies.append(sky_sums(visibilities, offsets, scale_row, s, part))
    factor = pixel_factor(screen_depth, corners[:, 0] % SUB, vis_count)
    if by_mask:
        lines = au_lines(line)
        lines, skies = lax.optimization_barrier((lines, skies))
        tables = with_core(lines)
    else:
        tables = whole_gather(sent)
    coded = [
        piece.reshape(-1, own_stations + 1, HALF, PACK)[:, own_stations] for piece in tables
    ]
    corners_all = decoded_corners(jnp.concatenate(coded, axis=0), count)
    owners = stations // own_stations
    station_rows = gathered_place(owners, by_mask) * (own_stations + 1) + stations % own_stations
    uv_own = corrected_subgrids(station_rows, tables, skies, factor)

    per_row = vert_count * count

    def row_place(index):
        return gathered_place(index * vert_count + vert_index, by_mask) // vert_count

    def places_of(place, spilled):
        chosen = [lax.dynamic_slice_in_dim(x, place * per_row, per_row) for x in corners_all]
        return tile_places(chosen, au_index, vert_index, au_count, vert_count, spilled)

    own_place = row_place(au_index)
    before_place = row_place(lax.rem(au_index + au_count - 1, au_count))
    own_list, spill_list = places_of(own_place, False), places_of(before_place, True)
    if by_mask:
        lines = au_lines(z_line(uv_own))
        own_row = with_core(lines[:1])
        tile = uv_tile_own(own_row, own_place, own_list, au_count, vert_count)
        lines, own_row, tile = lax.optimization_barrier((lines, own_row, tile))
        uv = own_row + with_core(lines[1:])
        before = [
            lax.select_n(before_place, *uv[core::2]) if au_count > 2 else uv[core + 2]
            for core in range(2)
        ]
        before_block = jnp.zeros((), jnp.int32)
    else:
        uv = before = whole_gather(uv_own)
        tile = uv_tile_own(uv, own_place, own_list, au_count, vert_count)
        before_block = before_place
    gridded = uv_tile_spill(tile, before, before_block, spill_list, au_count, vert_count)
    first_row = (au_index * vert_count + vert_index) * image_rows
    dirty_image = image_rows_of(uv, corners_all, first_row, image_rows)
    return (gridded, dirty_image)


def solution(mesh):
    return jax.shard_map(
        on_device,
        mesh=mesh,
        in_specs=(
            P(("au", "vert"), None, None),
            P(("au", "vert"), None, None),
            P(),
            P(("au", "vert")),
            P(("au", "vert"), None),
            P(("au", "vert"), None),
            P(("au", "vert"), None, None),
        ),
        out_specs=(P("au", None, "vert"), P(("au", "vert"), None, None)),
        check_vma=False,
    )
```

```python
import functools
import math

import jax
import jax.numpy as jnp
import numpy as np
from jax import lax
from jax.experimental import pallas as pl
from jax.experimental.pallas import tpu as pltpu
from jax.sharding import PartitionSpec as P

G = 8192
SUB = 32
HALF = SUB // 2
PACK = 4 * SUB
LANES = 128
FINE = G // SUB
LOW = FINE // 2
CHUNK = 768
MASK_VALUES = 1 << 22
field_view = 0.1
bf16 = jnp.bfloat16
f32 = jnp.float32
VMEM_BYTES = 58 * 1024 * 1024


def cmul(a, b):
    return (a[0] * b[0] - a[1] * b[1], a[0] * b[1] + a[1] * b[0])


def conj(a):
    return (a[0], -a[1])


def sky_kernel(vis_ref, offset_ref, scale_ref, out_ref, power_ref):
    count, _, vis_count = vis_ref.shape
    times = offset_ref.shape[1]
    step = math.gcd(vis_count, 256)
    row = lax.broadcasted_iota(jnp.int32, (8, step), 0)
    bits = [(row >> bit) % 2 == 1 for bit in range(3)]

    offsets = offset_ref[...]
    parts = []
    for _ in range(3):
        parts.append(offsets.astype(bf16))
        offsets = offsets - parts[-1].astype(f32)
    channels = vis_count // times
    repeats = max(1, LANES // channels)
    scale = jnp.concatenate([scale_ref[...]] * repeats, axis=1)
    width = math.gcd(vis_count, 512)
    scale = jnp.concatenate([scale] * (width // (repeats * channels)), axis=1)
    for start in range(0, vis_count, width):
        at = pl.ds(start, width)
        time = lax.broadcasted_iota(jnp.int32, (times, width), 0)
        place = lax.broadcasted_iota(jnp.int32, (times, width), 1) + start
        one = (place // channels == time).astype(f32).astype(bf16)
        shifts = sum(jnp.dot(part, one, preferred_element_type=f32) for part in parts)
        half = (math.pi / SUB) * (shifts * scale)
        square = half * half
        sine, cosine = 1.0, 1.0
        for term in (12, 10, 8, 6, 4, 2):
            sine = 1.0 - square * (1.0 / (term * (term + 1))) * sine
            cosine = 1.0 - square * (1.0 / (term * (term - 1))) * cosine
        sine = sine * half
        power = (1.0 - 2.0 * sine * sine, 2.0 * sine * cosine)
        for bit in range(5):
            power_ref[bit, 0, :, at] = power[0]
            power_ref[bit, 1, :, at] = power[1]
            power = (power[0] * power[0] - power[1] * power[1], 2.0 * power[0] * power[1])

    def powers(row, at, extra):
        z = [
            tuple(
                jnp.broadcast_to(power_ref[bit, part, pl.ds(row, 1), at], (8, step))
                for part in range(2)
            )
            for bit in range(5)
        ]
        low = (jnp.where(bits[0], z[0][0], 1.0), jnp.where(bits[0], z[0][1], 0.0))
        for bit in (1, 2):
            more = cmul(low, z[bit])
            low = (jnp.where(bits[bit], more[0], low[0]), jnp.where(bits[bit], more[1], low[1]))
        if extra is not None:
            low = cmul(low, extra)
        blocks = [cmul(low, conj(z[4])), cmul(low, conj(z[3])), low, cmul(low, z[3])]
        return jnp.concatenate([block[part] for part in range(2) for block in blocks], axis=0).astype(bf16)

    def one_subgrid(s):
        both = jnp.zeros((2 * SUB, 2 * SUB), f32)
        for start in range(0, vis_count, step):
            at = pl.ds(start, step)
            vis = tuple(
                jnp.broadcast_to(vis_ref[s, part : part + 1, at].astype(f32), (8, step))
                for part in range(2)
            )
            left = powers(2 * s, at, vis)
            right = powers(2 * s + 1, at, None)
            both += lax.dot_general(
                left, right, (((1,), (1,)), ((), ())), preferred_element_type=f32
            )
        real = both[:SUB, :SUB] - both[SUB:, SUB:]
        image = both[:SUB, SUB:] + both[SUB:, :SUB]
        out_ref[s] = jnp.concatenate(
            [real[:HALF], image[:HALF], real[HALF:], image[HALF:]], axis=1
        )

    def some(i, carry):
        for k in range(math.gcd(count, 2)):
            one_subgrid(i * math.gcd(count, 2) + k)
        return carry

    lax.fori_loop(0, count // math.gcd(count, 2), some, 0)


def sky_sums(visibilities, offsets, scale_row, first, count, interpret=False):
    vis_count = visibilities.shape[2]
    times = offsets.shape[1]
    at = first // count
    return pl.pallas_call(
        sky_kernel,
        grid=(1,),
        in_specs=[
            pl.BlockSpec((count, 2, vis_count), lambda i: (at, 0, 0)),
            pl.BlockSpec((2 * count, times), lambda i: (at, 0)),
            pl.BlockSpec(scale_row.shape, lambda i: (0, 0)),
        ],
        out_specs=pl.BlockSpec((count, HALF, PACK), lambda i: (0, 0, 0)),
        out_shape=jax.ShapeDtypeStruct((count, HALF, PACK), f32),
        scratch_shapes=[pltpu.VMEM((5, 2, 2 * count, vis_count), f32)],
        compiler_params=pltpu.CompilerParams(vmem_limit_bytes=VMEM_BYTES),
        cost_estimate=pl.CostEstimate(
            flops=0, bytes_accessed=count * 2_500_000, transcendentals=0
        ),
        name="sky_sums",
        interpret=interpret,
    )(visibilities, offsets, scale_row)


def correct_kernel(stations_ref, *refs, pieces, skies):
    table_refs, refs = refs[:pieces], refs[pieces:]
    sky_refs, refs = refs[:skies], refs[skies:]
    factor_ref, right_ref, left_ref, out_ref, table_ref, mid_ref = refs
    count = factor_ref.shape[0]
    lane = lax.broadcasted_iota(jnp.int32, (HALF, PACK), 1)
    imag = (lane // SUB) % 2 == 1
    sign = jnp.where(imag, 1.0, -1.0)

    def up(x):
        return pltpu.roll(x, SUB, 1)

    def down(x):
        return pltpu.roll(x, PACK - SUB, 1)

    def product(a, b):
        swapped = jnp.where(imag, up(a), down(a))
        return a * jnp.where(imag, up(b), b) + sign * swapped * jnp.where(imag, b, down(b))

    held = 0
    for piece in table_refs:
        table_ref[held : held + piece.shape[0]] = piece[...]
        held += piece.shape[0]
    for s in range(count):
        first = table_ref[stations_ref[2 * s]].astype(f32)
        second = table_ref[stations_ref[2 * s + 1]].astype(f32)
        pair = product(first, -sign * second)
        per = count // skies
        sky = product(sky_refs[s // per][s % per], factor_ref[s])
        mid_ref[HALF * s : HALF * (s + 1), :] = product(sky, pair).astype(bf16)
    mid = jnp.dot(mid_ref[...], right_ref[...], preferred_element_type=f32).astype(bf16)
    wide = jnp.concatenate([mid[HALF * s : HALF * (s + 1)] for s in range(count)], axis=1)
    every = jnp.dot(left_ref[...], wide, preferred_element_type=f32)
    for s in range(count):
        block = every[:, PACK * s : PACK * (s + 1)]
        four = block[: 2 * SUB, : 2 * SUB] + block[2 * SUB :, 2 * SUB :]
        real = four[:SUB, :SUB] - four[SUB:, SUB:]
        image = four[:SUB, SUB:] + four[SUB:, :SUB]
        out_ref[s] = jnp.concatenate(
            [real[:HALF], image[:HALF], real[HALF:], image[HALF:]], axis=1
        ).astype(bf16)


def corrected_subgrids(stations, tables, skies, factor, interpret=False):
    count = factor.shape[0]
    centred = np.arange(SUB) - HALF
    angle = 2.0 * math.pi / SUB * (centred[:, None] * centred[None, :] % SUB)
    re, im = np.cos(angle) / SUB, -np.sin(angle) / SUB
    right = jnp.asarray(np.kron(np.eye(2), np.block([[re, im], [-im, re]])), bf16)
    left = np.concatenate([re, im], axis=0)
    left = jnp.asarray(np.concatenate([left[:, :HALF], left[:, HALF:]], axis=0), bf16)
    rows = sum(piece.shape[0] for piece in tables)
    operands = [*tables, *skies, factor, right, left]

    def whole(operand):
        return pl.BlockSpec(operand.shape, lambda i, *_: (0,) * operand.ndim)

    return pl.pallas_call(
        functools.partial(correct_kernel, pieces=len(tables), skies=len(skies)),
        grid_spec=pltpu.PrefetchScalarGridSpec(
            num_scalar_prefetch=1,
            grid=(1,),
            in_specs=[whole(operand) for operand in operands],
            out_specs=pl.BlockSpec((count, HALF, PACK), lambda i, *_: (0, 0, 0)),
            scratch_shapes=[
                pltpu.VMEM((rows, HALF, PACK), bf16),
                pltpu.VMEM((HALF * count, PACK), bf16),
            ],
        ),
        out_shape=jax.ShapeDtypeStruct((count, HALF, PACK), bf16),
        compiler_params=pltpu.CompilerParams(vmem_limit_bytes=VMEM_BYTES),
        cost_estimate=pl.CostEstimate(flops=0, bytes_accessed=16_000_000, transcendentals=0),
        name="correct",
        interpret=interpret,
    )(stations.reshape(-1), *operands)


def listed(list_ref, first, count, wanted):
    def scan(i, found):
        list_ref[found] = first + i
        return found + wanted(first + i).astype(jnp.int32)

    return lax.fori_loop(0, count, scan, jnp.int32(0), unroll=math.gcd(count, 8))


def add_subgrid(packed, row_at, col_at, total_ref, lanes):
    lane = lax.broadcasted_iota(jnp.int32, (8, LANES), 1)
    row = lax.broadcasted_iota(jnp.int32, (8, LANES), 0)
    tile = col_at // LANES
    offset = col_at % LANES
    shift = row_at % SUB
    base = row_at - shift

    def place(over):
        inside = lane < offset + SUB - LANES
        if not over:
            inside = (lane >= offset) & (lane < offset + SUB)
        for h in range(2):
            for part in range(2):
                from_lane = (2 * h + part) * SUB
                moved = pltpu.roll(packed, lax.rem(offset - from_lane + LANES, LANES), 1)
                for group in range(2):
                    values = moved[8 * group : 8 * (group + 1)]
                    first_row = HALF * h + 8 * group
                    late = row + first_row >= shift
                    for wrapped in range(2):
                        keep = jnp.logical_and(inside, late if wrapped == 0 else ~late)
                        start = (base + SUB * wrapped + first_row) * lanes
                        start = start + 2 * (tile + over) + part
                        at = pl.ds(start, 8, stride=lanes)
                        total_ref[at, :] = total_ref[at, :] + jnp.where(keep, values, 0.0)

    place(0)

    @pl.when(offset + SUB > LANES)
    def _():
        place(1)


def tile_kernel(info_ref, row_ref, col_ref, *refs, pieces, tile_rows, tile_cols):
    uv_refs = refs[:pieces]
    out_ref, held_ref, total_ref, list_ref, sems = refs[pieces:]
    lanes = 2 * tile_cols // LANES
    count = held_ref.shape[0] // HALF
    first, row_first, col_first = info_ref[0] * count, info_ref[1], info_ref[2]
    rows_all = total_ref.shape[0]
    zero_rows = math.gcd(rows_all, 1024)

    def clear(i, carry):
        at = pl.ds(pl.multiple_of(i * zero_rows, zero_rows), zero_rows)
        total_ref[at, :] = jnp.zeros((zero_rows, LANES), f32)
        return carry

    lax.fori_loop(0, rows_all // zero_rows, clear, 0)
    held = 0
    for piece in uv_refs:
        held_ref[held : held + piece.shape[0]] = piece[...]
        held += piece.shape[0]

    def wanted(s):
        col_at = col_ref[s] - col_first
        return (col_at >= 0) & (col_at < tile_cols)

    def one(entry, carry):
        s = list_ref[entry]
        at = pl.ds(pl.multiple_of((s - first) * HALF, HALF), HALF)
        packed = held_ref[at, :].astype(f32)
        add_subgrid(packed, row_ref[s] - row_first, col_ref[s] - col_first, total_ref, lanes)
        return carry

    lax.fori_loop(0, listed(list_ref, first, count, wanted), one, 0)
    parts = sems.shape[0]
    size = tile_rows * lanes // parts
    copies = [
        pltpu.make_async_copy(
            total_ref.at[pl.ds(i * size, size), :], out_ref.at[pl.ds(i * size, size), :], sems.at[i]
        )
        for i in range(parts)
    ]
    for copy in copies:
        copy.start()
    for copy in copies:
        copy.wait()


def uv_tile_own(uv, info, corners, count, tile_rows, tile_cols, interpret=False):
    lanes = 2 * tile_cols // LANES
    rows = count * HALF // len(uv)
    return pl.pallas_call(
        functools.partial(
            tile_kernel, pieces=len(uv), tile_rows=tile_rows, tile_cols=tile_cols
        ),
        grid_spec=pltpu.PrefetchScalarGridSpec(
            num_scalar_prefetch=3,
            grid=(1,),
            in_specs=[pl.BlockSpec((rows, PACK), lambda i, info, *_: (info[0], 0))] * len(uv),
            out_specs=pl.BlockSpec(memory_space=pl.ANY),
            scratch_shapes=[
                pltpu.VMEM((count * HALF, PACK), bf16),
                pltpu.VMEM(((tile_rows + 2 * SUB) * lanes, LANES), f32),
                pltpu.SMEM((count + 1,), jnp.int32),
                pltpu.SemaphoreType.DMA((4,)),
            ],
        ),
        out_shape=jax.ShapeDtypeStruct((tile_rows * lanes, LANES), f32),
        compiler_params=pltpu.CompilerParams(vmem_limit_bytes=VMEM_BYTES),
        cost_estimate=pl.CostEstimate(
            flops=0, bytes_accessed=20 * tile_rows * tile_cols, transcendentals=0
        ),
        name="uv_tile",
        interpret=interpret,
    )(info, *corners, *[piece.reshape(-1, PACK) for piece in uv])


def short_transform(values):
    count = len(values)
    if count == 1:
        return values
    even = short_transform(values[0::2])
    odd = short_transform(values[1::2])
    low, high = [], []
    for k in range(count // 2):
        re, im = odd[k]
        if k == 0:
            turned = (re, im)
        elif 4 * k == count:
            turned = (-im, re)
        elif 8 * k == count:
            root = math.sqrt(0.5)
            turned = ((re - im) * root, (re + im) * root)
        elif 8 * k == 3 * count:
            root = math.sqrt(0.5)
            turned = ((re + im) * -root, (re - im) * root)
        else:
            c, s = math.cos(2 * math.pi * k / count), math.sin(2 * math.pi * k / count)
            turned = (re * c - im * s, re * s + im * c)
        low.append((even[k][0] + turned[0], even[k][1] + turned[1]))
        high.append((even[k][0] - turned[0], even[k][1] - turned[1]))
    return low + high


def image_kernel(
    info_ref, row_ref, col_ref, *refs, pieces, chunks, row_block, per_row, tile_cols
):
    uv_refs, refs = refs[:pieces], refs[pieces:]
    corner_ref, phase_ref, columns_ref, unit_ref, count_ref, twist_ref = refs[:6]
    out_ref, tile_ref, uv_wide, uv_rows, here, after, shifts, left_even, left_odd, total = refs[7:17]
    staged, spill, list_ref, sem = refs[17:]
    step = pl.program_id(0)
    lanes = 2 * tile_cols // LANES
    head = pltpu.make_async_copy(
        tile_ref.at[pl.ds(0, SUB * lanes), :], spill.at[pl.ds(SUB * lanes, SUB * lanes), :], sem
    )
    back = pltpu.make_async_copy(
        spill.at[pl.ds(SUB * lanes, SUB * lanes), :], tile_ref.at[pl.ds(0, SUB * lanes), :], sem
    )

    def add_spilled():
        def row_of(s):
            return lax.rem(row_ref[s] - info_ref[1] + SUB + G, G)

        def wanted(s):
            col_at = col_ref[s] - info_ref[2]
            mine = (col_at >= 0) & (col_at < tile_cols) & (row_of(s) < SUB)
            return mine & (s >= step * size) & (s < (step + 1) * size)

        def one(entry, carry):
            s = list_ref[entry]
            packed = uv_wide[pl.ds((s - step * size) * (HALF + 1), HALF), :]
            add_subgrid(packed, row_of(s), col_ref[s] - info_ref[2], spill, lanes)
            return carry

        found = listed(list_ref, info_ref[0] * per_row, per_row, wanted)
        lax.fori_loop(0, found, one, 0)

    size = uv_rows.shape[1]
    image_rows = phase_ref.shape[1]

    def products(pair, h, left):
        at = pl.ds(2 * image_rows * h, 2 * image_rows)
        spread = lax.dot_general(
            columns_ref[at, :], uv_rows[pair], (((1,), (1,)), ((), ())), preferred_element_type=f32
        ).astype(bf16)
        turned = cmul((spread[:image_rows], spread[image_rows:]), (phase_ref[0], phase_ref[1]))
        left[h, :image_rows] = turned[0]
        left[h, image_rows:] = turned[1]

    def sums(pair, h, left, first):
        index = pair + HALF * h
        late = shifts[...] > index.astype(f32)
        table = jnp.concatenate(
            [
                jnp.where(late, after[:, t : t + LANES], here[:, t : t + LANES])
                for t in range(0, FINE, LANES)
            ],
            axis=1,
        )
        four = jnp.dot(left[h], table, preferred_element_type=f32)
        even_re, odd_re = four[:image_rows, :LOW], four[:image_rows, LOW:]
        even_im, odd_im = four[image_rows:, :LOW], four[image_rows:, LOW:]
        edge = lax.broadcasted_iota(jnp.int32, (image_rows, LOW), 1) == 0
        low = (
            even_re - jnp.where(edge, 0.0, odd_im),
            even_im + jnp.where(edge, 0.0, odd_re),
        )
        high = (
            jnp.where(edge, odd_re, even_re + odd_im),
            jnp.where(edge, odd_im, even_im - odd_re),
        )
        twist = twist_ref[pl.ds(index, 1), :]
        for half, got in enumerate((low, high)):
            start = 2 * LOW * half
            done = cmul(
                got, (twist[:, start : start + LOW], twist[:, start + LOW : start + 2 * LOW])
            )
            for part in range(2):
                at = (index, part, slice(None), pl.ds(LOW * half, LOW))
                total[at] = done[part] if first else total[at] + done[part]

    def chunk(first):
        if first:
            head.start()
        held = 0
        for piece in uv_refs:

            def spread_out(s, carry, piece=piece, held=held):
                block = piece[pl.ds(pl.multiple_of(s * HALF, HALF), HALF), :]
                uv_wide[pl.ds((held + s) * (HALF + 1), HALF), :] = block.astype(f32)
                return carry

            count = piece.shape[0] // HALF
            lax.fori_loop(0, count, spread_out, 0, unroll=math.gcd(count, 8))
            held += count
        for row in range(HALF):
            uv_rows[row] = uv_wide[pl.ds(row, size, stride=HALF + 1), :].astype(bf16)
        if first:
            head.wait()
        add_spilled()
        pl.when(step == chunks - 1)(back.start)
        corner = corner_ref[...]
        coarse, shift = corner // SUB, corner % SUB

        def looked_up(index, length, table):
            place = lax.broadcasted_iota(jnp.int32, (length, size), 0)
            one = (place == index).astype(f32).astype(bf16)
            return lax.dot_general(one, table, (((0,), (0,)), ((), ())), preferred_element_type=f32)

        here[...] = looked_up(coarse, FINE, unit_ref[...]).astype(bf16)
        after[...] = looked_up(lax.rem(coarse + 1, FINE), FINE, unit_ref[...]).astype(bf16)
        shifts[...] = looked_up(shift, SUB, count_ref[...])
        for h in range(2):
            products(0, h, left_even)

        def two_pairs(i, carry):
            for h in range(2):
                products(2 * i + 1, h, left_odd)
                sums(2 * i, h, left_even, first)
            for h in range(2):
                products(jnp.minimum(2 * i + 2, HALF - 1), h, left_even)
                sums(2 * i + 1, h, left_odd, first)
            return carry

        lax.fori_loop(0, HALF // 2, two_pairs, 0)
        pl.when(step == chunks - 1)(back.wait)

    @pl.when(step == 0)
    def _():
        chunk(True)

    if chunks > 1:

        @pl.when((step > 0) & (step < chunks))
        def _():
            chunk(False)

    @pl.when(step >= chunks)
    def _():
        first = (step - chunks) * row_block
        wide = 2 * G // LANES
        backward = lax.rem(LOW - lax.broadcasted_iota(jnp.int32, (8, LOW), 1), LOW)

        def eight_rows(group, carry):
            at = pl.ds(pl.multiple_of(first + 8 * group, 8), 8)
            for tile in range(FINE // LANES):
                lanes = pl.ds(tile * LANES, LANES)
                values = [(total[n, 0, at, lanes], total[n, 1, at, lanes]) for n in range(SUB)]
                for k, value in enumerate(short_transform(values)):
                    for part in range(2):
                        ordered = value[part]
                        if tile > 0:
                            ordered = jnp.take_along_axis(
                                ordered, backward, axis=1, mode="promise_in_bounds"
                            )
                        column = 2 * (k * (FINE // LANES) + tile) + part
                        staged[pl.ds(column, 8, stride=wide + 1), :] = ordered
            for row in range(8):
                at = pl.ds(pl.multiple_of((8 * group + row) * wide, wide), wide)
                out_ref[at, :] = staged[row * (wide + 1) : row * (wide + 1) + wide, :]
            return carry

        lax.fori_loop(0, row_block // 8, eight_rows, 0)


def image_rows_of(uv, corners_all, first_row, image_rows, tile, info, per_row, tile_rows, tile_cols, interpret=False):
    lanes = 2 * tile_cols // LANES
    total = corners_all[0].shape[0]
    size = math.gcd(total, CHUNK) if len(uv) == 1 else total
    chunks = total // size
    row_block = math.gcd(image_rows, 32)
    outs = image_rows // row_block
    wide = 2 * G // LANES
    rows = first_row + jnp.arange(image_rows, dtype=jnp.int32)
    turn = 2.0 * math.pi / G
    angle = turn * (rows[:, None] * corners_all[1][None, :] % G).astype(f32)
    phase = jnp.stack([jnp.cos(angle), jnp.sin(angle)]).astype(bf16)
    angle = turn * (rows[:, None] * jnp.arange(SUB, dtype=jnp.int32)[None, :] % G).astype(f32)
    re, im = jnp.cos(angle), jnp.sin(angle)
    block = jnp.concatenate(
        [jnp.concatenate([re, -im], axis=1), jnp.concatenate([im, re], axis=1)], axis=0
    )
    columns = jnp.kron(jnp.eye(2, dtype=f32), block).astype(bf16)
    fine, low = np.arange(FINE), np.arange(LOW)
    angle = 2.0 * math.pi / FINE * (fine[:, None] * low[None, :] % FINE)
    odd = np.where(low == 0, 1.0 - 2.0 * (fine[:, None] % 2), np.sin(angle))
    unit = jnp.asarray(np.concatenate([np.cos(angle), odd], axis=1), bf16)
    scale = 1.0 / (SUB * math.sqrt(total))
    high = np.where(low == 0, LOW, FINE - low)
    angles = [2.0 * math.pi / G * (np.arange(SUB)[:, None] * k[None, :]) for k in (low, high)]
    twist = [f(angle) * scale for angle in angles for f in (np.cos, np.sin)]
    twist = jnp.asarray(np.concatenate(twist, axis=1), f32)
    counts = jnp.asarray(np.broadcast_to(np.arange(SUB)[:, None], (SUB, LANES)), bf16)
    last = chunks - 1

    def chunk_of(i):
        return jnp.minimum(i, last)

    def fixed(operand):
        return pl.BlockSpec(operand.shape, lambda i, *_: (0, 0))

    image, tile = pl.pallas_call(
        functools.partial(
            image_kernel, pieces=len(uv), chunks=chunks, row_block=row_block, per_row=per_row,
            tile_cols=tile_cols,
        ),
        grid_spec=pltpu.PrefetchScalarGridSpec(
            num_scalar_prefetch=3,
            grid=(chunks + outs,),
            in_specs=[
                *[pl.BlockSpec((size * HALF // len(uv), PACK), lambda i, *_: (chunk_of(i), 0))]
                * len(uv),
                pl.BlockSpec((1, size), lambda i, *_: (0, chunk_of(i))),
                pl.BlockSpec((2, image_rows, size), lambda i, *_: (0, 0, chunk_of(i))),
                fixed(columns),
                fixed(unit),
                fixed(counts),
                fixed(twist),
                pl.BlockSpec(memory_space=pl.ANY),
            ],
            out_specs=[
                pl.BlockSpec(
                    (row_block * wide, LANES), lambda i, *_: (jnp.maximum(i - chunks, 0), 0)
                ),
                pl.BlockSpec(memory_space=pl.ANY),
            ],
            scratch_shapes=[
                pltpu.VMEM((size * (HALF + 1) + HALF, PACK), f32),
                pltpu.VMEM((HALF, size, PACK), bf16),
                pltpu.VMEM((size, FINE), bf16),
                pltpu.VMEM((size, FINE), bf16),
                pltpu.VMEM((size, LANES), f32),
                pltpu.VMEM((2, 2 * image_rows, size), bf16),
                pltpu.VMEM((2, 2 * image_rows, size), bf16),
                pltpu.VMEM((SUB, 2, image_rows, FINE), f32),
                pltpu.VMEM((8 * (wide + 1) + wide, LANES), f32),
                pltpu.VMEM((3 * SUB * lanes, LANES), f32),
                pltpu.SMEM((per_row + 1,), jnp.int32),
                pltpu.SemaphoreType.DMA(()),
            ],
        ),
        out_shape=[
            jax.ShapeDtypeStruct((image_rows * wide, LANES), f32),
            jax.ShapeDtypeStruct(tile.shape, f32),
        ],
        input_output_aliases={9 + len(uv): 1},
        compiler_params=pltpu.CompilerParams(vmem_limit_bytes=VMEM_BYTES),
        name="image",
        interpret=interpret,
    )(
        info, *corners_all, *[piece.reshape(-1, PACK) for piece in uv],
        corners_all[0].reshape(1, total), phase, columns, unit, counts, twist, tile,
    )
    image = image.reshape(image_rows, G // LANES, 2, LANES)
    tile = tile.reshape(tile_rows, tile_cols // LANES, 2, LANES)
    return (
        jnp.transpose(tile, (0, 2, 1, 3)).reshape(tile_rows, 2, tile_cols),
        jnp.transpose(image, (0, 2, 1, 3)).reshape(image_rows, 2, G),
    )


def packed_beams(beam_terms):
    count = beam_terms.shape[0]
    parts = beam_terms.reshape(count, 2, 2, HALF, SUB)
    return jnp.transpose(parts, (0, 3, 2, 1, 4)).reshape(count, HALF, PACK)


def pixel_factor(screen_depth, shift, vis_count):
    lane = jnp.arange(PACK, dtype=jnp.int32)
    col = lane % SUB
    imag = (lane // SUB) % 2
    row = jnp.arange(HALF, dtype=jnp.int32)[:, None] + (lane // (2 * SUB) * HALF)[None, :]

    def taper(x):
        return 1.0 - ((2.0 * x.astype(f32) + 1.0 - SUB) / SUB) ** 2

    def angle_sq(x):
        return ((x - HALF).astype(f32) * (field_view / SUB)) ** 2

    weight = taper(row) * taper(col) / math.sqrt(vis_count)
    turns = shift[:, None, None] * (row - HALF) % SUB
    angle = (
        -math.pi * screen_depth[:, None, None] * (angle_sq(row) + angle_sq(col))
        + 2.0 * math.pi / SUB * turns.astype(f32)
        - 0.5 * math.pi * imag.astype(f32)
    )
    return jnp.cos(angle) * weight


def from_partner(value, axis, mask):
    count = lax.axis_size(axis)
    return lax.ppermute(value, axis, [(i, i ^ mask) for i in range(count)])


def z_line(own):
    vert_count = lax.axis_size("vert")
    line = [own] + [from_partner(own, "vert", 2 * mask) for mask in range(1, vert_count // 2)]
    return jnp.concatenate(line, axis=0)


def au_lines(line):
    return [line] + [from_partner(line, "au", mask) for mask in range(1, lax.axis_size("au"))]


def with_core(lines):
    return [piece for line in lines for piece in (line, from_partner(line, "vert", 1))]


def whole_gather(own):
    return [lax.all_gather(own, ("au", "vert"), axis=0, tiled=True)]


def gathered_place(owner, by_mask):
    if not by_mask:
        return owner
    vert_count = lax.axis_size("vert")
    au_mask = (owner // vert_count) ^ lax.axis_index("au")
    vert_mask = (owner % vert_count) ^ lax.axis_index("vert")
    return au_mask * vert_count + vert_mask % 2 * (vert_count // 2) + vert_mask // 2


def coded_corners(corners):
    digits = jnp.stack([corners[:, 0] // 128, corners[:, 0] % 128, corners[:, 1] // 128, corners[:, 1] % 128])
    flat = digits.astype(f32).astype(bf16).reshape(-1)
    return jnp.pad(flat, (0, HALF * PACK - flat.shape[0])).reshape(1, HALF, PACK)


def decoded_corners(blocks, count):
    digits = blocks.reshape(blocks.shape[0], HALF * PACK).astype(jnp.int32)
    high_row, low_row, high_col, low_col = [
        digits[:, i * count : (i + 1) * count].reshape(-1) for i in range(4)
    ]
    return (high_row * 128 + low_row, high_col * 128 + low_col)


def on_device(
    visibilities, baseline_offsets, channel_scale, screen_depth, stations, corners, beam_terms
):
    au_count = lax.axis_size("au")
    vert_count = lax.axis_size("vert")
    au_index, vert_index = lax.axis_index("au"), lax.axis_index("vert")
    image_rows = G // (au_count * vert_count)
    count, _, vis_count = visibilities.shape
    own_stations = beam_terms.shape[0]
    held = au_count * vert_count * count * HALF * PACK
    by_mask = held <= MASK_VALUES

    sent = jnp.concatenate([packed_beams(beam_terms), coded_corners(corners)], axis=0)
    offsets = baseline_offsets.reshape(2 * count, -1)
    scale_row = channel_scale.reshape(1, -1)
    part = math.gcd(count, 8)
    skies = [sky_sums(visibilities, offsets, scale_row, 0, part)]
    if by_mask:
        line = z_line(sent)
        line, offsets, skies[0], corners, stations, screen_depth = lax.optimization_barrier(
            (line, offsets, skies[0], corners, stations, screen_depth)
        )
    for s in range(part, count, part):
        skies.append(sky_sums(visibilities, offsets, scale_row, s, part))
    factor = pixel_factor(screen_depth, corners[:, 0] % SUB, vis_count)
    if by_mask:
        lines = au_lines(line)
        lines, skies = lax.optimization_barrier((lines, skies))
        tables = with_core(lines)
    else:
        tables = whole_gather(sent)
    coded = [
        piece.reshape(-1, own_stations + 1, HALF, PACK)[:, own_stations] for piece in tables
    ]
    corners_all = decoded_corners(jnp.concatenate(coded, axis=0), count)
    owners = stations // own_stations
    station_rows = gathered_place(owners, by_mask) * (own_stations + 1) + stations % own_stations
    uv_own = corrected_subgrids(station_rows, tables, skies, factor)

    per_row = vert_count * count
    tile_rows, tile_cols = G // au_count, G // vert_count

    def tile_info(row):
        place = gathered_place(row * vert_count + vert_index, by_mask) // vert_count
        return jnp.stack([place, au_index * tile_rows, vert_index * tile_cols])

    own_info = tile_info(au_index)
    before_info = tile_info(lax.rem(au_index + au_count - 1, au_count))
    if by_mask:
        lines = au_lines(z_line(uv_own))
        own_row = with_core(lines[:1])
        tile = uv_tile_own(own_row, own_info, corners_all, per_row, tile_rows, tile_cols)
        lines, own_row, tile = lax.optimization_barrier((lines, own_row, tile))
        uv = own_row + with_core(lines[1:])
    else:
        uv = whole_gather(uv_own)
        tile = uv_tile_own(uv, own_info, corners_all, per_row, tile_rows, tile_cols)
    first_row = (au_index * vert_count + vert_index) * image_rows
    return image_rows_of(
        uv, corners_all, first_row, image_rows, tile, before_info, per_row, tile_rows, tile_cols
    )


def solution(mesh):
    return jax.shard_map(
        on_device,
        mesh=mesh,
        in_specs=(
            P(("au", "vert"), None, None),
            P(("au", "vert"), None, None),
            P(),
            P(("au", "vert")),
            P(("au", "vert"), None),
            P(("au", "vert"), None),
            P(("au", "vert"), None, None),
        ),
        out_specs=(P("au", None, "vert"), P(("au", "vert"), None, None)),
        check_vma=False,
    )
```

```python
import functools
import math

import jax
import jax.numpy as jnp
import numpy as np
from jax import lax
from jax.experimental import pallas as pl
from jax.experimental.pallas import tpu as pltpu
from jax.sharding import PartitionSpec as P

G = 8192
SUB = 32
HALF = SUB // 2
PACK = 4 * SUB
LANES = 128
FINE = G // SUB
LOW = FINE // 2
CHUNK = 768
MASK_VALUES = 1 << 22
field_view = 0.1
bf16 = jnp.bfloat16
f32 = jnp.float32
VMEM_BYTES = 58 * 1024 * 1024


def cmul(a, b):
    return (a[0] * b[0] - a[1] * b[1], a[0] * b[1] + a[1] * b[0])


def conj(a):
    return (a[0], -a[1])


def sky_kernel(vis_ref, offset_ref, scale_ref, out_ref, power_ref):
    count, _, vis_count = vis_ref.shape
    times = offset_ref.shape[1]
    step = math.gcd(vis_count, 256)
    row = lax.broadcasted_iota(jnp.int32, (8, step), 0)
    bits = [(row >> bit) % 2 == 1 for bit in range(3)]

    offsets = offset_ref[...]
    parts = []
    for _ in range(3):
        parts.append(offsets.astype(bf16))
        offsets = offsets - parts[-1].astype(f32)
    channels = vis_count // times
    repeats = max(1, LANES // channels)
    scale = jnp.concatenate([scale_ref[...]] * repeats, axis=1)
    width = math.gcd(vis_count, 512)
    scale = jnp.concatenate([scale] * (width // (repeats * channels)), axis=1)
    for start in range(0, vis_count, width):
        at = pl.ds(start, width)
        time = lax.broadcasted_iota(jnp.int32, (times, width), 0)
        place = lax.broadcasted_iota(jnp.int32, (times, width), 1) + start
        one = (place // channels == time).astype(f32).astype(bf16)
        shifts = sum(jnp.dot(part, one, preferred_element_type=f32) for part in parts)
        half = (math.pi / SUB) * (shifts * scale)
        square = half * half
        sine, cosine = 1.0, 1.0
        for term in (12, 10, 8, 6, 4, 2):
            sine = 1.0 - square * (1.0 / (term * (term + 1))) * sine
            cosine = 1.0 - square * (1.0 / (term * (term - 1))) * cosine
        sine = sine * half
        power = (1.0 - 2.0 * sine * sine, 2.0 * sine * cosine)
        for bit in range(5):
            power_ref[bit, 0, :, at] = power[0]
            power_ref[bit, 1, :, at] = power[1]
            power = (power[0] * power[0] - power[1] * power[1], 2.0 * power[0] * power[1])

    def powers(row, at, extra):
        z = [
            tuple(
                jnp.broadcast_to(power_ref[bit, part, pl.ds(row, 1), at], (8, step))
                for part in range(2)
            )
            for bit in range(5)
        ]
        low = (jnp.where(bits[0], z[0][0], 1.0), jnp.where(bits[0], z[0][1], 0.0))
        for bit in (1, 2):
            more = cmul(low, z[bit])
            low = (jnp.where(bits[bit], more[0], low[0]), jnp.where(bits[bit], more[1], low[1]))
        if extra is not None:
            low = cmul(low, extra)
        blocks = [cmul(low, conj(z[4])), cmul(low, conj(z[3])), low, cmul(low, z[3])]
        return jnp.concatenate([block[part] for part in range(2) for block in blocks], axis=0).astype(bf16)

    def one_subgrid(s):
        both = jnp.zeros((2 * SUB, 2 * SUB), f32)
        for start in range(0, vis_count, step):
            at = pl.ds(start, step)
            vis = tuple(
                jnp.broadcast_to(vis_ref[s, part : part + 1, at].astype(f32), (8, step))
                for part in range(2)
            )
            left = powers(2 * s, at, vis)
            right = powers(2 * s + 1, at, None)
            both += lax.dot_general(
                left, right, (((1,), (1,)), ((), ())), preferred_element_type=f32
            )
        real = both[:SUB, :SUB] - both[SUB:, SUB:]
        image = both[:SUB, SUB:] + both[SUB:, :SUB]
        out_ref[s] = jnp.concatenate(
            [real[:HALF], image[:HALF], real[HALF:], image[HALF:]], axis=1
        )

    def some(i, carry):
        for k in range(math.gcd(count, 2)):
            one_subgrid(i * math.gcd(count, 2) + k)
        return carry

    lax.fori_loop(0, count // math.gcd(count, 2), some, 0)


def sky_sums(visibilities, offsets, scale_row, first, count, interpret=False):
    vis_count = visibilities.shape[2]
    times = offsets.shape[1]
    at = first // count
    return pl.pallas_call(
        sky_kernel,
        grid=(1,),
        in_specs=[
            pl.BlockSpec((count, 2, vis_count), lambda i: (at, 0, 0)),
            pl.BlockSpec((2 * count, times), lambda i: (at, 0)),
            pl.BlockSpec(scale_row.shape, lambda i: (0, 0)),
        ],
        out_specs=pl.BlockSpec((count, HALF, PACK), lambda i: (0, 0, 0)),
        out_shape=jax.ShapeDtypeStruct((count, HALF, PACK), f32),
        scratch_shapes=[pltpu.VMEM((5, 2, 2 * count, vis_count), f32)],
        compiler_params=pltpu.CompilerParams(vmem_limit_bytes=VMEM_BYTES),
        cost_estimate=pl.CostEstimate(
            flops=0, bytes_accessed=count * 2_500_000, transcendentals=0
        ),
        name="sky_sums",
        interpret=interpret,
    )(visibilities, offsets, scale_row)


def correct_kernel(stations_ref, *refs, pieces, skies):
    table_refs, refs = refs[:pieces], refs[pieces:]
    sky_refs, refs = refs[:skies], refs[skies:]
    factor_ref, right_ref, left_ref, out_ref, table_ref, mid_ref = refs
    count = factor_ref.shape[0]
    lane = lax.broadcasted_iota(jnp.int32, (HALF, PACK), 1)
    imag = (lane // SUB) % 2 == 1
    sign = jnp.where(imag, 1.0, -1.0)

    def up(x):
        return pltpu.roll(x, SUB, 1)

    def down(x):
        return pltpu.roll(x, PACK - SUB, 1)

    def product(a, b):
        swapped = jnp.where(imag, up(a), down(a))
        return a * jnp.where(imag, up(b), b) + sign * swapped * jnp.where(imag, b, down(b))

    held = 0
    for piece in table_refs:
        table_ref[held : held + piece.shape[0]] = piece[...]
        held += piece.shape[0]
    for s in range(count):
        first = table_ref[stations_ref[2 * s]].astype(f32)
        second = table_ref[stations_ref[2 * s + 1]].astype(f32)
        pair = product(first, -sign * second)
        per = count // skies
        sky = product(sky_refs[s // per][s % per], factor_ref[s])
        mid_ref[HALF * s : HALF * (s + 1), :] = product(sky, pair).astype(bf16)
    mid = jnp.dot(mid_ref[...], right_ref[...], preferred_element_type=f32).astype(bf16)
    for s in range(count):
        rows = mid[HALF * s : HALF * (s + 1)]
        tall = jnp.concatenate([rows[:, : 2 * SUB], rows[:, 2 * SUB :]], axis=0)
        four = jnp.dot(left_ref[...], tall, preferred_element_type=f32)
        real = four[:SUB, :SUB] - four[SUB:, SUB:]
        image = four[:SUB, SUB:] + four[SUB:, :SUB]
        out_ref[s] = jnp.concatenate(
            [real[:HALF], image[:HALF], real[HALF:], image[HALF:]], axis=1
        ).astype(bf16)


def corrected_subgrids(stations, tables, skies, factor, interpret=False):
    count = factor.shape[0]
    centred = np.arange(SUB) - HALF
    angle = 2.0 * math.pi / SUB * (centred[:, None] * centred[None, :] % SUB)
    re, im = np.cos(angle) / SUB, -np.sin(angle) / SUB
    right = jnp.asarray(np.kron(np.eye(2), np.block([[re, im], [-im, re]])), bf16)
    left = jnp.asarray(np.concatenate([re, im], axis=0), bf16)
    rows = sum(piece.shape[0] for piece in tables)
    operands = [*tables, *skies, factor, right, left]

    def whole(operand):
        return pl.BlockSpec(operand.shape, lambda i, *_: (0,) * operand.ndim)

    return pl.pallas_call(
        functools.partial(correct_kernel, pieces=len(tables), skies=len(skies)),
        grid_spec=pltpu.PrefetchScalarGridSpec(
            num_scalar_prefetch=1,
            grid=(1,),
            in_specs=[whole(operand) for operand in operands],
            out_specs=pl.BlockSpec((count, HALF, PACK), lambda i, *_: (0, 0, 0)),
            scratch_shapes=[
                pltpu.VMEM((rows, HALF, PACK), bf16),
                pltpu.VMEM((HALF * count, PACK), bf16),
            ],
        ),
        out_shape=jax.ShapeDtypeStruct((count, HALF, PACK), bf16),
        compiler_params=pltpu.CompilerParams(vmem_limit_bytes=VMEM_BYTES),
        cost_estimate=pl.CostEstimate(flops=0, bytes_accessed=16_000_000, transcendentals=0),
        name="correct",
        interpret=interpret,
    )(stations.reshape(-1), *operands)


def listed(list_ref, first, count, wanted):
    def scan(i, found):
        list_ref[found] = first + i
        return found + wanted(first + i).astype(jnp.int32)

    return lax.fori_loop(0, count, scan, jnp.int32(0), unroll=math.gcd(count, 8))


def add_subgrid(packed, row_at, col_at, total_ref, lanes):
    lane = lax.broadcasted_iota(jnp.int32, (8, LANES), 1)
    row = lax.broadcasted_iota(jnp.int32, (8, LANES), 0)
    tile = col_at // LANES
    offset = col_at % LANES
    shift = row_at % SUB
    base = row_at - shift

    def place(over):
        inside = lane < offset + SUB - LANES
        if not over:
            inside = (lane >= offset) & (lane < offset + SUB)
        for h in range(2):
            for part in range(2):
                from_lane = (2 * h + part) * SUB
                moved = pltpu.roll(packed, lax.rem(offset - from_lane + LANES, LANES), 1)
                for group in range(2):
                    values = moved[8 * group : 8 * (group + 1)]
                    first_row = HALF * h + 8 * group
                    late = row + first_row >= shift
                    for wrapped in range(2):
                        keep = jnp.logical_and(inside, late if wrapped == 0 else ~late)
                        start = (base + SUB * wrapped + first_row) * lanes
                        start = start + 2 * (tile + over) + part
                        at = pl.ds(start, 8, stride=lanes)
                        total_ref[at, :] = total_ref[at, :] + jnp.where(keep, values, 0.0)

    place(0)

    @pl.when(offset + SUB > LANES)
    def _():
        place(1)


def tile_kernel(info_ref, row_ref, col_ref, *refs, pieces, tile_rows, tile_cols):
    uv_refs = refs[:pieces]
    out_ref, held_ref, total_ref, list_ref, sems = refs[pieces:]
    lanes = 2 * tile_cols // LANES
    count = held_ref.shape[0] // HALF
    first, row_first, col_first = info_ref[0] * count, info_ref[1], info_ref[2]
    rows_all = total_ref.shape[0]
    zero_rows = math.gcd(rows_all, 1024)

    def clear(i, carry):
        at = pl.ds(pl.multiple_of(i * zero_rows, zero_rows), zero_rows)
        total_ref[at, :] = jnp.zeros((zero_rows, LANES), f32)
        return carry

    lax.fori_loop(0, rows_all // zero_rows, clear, 0)
    held = 0
    for piece in uv_refs:
        held_ref[held : held + piece.shape[0]] = piece[...]
        held += piece.shape[0]

    def wanted(s):
        col_at = col_ref[s] - col_first
        return (col_at >= 0) & (col_at < tile_cols)

    def one(entry, carry):
        s = list_ref[entry]
        at = pl.ds(pl.multiple_of((s - first) * HALF, HALF), HALF)
        packed = held_ref[at, :].astype(f32)
        add_subgrid(packed, row_ref[s] - row_first, col_ref[s] - col_first, total_ref, lanes)
        return carry

    lax.fori_loop(0, listed(list_ref, first, count, wanted), one, 0)
    parts = sems.shape[0]
    size = tile_rows * lanes // parts
    copies = [
        pltpu.make_async_copy(
            total_ref.at[pl.ds(i * size, size), :], out_ref.at[pl.ds(i * size, size), :], sems.at[i]
        )
        for i in range(parts)
    ]
    for copy in copies:
        copy.start()
    for copy in copies:
        copy.wait()


def uv_tile_own(uv, info, corners, count, tile_rows, tile_cols, interpret=False):
    lanes = 2 * tile_cols // LANES
    uv = [piece.reshape(-1, PACK) for piece in uv]
    if len(uv) == 1:
        uv_specs = [pl.BlockSpec((count * HALF, PACK), lambda i, info, *_: (info[0], 0))]
    else:
        uv_specs = [pl.BlockSpec(piece.shape, lambda i, *_: (0, 0)) for piece in uv]
    return pl.pallas_call(
        functools.partial(
            tile_kernel, pieces=len(uv), tile_rows=tile_rows, tile_cols=tile_cols
        ),
        grid_spec=pltpu.PrefetchScalarGridSpec(
            num_scalar_prefetch=3,
            grid=(1,),
            in_specs=uv_specs,
            out_specs=pl.BlockSpec(memory_space=pl.ANY),
            scratch_shapes=[
                pltpu.VMEM((count * HALF, PACK), bf16),
                pltpu.VMEM(((tile_rows + 2 * SUB) * lanes, LANES), f32),
                pltpu.SMEM((count + 1,), jnp.int32),
                pltpu.SemaphoreType.DMA((4,)),
            ],
        ),
        out_shape=jax.ShapeDtypeStruct((tile_rows * lanes, LANES), f32),
        compiler_params=pltpu.CompilerParams(vmem_limit_bytes=VMEM_BYTES),
        cost_estimate=pl.CostEstimate(
            flops=0, bytes_accessed=20 * tile_rows * tile_cols, transcendentals=0
        ),
        name="uv_tile",
        interpret=interpret,
    )(info, *corners, *uv)


def short_transform(values):
    count = len(values)
    if count == 1:
        return values
    even = short_transform(values[0::2])
    odd = short_transform(values[1::2])
    low, high = [], []
    for k in range(count // 2):
        re, im = odd[k]
        if k == 0:
            turned = (re, im)
        elif 4 * k == count:
            turned = (-im, re)
        elif 8 * k == count:
            root = math.sqrt(0.5)
            turned = ((re - im) * root, (re + im) * root)
        elif 8 * k == 3 * count:
            root = math.sqrt(0.5)
            turned = ((re + im) * -root, (re - im) * root)
        else:
            c, s = math.cos(2 * math.pi * k / count), math.sin(2 * math.pi * k / count)
            turned = (re * c - im * s, re * s + im * c)
        low.append((even[k][0] + turned[0], even[k][1] + turned[1]))
        high.append((even[k][0] - turned[0], even[k][1] - turned[1]))
    return low + high


def image_kernel(
    info_ref, row_ref, col_ref, *refs, pieces, chunks, row_block, per_row, tile_cols
):
    uv_refs, refs = refs[:pieces], refs[pieces:]
    corner_ref, phase_ref, columns_ref, unit_ref, count_ref, twist_ref = refs[:6]
    out_ref, tile_ref, uv_wide, uv_rows, here, after, shifts, left_even, left_odd, total = refs[7:17]
    staged, spill, list_ref, sem = refs[17:]
    step = pl.program_id(0)
    lanes = 2 * tile_cols // LANES
    head = pltpu.make_async_copy(
        tile_ref.at[pl.ds(0, SUB * lanes), :], spill.at[pl.ds(SUB * lanes, SUB * lanes), :], sem
    )
    back = pltpu.make_async_copy(
        spill.at[pl.ds(SUB * lanes, SUB * lanes), :], tile_ref.at[pl.ds(0, SUB * lanes), :], sem
    )

    def add_spilled():
        def row_of(s):
            return lax.rem(row_ref[s] - info_ref[1] + SUB + G, G)

        def wanted(s):
            col_at = col_ref[s] - info_ref[2]
            mine = (col_at >= 0) & (col_at < tile_cols) & (row_of(s) < SUB)
            return mine & (s >= step * size) & (s < (step + 1) * size)

        def one(entry, carry):
            s = list_ref[entry]
            packed = uv_wide[pl.ds((s - step * size) * (HALF + 1), HALF), :]
            add_subgrid(packed, row_of(s), col_ref[s] - info_ref[2], spill, lanes)
            return carry

        found = listed(list_ref, info_ref[0] * per_row, per_row, wanted)
        lax.fori_loop(0, found, one, 0)

    size = uv_rows.shape[1]
    image_rows = phase_ref.shape[1]

    def products(pair, h, left):
        at = pl.ds(2 * image_rows * h, 2 * image_rows)
        spread = lax.dot_general(
            columns_ref[at, :], uv_rows[pair], (((1,), (1,)), ((), ())), preferred_element_type=f32
        ).astype(bf16)
        turned = cmul((spread[:image_rows], spread[image_rows:]), (phase_ref[0], phase_ref[1]))
        left[h, :image_rows] = turned[0]
        left[h, image_rows:] = turned[1]

    def sums(pair, h, left, first):
        index = pair + HALF * h
        late = shifts[...] > index.astype(f32)
        table = jnp.concatenate(
            [
                jnp.where(late, after[:, t : t + LANES], here[:, t : t + LANES])
                for t in range(0, FINE, LANES)
            ],
            axis=1,
        )
        four = jnp.dot(left[h], table, preferred_element_type=f32)
        even_re, odd_re = four[:image_rows, :LOW], four[:image_rows, LOW:]
        even_im, odd_im = four[image_rows:, :LOW], four[image_rows:, LOW:]
        edge = lax.broadcasted_iota(jnp.int32, (image_rows, LOW), 1) == 0
        low = (
            even_re - jnp.where(edge, 0.0, odd_im),
            even_im + jnp.where(edge, 0.0, odd_re),
        )
        high = (
            jnp.where(edge, odd_re, even_re + odd_im),
            jnp.where(edge, odd_im, even_im - odd_re),
        )
        twist = twist_ref[pl.ds(index, 1), :]
        for half, got in enumerate((low, high)):
            start = 2 * LOW * half
            done = cmul(
                got, (twist[:, start : start + LOW], twist[:, start + LOW : start + 2 * LOW])
            )
            for part in range(2):
                at = (index, part, slice(None), pl.ds(LOW * half, LOW))
                total[at] = done[part] if first else total[at] + done[part]

    def chunk(first):
        if first:
            head.start()
        held = 0
        for piece in uv_refs:

            def spread_out(s, carry, piece=piece, held=held):
                block = piece[pl.ds(pl.multiple_of(s * HALF, HALF), HALF), :]
                uv_wide[pl.ds((held + s) * (HALF + 1), HALF), :] = block.astype(f32)
                return carry

            count = piece.shape[0] // HALF
            lax.fori_loop(0, count, spread_out, 0, unroll=math.gcd(count, 8))
            held += count
        for row in range(HALF):
            uv_rows[row] = uv_wide[pl.ds(row, size, stride=HALF + 1), :].astype(bf16)
        if first:
            head.wait()
        add_spilled()
        pl.when(step == chunks - 1)(back.start)
        corner = corner_ref[...]
        coarse, shift = corner // SUB, corner % SUB

        def looked_up(index, length, table):
            place = lax.broadcasted_iota(jnp.int32, (length, size), 0)
            one = (place == index).astype(f32).astype(bf16)
            return lax.dot_general(one, table, (((0,), (0,)), ((), ())), preferred_element_type=f32)

        here[...] = looked_up(coarse, FINE, unit_ref[...]).astype(bf16)
        after[...] = looked_up(lax.rem(coarse + 1, FINE), FINE, unit_ref[...]).astype(bf16)
        shifts[...] = looked_up(shift, SUB, count_ref[...])
        for h in range(2):
            products(0, h, left_even)

        def two_pairs(i, carry):
            for h in range(2):
                products(2 * i + 1, h, left_odd)
                sums(2 * i, h, left_even, first)
            for h in range(2):
                products(jnp.minimum(2 * i + 2, HALF - 1), h, left_even)
                sums(2 * i + 1, h, left_odd, first)
            return carry

        lax.fori_loop(0, HALF // 2, two_pairs, 0)
        pl.when(step == chunks - 1)(back.wait)

    @pl.when(step == 0)
    def _():
        chunk(True)

    if chunks > 1:

        @pl.when((step > 0) & (step < chunks))
        def _():
            chunk(False)

    @pl.when(step >= chunks)
    def _():
        first = (step - chunks) * row_block
        wide = 2 * G // LANES
        backward = lax.rem(LOW - lax.broadcasted_iota(jnp.int32, (8, LOW), 1), LOW)

        def eight_rows(group, carry):
            at = pl.ds(pl.multiple_of(first + 8 * group, 8), 8)
            for tile in range(FINE // LANES):
                lanes = pl.ds(tile * LANES, LANES)
                values = [(total[n, 0, at, lanes], total[n, 1, at, lanes]) for n in range(SUB)]
                for k, value in enumerate(short_transform(values)):
                    for part in range(2):
                        ordered = value[part]
                        if tile > 0:
                            ordered = jnp.take_along_axis(
                                ordered, backward, axis=1, mode="promise_in_bounds"
                            )
                        column = 2 * (k * (FINE // LANES) + tile) + part
                        staged[pl.ds(column, 8, stride=wide + 1), :] = ordered
            for row in range(8):
                at = pl.ds(pl.multiple_of((8 * group + row) * wide, wide), wide)
                out_ref[at, :] = staged[row * (wide + 1) : row * (wide + 1) + wide, :]
            return carry

        lax.fori_loop(0, row_block // 8, eight_rows, 0)


def image_tables(corner_cols, first_row, image_rows):
    rows = first_row + jnp.arange(image_rows, dtype=jnp.int32)
    turn = 2.0 * math.pi / G
    angle = turn * (rows[:, None] * corner_cols[None, :] % G).astype(f32)
    phase = jnp.stack([jnp.cos(angle), jnp.sin(angle)]).astype(bf16)
    angle = turn * (rows[:, None] * jnp.arange(SUB, dtype=jnp.int32)[None, :] % G).astype(f32)
    re, im = jnp.cos(angle), jnp.sin(angle)
    block = jnp.concatenate(
        [jnp.concatenate([re, -im], axis=1), jnp.concatenate([im, re], axis=1)], axis=0
    )
    columns = jnp.kron(jnp.eye(2, dtype=f32), block).astype(bf16)
    return phase, columns


def image_rows_of(
    uv, corners_all, tables, tile, info, per_row, tile_rows, tile_cols, interpret=False
):
    phase, columns = tables
    image_rows = phase.shape[1]
    lanes = 2 * tile_cols // LANES
    uv = [piece.reshape(-1, PACK) for piece in uv]
    total = corners_all[0].shape[0]
    size = math.gcd(total, CHUNK) if len(uv) == 1 else total
    chunks = total // size
    row_block = math.gcd(image_rows, 32)
    outs = image_rows // row_block
    wide = 2 * G // LANES
    fine, low = np.arange(FINE), np.arange(LOW)
    angle = 2.0 * math.pi / FINE * (fine[:, None] * low[None, :] % FINE)
    odd = np.where(low == 0, 1.0 - 2.0 * (fine[:, None] % 2), np.sin(angle))
    unit = jnp.asarray(np.concatenate([np.cos(angle), odd], axis=1), bf16)
    scale = 1.0 / (SUB * math.sqrt(total))
    high = np.where(low == 0, LOW, FINE - low)
    angles = [2.0 * math.pi / G * (np.arange(SUB)[:, None] * k[None, :]) for k in (low, high)]
    twist = [f(angle) * scale for angle in angles for f in (np.cos, np.sin)]
    twist = jnp.asarray(np.concatenate(twist, axis=1), f32)
    counts = jnp.asarray(np.broadcast_to(np.arange(SUB)[:, None], (SUB, LANES)), bf16)
    last = chunks - 1

    def chunk_of(i):
        return jnp.minimum(i, last)

    if len(uv) == 1:
        uv_specs = [pl.BlockSpec((size * HALF, PACK), lambda i, *_: (chunk_of(i), 0))]
    else:
        uv_specs = [pl.BlockSpec(piece.shape, lambda i, *_: (0, 0)) for piece in uv]

    def fixed(operand):
        return pl.BlockSpec(operand.shape, lambda i, *_: (0, 0))

    image, tile = pl.pallas_call(
        functools.partial(
            image_kernel, pieces=len(uv), chunks=chunks, row_block=row_block, per_row=per_row,
            tile_cols=tile_cols,
        ),
        grid_spec=pltpu.PrefetchScalarGridSpec(
            num_scalar_prefetch=3,
            grid=(chunks + outs,),
            in_specs=[
                *uv_specs,
                pl.BlockSpec((1, size), lambda i, *_: (0, chunk_of(i))),
                pl.BlockSpec((2, image_rows, size), lambda i, *_: (0, 0, chunk_of(i))),
                fixed(columns),
                fixed(unit),
                fixed(counts),
                fixed(twist),
                pl.BlockSpec(memory_space=pl.ANY),
            ],
            out_specs=[
                pl.BlockSpec(
                    (row_block * wide, LANES), lambda i, *_: (jnp.maximum(i - chunks, 0), 0)
                ),
                pl.BlockSpec(memory_space=pl.ANY),
            ],
            scratch_shapes=[
                pltpu.VMEM((size * (HALF + 1) + HALF, PACK), f32),
                pltpu.VMEM((HALF, size, PACK), bf16),
                pltpu.VMEM((size, FINE), bf16),
                pltpu.VMEM((size, FINE), bf16),
                pltpu.VMEM((size, LANES), f32),
                pltpu.VMEM((2, 2 * image_rows, size), bf16),
                pltpu.VMEM((2, 2 * image_rows, size), bf16),
                pltpu.VMEM((SUB, 2, image_rows, FINE), f32),
                pltpu.VMEM((8 * (wide + 1) + wide, LANES), f32),
                pltpu.VMEM((3 * SUB * lanes, LANES), f32),
                pltpu.SMEM((per_row + 1,), jnp.int32),
                pltpu.SemaphoreType.DMA(()),
            ],
        ),
        out_shape=[
            jax.ShapeDtypeStruct((image_rows * wide, LANES), f32),
            jax.ShapeDtypeStruct(tile.shape, f32),
        ],
        input_output_aliases={9 + len(uv): 1},
        compiler_params=pltpu.CompilerParams(vmem_limit_bytes=VMEM_BYTES),
        name="image",
        interpret=interpret,
    )(
        info, *corners_all, *uv,
        corners_all[0].reshape(1, total), phase, columns, unit, counts, twist, tile,
    )
    image = image.reshape(image_rows, G // LANES, 2, LANES)
    tile = tile.reshape(tile_rows, tile_cols // LANES, 2, LANES)
    return (
        jnp.transpose(tile, (0, 2, 1, 3)).reshape(tile_rows, 2, tile_cols),
        jnp.transpose(image, (0, 2, 1, 3)).reshape(image_rows, 2, G),
    )


def packed_beams(beam_terms):
    count = beam_terms.shape[0]
    parts = beam_terms.reshape(count, 2, 2, HALF, SUB)
    return jnp.transpose(parts, (0, 3, 2, 1, 4)).reshape(count, HALF, PACK)


def pixel_factor(screen_depth, shift, vis_count):
    lane = jnp.arange(PACK, dtype=jnp.int32)
    col = lane % SUB
    imag = (lane // SUB) % 2
    row = jnp.arange(HALF, dtype=jnp.int32)[:, None] + (lane // (2 * SUB) * HALF)[None, :]

    def taper(x):
        return 1.0 - ((2.0 * x.astype(f32) + 1.0 - SUB) / SUB) ** 2

    def angle_sq(x):
        return ((x - HALF).astype(f32) * (field_view / SUB)) ** 2

    weight = taper(row) * taper(col) / math.sqrt(vis_count)
    turns = shift[:, None, None] * (row - HALF) % SUB
    angle = (
        -math.pi * screen_depth[:, None, None] * (angle_sq(row) + angle_sq(col))
        + 2.0 * math.pi / SUB * turns.astype(f32)
        - 0.5 * math.pi * imag.astype(f32)
    )
    return jnp.cos(angle) * weight


def from_partner(value, axis, mask):
    count = lax.axis_size(axis)
    return lax.ppermute(value, axis, [(i, i ^ mask) for i in range(count)])


def z_line(own, with_own):
    vert_count = lax.axis_size("vert")
    line = [from_partner(own, "vert", 2 * mask) for mask in range(1, vert_count // 2)]
    return jnp.concatenate([own] * with_own + line, axis=0)


def au_lines(line):
    return [line] + [from_partner(line, "au", mask) for mask in range(1, lax.axis_size("au"))]


def with_core(lines):
    return [piece for line in lines for piece in (line, from_partner(line, "vert", 1))]


def whole_gather(own):
    return [lax.all_gather(own, ("au", "vert"), axis=0, tiled=True)]


def gathered_place(owner, by_mask):
    if not by_mask:
        return owner
    vert_count = lax.axis_size("vert")
    au_mask = (owner // vert_count) ^ lax.axis_index("au")
    vert_mask = (owner % vert_count) ^ lax.axis_index("vert")
    return au_mask * vert_count + vert_mask % 2 * (vert_count // 2) + vert_mask // 2


def coded_corners(corners):
    digits = jnp.stack([corners[:, 0] // 128, corners[:, 0] % 128, corners[:, 1] // 128, corners[:, 1] % 128])
    flat = digits.astype(f32).astype(bf16).reshape(-1)
    return jnp.pad(flat, (0, HALF * PACK - flat.shape[0])).reshape(1, HALF, PACK)


def decoded_corners(blocks, count):
    digits = blocks.reshape(blocks.shape[0], HALF * PACK).astype(jnp.int32)
    high_row, low_row, high_col, low_col = [
        digits[:, i * count : (i + 1) * count].reshape(-1) for i in range(4)
    ]
    return (high_row * 128 + low_row, high_col * 128 + low_col)


def on_device(
    visibilities, baseline_offsets, channel_scale, screen_depth, stations, corners, beam_terms
):
    au_count = lax.axis_size("au")
    vert_count = lax.axis_size("vert")
    au_index, vert_index = lax.axis_index("au"), lax.axis_index("vert")
    image_rows = G // (au_count * vert_count)
    count, _, vis_count = visibilities.shape
    own_stations = beam_terms.shape[0]
    held = au_count * vert_count * count * HALF * PACK
    by_mask = held <= MASK_VALUES

    sent = jnp.concatenate([packed_beams(beam_terms), coded_corners(corners)], axis=0)
    offsets = baseline_offsets.reshape(2 * count, -1)
    scale_row = channel_scale.reshape(1, -1)
    part = math.gcd(count, 8)
    skies = [sky_sums(visibilities, offsets, scale_row, 0, part)]
    if by_mask:
        line = z_line(sent, True)
        line, offsets, skies[0], corners, stations, screen_depth = lax.optimization_barrier(
            (line, offsets, skies[0], corners, stations, screen_depth)
        )
    for s in range(part, count, part):
        skies.append(sky_sums(visibilities, offsets, scale_row, s, part))
    factor = pixel_factor(screen_depth, corners[:, 0] % SUB, vis_count)
    if by_mask:
        lines = au_lines(line)
        lines, skies = lax.optimization_barrier((lines, skies))
        tables = with_core(lines)
    else:
        tables = whole_gather(sent)
    coded = [
        piece.reshape(-1, own_stations + 1, HALF, PACK)[:, own_stations] for piece in tables
    ]
    corners_all = decoded_corners(jnp.concatenate(coded, axis=0), count)
    owners = stations // own_stations
    station_rows = gathered_place(owners, by_mask) * (own_stations + 1) + stations % own_stations
    uv_own = corrected_subgrids(station_rows, tables, skies, factor)

    per_row = vert_count * count
    tile_rows, tile_cols = G // au_count, G // vert_count

    def tile_info(row):
        place = gathered_place(row * vert_count + vert_index, by_mask) // vert_count
        return jnp.stack([place, au_index * tile_rows, vert_index * tile_cols])

    own_info = tile_info(au_index)
    before_info = tile_info(lax.rem(au_index + au_count - 1, au_count))
    first_row = (au_index * vert_count + vert_index) * image_rows
    tables = image_tables(corners_all[1], first_row, image_rows)
    if by_mask:
        blocks, line = au_lines(uv_own), z_line(uv_own, False)
        blocks, line, tables, corners_all, own_info, before_info = lax.optimization_barrier(
            (blocks, line, tables, corners_all, own_info, before_info)
        )
        lines = au_lines(line)
        own_row = [uv_own, line] + [from_partner(piece, "vert", 1) for piece in (uv_own, line)]
        tile = uv_tile_own(own_row, own_info, corners_all, per_row, tile_rows, tile_cols)
        lines, own_row, tile = lax.optimization_barrier((lines, own_row, tile))
        uv = own_row
        for pair in zip(blocks[1:], lines[1:]):
            uv = uv + [*pair, *[from_partner(piece, "vert", 1) for piece in pair]]
    else:
        uv = whole_gather(uv_own)
        tile = uv_tile_own(uv, own_info, corners_all, per_row, tile_rows, tile_cols)
    return image_rows_of(
        uv, corners_all, tables, tile, before_info, per_row, tile_rows, tile_cols
    )


def solution(mesh):
    return jax.shard_map(
        on_device,
        mesh=mesh,
        in_specs=(
            P(("au", "vert"), None, None),
            P(("au", "vert"), None, None),
            P(),
            P(("au", "vert")),
            P(("au", "vert"), None),
            P(("au", "vert"), None),
            P(("au", "vert"), None, None),
        ),
        out_specs=(P("au", None, "vert"), P(("au", "vert"), None, None)),
        check_vma=False,
    )
```

```python
import functools
import math

import jax
import jax.numpy as jnp
import numpy as np
from jax import lax
from jax.experimental import pallas as pl
from jax.experimental.pallas import tpu as pltpu
from jax.sharding import PartitionSpec as P

G = 8192
SUB = 32
HALF = SUB // 2
PACK = 4 * SUB
LANES = 128
FINE = G // SUB
LOW = FINE // 2
CHUNK = 768
MASK_VALUES = 1 << 22
field_view = 0.1
bf16 = jnp.bfloat16
f32 = jnp.float32
VMEM_BYTES = 58 * 1024 * 1024


def cmul(a, b):
    return (a[0] * b[0] - a[1] * b[1], a[0] * b[1] + a[1] * b[0])


def conj(a):
    return (a[0], -a[1])


def sky_kernel(vis_ref, offset_ref, scale_ref, out_ref, power_ref):
    count, _, vis_count = vis_ref.shape
    times = offset_ref.shape[1]
    step = math.gcd(vis_count, 256)
    row = lax.broadcasted_iota(jnp.int32, (8, step), 0)
    bits = [(row >> bit) % 2 == 1 for bit in range(3)]

    offsets = offset_ref[...]
    parts = []
    for _ in range(3):
        parts.append(offsets.astype(bf16))
        offsets = offsets - parts[-1].astype(f32)
    channels = vis_count // times
    repeats = max(1, LANES // channels)
    scale = jnp.concatenate([scale_ref[...]] * repeats, axis=1)
    width = math.gcd(vis_count, 512)
    scale = jnp.concatenate([scale] * (width // (repeats * channels)), axis=1)
    for start in range(0, vis_count, width):
        at = pl.ds(start, width)
        time = lax.broadcasted_iota(jnp.int32, (times, width), 0)
        place = lax.broadcasted_iota(jnp.int32, (times, width), 1) + start
        one = (place // channels == time).astype(f32).astype(bf16)
        shifts = sum(jnp.dot(part, one, preferred_element_type=f32) for part in parts)
        half = (math.pi / SUB) * (shifts * scale)
        square = half * half
        sine, cosine = 1.0, 1.0
        for term in (12, 10, 8, 6, 4, 2):
            sine = 1.0 - square * (1.0 / (term * (term + 1))) * sine
            cosine = 1.0 - square * (1.0 / (term * (term - 1))) * cosine
        sine = sine * half
        power = (1.0 - 2.0 * sine * sine, 2.0 * sine * cosine)
        for bit in range(5):
            power_ref[bit, 0, :, at] = power[0]
            power_ref[bit, 1, :, at] = power[1]
            power = (power[0] * power[0] - power[1] * power[1], 2.0 * power[0] * power[1])

    def powers(row, at, extra):
        z = [
            tuple(
                jnp.broadcast_to(power_ref[bit, part, pl.ds(row, 1), at], (8, step))
                for part in range(2)
            )
            for bit in range(5)
        ]
        low = (jnp.where(bits[0], z[0][0], 1.0), jnp.where(bits[0], z[0][1], 0.0))
        for bit in (1, 2):
            more = cmul(low, z[bit])
            low = (jnp.where(bits[bit], more[0], low[0]), jnp.where(bits[bit], more[1], low[1]))
        if extra is not None:
            low = cmul(low, extra)
        blocks = [cmul(low, conj(z[4])), cmul(low, conj(z[3])), low, cmul(low, z[3])]
        return jnp.concatenate([block[part] for part in range(2) for block in blocks], axis=0).astype(bf16)

    def one_subgrid(s):
        both = jnp.zeros((2 * SUB, 2 * SUB), f32)
        for start in range(0, vis_count, step):
            at = pl.ds(start, step)
            vis = tuple(
                jnp.broadcast_to(vis_ref[s, part : part + 1, at].astype(f32), (8, step))
                for part in range(2)
            )
            left = powers(2 * s, at, vis)
            right = powers(2 * s + 1, at, None)
            both += lax.dot_general(
                left, right, (((1,), (1,)), ((), ())), preferred_element_type=f32
            )
        real = both[:SUB, :SUB] - both[SUB:, SUB:]
        image = both[:SUB, SUB:] + both[SUB:, :SUB]
        out_ref[s] = jnp.concatenate(
            [real[:HALF], image[:HALF], real[HALF:], image[HALF:]], axis=1
        )

    def some(i, carry):
        for k in range(math.gcd(count, 2)):
            one_subgrid(i * math.gcd(count, 2) + k)
        return carry

    lax.fori_loop(0, count // math.gcd(count, 2), some, 0)


def sky_sums(visibilities, offsets, scale_row, first, count, interpret=False):
    vis_count = visibilities.shape[2]
    times = offsets.shape[1]
    at = first // count
    return pl.pallas_call(
        sky_kernel,
        grid=(1,),
        in_specs=[
            pl.BlockSpec((count, 2, vis_count), lambda i: (at, 0, 0)),
            pl.BlockSpec((2 * count, times), lambda i: (at, 0)),
            pl.BlockSpec(scale_row.shape, lambda i: (0, 0)),
        ],
        out_specs=pl.BlockSpec((count, HALF, PACK), lambda i: (0, 0, 0)),
        out_shape=jax.ShapeDtypeStruct((count, HALF, PACK), f32),
        scratch_shapes=[pltpu.VMEM((5, 2, 2 * count, vis_count), f32)],
        compiler_params=pltpu.CompilerParams(vmem_limit_bytes=VMEM_BYTES),
        cost_estimate=pl.CostEstimate(
            flops=0, bytes_accessed=count * 2_500_000, transcendentals=0
        ),
        name="sky_sums",
        interpret=interpret,
    )(visibilities, offsets, scale_row)


def correct_kernel(stations_ref, *refs, pieces, skies):
    table_refs, refs = refs[:pieces], refs[pieces:]
    sky_refs, refs = refs[:skies], refs[skies:]
    factor_ref, right_ref, left_ref, out_ref, table_ref, mid_ref = refs
    count = factor_ref.shape[0]
    lane = lax.broadcasted_iota(jnp.int32, (HALF, PACK), 1)
    imag = (lane // SUB) % 2 == 1
    sign = jnp.where(imag, 1.0, -1.0)

    def up(x):
        return pltpu.roll(x, SUB, 1)

    def down(x):
        return pltpu.roll(x, PACK - SUB, 1)

    def product(a, b):
        swapped = jnp.where(imag, up(a), down(a))
        return a * jnp.where(imag, up(b), b) + sign * swapped * jnp.where(imag, b, down(b))

    held = 0
    for piece in table_refs:
        table_ref[held : held + piece.shape[0]] = piece[...]
        held += piece.shape[0]
    for s in range(count):
        first = table_ref[stations_ref[2 * s]].astype(f32)
        second = table_ref[stations_ref[2 * s + 1]].astype(f32)
        pair = product(first, -sign * second)
        per = count // skies
        sky = product(sky_refs[s // per][s % per], factor_ref[s])
        mid_ref[HALF * s : HALF * (s + 1), :] = product(sky, pair).astype(bf16)
    mid = jnp.dot(mid_ref[...], right_ref[...], preferred_element_type=f32).astype(bf16)
    for s in range(count):
        rows = mid[HALF * s : HALF * (s + 1)]
        tall = jnp.concatenate([rows[:, : 2 * SUB], rows[:, 2 * SUB :]], axis=0)
        four = jnp.dot(left_ref[...], tall, preferred_element_type=f32)
        real = four[:SUB, :SUB] - four[SUB:, SUB:]
        image = four[:SUB, SUB:] + four[SUB:, :SUB]
        out_ref[s] = jnp.concatenate(
            [real[:HALF], image[:HALF], real[HALF:], image[HALF:]], axis=1
        ).astype(bf16)


def corrected_subgrids(stations, tables, skies, factor, interpret=False):
    count = factor.shape[0]
    centred = np.arange(SUB) - HALF
    angle = 2.0 * math.pi / SUB * (centred[:, None] * centred[None, :] % SUB)
    re, im = np.cos(angle) / SUB, -np.sin(angle) / SUB
    right = jnp.asarray(np.kron(np.eye(2), np.block([[re, im], [-im, re]])), bf16)
    left = jnp.asarray(np.concatenate([re, im], axis=0), bf16)
    rows = sum(piece.shape[0] for piece in tables)
    operands = [*tables, *skies, factor, right, left]

    def whole(operand):
        return pl.BlockSpec(operand.shape, lambda i, *_: (0,) * operand.ndim)

    return pl.pallas_call(
        functools.partial(correct_kernel, pieces=len(tables), skies=len(skies)),
        grid_spec=pltpu.PrefetchScalarGridSpec(
            num_scalar_prefetch=1,
            grid=(1,),
            in_specs=[whole(operand) for operand in operands],
            out_specs=pl.BlockSpec((count, HALF, PACK), lambda i, *_: (0, 0, 0)),
            scratch_shapes=[
                pltpu.VMEM((rows, HALF, PACK), bf16),
                pltpu.VMEM((HALF * count, PACK), bf16),
            ],
        ),
        out_shape=jax.ShapeDtypeStruct((count, HALF, PACK), bf16),
        compiler_params=pltpu.CompilerParams(vmem_limit_bytes=VMEM_BYTES),
        cost_estimate=pl.CostEstimate(flops=0, bytes_accessed=16_000_000, transcendentals=0),
        name="correct",
        interpret=interpret,
    )(stations.reshape(-1), *operands)


def listed(list_ref, first, count, wanted):
    def scan(i, found):
        list_ref[found] = first + i
        return found + wanted(first + i).astype(jnp.int32)

    return lax.fori_loop(0, count, scan, jnp.int32(0), unroll=math.gcd(count, 8))


def add_subgrid(packed, row_at, col_at, total_ref, lanes):
    lane = lax.broadcasted_iota(jnp.int32, (8, LANES), 1)
    row = lax.broadcasted_iota(jnp.int32, (8, LANES), 0)
    tile = col_at // LANES
    offset = col_at % LANES
    shift = row_at % SUB
    base = row_at - shift

    def place(over):
        inside = lane < offset + SUB - LANES
        if not over:
            inside = (lane >= offset) & (lane < offset + SUB)
        for h in range(2):
            for part in range(2):
                from_lane = (2 * h + part) * SUB
                moved = pltpu.roll(packed, lax.rem(offset - from_lane + LANES, LANES), 1)
                for group in range(2):
                    values = moved[8 * group : 8 * (group + 1)]
                    first_row = HALF * h + 8 * group
                    late = row + first_row >= shift
                    for wrapped in range(2):
                        keep = jnp.logical_and(inside, late if wrapped == 0 else ~late)
                        start = (base + SUB * wrapped + first_row) * lanes
                        start = start + 2 * (tile + over) + part
                        at = pl.ds(start, 8, stride=lanes)
                        total_ref[at, :] = total_ref[at, :] + jnp.where(keep, values, 0.0)

    place(0)

    @pl.when(offset + SUB > LANES)
    def _():
        place(1)


def tile_kernel(info_ref, row_ref, col_ref, *refs, pieces, tile_rows, tile_cols):
    uv_refs = refs[:pieces]
    out_ref, held_ref, total_ref, list_ref, sems = refs[pieces:]
    lanes = 2 * tile_cols // LANES
    count = held_ref.shape[0] // HALF
    first, row_first, col_first = info_ref[0] * count, info_ref[1], info_ref[2]
    rows_all = total_ref.shape[0]
    zero_rows = math.gcd(rows_all, 1024)

    def clear(i, carry):
        at = pl.ds(pl.multiple_of(i * zero_rows, zero_rows), zero_rows)
        total_ref[at, :] = jnp.zeros((zero_rows, LANES), f32)
        return carry

    lax.fori_loop(0, rows_all // zero_rows, clear, 0)
    held = 0
    for piece in uv_refs:
        held_ref[held : held + piece.shape[0]] = piece[...]
        held += piece.shape[0]

    def wanted(s):
        col_at = col_ref[s] - col_first
        return (col_at >= 0) & (col_at < tile_cols)

    def one(entry, carry):
        s = list_ref[entry]
        at = pl.ds(pl.multiple_of((s - first) * HALF, HALF), HALF)
        packed = held_ref[at, :].astype(f32)
        add_subgrid(packed, row_ref[s] - row_first, col_ref[s] - col_first, total_ref, lanes)
        return carry

    lax.fori_loop(0, listed(list_ref, first, count, wanted), one, 0)
    parts = sems.shape[0]
    size = tile_rows * lanes // parts
    copies = [
        pltpu.make_async_copy(
            total_ref.at[pl.ds(i * size, size), :], out_ref.at[pl.ds(i * size, size), :], sems.at[i]
        )
        for i in range(parts)
    ]
    for copy in copies:
        copy.start()
    for copy in copies:
        copy.wait()


def uv_tile_own(uv, info, corners, count, tile_rows, tile_cols, interpret=False):
    lanes = 2 * tile_cols // LANES
    uv = [piece.reshape(-1, PACK) for piece in uv]
    if len(uv) == 1:
        uv_specs = [pl.BlockSpec((count * HALF, PACK), lambda i, info, *_: (info[0], 0))]
    else:
        uv_specs = [pl.BlockSpec(piece.shape, lambda i, *_: (0, 0)) for piece in uv]
    return pl.pallas_call(
        functools.partial(
            tile_kernel, pieces=len(uv), tile_rows=tile_rows, tile_cols=tile_cols
        ),
        grid_spec=pltpu.PrefetchScalarGridSpec(
            num_scalar_prefetch=3,
            grid=(1,),
            in_specs=uv_specs,
            out_specs=pl.BlockSpec(memory_space=pl.ANY),
            scratch_shapes=[
                pltpu.VMEM((count * HALF, PACK), bf16),
                pltpu.VMEM(((tile_rows + 2 * SUB) * lanes, LANES), f32),
                pltpu.SMEM((count + 1,), jnp.int32),
                pltpu.SemaphoreType.DMA((4,)),
            ],
        ),
        out_shape=jax.ShapeDtypeStruct((tile_rows * lanes, LANES), f32),
        compiler_params=pltpu.CompilerParams(vmem_limit_bytes=VMEM_BYTES),
        cost_estimate=pl.CostEstimate(
            flops=0, bytes_accessed=20 * tile_rows * tile_cols, transcendentals=0
        ),
        name="uv_tile",
        interpret=interpret,
    )(info, *corners, *uv)


def short_transform(values):
    count = len(values)
    if count == 1:
        return values
    even = short_transform(values[0::2])
    odd = short_transform(values[1::2])
    low, high = [], []
    for k in range(count // 2):
        re, im = odd[k]
        if k == 0:
            turned = (re, im)
        elif 4 * k == count:
            turned = (-im, re)
        elif 8 * k == count:
            root = math.sqrt(0.5)
            turned = ((re - im) * root, (re + im) * root)
        elif 8 * k == 3 * count:
            root = math.sqrt(0.5)
            turned = ((re + im) * -root, (re - im) * root)
        else:
            c, s = math.cos(2 * math.pi * k / count), math.sin(2 * math.pi * k / count)
            turned = (re * c - im * s, re * s + im * c)
        low.append((even[k][0] + turned[0], even[k][1] + turned[1]))
        high.append((even[k][0] - turned[0], even[k][1] - turned[1]))
    return low + high


def image_kernel(
    info_ref, row_ref, col_ref, *refs, pieces, chunks, row_block, per_row, tile_cols
):
    uv_refs, refs = refs[:pieces], refs[pieces:]
    corner_ref, phase_ref, columns_ref, unit_ref, count_ref, twist_ref = refs[:6]
    out_ref, tile_ref, uv_wide, uv_rows, here, after, shifts, left_even, left_odd, total = refs[7:17]
    staged, spill, list_ref, sem = refs[17:]
    step = pl.program_id(0)
    lanes = 2 * tile_cols // LANES
    head = pltpu.make_async_copy(
        tile_ref.at[pl.ds(0, SUB * lanes), :], spill.at[pl.ds(SUB * lanes, SUB * lanes), :], sem
    )
    back = pltpu.make_async_copy(
        spill.at[pl.ds(SUB * lanes, SUB * lanes), :], tile_ref.at[pl.ds(0, SUB * lanes), :], sem
    )

    def add_spilled():
        def row_of(s):
            return lax.rem(row_ref[s] - info_ref[1] + SUB + G, G)

        def wanted(s):
            col_at = col_ref[s] - info_ref[2]
            mine = (col_at >= 0) & (col_at < tile_cols) & (row_of(s) < SUB)
            return mine & (s >= step * size) & (s < (step + 1) * size)

        def one(entry, carry):
            s = list_ref[entry]
            packed = uv_wide[pl.ds((s - step * size) * (HALF + 1), HALF), :]
            add_subgrid(packed, row_of(s), col_ref[s] - info_ref[2], spill, lanes)
            return carry

        found = listed(list_ref, info_ref[0] * per_row, per_row, wanted)
        lax.fori_loop(0, found, one, 0)

    size = uv_rows.shape[1]
    image_rows = phase_ref.shape[1]

    def products(pair, h, left, start, width):
        at = pl.ds(2 * image_rows * h, 2 * image_rows)
        items = pl.ds(start, width)
        spread = lax.dot_general(
            columns_ref[at, :], uv_rows[pair, items, :], (((1,), (1,)), ((), ())),
            preferred_element_type=f32,
        ).astype(bf16)
        turned = cmul(
            (spread[:image_rows], spread[image_rows:]), (phase_ref[0, :, items], phase_ref[1, :, items])
        )
        left[h, :image_rows, items] = turned[0]
        left[h, image_rows:, items] = turned[1]

    def table_of(index):
        late = shifts[...] > index.astype(f32)
        return jnp.concatenate(
            [
                jnp.where(late, after[:, t : t + LANES], here[:, t : t + LANES])
                for t in range(0, FINE, LANES)
            ],
            axis=1,
        )

    def keep_sums(index, real, image, first):
        even_re, odd_re = real[:, :LOW], real[:, LOW:]
        even_im, odd_im = image[:, :LOW], image[:, LOW:]
        edge = lax.broadcasted_iota(jnp.int32, (image_rows, LOW), 1) == 0
        low = (
            even_re - jnp.where(edge, 0.0, odd_im),
            even_im + jnp.where(edge, 0.0, odd_re),
        )
        high = (
            jnp.where(edge, odd_re, even_re + odd_im),
            jnp.where(edge, odd_im, even_im - odd_re),
        )
        twist = twist_ref[pl.ds(index, 1), :]
        for half, got in enumerate((low, high)):
            start = 2 * LOW * half
            done = cmul(
                got, (twist[:, start : start + LOW], twist[:, start + LOW : start + 2 * LOW])
            )
            for part in range(2):
                at = (index, part, slice(None), pl.ds(LOW * half, LOW))
                total[at] = done[part] if first else total[at] + done[part]

    third = size // 3 if size % (3 * LANES) == 0 else size

    def products_and_sums(later, left_later, pair, left, first):
        for h in range(2):
            starts = list(range(0, size, third))
            index = pair + HALF * h
            products(later, h, left_later, starts[0], third)
            table = table_of(index)
            real = jnp.dot(left[h, :image_rows], table, preferred_element_type=f32)
            for start in starts[1:2]:
                products(later, h, left_later, start, third)
            image = jnp.dot(left[h, image_rows:], table, preferred_element_type=f32)
            for start in starts[2:]:
                products(later, h, left_later, start, third)
            keep_sums(index, real, image, first)

    def chunk(first):
        if first:
            head.start()
        held = 0
        for piece in uv_refs:

            def spread_out(s, carry, piece=piece, held=held):
                block = piece[pl.ds(pl.multiple_of(s * HALF, HALF), HALF), :]
                uv_wide[pl.ds((held + s) * (HALF + 1), HALF), :] = block.astype(f32)
                return carry

            count = piece.shape[0] // HALF
            lax.fori_loop(0, count, spread_out, 0, unroll=math.gcd(count, 8))
            held += count
        for row in range(HALF):
            uv_rows[row] = uv_wide[pl.ds(row, size, stride=HALF + 1), :].astype(bf16)
        if first:
            head.wait()
        add_spilled()
        pl.when(step == chunks - 1)(back.start)
        corner = corner_ref[...]
        coarse, shift = corner // SUB, corner % SUB

        def looked_up(index, length, table):
            place = lax.broadcasted_iota(jnp.int32, (length, size), 0)
            one = (place == index).astype(f32).astype(bf16)
            return lax.dot_general(one, table, (((0,), (0,)), ((), ())), preferred_element_type=f32)

        here[...] = looked_up(coarse, FINE, unit_ref[...]).astype(bf16)
        after[...] = looked_up(lax.rem(coarse + 1, FINE), FINE, unit_ref[...]).astype(bf16)
        shifts[...] = looked_up(shift, SUB, count_ref[...])
        for h in range(2):
            products(0, h, left_even, 0, size)

        def two_pairs(i, carry):
            products_and_sums(2 * i + 1, left_odd, 2 * i, left_even, first)
            products_and_sums(
                jnp.minimum(2 * i + 2, HALF - 1), left_even, 2 * i + 1, left_odd, first
            )
            return carry

        lax.fori_loop(0, HALF // 2, two_pairs, 0)
        pl.when(step == chunks - 1)(back.wait)

    @pl.when(step == 0)
    def _():
        chunk(True)

    if chunks > 1:

        @pl.when((step > 0) & (step < chunks))
        def _():
            chunk(False)

    @pl.when(step >= chunks)
    def _():
        first = (step - chunks) * row_block
        wide = 2 * G // LANES
        backward = lax.rem(LOW - lax.broadcasted_iota(jnp.int32, (8, LOW), 1), LOW)

        def eight_rows(group, carry):
            at = pl.ds(pl.multiple_of(first + 8 * group, 8), 8)
            for tile in range(FINE // LANES):
                lanes = pl.ds(tile * LANES, LANES)
                values = [(total[n, 0, at, lanes], total[n, 1, at, lanes]) for n in range(SUB)]
                for k, value in enumerate(short_transform(values)):
                    for part in range(2):
                        ordered = value[part]
                        if tile > 0:
                            ordered = jnp.take_along_axis(
                                ordered, backward, axis=1, mode="promise_in_bounds"
                            )
                        column = 2 * (k * (FINE // LANES) + tile) + part
                        staged[pl.ds(column, 8, stride=wide + 1), :] = ordered
            for row in range(8):
                at = pl.ds(pl.multiple_of((8 * group + row) * wide, wide), wide)
                out_ref[at, :] = staged[row * (wide + 1) : row * (wide + 1) + wide, :]
            return carry

        lax.fori_loop(0, row_block // 8, eight_rows, 0)


def image_tables(corner_cols, first_row, image_rows):
    rows = first_row + jnp.arange(image_rows, dtype=jnp.int32)
    turn = 2.0 * math.pi / G
    angle = turn * (rows[:, None] * corner_cols[None, :] % G).astype(f32)
    phase = jnp.stack([jnp.cos(angle), jnp.sin(angle)]).astype(bf16)
    angle = turn * (rows[:, None] * jnp.arange(SUB, dtype=jnp.int32)[None, :] % G).astype(f32)
    re, im = jnp.cos(angle), jnp.sin(angle)
    block = jnp.concatenate(
        [jnp.concatenate([re, -im], axis=1), jnp.concatenate([im, re], axis=1)], axis=0
    )
    columns = jnp.kron(jnp.eye(2, dtype=f32), block).astype(bf16)
    return phase, columns


def image_rows_of(
    uv, corners_all, tables, tile, info, per_row, tile_rows, tile_cols, interpret=False
):
    phase, columns = tables
    image_rows = phase.shape[1]
    lanes = 2 * tile_cols // LANES
    uv = [piece.reshape(-1, PACK) for piece in uv]
    total = corners_all[0].shape[0]
    size = math.gcd(total, CHUNK) if len(uv) == 1 else total
    chunks = total // size
    row_block = math.gcd(image_rows, 32)
    outs = image_rows // row_block
    wide = 2 * G // LANES
    fine, low = np.arange(FINE), np.arange(LOW)
    angle = 2.0 * math.pi / FINE * (fine[:, None] * low[None, :] % FINE)
    odd = np.where(low == 0, 1.0 - 2.0 * (fine[:, None] % 2), np.sin(angle))
    unit = jnp.asarray(np.concatenate([np.cos(angle), odd], axis=1), bf16)
    scale = 1.0 / (SUB * math.sqrt(total))
    high = np.where(low == 0, LOW, FINE - low)
    angles = [2.0 * math.pi / G * (np.arange(SUB)[:, None] * k[None, :]) for k in (low, high)]
    twist = [f(angle) * scale for angle in angles for f in (np.cos, np.sin)]
    twist = jnp.asarray(np.concatenate(twist, axis=1), f32)
    counts = jnp.asarray(np.broadcast_to(np.arange(SUB)[:, None], (SUB, LANES)), bf16)
    last = chunks - 1

    def chunk_of(i):
        return jnp.minimum(i, last)

    if len(uv) == 1:
        uv_specs = [pl.BlockSpec((size * HALF, PACK), lambda i, *_: (chunk_of(i), 0))]
    else:
        uv_specs = [pl.BlockSpec(piece.shape, lambda i, *_: (0, 0)) for piece in uv]

    def fixed(operand):
        return pl.BlockSpec(operand.shape, lambda i, *_: (0, 0))

    image, tile = pl.pallas_call(
        functools.partial(
            image_kernel, pieces=len(uv), chunks=chunks, row_block=row_block, per_row=per_row,
            tile_cols=tile_cols,
        ),
        grid_spec=pltpu.PrefetchScalarGridSpec(
            num_scalar_prefetch=3,
            grid=(chunks + outs,),
            in_specs=[
                *uv_specs,
                pl.BlockSpec((1, size), lambda i, *_: (0, chunk_of(i))),
                pl.BlockSpec((2, image_rows, size), lambda i, *_: (0, 0, chunk_of(i))),
                fixed(columns),
                fixed(unit),
                fixed(counts),
                fixed(twist),
                pl.BlockSpec(memory_space=pl.ANY),
            ],
            out_specs=[
                pl.BlockSpec(
                    (row_block * wide, LANES), lambda i, *_: (jnp.maximum(i - chunks, 0), 0)
                ),
                pl.BlockSpec(memory_space=pl.ANY),
            ],
            scratch_shapes=[
                pltpu.VMEM((size * (HALF + 1) + HALF, PACK), f32),
                pltpu.VMEM((HALF, size, PACK), bf16),
                pltpu.VMEM((size, FINE), bf16),
                pltpu.VMEM((size, FINE), bf16),
                pltpu.VMEM((size, LANES), f32),
                pltpu.VMEM((2, 2 * image_rows, size), bf16),
                pltpu.VMEM((2, 2 * image_rows, size), bf16),
                pltpu.VMEM((SUB, 2, image_rows, FINE), f32),
                pltpu.VMEM((8 * (wide + 1) + wide, LANES), f32),
                pltpu.VMEM((3 * SUB * lanes, LANES), f32),
                pltpu.SMEM((per_row + 1,), jnp.int32),
                pltpu.SemaphoreType.DMA(()),
            ],
        ),
        out_shape=[
            jax.ShapeDtypeStruct((image_rows * wide, LANES), f32),
            jax.ShapeDtypeStruct(tile.shape, f32),
        ],
        input_output_aliases={9 + len(uv): 1},
        compiler_params=pltpu.CompilerParams(vmem_limit_bytes=VMEM_BYTES),
        name="image",
        interpret=interpret,
    )(
        info, *corners_all, *uv,
        corners_all[0].reshape(1, total), phase, columns, unit, counts, twist, tile,
    )
    image = image.reshape(image_rows, G // LANES, 2, LANES)
    tile = tile.reshape(tile_rows, tile_cols // LANES, 2, LANES)
    return (
        jnp.transpose(tile, (0, 2, 1, 3)).reshape(tile_rows, 2, tile_cols),
        jnp.transpose(image, (0, 2, 1, 3)).reshape(image_rows, 2, G),
    )


def packed_beams(beam_terms):
    count = beam_terms.shape[0]
    parts = beam_terms.reshape(count, 2, 2, HALF, SUB)
    return jnp.transpose(parts, (0, 3, 2, 1, 4)).reshape(count, HALF, PACK)


def pixel_factor(screen_depth, shift, vis_count):
    lane = jnp.arange(PACK, dtype=jnp.int32)
    col = lane % SUB
    imag = (lane // SUB) % 2
    row = jnp.arange(HALF, dtype=jnp.int32)[:, None] + (lane // (2 * SUB) * HALF)[None, :]

    def taper(x):
        return 1.0 - ((2.0 * x.astype(f32) + 1.0 - SUB) / SUB) ** 2

    def angle_sq(x):
        return ((x - HALF).astype(f32) * (field_view / SUB)) ** 2

    weight = taper(row) * taper(col) / math.sqrt(vis_count)
    turns = shift[:, None, None] * (row - HALF) % SUB
    angle = (
        -math.pi * screen_depth[:, None, None] * (angle_sq(row) + angle_sq(col))
        + 2.0 * math.pi / SUB * turns.astype(f32)
        - 0.5 * math.pi * imag.astype(f32)
    )
    return jnp.cos(angle) * weight


def from_partner(value, axis, mask):
    count = lax.axis_size(axis)
    return lax.ppermute(value, axis, [(i, i ^ mask) for i in range(count)])


def z_line(own):
    vert_count = lax.axis_size("vert")
    line = [own] + [from_partner(own, "vert", 2 * mask) for mask in range(1, vert_count // 2)]
    return jnp.concatenate(line, axis=0)


def au_lines(line):
    return [line] + [from_partner(line, "au", mask) for mask in range(1, lax.axis_size("au"))]


def with_core(lines):
    return [piece for line in lines for piece in (line, from_partner(line, "vert", 1))]


def whole_gather(own):
    return [lax.all_gather(own, ("au", "vert"), axis=0, tiled=True)]


def gathered_place(owner, by_mask):
    if not by_mask:
        return owner
    vert_count = lax.axis_size("vert")
    au_mask = (owner // vert_count) ^ lax.axis_index("au")
    vert_mask = (owner % vert_count) ^ lax.axis_index("vert")
    return au_mask * vert_count + vert_mask % 2 * (vert_count // 2) + vert_mask // 2


def coded_corners(corners):
    digits = jnp.stack([corners[:, 0] // 128, corners[:, 0] % 128, corners[:, 1] // 128, corners[:, 1] % 128])
    flat = digits.astype(f32).astype(bf16).reshape(-1)
    return jnp.pad(flat, (0, HALF * PACK - flat.shape[0])).reshape(1, HALF, PACK)


def decoded_corners(blocks, count):
    digits = blocks.reshape(blocks.shape[0], HALF * PACK).astype(jnp.int32)
    high_row, low_row, high_col, low_col = [
        digits[:, i * count : (i + 1) * count].reshape(-1) for i in range(4)
    ]
    return (high_row * 128 + low_row, high_col * 128 + low_col)


def on_device(
    visibilities, baseline_offsets, channel_scale, screen_depth, stations, corners, beam_terms
):
    au_count = lax.axis_size("au")
    vert_count = lax.axis_size("vert")
    au_index, vert_index = lax.axis_index("au"), lax.axis_index("vert")
    image_rows = G // (au_count * vert_count)
    count, _, vis_count = visibilities.shape
    own_stations = beam_terms.shape[0]
    held = au_count * vert_count * count * HALF * PACK
    by_mask = held <= MASK_VALUES

    sent = jnp.concatenate([packed_beams(beam_terms), coded_corners(corners)], axis=0)
    offsets = baseline_offsets.reshape(2 * count, -1)
    scale_row = channel_scale.reshape(1, -1)
    part = math.gcd(count, 8)
    skies = [sky_sums(visibilities, offsets, scale_row, 0, part)]
    if by_mask:
        line = z_line(sent)
        line, offsets, skies[0], corners, stations, screen_depth = lax.optimization_barrier(
            (line, offsets, skies[0], corners, stations, screen_depth)
        )
    for s in range(part, count, part):
        skies.append(sky_sums(visibilities, offsets, scale_row, s, part))
    factor = pixel_factor(screen_depth, corners[:, 0] % SUB, vis_count)
    if by_mask:
        lines = au_lines(line)
        lines, skies = lax.optimization_barrier((lines, skies))
        tables = with_core(lines)
    else:
        tables = whole_gather(sent)
    coded = [
        piece.reshape(-1, own_stations + 1, HALF, PACK)[:, own_stations] for piece in tables
    ]
    corners_all = decoded_corners(jnp.concatenate(coded, axis=0), count)
    owners = stations // own_stations
    station_rows = gathered_place(owners, by_mask) * (own_stations + 1) + stations % own_stations
    uv_own = corrected_subgrids(station_rows, tables, skies, factor)

    per_row = vert_count * count
    tile_rows, tile_cols = G // au_count, G // vert_count

    def tile_info(row):
        place = gathered_place(row * vert_count + vert_index, by_mask) // vert_count
        return jnp.stack([place, au_index * tile_rows, vert_index * tile_cols])

    own_info = tile_info(au_index)
    before_info = tile_info(lax.rem(au_index + au_count - 1, au_count))
    first_row = (au_index * vert_count + vert_index) * image_rows
    tables = image_tables(corners_all[1], first_row, image_rows)
    if by_mask:
        line = z_line(uv_own)
        line, tables, corners_all, own_info, before_info = lax.optimization_barrier(
            (line, tables, corners_all, own_info, before_info)
        )
        lines = au_lines(line)
        own_row = with_core(lines[:1])
        tile = uv_tile_own(own_row, own_info, corners_all, per_row, tile_rows, tile_cols)
        lines, own_row, tile = lax.optimization_barrier((lines, own_row, tile))
        uv = own_row + with_core(lines[1:])
    else:
        uv = whole_gather(uv_own)
        tile = uv_tile_own(uv, own_info, corners_all, per_row, tile_rows, tile_cols)
    return image_rows_of(
        uv, corners_all, tables, tile, before_info, per_row, tile_rows, tile_cols
    )


def solution(mesh):
    return jax.shard_map(
        on_device,
        mesh=mesh,
        in_specs=(
            P(("au", "vert"), None, None),
            P(("au", "vert"), None, None),
            P(),
            P(("au", "vert")),
            P(("au", "vert"), None),
            P(("au", "vert"), None),
            P(("au", "vert"), None, None),
        ),
        out_specs=(P("au", None, "vert"), P(("au", "vert"), None, None)),
        check_vma=False,
    )
```

```python
import functools
import math

import jax
import jax.numpy as jnp
import numpy as np
from jax import lax
from jax.experimental import pallas as pl
from jax.experimental.pallas import tpu as pltpu
from jax.sharding import PartitionSpec as P

G = 8192
SUB = 32
HALF = SUB // 2
PACK = 4 * SUB
LANES = 128
FINE = G // SUB
LOW = FINE // 2
CHUNK = 768
MASK_VALUES = 1 << 22
field_view = 0.1
bf16 = jnp.bfloat16
f32 = jnp.float32
VMEM_BYTES = 58 * 1024 * 1024


def cmul(a, b):
    return (a[0] * b[0] - a[1] * b[1], a[0] * b[1] + a[1] * b[0])


def conj(a):
    return (a[0], -a[1])


def sky_kernel(vis_ref, offset_ref, scale_ref, out_ref, power_ref):
    count, _, vis_count = vis_ref.shape
    times = offset_ref.shape[1]
    step = math.gcd(vis_count, 256)
    row = lax.broadcasted_iota(jnp.int32, (8, step), 0)
    bits = [(row >> bit) % 2 == 1 for bit in range(3)]

    offsets = offset_ref[...]
    parts = []
    for _ in range(3):
        parts.append(offsets.astype(bf16))
        offsets = offsets - parts[-1].astype(f32)
    channels = vis_count // times
    repeats = max(1, LANES // channels)
    scale = jnp.concatenate([scale_ref[...]] * repeats, axis=1)
    width = math.gcd(vis_count, 512)
    scale = jnp.concatenate([scale] * (width // (repeats * channels)), axis=1)
    for start in range(0, vis_count, width):
        at = pl.ds(start, width)
        time = lax.broadcasted_iota(jnp.int32, (times, width), 0)
        place = lax.broadcasted_iota(jnp.int32, (times, width), 1) + start
        one = (place // channels == time).astype(f32).astype(bf16)
        shifts = sum(jnp.dot(part, one, preferred_element_type=f32) for part in parts)
        half = (math.pi / SUB) * (shifts * scale)
        square = half * half
        sine, cosine = 1.0, 1.0
        for term in (12, 10, 8, 6, 4, 2):
            sine = 1.0 - square * (1.0 / (term * (term + 1))) * sine
            cosine = 1.0 - square * (1.0 / (term * (term - 1))) * cosine
        sine = sine * half
        power = (1.0 - 2.0 * sine * sine, 2.0 * sine * cosine)
        for bit in range(5):
            power_ref[bit, 0, :, at] = power[0]
            power_ref[bit, 1, :, at] = power[1]
            power = (power[0] * power[0] - power[1] * power[1], 2.0 * power[0] * power[1])

    def powers(row, at, extra):
        z = [
            tuple(
                jnp.broadcast_to(power_ref[bit, part, pl.ds(row, 1), at], (8, step))
                for part in range(2)
            )
            for bit in range(5)
        ]
        low = (jnp.where(bits[0], z[0][0], 1.0), jnp.where(bits[0], z[0][1], 0.0))
        for bit in (1, 2):
            more = cmul(low, z[bit])
            low = (jnp.where(bits[bit], more[0], low[0]), jnp.where(bits[bit], more[1], low[1]))
        if extra is not None:
            low = cmul(low, extra)
        blocks = [cmul(low, conj(z[4])), cmul(low, conj(z[3])), low, cmul(low, z[3])]
        return jnp.concatenate([block[part] for part in range(2) for block in blocks], axis=0).astype(bf16)

    def one_subgrid(s):
        both = jnp.zeros((2 * SUB, 2 * SUB), f32)
        for start in range(0, vis_count, step):
            at = pl.ds(start, step)
            vis = tuple(
                jnp.broadcast_to(vis_ref[s, part : part + 1, at].astype(f32), (8, step))
                for part in range(2)
            )
            left = powers(2 * s, at, vis)
            right = powers(2 * s + 1, at, None)
            both += lax.dot_general(
                left, right, (((1,), (1,)), ((), ())), preferred_element_type=f32
            )
        real = both[:SUB, :SUB] - both[SUB:, SUB:]
        image = both[:SUB, SUB:] + both[SUB:, :SUB]
        out_ref[s] = jnp.concatenate(
            [real[:HALF], image[:HALF], real[HALF:], image[HALF:]], axis=1
        )

    def some(i, carry):
        for k in range(math.gcd(count, 2)):
            one_subgrid(i * math.gcd(count, 2) + k)
        return carry

    lax.fori_loop(0, count // math.gcd(count, 2), some, 0)


def sky_sums(visibilities, offsets, scale_row, first, count, interpret=False):
    vis_count = visibilities.shape[2]
    times = offsets.shape[1]
    at = first // count
    return pl.pallas_call(
        sky_kernel,
        grid=(1,),
        in_specs=[
            pl.BlockSpec((count, 2, vis_count), lambda i: (at, 0, 0)),
            pl.BlockSpec((2 * count, times), lambda i: (at, 0)),
            pl.BlockSpec(scale_row.shape, lambda i: (0, 0)),
        ],
        out_specs=pl.BlockSpec((count, HALF, PACK), lambda i: (0, 0, 0)),
        out_shape=jax.ShapeDtypeStruct((count, HALF, PACK), f32),
        scratch_shapes=[pltpu.VMEM((5, 2, 2 * count, vis_count), f32)],
        compiler_params=pltpu.CompilerParams(vmem_limit_bytes=VMEM_BYTES),
        cost_estimate=pl.CostEstimate(
            flops=0, bytes_accessed=count * 2_500_000, transcendentals=0
        ),
        name="sky_sums",
        interpret=interpret,
    )(visibilities, offsets, scale_row)


def correct_kernel(stations_ref, *refs, pieces, skies):
    table_refs, refs = refs[:pieces], refs[pieces:]
    sky_refs, refs = refs[:skies], refs[skies:]
    factor_ref, right_ref, left_ref, out_ref, table_ref, mid_ref = refs
    count = factor_ref.shape[0]
    lane = lax.broadcasted_iota(jnp.int32, (HALF, PACK), 1)
    imag = (lane // SUB) % 2 == 1
    sign = jnp.where(imag, 1.0, -1.0)

    def up(x):
        return pltpu.roll(x, SUB, 1)

    def down(x):
        return pltpu.roll(x, PACK - SUB, 1)

    def product(a, b):
        swapped = jnp.where(imag, up(a), down(a))
        return a * jnp.where(imag, up(b), b) + sign * swapped * jnp.where(imag, b, down(b))

    held = 0
    for piece in table_refs:
        table_ref[held : held + piece.shape[0]] = piece[...]
        held += piece.shape[0]
    for s in range(count):
        first = table_ref[stations_ref[2 * s]].astype(f32)
        second = table_ref[stations_ref[2 * s + 1]].astype(f32)
        pair = product(first, -sign * second)
        per = count // skies
        sky = product(sky_refs[s // per][s % per], factor_ref[s])
        mid_ref[HALF * s : HALF * (s + 1), :] = product(sky, pair).astype(bf16)
    mid = jnp.dot(mid_ref[...], right_ref[...], preferred_element_type=f32).astype(bf16)
    for s in range(count):
        rows = mid[HALF * s : HALF * (s + 1)]
        tall = jnp.concatenate([rows[:, : 2 * SUB], rows[:, 2 * SUB :]], axis=0)
        four = jnp.dot(left_ref[...], tall, preferred_element_type=f32)
        real = four[:SUB, :SUB] - four[SUB:, SUB:]
        image = four[:SUB, SUB:] + four[SUB:, :SUB]
        out_ref[s] = jnp.concatenate(
            [real[:HALF], image[:HALF], real[HALF:], image[HALF:]], axis=1
        ).astype(bf16)


def corrected_subgrids(stations, tables, skies, factor, interpret=False):
    count = factor.shape[0]
    centred = np.arange(SUB) - HALF
    angle = 2.0 * math.pi / SUB * (centred[:, None] * centred[None, :] % SUB)
    re, im = np.cos(angle) / SUB, -np.sin(angle) / SUB
    right = jnp.asarray(np.kron(np.eye(2), np.block([[re, im], [-im, re]])), bf16)
    left = jnp.asarray(np.concatenate([re, im], axis=0), bf16)
    rows = sum(piece.shape[0] for piece in tables)
    operands = [*tables, *skies, factor, right, left]

    def whole(operand):
        return pl.BlockSpec(operand.shape, lambda i, *_: (0,) * operand.ndim)

    return pl.pallas_call(
        functools.partial(correct_kernel, pieces=len(tables), skies=len(skies)),
        grid_spec=pltpu.PrefetchScalarGridSpec(
            num_scalar_prefetch=1,
            grid=(1,),
            in_specs=[whole(operand) for operand in operands],
            out_specs=pl.BlockSpec((count, HALF, PACK), lambda i, *_: (0, 0, 0)),
            scratch_shapes=[
                pltpu.VMEM((rows, HALF, PACK), bf16),
                pltpu.VMEM((HALF * count, PACK), bf16),
            ],
        ),
        out_shape=jax.ShapeDtypeStruct((count, HALF, PACK), bf16),
        compiler_params=pltpu.CompilerParams(vmem_limit_bytes=VMEM_BYTES),
        cost_estimate=pl.CostEstimate(flops=0, bytes_accessed=16_000_000, transcendentals=0),
        name="correct",
        interpret=interpret,
    )(stations.reshape(-1), *operands)


def listed(list_ref, first, count, wanted):
    def scan(i, found):
        list_ref[found] = first + i
        return found + wanted(first + i).astype(jnp.int32)

    return lax.fori_loop(0, count, scan, jnp.int32(0), unroll=math.gcd(count, 8))


def add_subgrid(packed, row_at, col_at, total_ref, lanes):
    lane = lax.broadcasted_iota(jnp.int32, (8, LANES), 1)
    row = lax.broadcasted_iota(jnp.int32, (8, LANES), 0)
    tile = col_at // LANES
    offset = col_at % LANES
    shift = row_at % SUB
    base = row_at - shift

    def place(over):
        inside = lane < offset + SUB - LANES
        if not over:
            inside = (lane >= offset) & (lane < offset + SUB)
        for h in range(2):
            for part in range(2):
                from_lane = (2 * h + part) * SUB
                moved = pltpu.roll(packed, lax.rem(offset - from_lane + LANES, LANES), 1)
                for group in range(2):
                    values = moved[8 * group : 8 * (group + 1)]
                    first_row = HALF * h + 8 * group
                    late = row + first_row >= shift
                    for wrapped in range(2):
                        keep = jnp.logical_and(inside, late if wrapped == 0 else ~late)
                        start = (base + SUB * wrapped + first_row) * lanes
                        start = start + 2 * (tile + over) + part
                        at = pl.ds(start, 8, stride=lanes)
                        total_ref[at, :] = total_ref[at, :] + jnp.where(keep, values, 0.0)

    place(0)

    @pl.when(offset + SUB > LANES)
    def _():
        place(1)


def tile_kernel(info_ref, row_ref, col_ref, *refs, pieces, tile_rows, tile_cols):
    uv_refs = refs[:pieces]
    out_ref, held_ref, total_ref, list_ref, sems = refs[pieces:]
    lanes = 2 * tile_cols // LANES
    count = held_ref.shape[0] // HALF
    first, row_first, col_first = info_ref[0] * count, info_ref[1], info_ref[2]
    rows_all = total_ref.shape[0]
    zero_rows = math.gcd(rows_all, 1024)

    def clear(i, carry):
        at = pl.ds(pl.multiple_of(i * zero_rows, zero_rows), zero_rows)
        total_ref[at, :] = jnp.zeros((zero_rows, LANES), f32)
        return carry

    lax.fori_loop(0, rows_all // zero_rows, clear, 0)
    held = 0
    for piece in uv_refs:
        held_ref[held : held + piece.shape[0]] = piece[...]
        held += piece.shape[0]

    def wanted(s):
        col_at = col_ref[s] - col_first
        return (col_at >= 0) & (col_at < tile_cols)

    def one(entry, carry):
        s = list_ref[entry]
        at = pl.ds(pl.multiple_of((s - first) * HALF, HALF), HALF)
        packed = held_ref[at, :].astype(f32)
        add_subgrid(packed, row_ref[s] - row_first, col_ref[s] - col_first, total_ref, lanes)
        return carry

    lax.fori_loop(0, listed(list_ref, first, count, wanted), one, 0)
    parts = sems.shape[0]
    size = tile_rows * lanes // parts
    copies = [
        pltpu.make_async_copy(
            total_ref.at[pl.ds(i * size, size), :], out_ref.at[pl.ds(i * size, size), :], sems.at[i]
        )
        for i in range(parts)
    ]
    for copy in copies:
        copy.start()
    for copy in copies:
        copy.wait()


def uv_tile_own(uv, info, corners, count, tile_rows, tile_cols, interpret=False):
    lanes = 2 * tile_cols // LANES
    uv = [piece.reshape(-1, PACK) for piece in uv]
    if len(uv) == 1:
        uv_specs = [pl.BlockSpec((count * HALF, PACK), lambda i, info, *_: (info[0], 0))]
    else:
        uv_specs = [pl.BlockSpec(piece.shape, lambda i, *_: (0, 0)) for piece in uv]
    return pl.pallas_call(
        functools.partial(
            tile_kernel, pieces=len(uv), tile_rows=tile_rows, tile_cols=tile_cols
        ),
        grid_spec=pltpu.PrefetchScalarGridSpec(
            num_scalar_prefetch=3,
            grid=(1,),
            in_specs=uv_specs,
            out_specs=pl.BlockSpec(memory_space=pl.ANY),
            scratch_shapes=[
                pltpu.VMEM((count * HALF, PACK), bf16),
                pltpu.VMEM(((tile_rows + 2 * SUB) * lanes, LANES), f32),
                pltpu.SMEM((count + 1,), jnp.int32),
                pltpu.SemaphoreType.DMA((4,)),
            ],
        ),
        out_shape=jax.ShapeDtypeStruct((tile_rows * lanes, LANES), f32),
        compiler_params=pltpu.CompilerParams(vmem_limit_bytes=VMEM_BYTES),
        cost_estimate=pl.CostEstimate(
            flops=0, bytes_accessed=20 * tile_rows * tile_cols, transcendentals=0
        ),
        name="uv_tile",
        interpret=interpret,
    )(info, *corners, *uv)


def short_transform(values):
    count = len(values)
    if count == 1:
        return values
    even = short_transform(values[0::2])
    odd = short_transform(values[1::2])
    low, high = [], []
    for k in range(count // 2):
        re, im = odd[k]
        if k == 0:
            turned = (re, im)
        elif 4 * k == count:
            turned = (-im, re)
        elif 8 * k == count:
            root = math.sqrt(0.5)
            turned = ((re - im) * root, (re + im) * root)
        elif 8 * k == 3 * count:
            root = math.sqrt(0.5)
            turned = ((re + im) * -root, (re - im) * root)
        else:
            c, s = math.cos(2 * math.pi * k / count), math.sin(2 * math.pi * k / count)
            turned = (re * c - im * s, re * s + im * c)
        low.append((even[k][0] + turned[0], even[k][1] + turned[1]))
        high.append((even[k][0] - turned[0], even[k][1] - turned[1]))
    return low + high


def fill_lookups(corner, unit, counts, here, after, shifts):
    size = corner.shape[1]
    coarse, shift = corner // SUB, corner % SUB

    def looked_up(index, length, table):
        place = lax.broadcasted_iota(jnp.int32, (length, size), 0)
        one = (place == index).astype(f32).astype(bf16)
        return lax.dot_general(one, table, (((0,), (0,)), ((), ())), preferred_element_type=f32)

    here[...] = looked_up(coarse, FINE, unit).astype(bf16)
    after[...] = looked_up(lax.rem(coarse + 1, FINE), FINE, unit).astype(bf16)
    shifts[...] = looked_up(shift, SUB, counts)


def lookup_kernel(corner_ref, unit_ref, count_ref, here, after, shifts):
    fill_lookups(corner_ref[...], unit_ref[...], count_ref[...], here, after, shifts)


def lookup_tables():
    fine, low = np.arange(FINE), np.arange(LOW)
    angle = 2.0 * math.pi / FINE * (fine[:, None] * low[None, :] % FINE)
    odd = np.where(low == 0, 1.0 - 2.0 * (fine[:, None] % 2), np.sin(angle))
    unit = jnp.asarray(np.concatenate([np.cos(angle), odd], axis=1), bf16)
    counts = jnp.asarray(np.broadcast_to(np.arange(SUB)[:, None], (SUB, LANES)), bf16)
    return unit, counts


def lookups(corner_rows, interpret=False):
    total = corner_rows.shape[0]
    return pl.pallas_call(
        lookup_kernel,
        out_shape=[
            jax.ShapeDtypeStruct((total, FINE), bf16),
            jax.ShapeDtypeStruct((total, FINE), bf16),
            jax.ShapeDtypeStruct((total, LANES), f32),
        ],
        compiler_params=pltpu.CompilerParams(vmem_limit_bytes=VMEM_BYTES),
        cost_estimate=pl.CostEstimate(flops=0, bytes_accessed=8_000_000, transcendentals=0),
        name="lookups",
        interpret=interpret,
    )(corner_rows.reshape(1, total), *lookup_tables())


def image_kernel(
    info_ref, row_ref, col_ref, *refs, pieces, chunks, row_block, per_row, tile_cols
):
    uv_refs, refs = refs[:pieces], refs[pieces:]
    given, (phase_ref, columns_ref, twist_ref), refs = refs[:3], refs[3:6], refs[7:]
    out_ref, tile_ref, uv_wide, uv_rows, left_even, left_odd, total, staged, ready = refs[:9]
    spill, list_ref, sem, out_sems = refs[9:13]
    here, after, shifts = refs[13:] or given
    step = pl.program_id(0)
    lanes = 2 * tile_cols // LANES
    head = pltpu.make_async_copy(
        tile_ref.at[pl.ds(0, SUB * lanes), :], spill.at[pl.ds(SUB * lanes, SUB * lanes), :], sem
    )
    back = pltpu.make_async_copy(
        spill.at[pl.ds(SUB * lanes, SUB * lanes), :], tile_ref.at[pl.ds(0, SUB * lanes), :], sem
    )

    def add_spilled():
        def row_of(s):
            return lax.rem(row_ref[s] - info_ref[1] + SUB + G, G)

        def wanted(s):
            col_at = col_ref[s] - info_ref[2]
            mine = (col_at >= 0) & (col_at < tile_cols) & (row_of(s) < SUB)
            return mine & (s >= step * size) & (s < (step + 1) * size)

        def one(entry, carry):
            s = list_ref[entry]
            packed = uv_wide[pl.ds((s - step * size) * (HALF + 1), HALF), :]
            add_subgrid(packed, row_of(s), col_ref[s] - info_ref[2], spill, lanes)
            return carry

        found = listed(list_ref, info_ref[0] * per_row, per_row, wanted)
        lax.fori_loop(0, found, one, 0)

    size = uv_rows.shape[1]
    image_rows = phase_ref.shape[1]

    def products(pair, h, left, start, width):
        at = pl.ds(2 * image_rows * h, 2 * image_rows)
        items = pl.ds(start, width)
        spread = lax.dot_general(
            columns_ref[at, :], uv_rows[pair, items, :], (((1,), (1,)), ((), ())),
            preferred_element_type=f32,
        ).astype(bf16)
        turned = cmul(
            (spread[:image_rows], spread[image_rows:]), (phase_ref[0, :, items], phase_ref[1, :, items])
        )
        left[h, :image_rows, items] = turned[0]
        left[h, image_rows:, items] = turned[1]

    def table_of(index):
        late = shifts[...] > index.astype(f32)
        return jnp.concatenate(
            [
                jnp.where(late, after[:, t : t + LANES], here[:, t : t + LANES])
                for t in range(0, FINE, LANES)
            ],
            axis=1,
        )

    def keep_sums(index, real, image, first):
        even_re, odd_re = real[:, :LOW], real[:, LOW:]
        even_im, odd_im = image[:, :LOW], image[:, LOW:]
        edge = lax.broadcasted_iota(jnp.int32, (image_rows, LOW), 1) == 0
        low = (
            even_re - jnp.where(edge, 0.0, odd_im),
            even_im + jnp.where(edge, 0.0, odd_re),
        )
        high = (
            jnp.where(edge, odd_re, even_re + odd_im),
            jnp.where(edge, odd_im, even_im - odd_re),
        )
        twist = twist_ref[pl.ds(index, 1), :]
        for half, got in enumerate((low, high)):
            start = 2 * LOW * half
            done = cmul(
                got, (twist[:, start : start + LOW], twist[:, start + LOW : start + 2 * LOW])
            )
            for part in range(2):
                at = (index, part, slice(None), pl.ds(LOW * half, LOW))
                total[at] = done[part] if first else total[at] + done[part]

    third = size // 3 if size % (3 * LANES) == 0 else size

    def products_and_sums(later, left_later, pair, left, first):
        for h in range(2):
            starts = list(range(0, size, third))
            index = pair + HALF * h
            products(later, h, left_later, starts[0], third)
            table = table_of(index)
            real = jnp.dot(left[h, :image_rows], table, preferred_element_type=f32)
            for start in starts[1:2]:
                products(later, h, left_later, start, third)
            image = jnp.dot(left[h, image_rows:], table, preferred_element_type=f32)
            for start in starts[2:]:
                products(later, h, left_later, start, third)
            keep_sums(index, real, image, first)

    def chunk(first):
        if first:
            head.start()
        held = 0
        for piece in uv_refs:

            def spread_out(s, carry, piece=piece, held=held):
                block = piece[pl.ds(pl.multiple_of(s * HALF, HALF), HALF), :]
                uv_wide[pl.ds((held + s) * (HALF + 1), HALF), :] = block.astype(f32)
                return carry

            count = piece.shape[0] // HALF
            lax.fori_loop(0, count, spread_out, 0, unroll=math.gcd(count, 8))
            held += count
        for row in range(HALF):
            uv_rows[row] = uv_wide[pl.ds(row, size, stride=HALF + 1), :].astype(bf16)
        if first:
            head.wait()
        add_spilled()
        pl.when(step == chunks - 1)(back.start)
        if refs[13:]:
            fill_lookups(given[0][...], given[1][...], given[2][...], here, after, shifts)
        for h in range(2):
            products(0, h, left_even, 0, size)

        def two_pairs(i, carry):
            products_and_sums(2 * i + 1, left_odd, 2 * i, left_even, first)
            products_and_sums(
                jnp.minimum(2 * i + 2, HALF - 1), left_even, 2 * i + 1, left_odd, first
            )
            return carry

        lax.fori_loop(0, HALF // 2, two_pairs, 0)
        pl.when(step == chunks - 1)(back.wait)

    @pl.when(step == 0)
    def _():
        chunk(True)

    if chunks > 1:

        @pl.when((step > 0) & (step < chunks))
        def _():
            chunk(False)

    wide = 2 * G // LANES

    def eight_rows(first, slot, group):
        backward = lax.rem(LOW - lax.broadcasted_iota(jnp.int32, (8, LOW), 1), LOW)
        at = pl.ds(pl.multiple_of(first, 8), 8)
        for tile in range(FINE // LANES):
            at_lanes = pl.ds(tile * LANES, LANES)
            values = [(total[n, 0, at, at_lanes], total[n, 1, at, at_lanes]) for n in range(SUB)]
            for k, value in enumerate(short_transform(values)):
                for part in range(2):
                    ordered = value[part]
                    if tile > 0:
                        ordered = jnp.take_along_axis(
                            ordered, backward, axis=1, mode="promise_in_bounds"
                        )
                    column = 2 * (k * (FINE // LANES) + tile) + part
                    staged[pl.ds(column, 8, stride=wide + 1), :] = ordered
        for row in range(8):
            ready[slot, pl.ds((8 * group + row) * wide, wide), :] = staged[
                row * (wide + 1) : row * (wide + 1) + wide, :
            ]

    @pl.when(step == chunks - 1)
    def _():
        block = row_block * wide
        blocks = image_rows // row_block

        def sent(number, slot):
            return pltpu.make_async_copy(
                ready.at[slot], out_ref.at[pl.ds(pl.multiple_of(number * block, block), block), :],
                out_sems.at[slot],
            )

        def two_blocks(i, carry):
            for slot in range(2):
                number = 2 * i + slot

                @pl.when(i > 0)
                def _():
                    sent(number - 2, slot).wait()

                for group in range(row_block // 8):
                    eight_rows(number * row_block + 8 * group, slot, group)
                sent(number, slot).start()
            return carry

        lax.fori_loop(0, blocks // 2, two_blocks, 0)
        for slot in range(2):
            sent(blocks - 2 + slot, slot).wait()


def image_tables(corner_cols, first_row, image_rows):
    rows = first_row + jnp.arange(image_rows, dtype=jnp.int32)
    turn = 2.0 * math.pi / G
    angle = turn * (rows[:, None] * corner_cols[None, :] % G).astype(f32)
    phase = jnp.stack([jnp.cos(angle), jnp.sin(angle)]).astype(bf16)
    lane = jnp.arange(PACK, dtype=jnp.int32)[None, None, :]
    line = jnp.arange(4, dtype=jnp.int32)[:, None, None]
    angle = turn * (rows[None, :, None] * (lane % SUB) % G).astype(f32)
    angle = angle + (0.5 * math.pi) * (lane // SUB % 2 - line % 2).astype(f32)
    columns = jnp.where(lane // (2 * SUB) == line // 2, jnp.cos(angle), 0.0).astype(bf16)
    columns = columns.reshape(4 * image_rows, PACK)
    return phase, columns


def image_rows_of(
    uv, corners_all, tables, given, tile, info, per_row, tile_rows, tile_cols, interpret=False
):
    phase, columns = tables
    image_rows = phase.shape[1]
    lanes = 2 * tile_cols // LANES
    uv = [piece.reshape(-1, PACK) for piece in uv]
    total = corners_all[0].shape[0]
    size = math.gcd(total, CHUNK) if len(uv) == 1 else total
    chunks = total // size
    row_block = math.gcd(image_rows // 2, 16)
    wide = 2 * G // LANES
    fine, low = np.arange(FINE), np.arange(LOW)
    scale = 1.0 / (SUB * math.sqrt(total))
    high = np.where(low == 0, LOW, FINE - low)
    angles = [2.0 * math.pi / G * (np.arange(SUB)[:, None] * k[None, :]) for k in (low, high)]
    twist = [f(angle) * scale for angle in angles for f in (np.cos, np.sin)]
    twist = jnp.asarray(np.concatenate(twist, axis=1), f32)
    if len(uv) == 1:
        uv_specs = [pl.BlockSpec((size * HALF, PACK), lambda i, *_: (i, 0))]
    else:
        uv_specs = [pl.BlockSpec(piece.shape, lambda i, *_: (0, 0)) for piece in uv]

    def fixed(operand):
        return pl.BlockSpec(operand.shape, lambda i, *_: (0, 0))

    given_specs = [fixed(operand) for operand in given or ()]
    scratch = []
    if not given:
        given = [corners_all[0].reshape(1, total), *lookup_tables()]
        given_specs = [pl.BlockSpec((1, size), lambda i, *_: (0, i)), *map(fixed, given[1:])]
        scratch = [
            pltpu.VMEM((size, FINE), bf16),
            pltpu.VMEM((size, FINE), bf16),
            pltpu.VMEM((size, LANES), f32),
        ]

    image, tile = pl.pallas_call(
        functools.partial(
            image_kernel, pieces=len(uv), chunks=chunks, row_block=row_block, per_row=per_row,
            tile_cols=tile_cols,
        ),
        grid_spec=pltpu.PrefetchScalarGridSpec(
            num_scalar_prefetch=3,
            grid=(chunks,),
            in_specs=[
                *uv_specs,
                *given_specs,
                pl.BlockSpec((2, image_rows, size), lambda i, *_: (0, 0, i)),
                fixed(columns),
                fixed(twist),
                pl.BlockSpec(memory_space=pl.ANY),
            ],
            out_specs=[pl.BlockSpec(memory_space=pl.ANY)] * 2,
            scratch_shapes=[
                pltpu.VMEM((size * (HALF + 1) + HALF, PACK), f32),
                pltpu.VMEM((HALF, size, PACK), bf16),
                pltpu.VMEM((2, 2 * image_rows, size), bf16),
                pltpu.VMEM((2, 2 * image_rows, size), bf16),
                pltpu.VMEM((SUB, 2, image_rows, FINE), f32),
                pltpu.VMEM((8 * (wide + 1) + wide, LANES), f32),
                pltpu.VMEM((2, row_block * wide, LANES), f32),
                pltpu.VMEM((3 * SUB * lanes, LANES), f32),
                pltpu.SMEM((per_row + 1,), jnp.int32),
                pltpu.SemaphoreType.DMA(()),
                pltpu.SemaphoreType.DMA((2,)),
                *scratch,
            ],
        ),
        out_shape=[
            jax.ShapeDtypeStruct((image_rows * wide, LANES), f32),
            jax.ShapeDtypeStruct(tile.shape, f32),
        ],
        input_output_aliases={9 + len(uv): 1},
        compiler_params=pltpu.CompilerParams(vmem_limit_bytes=VMEM_BYTES),
        name="image",
        interpret=interpret,
    )(
        info, *corners_all, *uv,
        *given, phase, columns, twist, tile,
    )
    image = image.reshape(image_rows, G // LANES, 2, LANES)
    tile = tile.reshape(tile_rows, tile_cols // LANES, 2, LANES)
    return (
        jnp.transpose(tile, (0, 2, 1, 3)).reshape(tile_rows, 2, tile_cols),
        jnp.transpose(image, (0, 2, 1, 3)).reshape(image_rows, 2, G),
    )


def packed_beams(beam_terms):
    count = beam_terms.shape[0]
    parts = beam_terms.reshape(count, 2, 2, HALF, SUB)
    return jnp.transpose(parts, (0, 3, 2, 1, 4)).reshape(count, HALF, PACK)


def pixel_factor(screen_depth, shift, vis_count):
    lane = jnp.arange(PACK, dtype=jnp.int32)
    col = lane % SUB
    imag = (lane // SUB) % 2
    row = jnp.arange(HALF, dtype=jnp.int32)[:, None] + (lane // (2 * SUB) * HALF)[None, :]

    def taper(x):
        return 1.0 - ((2.0 * x.astype(f32) + 1.0 - SUB) / SUB) ** 2

    def angle_sq(x):
        return ((x - HALF).astype(f32) * (field_view / SUB)) ** 2

    weight = taper(row) * taper(col) / math.sqrt(vis_count)
    turns = shift[:, None, None] * (row - HALF) % SUB
    angle = (
        -math.pi * screen_depth[:, None, None] * (angle_sq(row) + angle_sq(col))
        + 2.0 * math.pi / SUB * turns.astype(f32)
        - 0.5 * math.pi * imag.astype(f32)
    )
    return jnp.cos(angle) * weight


def from_partner(value, axis, mask):
    count = lax.axis_size(axis)
    return lax.ppermute(value, axis, [(i, i ^ mask) for i in range(count)])


def z_line(own):
    vert_count = lax.axis_size("vert")
    line = [own] + [from_partner(own, "vert", 2 * mask) for mask in range(1, vert_count // 2)]
    return jnp.concatenate(line, axis=0)


def au_lines(line):
    return [line] + [from_partner(line, "au", mask) for mask in range(1, lax.axis_size("au"))]


def with_core(lines):
    return [piece for line in lines for piece in (line, from_partner(line, "vert", 1))]


def whole_gather(own):
    return [lax.all_gather(own, ("au", "vert"), axis=0, tiled=True)]


def gathered_place(owner, by_mask):
    if not by_mask:
        return owner
    vert_count = lax.axis_size("vert")
    au_mask = (owner // vert_count) ^ lax.axis_index("au")
    vert_mask = (owner % vert_count) ^ lax.axis_index("vert")
    return au_mask * vert_count + vert_mask % 2 * (vert_count // 2) + vert_mask // 2


def coded_corners(corners):
    digits = jnp.stack([corners[:, 0] // 128, corners[:, 0] % 128, corners[:, 1] // 128, corners[:, 1] % 128])
    flat = digits.astype(f32).astype(bf16).reshape(-1)
    return jnp.pad(flat, (0, HALF * PACK - flat.shape[0])).reshape(1, HALF, PACK)


def decoded_corners(blocks, count):
    digits = blocks.reshape(blocks.shape[0], HALF * PACK).astype(jnp.int32)
    high_row, low_row, high_col, low_col = [
        digits[:, i * count : (i + 1) * count].reshape(-1) for i in range(4)
    ]
    return (high_row * 128 + low_row, high_col * 128 + low_col)


def on_device(
    visibilities, baseline_offsets, channel_scale, screen_depth, stations, corners, beam_terms
):
    au_count = lax.axis_size("au")
    vert_count = lax.axis_size("vert")
    au_index, vert_index = lax.axis_index("au"), lax.axis_index("vert")
    image_rows = G // (au_count * vert_count)
    count, _, vis_count = visibilities.shape
    own_stations = beam_terms.shape[0]
    held = au_count * vert_count * count * HALF * PACK
    by_mask = held <= MASK_VALUES

    sent = jnp.concatenate([packed_beams(beam_terms), coded_corners(corners)], axis=0)
    offsets = baseline_offsets.reshape(2 * count, -1)
    scale_row = channel_scale.reshape(1, -1)
    part = math.gcd(count, 8)
    skies = [sky_sums(visibilities, offsets, scale_row, 0, part)]
    if by_mask:
        line = z_line(sent)
        line, offsets, skies[0], corners, stations, screen_depth = lax.optimization_barrier(
            (line, offsets, skies[0], corners, stations, screen_depth)
        )
    for s in range(part, count, part):
        skies.append(sky_sums(visibilities, offsets, scale_row, s, part))
    factor = pixel_factor(screen_depth, corners[:, 0] % SUB, vis_count)
    if by_mask:
        lines = au_lines(line)
        lines, skies = lax.optimization_barrier((lines, skies))
        tables = with_core(lines)
    else:
        tables = whole_gather(sent)
    coded = [
        piece.reshape(-1, own_stations + 1, HALF, PACK)[:, own_stations] for piece in tables
    ]
    corners_all = decoded_corners(jnp.concatenate(coded, axis=0), count)
    owners = stations // own_stations
    station_rows = gathered_place(owners, by_mask) * (own_stations + 1) + stations % own_stations
    uv_own = corrected_subgrids(station_rows, tables, skies, factor)

    per_row = vert_count * count
    tile_rows, tile_cols = G // au_count, G // vert_count

    def tile_info(row):
        place = gathered_place(row * vert_count + vert_index, by_mask) // vert_count
        return jnp.stack([place, au_index * tile_rows, vert_index * tile_cols])

    own_info = tile_info(au_index)
    before_info = tile_info(lax.rem(au_index + au_count - 1, au_count))
    first_row = (au_index * vert_count + vert_index) * image_rows
    tables = image_tables(corners_all[1], first_row, image_rows)
    if by_mask:
        line = z_line(uv_own)
        line, tables, corners_all, own_info, before_info = lax.optimization_barrier(
            (line, tables, corners_all, own_info, before_info)
        )
        lines = au_lines(line)
        own_row = with_core(lines[:1])
        tile = uv_tile_own(own_row, own_info, corners_all, per_row, tile_rows, tile_cols)
        given = lookups(corners_all[0])
        lines, own_row, tile, given = lax.optimization_barrier((lines, own_row, tile, given))
        uv = own_row + with_core(lines[1:])
    else:
        uv, given = whole_gather(uv_own), None
        tile = uv_tile_own(uv, own_info, corners_all, per_row, tile_rows, tile_cols)
    return image_rows_of(
        uv, corners_all, tables, given, tile, before_info, per_row, tile_rows, tile_cols
    )


def solution(mesh):
    return jax.shard_map(
        on_device,
        mesh=mesh,
        in_specs=(
            P(("au", "vert"), None, None),
            P(("au", "vert"), None, None),
            P(),
            P(("au", "vert")),
            P(("au", "vert"), None),
            P(("au", "vert"), None),
            P(("au", "vert"), None, None),
        ),
        out_specs=(P("au", None, "vert"), P(("au", "vert"), None, None)),
        check_vma=False,
    )
```

```python
import functools
import math

import jax
import jax.numpy as jnp
import numpy as np
from jax import lax
from jax.experimental import pallas as pl
from jax.experimental.pallas import tpu as pltpu
from jax.sharding import PartitionSpec as P

G = 8192
SUB = 32
HALF = SUB // 2
PACK = 4 * SUB
LANES = 128
FINE = G // SUB
LOW = FINE // 2
CHUNK = 768
MASK_VALUES = 1 << 22
field_view = 0.1
bf16 = jnp.bfloat16
f32 = jnp.float32
VMEM_BYTES = 58 * 1024 * 1024


def cmul(a, b):
    return (a[0] * b[0] - a[1] * b[1], a[0] * b[1] + a[1] * b[0])


def conj(a):
    return (a[0], -a[1])


def sky_kernel(vis_ref, offset_ref, scale_ref, out_ref, power_ref):
    count, _, vis_count = vis_ref.shape
    times = offset_ref.shape[1]
    step = math.gcd(vis_count, 256)
    row = lax.broadcasted_iota(jnp.int32, (8, step), 0)
    bits = [(row >> bit) % 2 == 1 for bit in range(3)]

    offsets = offset_ref[...]
    parts = []
    for _ in range(3):
        parts.append(offsets.astype(bf16))
        offsets = offsets - parts[-1].astype(f32)
    channels = vis_count // times
    repeats = max(1, LANES // channels)
    scale = jnp.concatenate([scale_ref[...]] * repeats, axis=1)
    width = math.gcd(vis_count, 512)
    scale = jnp.concatenate([scale] * (width // (repeats * channels)), axis=1)
    for start in range(0, vis_count, width):
        at = pl.ds(start, width)
        time = lax.broadcasted_iota(jnp.int32, (times, width), 0)
        place = lax.broadcasted_iota(jnp.int32, (times, width), 1) + start
        one = (place // channels == time).astype(f32).astype(bf16)
        shifts = sum(jnp.dot(part, one, preferred_element_type=f32) for part in parts)
        half = (math.pi / SUB) * (shifts * scale)
        square = half * half
        sine, cosine = 1.0, 1.0
        for term in (12, 10, 8, 6, 4, 2):
            sine = 1.0 - square * (1.0 / (term * (term + 1))) * sine
            cosine = 1.0 - square * (1.0 / (term * (term - 1))) * cosine
        sine = sine * half
        power = (1.0 - 2.0 * sine * sine, 2.0 * sine * cosine)
        for bit in range(5):
            power_ref[bit, 0, :, at] = power[0]
            power_ref[bit, 1, :, at] = power[1]
            power = (power[0] * power[0] - power[1] * power[1], 2.0 * power[0] * power[1])

    def powers(row, at, extra):
        z = [
            tuple(
                jnp.broadcast_to(power_ref[bit, part, pl.ds(row, 1), at], (8, step))
                for part in range(2)
            )
            for bit in range(5)
        ]
        low = (jnp.where(bits[0], z[0][0], 1.0), jnp.where(bits[0], z[0][1], 0.0))
        for bit in (1, 2):
            more = cmul(low, z[bit])
            low = (jnp.where(bits[bit], more[0], low[0]), jnp.where(bits[bit], more[1], low[1]))
        if extra is not None:
            low = cmul(low, extra)
        blocks = [cmul(low, conj(z[4])), cmul(low, conj(z[3])), low, cmul(low, z[3])]
        return jnp.concatenate([block[part] for part in range(2) for block in blocks], axis=0).astype(bf16)

    def one_subgrid(s):
        both = jnp.zeros((2 * SUB, 2 * SUB), f32)
        for start in range(0, vis_count, step):
            at = pl.ds(start, step)
            vis = tuple(
                jnp.broadcast_to(vis_ref[s, part : part + 1, at].astype(f32), (8, step))
                for part in range(2)
            )
            left = powers(2 * s, at, vis)
            right = powers(2 * s + 1, at, None)
            both += lax.dot_general(
                left, right, (((1,), (1,)), ((), ())), preferred_element_type=f32
            )
        real = both[:SUB, :SUB] - both[SUB:, SUB:]
        image = both[:SUB, SUB:] + both[SUB:, :SUB]
        out_ref[s] = jnp.concatenate(
            [real[:HALF], image[:HALF], real[HALF:], image[HALF:]], axis=1
        )

    def some(i, carry):
        for k in range(math.gcd(count, 2)):
            one_subgrid(i * math.gcd(count, 2) + k)
        return carry

    lax.fori_loop(0, count // math.gcd(count, 2), some, 0)


def sky_sums(visibilities, offsets, scale_row, first, count, interpret=False):
    vis_count = visibilities.shape[2]
    times = offsets.shape[1]
    at = first // count
    return pl.pallas_call(
        sky_kernel,
        grid=(1,),
        in_specs=[
            pl.BlockSpec((count, 2, vis_count), lambda i: (at, 0, 0)),
            pl.BlockSpec((2 * count, times), lambda i: (at, 0)),
            pl.BlockSpec(scale_row.shape, lambda i: (0, 0)),
        ],
        out_specs=pl.BlockSpec((count, HALF, PACK), lambda i: (0, 0, 0)),
        out_shape=jax.ShapeDtypeStruct((count, HALF, PACK), f32),
        scratch_shapes=[pltpu.VMEM((5, 2, 2 * count, vis_count), f32)],
        compiler_params=pltpu.CompilerParams(vmem_limit_bytes=VMEM_BYTES),
        cost_estimate=pl.CostEstimate(
            flops=0, bytes_accessed=count * 2_500_000, transcendentals=0
        ),
        name="sky_sums",
        interpret=interpret,
    )(visibilities, offsets, scale_row)


def correct_kernel(stations_ref, *refs, pieces, skies):
    table_refs, refs = refs[:pieces], refs[pieces:]
    sky_refs, refs = refs[:skies], refs[skies:]
    factor_ref, right_ref, left_ref, out_ref, table_ref, mid_ref = refs
    count = factor_ref.shape[0]
    lane = lax.broadcasted_iota(jnp.int32, (HALF, PACK), 1)
    imag = (lane // SUB) % 2 == 1
    sign = jnp.where(imag, 1.0, -1.0)

    def up(x):
        return pltpu.roll(x, SUB, 1)

    def down(x):
        return pltpu.roll(x, PACK - SUB, 1)

    def product(a, b):
        swapped = jnp.where(imag, up(a), down(a))
        return a * jnp.where(imag, up(b), b) + sign * swapped * jnp.where(imag, b, down(b))

    held = 0
    for piece in table_refs:
        table_ref[held : held + piece.shape[0]] = piece[...]
        held += piece.shape[0]
    for s in range(count):
        first = table_ref[stations_ref[2 * s]].astype(f32)
        second = table_ref[stations_ref[2 * s + 1]].astype(f32)
        pair = product(first, -sign * second)
        per = count // skies
        sky = product(sky_refs[s // per][s % per], factor_ref[s])
        mid_ref[HALF * s : HALF * (s + 1), :] = product(sky, pair).astype(bf16)
    mid = jnp.dot(mid_ref[...], right_ref[...], preferred_element_type=f32).astype(bf16)
    for s in range(count):
        rows = mid[HALF * s : HALF * (s + 1)]
        tall = jnp.concatenate([rows[:, : 2 * SUB], rows[:, 2 * SUB :]], axis=0)
        four = jnp.dot(left_ref[...], tall, preferred_element_type=f32)
        real = four[:SUB, :SUB] - four[SUB:, SUB:]
        image = four[:SUB, SUB:] + four[SUB:, :SUB]
        out_ref[s] = jnp.concatenate(
            [real[:HALF], image[:HALF], real[HALF:], image[HALF:]], axis=1
        ).astype(bf16)


def corrected_subgrids(stations, tables, skies, factor, interpret=False):
    count = factor.shape[0]
    centred = np.arange(SUB) - HALF
    angle = 2.0 * math.pi / SUB * (centred[:, None] * centred[None, :] % SUB)
    re, im = np.cos(angle) / SUB, -np.sin(angle) / SUB
    right = jnp.asarray(np.kron(np.eye(2), np.block([[re, im], [-im, re]])), bf16)
    left = jnp.asarray(np.concatenate([re, im], axis=0), bf16)
    rows = sum(piece.shape[0] for piece in tables)
    operands = [*tables, *skies, factor, right, left]

    def whole(operand):
        return pl.BlockSpec(operand.shape, lambda i, *_: (0,) * operand.ndim)

    return pl.pallas_call(
        functools.partial(correct_kernel, pieces=len(tables), skies=len(skies)),
        grid_spec=pltpu.PrefetchScalarGridSpec(
            num_scalar_prefetch=1,
            grid=(1,),
            in_specs=[whole(operand) for operand in operands],
            out_specs=pl.BlockSpec((count, HALF, PACK), lambda i, *_: (0, 0, 0)),
            scratch_shapes=[
                pltpu.VMEM((rows, HALF, PACK), bf16),
                pltpu.VMEM((HALF * count, PACK), bf16),
            ],
        ),
        out_shape=jax.ShapeDtypeStruct((count, HALF, PACK), bf16),
        compiler_params=pltpu.CompilerParams(vmem_limit_bytes=VMEM_BYTES),
        cost_estimate=pl.CostEstimate(flops=0, bytes_accessed=16_000_000, transcendentals=0),
        name="correct",
        interpret=interpret,
    )(stations.reshape(-1), *operands)


def listed(list_ref, first, count, wanted):
    def scan(i, found):
        list_ref[found] = first + i
        return found + wanted(first + i).astype(jnp.int32)

    return lax.fori_loop(0, count, scan, jnp.int32(0), unroll=math.gcd(count, 8))


def add_subgrid(packed, row_at, col_at, total_ref, lanes):
    lane = lax.broadcasted_iota(jnp.int32, (8, LANES), 1)
    row = lax.broadcasted_iota(jnp.int32, (8, LANES), 0)
    tile = col_at // LANES
    offset = col_at % LANES
    shift = row_at % SUB
    base = row_at - shift

    def place(over):
        inside = lane < offset + SUB - LANES
        if not over:
            inside = (lane >= offset) & (lane < offset + SUB)
        for h in range(2):
            for part in range(2):
                from_lane = (2 * h + part) * SUB
                moved = pltpu.roll(packed, lax.rem(offset - from_lane + LANES, LANES), 1)
                for group in range(2):
                    values = moved[8 * group : 8 * (group + 1)]
                    first_row = HALF * h + 8 * group
                    late = row + first_row >= shift
                    for wrapped in range(2):
                        keep = jnp.logical_and(inside, late if wrapped == 0 else ~late)
                        start = (base + SUB * wrapped + first_row) * lanes
                        start = start + 2 * (tile + over) + part
                        at = pl.ds(start, 8, stride=lanes)
                        total_ref[at, :] = total_ref[at, :] + jnp.where(keep, values, 0.0)

    place(0)

    @pl.when(offset + SUB > LANES)
    def _():
        place(1)


def tile_kernel(info_ref, row_ref, col_ref, *refs, pieces, tile_rows, tile_cols):
    uv_refs = refs[:pieces]
    out_ref, held_ref, total_ref, list_ref, sems = refs[pieces:]
    lanes = 2 * tile_cols // LANES
    count = held_ref.shape[0] // HALF
    first, row_first, col_first = info_ref[0] * count, info_ref[1], info_ref[2]
    rows_all = total_ref.shape[0]
    zero_rows = math.gcd(rows_all, 1024)

    def clear(i, carry):
        at = pl.ds(pl.multiple_of(i * zero_rows, zero_rows), zero_rows)
        total_ref[at, :] = jnp.zeros((zero_rows, LANES), f32)
        return carry

    lax.fori_loop(0, rows_all // zero_rows, clear, 0)
    held = 0
    for piece in uv_refs:
        held_ref[held : held + piece.shape[0]] = piece[...]
        held += piece.shape[0]

    def wanted(s):
        col_at = col_ref[s] - col_first
        return (col_at >= 0) & (col_at < tile_cols)

    def one(entry, carry):
        s = list_ref[entry]
        at = pl.ds(pl.multiple_of((s - first) * HALF, HALF), HALF)
        packed = held_ref[at, :].astype(f32)
        add_subgrid(packed, row_ref[s] - row_first, col_ref[s] - col_first, total_ref, lanes)
        return carry

    lax.fori_loop(0, listed(list_ref, first, count, wanted), one, 0)
    parts = sems.shape[0]
    size = tile_rows * lanes // parts
    copies = [
        pltpu.make_async_copy(
            total_ref.at[pl.ds(i * size, size), :], out_ref.at[pl.ds(i * size, size), :], sems.at[i]
        )
        for i in range(parts)
    ]
    for copy in copies:
        copy.start()
    for copy in copies:
        copy.wait()


def uv_tile_own(uv, info, corners, count, tile_rows, tile_cols, interpret=False):
    lanes = 2 * tile_cols // LANES
    uv = [piece.reshape(-1, PACK) for piece in uv]
    if len(uv) == 1:
        uv_specs = [pl.BlockSpec((count * HALF, PACK), lambda i, info, *_: (info[0], 0))]
    else:
        uv_specs = [pl.BlockSpec(piece.shape, lambda i, *_: (0, 0)) for piece in uv]
    return pl.pallas_call(
        functools.partial(
            tile_kernel, pieces=len(uv), tile_rows=tile_rows, tile_cols=tile_cols
        ),
        grid_spec=pltpu.PrefetchScalarGridSpec(
            num_scalar_prefetch=3,
            grid=(1,),
            in_specs=uv_specs,
            out_specs=pl.BlockSpec(memory_space=pl.ANY),
            scratch_shapes=[
                pltpu.VMEM((count * HALF, PACK), bf16),
                pltpu.VMEM(((tile_rows + 2 * SUB) * lanes, LANES), f32),
                pltpu.SMEM((count + 1,), jnp.int32),
                pltpu.SemaphoreType.DMA((4,)),
            ],
        ),
        out_shape=jax.ShapeDtypeStruct((tile_rows * lanes, LANES), f32),
        compiler_params=pltpu.CompilerParams(vmem_limit_bytes=VMEM_BYTES),
        cost_estimate=pl.CostEstimate(
            flops=0, bytes_accessed=20 * tile_rows * tile_cols, transcendentals=0
        ),
        name="uv_tile",
        interpret=interpret,
    )(info, *corners, *uv)


def short_transform(values):
    count = len(values)
    if count == 1:
        return values
    even = short_transform(values[0::2])
    odd = short_transform(values[1::2])
    low, high = [], []
    for k in range(count // 2):
        re, im = odd[k]
        if k == 0:
            turned = (re, im)
        elif 4 * k == count:
            turned = (-im, re)
        elif 8 * k == count:
            root = math.sqrt(0.5)
            turned = ((re - im) * root, (re + im) * root)
        elif 8 * k == 3 * count:
            root = math.sqrt(0.5)
            turned = ((re + im) * -root, (re - im) * root)
        else:
            c, s = math.cos(2 * math.pi * k / count), math.sin(2 * math.pi * k / count)
            turned = (re * c - im * s, re * s + im * c)
        low.append((even[k][0] + turned[0], even[k][1] + turned[1]))
        high.append((even[k][0] - turned[0], even[k][1] - turned[1]))
    return low + high


def fill_lookups(corner, unit, counts, here, after, shifts):
    size = corner.shape[1]
    coarse, shift = corner // SUB, corner % SUB

    def looked_up(index, length, table):
        place = lax.broadcasted_iota(jnp.int32, (length, size), 0)
        one = (place == index).astype(f32).astype(bf16)
        return lax.dot_general(one, table, (((0,), (0,)), ((), ())), preferred_element_type=f32)

    here[...] = looked_up(coarse, FINE, unit).astype(bf16)
    after[...] = looked_up(lax.rem(coarse + 1, FINE), FINE, unit).astype(bf16)
    shifts[...] = looked_up(shift, SUB, counts)


def lookup_kernel(corner_ref, unit_ref, count_ref, here, after, shifts):
    fill_lookups(corner_ref[...], unit_ref[...], count_ref[...], here, after, shifts)


def lookup_tables():
    fine, low = np.arange(FINE), np.arange(LOW)
    angle = 2.0 * math.pi / FINE * (fine[:, None] * low[None, :] % FINE)
    odd = np.where(low == 0, 1.0 - 2.0 * (fine[:, None] % 2), np.sin(angle))
    unit = jnp.asarray(np.concatenate([np.cos(angle), odd], axis=1), bf16)
    counts = jnp.asarray(np.broadcast_to(np.arange(SUB)[:, None], (SUB, LANES)), bf16)
    return unit, counts


def lookups(corner_rows, interpret=False):
    total = corner_rows.shape[0]
    return pl.pallas_call(
        lookup_kernel,
        out_shape=[
            jax.ShapeDtypeStruct((total, FINE), bf16),
            jax.ShapeDtypeStruct((total, FINE), bf16),
            jax.ShapeDtypeStruct((total, LANES), f32),
        ],
        compiler_params=pltpu.CompilerParams(vmem_limit_bytes=VMEM_BYTES),
        cost_estimate=pl.CostEstimate(flops=0, bytes_accessed=8_000_000, transcendentals=0),
        name="lookups",
        interpret=interpret,
    )(corner_rows.reshape(1, total), *lookup_tables())


def image_kernel(
    info_ref, row_ref, col_ref, *refs, pieces, chunks, row_block, per_row, tile_cols
):
    uv_refs, refs = refs[:pieces], refs[pieces:]
    given, (phase_ref, columns_ref, twist_ref), refs = refs[:3], refs[3:6], refs[7:]
    out_ref, tile_ref, uv_wide, uv_rows, left, total, staged, spill = refs[:8]
    list_ref, sem = refs[8:10]
    here, after, shifts = refs[10:] or given
    step = pl.program_id(0)
    lanes = 2 * tile_cols // LANES
    head = pltpu.make_async_copy(
        tile_ref.at[pl.ds(0, SUB * lanes), :], spill.at[pl.ds(SUB * lanes, SUB * lanes), :], sem
    )
    back = pltpu.make_async_copy(
        spill.at[pl.ds(SUB * lanes, SUB * lanes), :], tile_ref.at[pl.ds(0, SUB * lanes), :], sem
    )

    def add_spilled():
        def row_of(s):
            return lax.rem(row_ref[s] - info_ref[1] + SUB + G, G)

        def wanted(s):
            col_at = col_ref[s] - info_ref[2]
            mine = (col_at >= 0) & (col_at < tile_cols) & (row_of(s) < SUB)
            return mine & (s >= step * size) & (s < (step + 1) * size)

        def one(entry, carry):
            s = list_ref[entry]
            packed = uv_wide[pl.ds((s - step * size) * (HALF + 1), HALF), :]
            add_subgrid(packed, row_of(s), col_ref[s] - info_ref[2], spill, lanes)
            return carry

        found = listed(list_ref, info_ref[0] * per_row, per_row, wanted)
        lax.fori_loop(0, found, one, 0)

    size = uv_rows.shape[1]
    image_rows = phase_ref.shape[1]

    def products(pair, h):
        at = pl.ds(2 * image_rows * h, 2 * image_rows)
        spread = lax.dot_general(
            columns_ref[at, :], uv_rows[pair], (((1,), (1,)), ((), ())), preferred_element_type=f32
        ).astype(bf16)
        turned = cmul((spread[:image_rows], spread[image_rows:]), (phase_ref[0], phase_ref[1]))
        left[h, :image_rows] = turned[0]
        left[h, image_rows:] = turned[1]

    def table_of(index):
        late = shifts[...] > index.astype(f32)
        return jnp.concatenate(
            [
                jnp.where(late, after[:, t : t + LANES], here[:, t : t + LANES])
                for t in range(0, FINE, LANES)
            ],
            axis=1,
        )

    def keep_sums(index, real, image, first):
        even_re, odd_re = real[:, :LOW], real[:, LOW:]
        even_im, odd_im = image[:, :LOW], image[:, LOW:]
        edge = lax.broadcasted_iota(jnp.int32, (image_rows, LOW), 1) == 0
        low = (
            even_re - jnp.where(edge, 0.0, odd_im),
            even_im + jnp.where(edge, 0.0, odd_re),
        )
        high = (
            jnp.where(edge, odd_re, even_re + odd_im),
            jnp.where(edge, odd_im, even_im - odd_re),
        )
        twist = twist_ref[pl.ds(index, 1), :]
        for half, got in enumerate((low, high)):
            start = 2 * LOW * half
            done = cmul(
                got, (twist[:, start : start + LOW], twist[:, start + LOW : start + 2 * LOW])
            )
            for part in range(2):
                at = (index, part, slice(None), pl.ds(LOW * half, LOW))
                total[at] = done[part] if first else total[at] + done[part]

    def sums(pair, h, first):
        index = pair + HALF * h
        four = jnp.dot(left[h], table_of(index), preferred_element_type=f32)
        keep_sums(index, four[:image_rows], four[image_rows:], first)

    def chunk(first):
        if first:
            head.start()
        held = 0
        for piece in uv_refs:

            def spread_out(s, carry, piece=piece, held=held):
                block = piece[pl.ds(pl.multiple_of(s * HALF, HALF), HALF), :]
                uv_wide[pl.ds((held + s) * (HALF + 1), HALF), :] = block.astype(f32)
                return carry

            count = piece.shape[0] // HALF
            lax.fori_loop(0, count, spread_out, 0, unroll=math.gcd(count, 8))
            held += count
        for row in range(HALF):
            uv_rows[row] = uv_wide[pl.ds(row, size, stride=HALF + 1), :].astype(bf16)
        if first:
            head.wait()
        add_spilled()
        pl.when(step == chunks - 1)(back.start)
        if refs[10:]:
            fill_lookups(given[0][...], given[1][...], given[2][...], here, after, shifts)

        def one_pair(pair, carry):
            for h in range(2):
                products(pair, h)
            for h in range(2):
                sums(pair, h, first)
            return carry

        lax.fori_loop(0, HALF, one_pair, 0)
        pl.when(step == chunks - 1)(back.wait)

    @pl.when(step == 0)
    def _():
        chunk(True)

    if chunks > 1:

        @pl.when((step > 0) & (step < chunks))
        def _():
            chunk(False)

    @pl.when(step >= chunks)
    def _():
        first = (step - chunks) * row_block
        wide = 2 * G // LANES
        backward = lax.rem(LOW - lax.broadcasted_iota(jnp.int32, (8, LOW), 1), LOW)

        def eight_rows(group, carry):
            at = pl.ds(pl.multiple_of(first + 8 * group, 8), 8)
            for tile in range(FINE // LANES):
                lanes = pl.ds(tile * LANES, LANES)
                values = [(total[n, 0, at, lanes], total[n, 1, at, lanes]) for n in range(SUB)]
                for k, value in enumerate(short_transform(values)):
                    for part in range(2):
                        ordered = value[part]
                        if tile > 0:
                            ordered = jnp.take_along_axis(
                                ordered, backward, axis=1, mode="promise_in_bounds"
                            )
                        column = 2 * (k * (FINE // LANES) + tile) + part
                        staged[pl.ds(column, 8, stride=wide + 1), :] = ordered
            for row in range(8):
                at = pl.ds(pl.multiple_of((8 * group + row) * wide, wide), wide)
                out_ref[at, :] = staged[row * (wide + 1) : row * (wide + 1) + wide, :]
            return carry

        lax.fori_loop(0, row_block // 8, eight_rows, 0)


def phase_table(corner_cols, first_row, image_rows):
    rows = first_row + jnp.arange(image_rows, dtype=jnp.int32)
    angle = 2.0 * math.pi / G * (rows[:, None] * corner_cols[None, :] % G).astype(f32)
    return jnp.stack([jnp.cos(angle), jnp.sin(angle)]).astype(bf16)


def column_table(first_row, image_rows):
    lane, line = np.arange(PACK)[None, None, :], np.arange(4)[:, None, None]
    angle = 2.0 * math.pi / G * (np.arange(image_rows)[None, :, None] * (lane % SUB))
    angle = angle + 0.5 * math.pi * (lane // SUB % 2 - line % 2)
    same = lane // (2 * SUB) == line // 2
    re, im = [
        jnp.asarray(np.where(same, f(angle), 0.0).reshape(-1, PACK), f32) for f in (np.cos, np.sin)
    ]
    turn = first_row * (jnp.arange(PACK, dtype=jnp.int32) % SUB) % G
    turn = 2.0 * math.pi / G * turn.astype(f32)
    return (re * jnp.cos(turn) - im * jnp.sin(turn)).astype(bf16)


def image_rows_of(
    uv, corners_all, tables, given, tile, info, per_row, tile_rows, tile_cols, interpret=False
):
    phase, columns = tables
    image_rows = phase.shape[1]
    lanes = 2 * tile_cols // LANES
    uv = [piece.reshape(-1, PACK) for piece in uv]
    total = corners_all[0].shape[0]
    size = math.gcd(total, CHUNK) if len(uv) == 1 else total
    chunks = total // size
    row_block = math.gcd(image_rows, 32)
    outs = image_rows // row_block
    wide = 2 * G // LANES
    fine, low = np.arange(FINE), np.arange(LOW)
    scale = 1.0 / (SUB * math.sqrt(total))
    high = np.where(low == 0, LOW, FINE - low)
    angles = [2.0 * math.pi / G * (np.arange(SUB)[:, None] * k[None, :]) for k in (low, high)]
    twist = [f(angle) * scale for angle in angles for f in (np.cos, np.sin)]
    twist = jnp.asarray(np.concatenate(twist, axis=1), f32)
    last = chunks - 1

    def chunk_of(i):
        return jnp.minimum(i, last)

    if len(uv) == 1:
        uv_specs = [pl.BlockSpec((size * HALF, PACK), lambda i, *_: (chunk_of(i), 0))]
    else:
        uv_specs = [pl.BlockSpec(piece.shape, lambda i, *_: (0, 0)) for piece in uv]

    def fixed(operand):
        return pl.BlockSpec(operand.shape, lambda i, *_: (0, 0))

    given_specs = [fixed(operand) for operand in given or ()]
    scratch = []
    if not given:
        given = [corners_all[0].reshape(1, total), *lookup_tables()]
        given_specs = [pl.BlockSpec((1, size), lambda i, *_: (0, chunk_of(i))), *map(fixed, given[1:])]
        scratch = [
            pltpu.VMEM((size, FINE), bf16),
            pltpu.VMEM((size, FINE), bf16),
            pltpu.VMEM((size, LANES), f32),
        ]

    image, tile = pl.pallas_call(
        functools.partial(
            image_kernel, pieces=len(uv), chunks=chunks, row_block=row_block, per_row=per_row,
            tile_cols=tile_cols,
        ),
        grid_spec=pltpu.PrefetchScalarGridSpec(
            num_scalar_prefetch=3,
            grid=(chunks + outs,),
            in_specs=[
                *uv_specs,
                *given_specs,
                pl.BlockSpec((2, image_rows, size), lambda i, *_: (0, 0, chunk_of(i))),
                fixed(columns),
                fixed(twist),
                pl.BlockSpec(memory_space=pl.ANY),
            ],
            out_specs=[
                pl.BlockSpec(
                    (row_block * wide, LANES), lambda i, *_: (jnp.maximum(i - chunks, 0), 0)
                ),
                pl.BlockSpec(memory_space=pl.ANY),
            ],
            scratch_shapes=[
                pltpu.VMEM((size * (HALF + 1) + HALF, PACK), f32),
                pltpu.VMEM((HALF, size, PACK), bf16),
                pltpu.VMEM((2, 2 * image_rows, size), bf16),
                pltpu.VMEM((SUB, 2, image_rows, FINE), f32),
                pltpu.VMEM((8 * (wide + 1) + wide, LANES), f32),
                pltpu.VMEM((3 * SUB * lanes, LANES), f32),
                pltpu.SMEM((per_row + 1,), jnp.int32),
                pltpu.SemaphoreType.DMA(()),
                *scratch,
            ],
        ),
        out_shape=[
            jax.ShapeDtypeStruct((image_rows * wide, LANES), f32),
            jax.ShapeDtypeStruct(tile.shape, f32),
        ],
        input_output_aliases={9 + len(uv): 1},
        compiler_params=pltpu.CompilerParams(vmem_limit_bytes=VMEM_BYTES),
        name="image",
        interpret=interpret,
    )(
        info, *corners_all, *uv,
        *given, phase, columns, twist, tile,
    )
    image = image.reshape(image_rows, G // LANES, 2, LANES)
    tile = tile.reshape(tile_rows, tile_cols // LANES, 2, LANES)
    return (
        jnp.transpose(tile, (0, 2, 1, 3)).reshape(tile_rows, 2, tile_cols),
        jnp.transpose(image, (0, 2, 1, 3)).reshape(image_rows, 2, G),
    )


def packed_beams(beam_terms):
    count = beam_terms.shape[0]
    parts = beam_terms.reshape(count, 2, 2, HALF, SUB)
    return jnp.transpose(parts, (0, 3, 2, 1, 4)).reshape(count, HALF, PACK)


def pixel_factor(screen_depth, shift, vis_count):
    lane = jnp.arange(PACK, dtype=jnp.int32)
    col = lane % SUB
    imag = (lane // SUB) % 2
    row = jnp.arange(HALF, dtype=jnp.int32)[:, None] + (lane // (2 * SUB) * HALF)[None, :]

    def taper(x):
        return 1.0 - ((2.0 * x.astype(f32) + 1.0 - SUB) / SUB) ** 2

    def angle_sq(x):
        return ((x - HALF).astype(f32) * (field_view / SUB)) ** 2

    weight = taper(row) * taper(col) / math.sqrt(vis_count)
    turns = shift[:, None, None] * (row - HALF) % SUB
    angle = (
        -math.pi * screen_depth[:, None, None] * (angle_sq(row) + angle_sq(col))
        + 2.0 * math.pi / SUB * turns.astype(f32)
        - 0.5 * math.pi * imag.astype(f32)
    )
    return jnp.cos(angle) * weight


def from_partner(value, axis, mask):
    count = lax.axis_size(axis)
    return lax.ppermute(value, axis, [(i, i ^ mask) for i in range(count)])


def z_line(own):
    vert_count = lax.axis_size("vert")
    line = [own] + [from_partner(own, "vert", 2 * mask) for mask in range(1, vert_count // 2)]
    return jnp.concatenate(line, axis=0)


def au_lines(line):
    return [line] + [from_partner(line, "au", mask) for mask in range(1, lax.axis_size("au"))]


def with_core(lines):
    return [piece for line in lines for piece in (line, from_partner(line, "vert", 1))]


def whole_gather(own):
    return [lax.all_gather(own, ("au", "vert"), axis=0, tiled=True)]


def gathered_place(owner, by_mask):
    if not by_mask:
        return owner
    vert_count = lax.axis_size("vert")
    au_mask = (owner // vert_count) ^ lax.axis_index("au")
    vert_mask = (owner % vert_count) ^ lax.axis_index("vert")
    return au_mask * vert_count + vert_mask % 2 * (vert_count // 2) + vert_mask // 2


def coded_corners(corners):
    digits = jnp.stack([corners[:, 0] // 128, corners[:, 0] % 128, corners[:, 1] // 128, corners[:, 1] % 128])
    flat = digits.astype(f32).astype(bf16).reshape(-1)
    return jnp.pad(flat, (0, HALF * PACK - flat.shape[0])).reshape(1, HALF, PACK)


def decoded_corners(blocks, count):
    digits = blocks.reshape(blocks.shape[0], HALF * PACK).astype(jnp.int32)
    high_row, low_row, high_col, low_col = [
        digits[:, i * count : (i + 1) * count].reshape(-1) for i in range(4)
    ]
    return (high_row * 128 + low_row, high_col * 128 + low_col)


def on_device(
    visibilities, baseline_offsets, channel_scale, screen_depth, stations, corners, beam_terms
):
    au_count = lax.axis_size("au")
    vert_count = lax.axis_size("vert")
    au_index, vert_index = lax.axis_index("au"), lax.axis_index("vert")
    image_rows = G // (au_count * vert_count)
    count, _, vis_count = visibilities.shape
    own_stations = beam_terms.shape[0]
    held = au_count * vert_count * count * HALF * PACK
    by_mask = held <= MASK_VALUES

    sent = jnp.concatenate([packed_beams(beam_terms), coded_corners(corners)], axis=0)
    offsets = baseline_offsets.reshape(2 * count, -1)
    scale_row = channel_scale.reshape(1, -1)
    part = math.gcd(count, 8)
    skies = [sky_sums(visibilities, offsets, scale_row, 0, part)]
    if by_mask:
        line = z_line(sent)
        line, offsets, skies[0], corners, stations, screen_depth = lax.optimization_barrier(
            (line, offsets, skies[0], corners, stations, screen_depth)
        )
    for s in range(part, count, part):
        skies.append(sky_sums(visibilities, offsets, scale_row, s, part))
    factor = pixel_factor(screen_depth, corners[:, 0] % SUB, vis_count)
    if by_mask:
        lines = au_lines(line)
        lines, skies = lax.optimization_barrier((lines, skies))
        tables = with_core(lines)
    else:
        tables = whole_gather(sent)
    coded = [
        piece.reshape(-1, own_stations + 1, HALF, PACK)[:, own_stations] for piece in tables
    ]
    corners_all = decoded_corners(jnp.concatenate(coded, axis=0), count)
    owners = stations // own_stations
    station_rows = gathered_place(owners, by_mask) * (own_stations + 1) + stations % own_stations
    uv_own = corrected_subgrids(station_rows, tables, skies, factor)

    per_row = vert_count * count
    tile_rows, tile_cols = G // au_count, G // vert_count

    def tile_info(row):
        place = gathered_place(row * vert_count + vert_index, by_mask) // vert_count
        return jnp.stack([place, au_index * tile_rows, vert_index * tile_cols])

    own_info = tile_info(au_index)
    before_info = tile_info(lax.rem(au_index + au_count - 1, au_count))
    first_row = (au_index * vert_count + vert_index) * image_rows
    phase = phase_table(corners_all[1], first_row, image_rows)
    if by_mask:
        line = z_line(uv_own)
        line, phase, corners_all, own_info, before_info, first_row = lax.optimization_barrier(
            (line, phase, corners_all, own_info, before_info, first_row)
        )
        lines = au_lines(line)
        own_row = with_core(lines[:1])
        tile = uv_tile_own(own_row, own_info, corners_all, per_row, tile_rows, tile_cols)
        given = lookups(corners_all[0])
        columns = column_table(first_row, image_rows)
        lines, own_row, tile, given, columns = lax.optimization_barrier(
            (lines, own_row, tile, given, columns)
        )
        uv = own_row + with_core(lines[1:])
    else:
        uv, given = whole_gather(uv_own), None
        columns = column_table(first_row, image_rows)
        tile = uv_tile_own(uv, own_info, corners_all, per_row, tile_rows, tile_cols)
    return image_rows_of(
        uv, corners_all, (phase, columns), given, tile, before_info, per_row, tile_rows, tile_cols
    )


def solution(mesh):
    return jax.shard_map(
        on_device,
        mesh=mesh,
        in_specs=(
            P(("au", "vert"), None, None),
            P(("au", "vert"), None, None),
            P(),
            P(("au", "vert")),
            P(("au", "vert"), None),
            P(("au", "vert"), None),
            P(("au", "vert"), None, None),
        ),
        out_specs=(P("au", None, "vert"), P(("au", "vert"), None, None)),
        check_vma=False,
    )
```

```python
import functools
import math

import jax
import jax.numpy as jnp
import numpy as np
from jax import lax
from jax.experimental import pallas as pl
from jax.experimental.pallas import tpu as pltpu
from jax.sharding import PartitionSpec as P

G = 8192
SUB = 32
HALF = SUB // 2
PACK = 4 * SUB
LANES = 128
FINE = G // SUB
LOW = FINE // 2
CHUNK = 768
MASK_VALUES = 1 << 22
field_view = 0.1
bf16 = jnp.bfloat16
f32 = jnp.float32
VMEM_BYTES = 58 * 1024 * 1024


def cmul(a, b):
    return (a[0] * b[0] - a[1] * b[1], a[0] * b[1] + a[1] * b[0])


def conj(a):
    return (a[0], -a[1])


def sky_kernel(vis_ref, offset_ref, scale_ref, out_ref, power_ref):
    count, _, vis_count = vis_ref.shape
    times = offset_ref.shape[1]
    step = math.gcd(vis_count, 256)
    row = lax.broadcasted_iota(jnp.int32, (8, step), 0)
    bits = [(row >> bit) % 2 == 1 for bit in range(3)]

    offsets = offset_ref[...]
    parts = []
    for _ in range(3):
        parts.append(offsets.astype(bf16))
        offsets = offsets - parts[-1].astype(f32)
    channels = vis_count // times
    repeats = max(1, LANES // channels)
    scale = jnp.concatenate([scale_ref[...]] * repeats, axis=1)
    width = math.gcd(vis_count, 512)
    scale = jnp.concatenate([scale] * (width // (repeats * channels)), axis=1)
    for start in range(0, vis_count, width):
        at = pl.ds(start, width)
        time = lax.broadcasted_iota(jnp.int32, (times, width), 0)
        place = lax.broadcasted_iota(jnp.int32, (times, width), 1) + start
        one = (place // channels == time).astype(f32).astype(bf16)
        shifts = sum(jnp.dot(part, one, preferred_element_type=f32) for part in parts)
        half = (math.pi / SUB) * (shifts * scale)
        square = half * half
        sine, cosine = 1.0, 1.0
        for term in (12, 10, 8, 6, 4, 2):
            sine = 1.0 - square * (1.0 / (term * (term + 1))) * sine
            cosine = 1.0 - square * (1.0 / (term * (term - 1))) * cosine
        sine = sine * half
        power = (1.0 - 2.0 * sine * sine, 2.0 * sine * cosine)
        for bit in range(5):
            power_ref[bit, 0, :, at] = power[0]
            power_ref[bit, 1, :, at] = power[1]
            power = (power[0] * power[0] - power[1] * power[1], 2.0 * power[0] * power[1])

    def powers(row, at, extra):
        z = [
            tuple(
                jnp.broadcast_to(power_ref[bit, part, pl.ds(row, 1), at], (8, step))
                for part in range(2)
            )
            for bit in range(5)
        ]
        low = (jnp.where(bits[0], z[0][0], 1.0), jnp.where(bits[0], z[0][1], 0.0))
        for bit in (1, 2):
            more = cmul(low, z[bit])
            low = (jnp.where(bits[bit], more[0], low[0]), jnp.where(bits[bit], more[1], low[1]))
        if extra is not None:
            low = cmul(low, extra)
        blocks = [cmul(low, conj(z[4])), cmul(low, conj(z[3])), low, cmul(low, z[3])]
        return jnp.concatenate([block[part] for part in range(2) for block in blocks], axis=0).astype(bf16)

    def one_subgrid(s):
        both = jnp.zeros((2 * SUB, 2 * SUB), f32)
        for start in range(0, vis_count, step):
            at = pl.ds(start, step)
            vis = tuple(
                jnp.broadcast_to(vis_ref[s, part : part + 1, at].astype(f32), (8, step))
                for part in range(2)
            )
            left = powers(2 * s, at, vis)
            right = powers(2 * s + 1, at, None)
            both += lax.dot_general(
                left, right, (((1,), (1,)), ((), ())), preferred_element_type=f32
            )
        real = both[:SUB, :SUB] - both[SUB:, SUB:]
        image = both[:SUB, SUB:] + both[SUB:, :SUB]
        out_ref[s] = jnp.concatenate(
            [real[:HALF], image[:HALF], real[HALF:], image[HALF:]], axis=1
        )

    def some(i, carry):
        for k in range(math.gcd(count, 2)):
            one_subgrid(i * math.gcd(count, 2) + k)
        return carry

    lax.fori_loop(0, count // math.gcd(count, 2), some, 0)


def sky_sums(visibilities, offsets, scale_row, first, count, interpret=False):
    vis_count = visibilities.shape[2]
    times = offsets.shape[1]
    at = first // count
    return pl.pallas_call(
        sky_kernel,
        grid=(1,),
        in_specs=[
            pl.BlockSpec((count, 2, vis_count), lambda i: (at, 0, 0)),
            pl.BlockSpec((2 * count, times), lambda i: (at, 0)),
            pl.BlockSpec(scale_row.shape, lambda i: (0, 0)),
        ],
        out_specs=pl.BlockSpec((count, HALF, PACK), lambda i: (0, 0, 0)),
        out_shape=jax.ShapeDtypeStruct((count, HALF, PACK), f32),
        scratch_shapes=[pltpu.VMEM((5, 2, 2 * count, vis_count), f32)],
        compiler_params=pltpu.CompilerParams(vmem_limit_bytes=VMEM_BYTES),
        cost_estimate=pl.CostEstimate(
            flops=0, bytes_accessed=count * 2_500_000, transcendentals=0
        ),
        name="sky_sums",
        interpret=interpret,
    )(visibilities, offsets, scale_row)


def correct_kernel(stations_ref, *refs, pieces, skies):
    table_refs, refs = refs[:pieces], refs[pieces:]
    sky_refs, refs = refs[:skies], refs[skies:]
    factor_ref, right_ref, left_ref, out_ref, table_ref, mid_ref = refs
    count = factor_ref.shape[0]
    lane = lax.broadcasted_iota(jnp.int32, (HALF, PACK), 1)
    imag = (lane // SUB) % 2 == 1
    sign = jnp.where(imag, 1.0, -1.0)

    def up(x):
        return pltpu.roll(x, SUB, 1)

    def down(x):
        return pltpu.roll(x, PACK - SUB, 1)

    def product(a, b):
        swapped = jnp.where(imag, up(a), down(a))
        return a * jnp.where(imag, up(b), b) + sign * swapped * jnp.where(imag, b, down(b))

    held = 0
    for piece in table_refs:
        table_ref[held : held + piece.shape[0]] = piece[...]
        held += piece.shape[0]
    for s in range(count):
        first = table_ref[stations_ref[2 * s]].astype(f32)
        second = table_ref[stations_ref[2 * s + 1]].astype(f32)
        pair = product(first, -sign * second)
        per = count // skies
        sky = product(sky_refs[s // per][s % per], factor_ref[s])
        mid_ref[HALF * s : HALF * (s + 1), :] = product(sky, pair).astype(bf16)
    mid = jnp.dot(mid_ref[...], right_ref[...], preferred_element_type=f32).astype(bf16)
    for s in range(count):
        rows = mid[HALF * s : HALF * (s + 1)]
        tall = jnp.concatenate([rows[:, : 2 * SUB], rows[:, 2 * SUB :]], axis=0)
        four = jnp.dot(left_ref[...], tall, preferred_element_type=f32)
        real = four[:SUB, :SUB] - four[SUB:, SUB:]
        image = four[:SUB, SUB:] + four[SUB:, :SUB]
        out_ref[s] = jnp.concatenate(
            [real[:HALF], image[:HALF], real[HALF:], image[HALF:]], axis=1
        ).astype(bf16)


def corrected_subgrids(stations, tables, skies, factor, interpret=False):
    count = factor.shape[0]
    centred = np.arange(SUB) - HALF
    angle = 2.0 * math.pi / SUB * (centred[:, None] * centred[None, :] % SUB)
    re, im = np.cos(angle) / SUB, -np.sin(angle) / SUB
    right = jnp.asarray(np.kron(np.eye(2), np.block([[re, im], [-im, re]])), bf16)
    left = jnp.asarray(np.concatenate([re, im], axis=0), bf16)
    rows = sum(piece.shape[0] for piece in tables)
    operands = [*tables, *skies, factor, right, left]

    def whole(operand):
        return pl.BlockSpec(operand.shape, lambda i, *_: (0,) * operand.ndim)

    return pl.pallas_call(
        functools.partial(correct_kernel, pieces=len(tables), skies=len(skies)),
        grid_spec=pltpu.PrefetchScalarGridSpec(
            num_scalar_prefetch=1,
            grid=(1,),
            in_specs=[whole(operand) for operand in operands],
            out_specs=pl.BlockSpec((count, HALF, PACK), lambda i, *_: (0, 0, 0)),
            scratch_shapes=[
                pltpu.VMEM((rows, HALF, PACK), bf16),
                pltpu.VMEM((HALF * count, PACK), bf16),
            ],
        ),
        out_shape=jax.ShapeDtypeStruct((count, HALF, PACK), bf16),
        compiler_params=pltpu.CompilerParams(vmem_limit_bytes=VMEM_BYTES),
        cost_estimate=pl.CostEstimate(flops=0, bytes_accessed=16_000_000, transcendentals=0),
        name="correct",
        interpret=interpret,
    )(stations.reshape(-1), *operands)


def listed(list_ref, first, count, wanted):
    def scan(i, found):
        list_ref[found] = first + i
        return found + wanted(first + i).astype(jnp.int32)

    return lax.fori_loop(0, count, scan, jnp.int32(0), unroll=math.gcd(count, 8))


def add_subgrid(packed, row_at, col_at, total_ref, lanes):
    lane = lax.broadcasted_iota(jnp.int32, (8, LANES), 1)
    row = lax.broadcasted_iota(jnp.int32, (8, LANES), 0)
    tile = col_at // LANES
    offset = col_at % LANES
    shift = row_at % SUB
    base = row_at - shift

    def place(over):
        inside = lane < offset + SUB - LANES
        if not over:
            inside = (lane >= offset) & (lane < offset + SUB)
        for h in range(2):
            for part in range(2):
                from_lane = (2 * h + part) * SUB
                moved = pltpu.roll(packed, lax.rem(offset - from_lane + LANES, LANES), 1)
                for group in range(2):
                    values = moved[8 * group : 8 * (group + 1)]
                    first_row = HALF * h + 8 * group
                    late = row + first_row >= shift
                    early = first_row + 8 <= shift

                    def add(start_row, keep, values=values, part=part):
                        start = start_row * lanes + 2 * (tile + over) + part
                        at = pl.ds(start, 8, stride=lanes)
                        total_ref[at, :] = total_ref[at, :] + jnp.where(keep, values, 0.0)

                    here = base + first_row
                    add(here + SUB * early.astype(jnp.int32), inside & (late | early))

                    @pl.when((first_row < shift) & (shift < first_row + 8))
                    def _():
                        add(here + SUB, inside & ~late)

    place(0)

    @pl.when(offset + SUB > LANES)
    def _():
        place(1)


def tile_kernel(info_ref, row_ref, col_ref, *refs, pieces, tile_rows, tile_cols):
    uv_refs = refs[:pieces]
    out_ref, held_ref, total_ref, list_ref, sems = refs[pieces:]
    lanes = 2 * tile_cols // LANES
    count = held_ref.shape[0] // HALF
    first, row_first, col_first = info_ref[0] * count, info_ref[1], info_ref[2]
    rows_all = total_ref.shape[0]
    zero_rows = math.gcd(rows_all, 1024)

    def clear(i, carry):
        at = pl.ds(pl.multiple_of(i * zero_rows, zero_rows), zero_rows)
        total_ref[at, :] = jnp.zeros((zero_rows, LANES), f32)
        return carry

    lax.fori_loop(0, rows_all // zero_rows, clear, 0)
    held = 0
    for piece in uv_refs:
        held_ref[held : held + piece.shape[0]] = piece[...]
        held += piece.shape[0]

    def wanted(s):
        col_at = col_ref[s] - col_first
        return (col_at >= 0) & (col_at < tile_cols)

    def one(entry, carry):
        s = list_ref[entry]
        at = pl.ds(pl.multiple_of((s - first) * HALF, HALF), HALF)
        packed = held_ref[at, :].astype(f32)
        add_subgrid(packed, row_ref[s] - row_first, col_ref[s] - col_first, total_ref, lanes)
        return carry

    lax.fori_loop(0, listed(list_ref, first, count, wanted), one, 0)
    parts = sems.shape[0]
    size = tile_rows * lanes // parts
    copies = [
        pltpu.make_async_copy(
            total_ref.at[pl.ds(i * size, size), :], out_ref.at[pl.ds(i * size, size), :], sems.at[i]
        )
        for i in range(parts)
    ]
    for copy in copies:
        copy.start()
    for copy in copies:
        copy.wait()


def uv_tile_own(uv, info, corners, count, tile_rows, tile_cols, interpret=False):
    lanes = 2 * tile_cols // LANES
    uv = [piece.reshape(-1, PACK) for piece in uv]
    if len(uv) == 1:
        uv_specs = [pl.BlockSpec((count * HALF, PACK), lambda i, info, *_: (info[0], 0))]
    else:
        uv_specs = [pl.BlockSpec(piece.shape, lambda i, *_: (0, 0)) for piece in uv]
    return pl.pallas_call(
        functools.partial(
            tile_kernel, pieces=len(uv), tile_rows=tile_rows, tile_cols=tile_cols
        ),
        grid_spec=pltpu.PrefetchScalarGridSpec(
            num_scalar_prefetch=3,
            grid=(1,),
            in_specs=uv_specs,
            out_specs=pl.BlockSpec(memory_space=pl.ANY),
            scratch_shapes=[
                pltpu.VMEM((count * HALF, PACK), bf16),
                pltpu.VMEM(((tile_rows + 2 * SUB) * lanes, LANES), f32),
                pltpu.SMEM((count + 1,), jnp.int32),
                pltpu.SemaphoreType.DMA((4,)),
            ],
        ),
        out_shape=jax.ShapeDtypeStruct((tile_rows * lanes, LANES), f32),
        compiler_params=pltpu.CompilerParams(vmem_limit_bytes=VMEM_BYTES),
        cost_estimate=pl.CostEstimate(
            flops=0, bytes_accessed=20 * tile_rows * tile_cols, transcendentals=0
        ),
        name="uv_tile",
        interpret=interpret,
    )(info, *corners, *uv)


def short_transform(values):
    count = len(values)
    if count == 1:
        return values
    even = short_transform(values[0::2])
    odd = short_transform(values[1::2])
    low, high = [], []
    for k in range(count // 2):
        re, im = odd[k]
        if k == 0:
            turned = (re, im)
        elif 4 * k == count:
            turned = (-im, re)
        elif 8 * k == count:
            root = math.sqrt(0.5)
            turned = ((re - im) * root, (re + im) * root)
        elif 8 * k == 3 * count:
            root = math.sqrt(0.5)
            turned = ((re + im) * -root, (re - im) * root)
        else:
            c, s = math.cos(2 * math.pi * k / count), math.sin(2 * math.pi * k / count)
            turned = (re * c - im * s, re * s + im * c)
        low.append((even[k][0] + turned[0], even[k][1] + turned[1]))
        high.append((even[k][0] - turned[0], even[k][1] - turned[1]))
    return low + high


def fill_lookups(corner, unit, counts, here, after, shifts):
    size = corner.shape[1]
    coarse, shift = corner // SUB, corner % SUB

    def looked_up(index, length, table):
        place = lax.broadcasted_iota(jnp.int32, (length, size), 0)
        one = (place == index).astype(f32).astype(bf16)
        return lax.dot_general(one, table, (((0,), (0,)), ((), ())), preferred_element_type=f32)

    here[...] = looked_up(coarse, FINE, unit).astype(bf16)
    after[...] = looked_up(lax.rem(coarse + 1, FINE), FINE, unit).astype(bf16)
    shifts[...] = looked_up(shift, SUB, counts)


def lookup_kernel(corner_ref, unit_ref, count_ref, here, after, shifts):
    fill_lookups(corner_ref[...], unit_ref[...], count_ref[...], here, after, shifts)


def lookup_tables():
    fine, low = np.arange(FINE), np.arange(LOW)
    angle = 2.0 * math.pi / FINE * (fine[:, None] * low[None, :] % FINE)
    odd = np.where(low == 0, 1.0 - 2.0 * (fine[:, None] % 2), np.sin(angle))
    unit = jnp.asarray(np.concatenate([np.cos(angle), odd], axis=1), bf16)
    counts = jnp.asarray(np.broadcast_to(np.arange(SUB)[:, None], (SUB, LANES)), bf16)
    return unit, counts


def lookups(corner_rows, interpret=False):
    total = corner_rows.shape[0]
    return pl.pallas_call(
        lookup_kernel,
        out_shape=[
            jax.ShapeDtypeStruct((total, FINE), bf16),
            jax.ShapeDtypeStruct((total, FINE), bf16),
            jax.ShapeDtypeStruct((total, LANES), f32),
        ],
        compiler_params=pltpu.CompilerParams(vmem_limit_bytes=VMEM_BYTES),
        cost_estimate=pl.CostEstimate(flops=0, bytes_accessed=8_000_000, transcendentals=0),
        name="lookups",
        interpret=interpret,
    )(corner_rows.reshape(1, total), *lookup_tables())


def image_kernel(
    info_ref, row_ref, col_ref, *refs, pieces, chunks, row_block, per_row, tile_cols
):
    uv_refs, refs = refs[:pieces], refs[pieces:]
    given, (phase_ref, columns_ref, twist_ref), refs = refs[:3], refs[3:6], refs[7:]
    out_ref, tile_ref, uv_wide, uv_rows, left_even, left_odd, total, staged, spill = refs[:9]
    list_ref, sem = refs[9:11]
    here, after, shifts = refs[11:] or given
    step = pl.program_id(0)
    lanes = 2 * tile_cols // LANES
    head = pltpu.make_async_copy(
        tile_ref.at[pl.ds(0, SUB * lanes), :], spill.at[pl.ds(SUB * lanes, SUB * lanes), :], sem
    )
    back = pltpu.make_async_copy(
        spill.at[pl.ds(SUB * lanes, SUB * lanes), :], tile_ref.at[pl.ds(0, SUB * lanes), :], sem
    )

    def add_spilled():
        def row_of(s):
            return lax.rem(row_ref[s] - info_ref[1] + SUB + G, G)

        def wanted(s):
            col_at = col_ref[s] - info_ref[2]
            mine = (col_at >= 0) & (col_at < tile_cols) & (row_of(s) < SUB)
            return mine & (s >= step * size) & (s < (step + 1) * size)

        def one(entry, carry):
            s = list_ref[entry]
            packed = uv_wide[pl.ds((s - step * size) * (HALF + 1), HALF), :]
            add_subgrid(packed, row_of(s), col_ref[s] - info_ref[2], spill, lanes)
            return carry

        found = listed(list_ref, info_ref[0] * per_row, per_row, wanted)
        lax.fori_loop(0, found, one, 0)

    size = uv_rows.shape[1]
    image_rows = phase_ref.shape[1]

    def products(pair, h, left, start, width):
        at = pl.ds(2 * image_rows * h, 2 * image_rows)
        items = pl.ds(start, width)
        spread = lax.dot_general(
            columns_ref[at, :], uv_rows[pair, items, :], (((1,), (1,)), ((), ())),
            preferred_element_type=f32,
        ).astype(bf16)
        turned = cmul(
            (spread[:image_rows], spread[image_rows:]), (phase_ref[0, :, items], phase_ref[1, :, items])
        )
        left[h, :image_rows, items] = turned[0]
        left[h, image_rows:, items] = turned[1]

    def table_of(index):
        late = shifts[...] > index.astype(f32)
        return jnp.concatenate(
            [
                jnp.where(late, after[:, t : t + LANES], here[:, t : t + LANES])
                for t in range(0, FINE, LANES)
            ],
            axis=1,
        )

    def keep_sums(index, real, image, first):
        even_re, odd_re = real[:, :LOW], real[:, LOW:]
        even_im, odd_im = image[:, :LOW], image[:, LOW:]
        edge = lax.broadcasted_iota(jnp.int32, (image_rows, LOW), 1) == 0
        low = (
            even_re - jnp.where(edge, 0.0, odd_im),
            even_im + jnp.where(edge, 0.0, odd_re),
        )
        high = (
            jnp.where(edge, odd_re, even_re + odd_im),
            jnp.where(edge, odd_im, even_im - odd_re),
        )
        twist = twist_ref[pl.ds(index, 1), :]
        for half, got in enumerate((low, high)):
            start = 2 * LOW * half
            done = cmul(
                got, (twist[:, start : start + LOW], twist[:, start + LOW : start + 2 * LOW])
            )
            for part in range(2):
                at = (index, part, slice(None), pl.ds(LOW * half, LOW))
                total[at] = done[part] if first else total[at] + done[part]

    third = size // 3 if size % (3 * LANES) == 0 else size

    def products_and_sums(later, left_later, pair, left, first):
        for h in range(2):
            starts = list(range(0, size, third))
            index = pair + HALF * h
            products(later, h, left_later, starts[0], third)
            table = table_of(index)
            real = jnp.dot(left[h, :image_rows], table, preferred_element_type=f32)
            for start in starts[1:2]:
                products(later, h, left_later, start, third)
            image = jnp.dot(left[h, image_rows:], table, preferred_element_type=f32)
            for start in starts[2:]:
                products(later, h, left_later, start, third)
            keep_sums(index, real, image, first)

    def chunk(first):
        if first:
            head.start()
        held = 0
        for piece in uv_refs:

            def spread_out(s, carry, piece=piece, held=held):
                block = piece[pl.ds(pl.multiple_of(s * HALF, HALF), HALF), :]
                uv_wide[pl.ds((held + s) * (HALF + 1), HALF), :] = block.astype(f32)
                return carry

            count = piece.shape[0] // HALF
            lax.fori_loop(0, count, spread_out, 0, unroll=math.gcd(count, 8))
            held += count
        for row in range(HALF):
            uv_rows[row] = uv_wide[pl.ds(row, size, stride=HALF + 1), :].astype(bf16)
        if first:
            head.wait()
        add_spilled()
        pl.when(step == chunks - 1)(back.start)
        if refs[11:]:
            fill_lookups(given[0][...], given[1][...], given[2][...], here, after, shifts)
        for h in range(2):
            products(0, h, left_even, 0, size)

        def two_pairs(i, carry):
            products_and_sums(2 * i + 1, left_odd, 2 * i, left_even, first)
            products_and_sums(
                jnp.minimum(2 * i + 2, HALF - 1), left_even, 2 * i + 1, left_odd, first
            )
            return carry

        lax.fori_loop(0, HALF // 2, two_pairs, 0)
        pl.when(step == chunks - 1)(back.wait)

    @pl.when(step == 0)
    def _():
        chunk(True)

    if chunks > 1:

        @pl.when((step > 0) & (step < chunks))
        def _():
            chunk(False)

    @pl.when(step >= chunks)
    def _():
        first = (step - chunks) * row_block
        wide = 2 * G // LANES
        backward = lax.rem(LOW - lax.broadcasted_iota(jnp.int32, (8, LOW), 1), LOW)

        def eight_rows(group, carry):
            at = pl.ds(pl.multiple_of(first + 8 * group, 8), 8)
            for tile in range(FINE // LANES):
                lanes = pl.ds(tile * LANES, LANES)
                values = [(total[n, 0, at, lanes], total[n, 1, at, lanes]) for n in range(SUB)]
                for k, value in enumerate(short_transform(values)):
                    for part in range(2):
                        ordered = value[part]
                        if tile > 0:
                            ordered = jnp.take_along_axis(
                                ordered, backward, axis=1, mode="promise_in_bounds"
                            )
                        column = 2 * (k * (FINE // LANES) + tile) + part
                        staged[pl.ds(column, 8, stride=wide + 1), :] = ordered
            for row in range(8):
                at = pl.ds(pl.multiple_of((8 * group + row) * wide, wide), wide)
                out_ref[at, :] = staged[row * (wide + 1) : row * (wide + 1) + wide, :]
            return carry

        lax.fori_loop(0, row_block // 8, eight_rows, 0)


def phase_table(corner_cols, first_row, image_rows):
    rows = first_row + jnp.arange(image_rows, dtype=jnp.int32)
    angle = 2.0 * math.pi / G * (rows[:, None] * corner_cols[None, :] % G).astype(f32)
    return jnp.stack([jnp.cos(angle), jnp.sin(angle)]).astype(bf16)


def column_table(first_row, image_rows):
    lane, line = np.arange(PACK)[None, None, :], np.arange(4)[:, None, None]
    angle = 2.0 * math.pi / G * (np.arange(image_rows)[None, :, None] * (lane % SUB))
    angle = angle + 0.5 * math.pi * (lane // SUB % 2 - line % 2)
    same = lane // (2 * SUB) == line // 2
    re, im = [
        jnp.asarray(np.where(same, f(angle), 0.0).reshape(-1, PACK), f32) for f in (np.cos, np.sin)
    ]
    turn = first_row * (jnp.arange(PACK, dtype=jnp.int32) % SUB) % G
    turn = 2.0 * math.pi / G * turn.astype(f32)
    return (re * jnp.cos(turn) - im * jnp.sin(turn)).astype(bf16)


def image_rows_of(
    uv, corners_all, tables, given, tile, info, per_row, tile_rows, tile_cols, interpret=False
):
    phase, columns = tables
    image_rows = phase.shape[1]
    lanes = 2 * tile_cols // LANES
    uv = [piece.reshape(-1, PACK) for piece in uv]
    total = corners_all[0].shape[0]
    size = math.gcd(total, CHUNK) if len(uv) == 1 else total
    chunks = total // size
    row_block = math.gcd(image_rows, 32)
    outs = image_rows // row_block
    wide = 2 * G // LANES
    fine, low = np.arange(FINE), np.arange(LOW)
    scale = 1.0 / (SUB * math.sqrt(total))
    high = np.where(low == 0, LOW, FINE - low)
    angles = [2.0 * math.pi / G * (np.arange(SUB)[:, None] * k[None, :]) for k in (low, high)]
    twist = [f(angle) * scale for angle in angles for f in (np.cos, np.sin)]
    twist = jnp.asarray(np.concatenate(twist, axis=1), f32)
    last = chunks - 1

    def chunk_of(i):
        return jnp.minimum(i, last)

    if len(uv) == 1:
        uv_specs = [pl.BlockSpec((size * HALF, PACK), lambda i, *_: (chunk_of(i), 0))]
    else:
        uv_specs = [pl.BlockSpec(piece.shape, lambda i, *_: (0, 0)) for piece in uv]

    def fixed(operand):
        return pl.BlockSpec(operand.shape, lambda i, *_: (0, 0))

    given_specs = [fixed(operand) for operand in given or ()]
    scratch = []
    if not given:
        given = [corners_all[0].reshape(1, total), *lookup_tables()]
        given_specs = [pl.BlockSpec((1, size), lambda i, *_: (0, chunk_of(i))), *map(fixed, given[1:])]
        scratch = [
            pltpu.VMEM((size, FINE), bf16),
            pltpu.VMEM((size, FINE), bf16),
            pltpu.VMEM((size, LANES), f32),
        ]

    image, tile = pl.pallas_call(
        functools.partial(
            image_kernel, pieces=len(uv), chunks=chunks, row_block=row_block, per_row=per_row,
            tile_cols=tile_cols,
        ),
        grid_spec=pltpu.PrefetchScalarGridSpec(
            num_scalar_prefetch=3,
            grid=(chunks + outs,),
            in_specs=[
                *uv_specs,
                *given_specs,
                pl.BlockSpec((2, image_rows, size), lambda i, *_: (0, 0, chunk_of(i))),
                fixed(columns),
                fixed(twist),
                pl.BlockSpec(memory_space=pl.ANY),
            ],
            out_specs=[
                pl.BlockSpec(
                    (row_block * wide, LANES), lambda i, *_: (jnp.maximum(i - chunks, 0), 0)
                ),
                pl.BlockSpec(memory_space=pl.ANY),
            ],
            scratch_shapes=[
                pltpu.VMEM((size * (HALF + 1) + HALF, PACK), f32),
                pltpu.VMEM((HALF, size, PACK), bf16),
                pltpu.VMEM((2, 2 * image_rows, size), bf16),
                pltpu.VMEM((2, 2 * image_rows, size), bf16),
                pltpu.VMEM((SUB, 2, image_rows, FINE), f32),
                pltpu.VMEM((8 * (wide + 1) + wide, LANES), f32),
                pltpu.VMEM((3 * SUB * lanes, LANES), f32),
                pltpu.SMEM((per_row + 1,), jnp.int32),
                pltpu.SemaphoreType.DMA(()),
                *scratch,
            ],
        ),
        out_shape=[
            jax.ShapeDtypeStruct((image_rows * wide, LANES), f32),
            jax.ShapeDtypeStruct(tile.shape, f32),
        ],
        input_output_aliases={9 + len(uv): 1},
        compiler_params=pltpu.CompilerParams(vmem_limit_bytes=VMEM_BYTES),
        name="image",
        interpret=interpret,
    )(
        info, *corners_all, *uv,
        *given, phase, columns, twist, tile,
    )
    image = image.reshape(image_rows, G // LANES, 2, LANES)
    tile = tile.reshape(tile_rows, tile_cols // LANES, 2, LANES)
    return (
        jnp.transpose(tile, (0, 2, 1, 3)).reshape(tile_rows, 2, tile_cols),
        jnp.transpose(image, (0, 2, 1, 3)).reshape(image_rows, 2, G),
    )


def packed_beams(beam_terms):
    count = beam_terms.shape[0]
    parts = beam_terms.reshape(count, 2, 2, HALF, SUB)
    return jnp.transpose(parts, (0, 3, 2, 1, 4)).reshape(count, HALF, PACK)


def pixel_factor(screen_depth, shift, vis_count):
    lane = jnp.arange(PACK, dtype=jnp.int32)
    col = lane % SUB
    imag = (lane // SUB) % 2
    row = jnp.arange(HALF, dtype=jnp.int32)[:, None] + (lane // (2 * SUB) * HALF)[None, :]

    def taper(x):
        return 1.0 - ((2.0 * x.astype(f32) + 1.0 - SUB) / SUB) ** 2

    def angle_sq(x):
        return ((x - HALF).astype(f32) * (field_view / SUB)) ** 2

    weight = taper(row) * taper(col) / math.sqrt(vis_count)
    turns = shift[:, None, None] * (row - HALF) % SUB
    angle = (
        -math.pi * screen_depth[:, None, None] * (angle_sq(row) + angle_sq(col))
        + 2.0 * math.pi / SUB * turns.astype(f32)
        - 0.5 * math.pi * imag.astype(f32)
    )
    return jnp.cos(angle) * weight


def from_partner(value, axis, mask):
    count = lax.axis_size(axis)
    return lax.ppermute(value, axis, [(i, i ^ mask) for i in range(count)])


def z_line(own):
    vert_count = lax.axis_size("vert")
    line = [own] + [from_partner(own, "vert", 2 * mask) for mask in range(1, vert_count // 2)]
    return jnp.concatenate(line, axis=0)


def au_lines(line):
    return [line] + [from_partner(line, "au", mask) for mask in range(1, lax.axis_size("au"))]


def with_core(lines):
    return [piece for line in lines for piece in (line, from_partner(line, "vert", 1))]


def whole_gather(own):
    return [lax.all_gather(own, ("au", "vert"), axis=0, tiled=True)]


def gathered_place(owner, by_mask):
    if not by_mask:
        return owner
    vert_count = lax.axis_size("vert")
    au_mask = (owner // vert_count) ^ lax.axis_index("au")
    vert_mask = (owner % vert_count) ^ lax.axis_index("vert")
    return au_mask * vert_count + vert_mask % 2 * (vert_count // 2) + vert_mask // 2


def coded_corners(corners):
    digits = jnp.stack([corners[:, 0] // 128, corners[:, 0] % 128, corners[:, 1] // 128, corners[:, 1] % 128])
    flat = digits.astype(f32).astype(bf16).reshape(-1)
    return jnp.pad(flat, (0, HALF * PACK - flat.shape[0])).reshape(1, HALF, PACK)


def decoded_corners(blocks, count):
    digits = blocks.reshape(blocks.shape[0], HALF * PACK).astype(jnp.int32)
    high_row, low_row, high_col, low_col = [
        digits[:, i * count : (i + 1) * count].reshape(-1) for i in range(4)
    ]
    return (high_row * 128 + low_row, high_col * 128 + low_col)


def on_device(
    visibilities, baseline_offsets, channel_scale, screen_depth, stations, corners, beam_terms
):
    au_count = lax.axis_size("au")
    vert_count = lax.axis_size("vert")
    au_index, vert_index = lax.axis_index("au"), lax.axis_index("vert")
    image_rows = G // (au_count * vert_count)
    count, _, vis_count = visibilities.shape
    own_stations = beam_terms.shape[0]
    held = au_count * vert_count * count * HALF * PACK
    by_mask = held <= MASK_VALUES

    sent = jnp.concatenate([packed_beams(beam_terms), coded_corners(corners)], axis=0)
    offsets = baseline_offsets.reshape(2 * count, -1)
    scale_row = channel_scale.reshape(1, -1)
    part = math.gcd(count, 8)
    skies = [sky_sums(visibilities, offsets, scale_row, 0, part)]
    if by_mask:
        line = z_line(sent)
        line, offsets, skies[0], corners, stations, screen_depth = lax.optimization_barrier(
            (line, offsets, skies[0], corners, stations, screen_depth)
        )
    for s in range(part, count, part):
        skies.append(sky_sums(visibilities, offsets, scale_row, s, part))
    factor = pixel_factor(screen_depth, corners[:, 0] % SUB, vis_count)
    if by_mask:
        lines = au_lines(line)
        lines, skies = lax.optimization_barrier((lines, skies))
        tables = with_core(lines)
    else:
        tables = whole_gather(sent)
    coded = [
        piece.reshape(-1, own_stations + 1, HALF, PACK)[:, own_stations] for piece in tables
    ]
    corners_all = decoded_corners(jnp.concatenate(coded, axis=0), count)
    owners = stations // own_stations
    station_rows = gathered_place(owners, by_mask) * (own_stations + 1) + stations % own_stations
    uv_own = corrected_subgrids(station_rows, tables, skies, factor)

    per_row = vert_count * count
    tile_rows, tile_cols = G // au_count, G // vert_count

    def tile_info(row):
        place = gathered_place(row * vert_count + vert_index, by_mask) // vert_count
        return jnp.stack([place, au_index * tile_rows, vert_index * tile_cols])

    own_info = tile_info(au_index)
    before_info = tile_info(lax.rem(au_index + au_count - 1, au_count))
    first_row = (au_index * vert_count + vert_index) * image_rows
    phase = phase_table(corners_all[1], first_row, image_rows)
    if by_mask:
        line = z_line(uv_own)
        line, phase, corners_all, own_info, before_info, first_row = lax.optimization_barrier(
            (line, phase, corners_all, own_info, before_info, first_row)
        )
        lines = au_lines(line)
        own_row = with_core(lines[:1])
        tile = uv_tile_own(own_row, own_info, corners_all, per_row, tile_rows, tile_cols)
        given = lookups(corners_all[0])
        columns = column_table(first_row, image_rows)
        lines, own_row, tile, given, columns = lax.optimization_barrier(
            (lines, own_row, tile, given, columns)
        )
        uv = own_row + with_core(lines[1:])
    else:
        uv, given = whole_gather(uv_own), None
        columns = column_table(first_row, image_rows)
        tile = uv_tile_own(uv, own_info, corners_all, per_row, tile_rows, tile_cols)
    return image_rows_of(
        uv, corners_all, (phase, columns), given, tile, before_info, per_row, tile_rows, tile_cols
    )


def solution(mesh):
    return jax.shard_map(
        on_device,
        mesh=mesh,
        in_specs=(
            P(("au", "vert"), None, None),
            P(("au", "vert"), None, None),
            P(),
            P(("au", "vert")),
            P(("au", "vert"), None),
            P(("au", "vert"), None),
            P(("au", "vert"), None, None),
        ),
        out_specs=(P("au", None, "vert"), P(("au", "vert"), None, None)),
        check_vma=False,
    )
```

```python
import functools
import math

import jax
import jax.numpy as jnp
import numpy as np
from jax import lax
from jax.experimental import pallas as pl
from jax.experimental.pallas import tpu as pltpu
from jax.sharding import PartitionSpec as P

G = 8192
SUB = 32
HALF = SUB // 2
PACK = 4 * SUB
LANES = 128
FINE = G // SUB
LOW = FINE // 2
CHUNK = 768
MASK_VALUES = 1 << 22
field_view = 0.1
bf16 = jnp.bfloat16
f32 = jnp.float32
VMEM_BYTES = 58 * 1024 * 1024


def cmul(a, b):
    return (a[0] * b[0] - a[1] * b[1], a[0] * b[1] + a[1] * b[0])


def conj(a):
    return (a[0], -a[1])


def sky_kernel(vis_ref, offset_ref, scale_ref, out_ref, power_ref):
    count, _, vis_count = vis_ref.shape
    times = offset_ref.shape[1]
    step = math.gcd(vis_count, 256)
    row = lax.broadcasted_iota(jnp.int32, (8, step), 0)
    bits = [(row >> bit) % 2 == 1 for bit in range(3)]

    offsets = offset_ref[...]
    parts = []
    for _ in range(3):
        parts.append(offsets.astype(bf16))
        offsets = offsets - parts[-1].astype(f32)
    channels = vis_count // times
    repeats = max(1, LANES // channels)
    scale = jnp.concatenate([scale_ref[...]] * repeats, axis=1)
    width = math.gcd(vis_count, 512)
    scale = jnp.concatenate([scale] * (width // (repeats * channels)), axis=1)
    for start in range(0, vis_count, width):
        at = pl.ds(start, width)
        time = lax.broadcasted_iota(jnp.int32, (times, width), 0)
        place = lax.broadcasted_iota(jnp.int32, (times, width), 1) + start
        one = (place // channels == time).astype(f32).astype(bf16)
        shifts = sum(jnp.dot(part, one, preferred_element_type=f32) for part in parts)
        half = (math.pi / SUB) * (shifts * scale)
        square = half * half
        sine, cosine = 1.0, 1.0
        for term in (12, 10, 8, 6, 4, 2):
            sine = 1.0 - square * (1.0 / (term * (term + 1))) * sine
            cosine = 1.0 - square * (1.0 / (term * (term - 1))) * cosine
        sine = sine * half
        power = (1.0 - 2.0 * sine * sine, 2.0 * sine * cosine)
        for bit in range(5):
            power_ref[bit, 0, :, at] = power[0]
            power_ref[bit, 1, :, at] = power[1]
            power = (power[0] * power[0] - power[1] * power[1], 2.0 * power[0] * power[1])

    def powers(row, at, extra):
        z = [
            tuple(
                jnp.broadcast_to(power_ref[bit, part, pl.ds(row, 1), at], (8, step))
                for part in range(2)
            )
            for bit in range(5)
        ]
        low = (jnp.where(bits[0], z[0][0], 1.0), jnp.where(bits[0], z[0][1], 0.0))
        for bit in (1, 2):
            more = cmul(low, z[bit])
            low = (jnp.where(bits[bit], more[0], low[0]), jnp.where(bits[bit], more[1], low[1]))
        if extra is not None:
            low = cmul(low, extra)
        blocks = [cmul(low, conj(z[4])), cmul(low, conj(z[3])), low, cmul(low, z[3])]
        return jnp.concatenate([block[part] for part in range(2) for block in blocks], axis=0).astype(bf16)

    def one_subgrid(s):
        both = jnp.zeros((2 * SUB, 2 * SUB), f32)
        for start in range(0, vis_count, step):
            at = pl.ds(start, step)
            vis = tuple(
                jnp.broadcast_to(vis_ref[s, part : part + 1, at].astype(f32), (8, step))
                for part in range(2)
            )
            left = powers(2 * s, at, vis)
            right = powers(2 * s + 1, at, None)
            both += lax.dot_general(
                left, right, (((1,), (1,)), ((), ())), preferred_element_type=f32
            )
        real = both[:SUB, :SUB] - both[SUB:, SUB:]
        image = both[:SUB, SUB:] + both[SUB:, :SUB]
        out_ref[s] = jnp.concatenate(
            [real[:HALF], image[:HALF], real[HALF:], image[HALF:]], axis=1
        )

    def some(i, carry):
        for k in range(math.gcd(count, 2)):
            one_subgrid(i * math.gcd(count, 2) + k)
        return carry

    lax.fori_loop(0, count // math.gcd(count, 2), some, 0)


def sky_sums(visibilities, offsets, scale_row, first, count, interpret=False):
    vis_count = visibilities.shape[2]
    times = offsets.shape[1]
    at = first // count
    return pl.pallas_call(
        sky_kernel,
        grid=(1,),
        in_specs=[
            pl.BlockSpec((count, 2, vis_count), lambda i: (at, 0, 0)),
            pl.BlockSpec((2 * count, times), lambda i: (at, 0)),
            pl.BlockSpec(scale_row.shape, lambda i: (0, 0)),
        ],
        out_specs=pl.BlockSpec((count, HALF, PACK), lambda i: (0, 0, 0)),
        out_shape=jax.ShapeDtypeStruct((count, HALF, PACK), f32),
        scratch_shapes=[pltpu.VMEM((5, 2, 2 * count, vis_count), f32)],
        compiler_params=pltpu.CompilerParams(vmem_limit_bytes=VMEM_BYTES),
        cost_estimate=pl.CostEstimate(
            flops=0, bytes_accessed=count * 2_500_000, transcendentals=0
        ),
        name="sky_sums",
        interpret=interpret,
    )(visibilities, offsets, scale_row)


def correct_kernel(stations_ref, *refs, pieces, skies):
    table_refs, refs = refs[:pieces], refs[pieces:]
    sky_refs, refs = refs[:skies], refs[skies:]
    factor_ref, right_ref, left_ref, out_ref, table_ref, mid_ref = refs
    count = factor_ref.shape[0]
    lane = lax.broadcasted_iota(jnp.int32, (HALF, PACK), 1)
    imag = (lane // SUB) % 2 == 1
    sign = jnp.where(imag, 1.0, -1.0)

    def up(x):
        return pltpu.roll(x, SUB, 1)

    def down(x):
        return pltpu.roll(x, PACK - SUB, 1)

    def product(a, b):
        swapped = jnp.where(imag, up(a), down(a))
        return a * jnp.where(imag, up(b), b) + sign * swapped * jnp.where(imag, b, down(b))

    held = 0
    for piece in table_refs:
        table_ref[held : held + piece.shape[0]] = piece[...]
        held += piece.shape[0]
    for s in range(count):
        first = table_ref[stations_ref[2 * s]].astype(f32)
        second = table_ref[stations_ref[2 * s + 1]].astype(f32)
        pair = product(first, -sign * second)
        per = count // skies
        sky = product(sky_refs[s // per][s % per], factor_ref[s])
        mid_ref[HALF * s : HALF * (s + 1), :] = product(sky, pair).astype(bf16)
    mid = jnp.dot(mid_ref[...], right_ref[...], preferred_element_type=f32).astype(bf16)
    for s in range(count):
        rows = mid[HALF * s : HALF * (s + 1)]
        tall = jnp.concatenate([rows[:, : 2 * SUB], rows[:, 2 * SUB :]], axis=0)
        four = jnp.dot(left_ref[...], tall, preferred_element_type=f32)
        real = four[:SUB, :SUB] - four[SUB:, SUB:]
        image = four[:SUB, SUB:] + four[SUB:, :SUB]
        out_ref[s] = jnp.concatenate(
            [real[:HALF], image[:HALF], real[HALF:], image[HALF:]], axis=1
        ).astype(bf16)


def corrected_subgrids(stations, tables, skies, factor, interpret=False):
    count = factor.shape[0]
    centred = np.arange(SUB) - HALF
    angle = 2.0 * math.pi / SUB * (centred[:, None] * centred[None, :] % SUB)
    re, im = np.cos(angle) / SUB, -np.sin(angle) / SUB
    right = jnp.asarray(np.kron(np.eye(2), np.block([[re, im], [-im, re]])), bf16)
    left = jnp.asarray(np.concatenate([re, im], axis=0), bf16)
    rows = sum(piece.shape[0] for piece in tables)
    operands = [*tables, *skies, factor, right, left]

    def whole(operand):
        return pl.BlockSpec(operand.shape, lambda i, *_: (0,) * operand.ndim)

    return pl.pallas_call(
        functools.partial(correct_kernel, pieces=len(tables), skies=len(skies)),
        grid_spec=pltpu.PrefetchScalarGridSpec(
            num_scalar_prefetch=1,
            grid=(1,),
            in_specs=[whole(operand) for operand in operands],
            out_specs=pl.BlockSpec((count, HALF, PACK), lambda i, *_: (0, 0, 0)),
            scratch_shapes=[
                pltpu.VMEM((rows, HALF, PACK), bf16),
                pltpu.VMEM((HALF * count, PACK), bf16),
            ],
        ),
        out_shape=jax.ShapeDtypeStruct((count, HALF, PACK), bf16),
        compiler_params=pltpu.CompilerParams(vmem_limit_bytes=VMEM_BYTES),
        cost_estimate=pl.CostEstimate(flops=0, bytes_accessed=16_000_000, transcendentals=0),
        name="correct",
        interpret=interpret,
    )(stations.reshape(-1), *operands)


def listed(list_ref, first, count, wanted):
    def scan(i, found):
        list_ref[found] = first + i
        return found + wanted(first + i).astype(jnp.int32)

    return lax.fori_loop(0, count, scan, jnp.int32(0), unroll=math.gcd(count, 8))


def add_subgrid(packed, row_at, col_at, total_ref, lanes):
    lane = lax.broadcasted_iota(jnp.int32, (8, LANES), 1)
    row = lax.broadcasted_iota(jnp.int32, (8, LANES), 0)
    tile = col_at // LANES
    offset = col_at % LANES
    shift = row_at % SUB
    base = row_at - shift

    def place(over):
        inside = lane < offset + SUB - LANES
        if not over:
            inside = (lane >= offset) & (lane < offset + SUB)
        added = []
        for h in range(2):
            for part in range(2):
                from_lane = (2 * h + part) * SUB
                moved = pltpu.roll(packed, lax.rem(offset - from_lane + LANES, LANES), 1)
                for group in range(2):
                    values = moved[8 * group : 8 * (group + 1)]
                    first_row = HALF * h + 8 * group
                    late = row + first_row >= shift
                    for wrapped in range(2):
                        keep = jnp.logical_and(inside, late if wrapped == 0 else ~late)
                        start = (base + SUB * wrapped + first_row) * lanes
                        at = pl.ds(start + 2 * (tile + over) + part, 8, stride=lanes)
                        added.append((at, jnp.where(keep, values, 0.0)))
        sums = [total_ref[at, :] + values for at, values in added]
        for (at, _), value in zip(added, sums):
            total_ref[at, :] = value

    place(0)

    @pl.when(offset + SUB > LANES)
    def _():
        place(1)


def tile_kernel(info_ref, row_ref, col_ref, *refs, pieces, tile_rows, tile_cols):
    uv_refs = refs[:pieces]
    out_ref, held_ref, total_ref, list_ref, sems = refs[pieces:]
    lanes = 2 * tile_cols // LANES
    count = held_ref.shape[0] // HALF
    first, row_first, col_first = info_ref[0] * count, info_ref[1], info_ref[2]
    rows_all = total_ref.shape[0]
    zero_rows = math.gcd(rows_all, 1024)

    def clear(i, carry):
        at = pl.ds(pl.multiple_of(i * zero_rows, zero_rows), zero_rows)
        total_ref[at, :] = jnp.zeros((zero_rows, LANES), f32)
        return carry

    lax.fori_loop(0, rows_all // zero_rows, clear, 0)
    held = 0
    for piece in uv_refs:
        held_ref[held : held + piece.shape[0]] = piece[...]
        held += piece.shape[0]

    def wanted(s):
        col_at = col_ref[s] - col_first
        return (col_at >= 0) & (col_at < tile_cols)

    def one(entry, carry):
        s = list_ref[entry]
        at = pl.ds(pl.multiple_of((s - first) * HALF, HALF), HALF)
        packed = held_ref[at, :].astype(f32)
        add_subgrid(packed, row_ref[s] - row_first, col_ref[s] - col_first, total_ref, lanes)
        return carry

    lax.fori_loop(0, listed(list_ref, first, count, wanted), one, 0)
    parts = sems.shape[0]
    size = tile_rows * lanes // parts
    copies = [
        pltpu.make_async_copy(
            total_ref.at[pl.ds(i * size, size), :], out_ref.at[pl.ds(i * size, size), :], sems.at[i]
        )
        for i in range(parts)
    ]
    for copy in copies:
        copy.start()
    for copy in copies:
        copy.wait()


def uv_tile_own(uv, info, corners, count, tile_rows, tile_cols, interpret=False):
    lanes = 2 * tile_cols // LANES
    uv = [piece.reshape(-1, PACK) for piece in uv]
    if len(uv) == 1:
        uv_specs = [pl.BlockSpec((count * HALF, PACK), lambda i, info, *_: (info[0], 0))]
    else:
        uv_specs = [pl.BlockSpec(piece.shape, lambda i, *_: (0, 0)) for piece in uv]
    return pl.pallas_call(
        functools.partial(
            tile_kernel, pieces=len(uv), tile_rows=tile_rows, tile_cols=tile_cols
        ),
        grid_spec=pltpu.PrefetchScalarGridSpec(
            num_scalar_prefetch=3,
            grid=(1,),
            in_specs=uv_specs,
            out_specs=pl.BlockSpec(memory_space=pl.ANY),
            scratch_shapes=[
                pltpu.VMEM((count * HALF, PACK), bf16),
                pltpu.VMEM(((tile_rows + 2 * SUB) * lanes, LANES), f32),
                pltpu.SMEM((count + 1,), jnp.int32),
                pltpu.SemaphoreType.DMA((4,)),
            ],
        ),
        out_shape=jax.ShapeDtypeStruct((tile_rows * lanes, LANES), f32),
        compiler_params=pltpu.CompilerParams(vmem_limit_bytes=VMEM_BYTES),
        cost_estimate=pl.CostEstimate(
            flops=0, bytes_accessed=20 * tile_rows * tile_cols, transcendentals=0
        ),
        name="uv_tile",
        interpret=interpret,
    )(info, *corners, *uv)


def short_transform(values):
    count = len(values)
    if count == 1:
        return values
    even = short_transform(values[0::2])
    odd = short_transform(values[1::2])
    low, high = [], []
    for k in range(count // 2):
        re, im = odd[k]
        if k == 0:
            turned = (re, im)
        elif 4 * k == count:
            turned = (-im, re)
        elif 8 * k == count:
            root = math.sqrt(0.5)
            turned = ((re - im) * root, (re + im) * root)
        elif 8 * k == 3 * count:
            root = math.sqrt(0.5)
            turned = ((re + im) * -root, (re - im) * root)
        else:
            c, s = math.cos(2 * math.pi * k / count), math.sin(2 * math.pi * k / count)
            turned = (re * c - im * s, re * s + im * c)
        low.append((even[k][0] + turned[0], even[k][1] + turned[1]))
        high.append((even[k][0] - turned[0], even[k][1] - turned[1]))
    return low + high


def fill_lookups(corner, unit, counts, here, after, shifts):
    size = corner.shape[1]
    coarse, shift = corner // SUB, corner % SUB

    def looked_up(index, length, table):
        place = lax.broadcasted_iota(jnp.int32, (length, size), 0)
        one = (place == index).astype(f32).astype(bf16)
        return lax.dot_general(one, table, (((0,), (0,)), ((), ())), preferred_element_type=f32)

    here[...] = looked_up(coarse, FINE, unit).astype(bf16)
    after[...] = looked_up(lax.rem(coarse + 1, FINE), FINE, unit).astype(bf16)
    shifts[...] = looked_up(shift, SUB, counts)


def lookup_kernel(corner_ref, unit_ref, count_ref, here, after, shifts):
    fill_lookups(corner_ref[...], unit_ref[...], count_ref[...], here, after, shifts)


def lookup_tables():
    fine, low = np.arange(FINE), np.arange(LOW)
    angle = 2.0 * math.pi / FINE * (fine[:, None] * low[None, :] % FINE)
    odd = np.where(low == 0, 1.0 - 2.0 * (fine[:, None] % 2), np.sin(angle))
    unit = jnp.asarray(np.concatenate([np.cos(angle), odd], axis=1), bf16)
    counts = jnp.asarray(np.broadcast_to(np.arange(SUB)[:, None], (SUB, LANES)), bf16)
    return unit, counts


def lookups(corner_rows, interpret=False):
    total = corner_rows.shape[0]
    return pl.pallas_call(
        lookup_kernel,
        out_shape=[
            jax.ShapeDtypeStruct((total, FINE), bf16),
            jax.ShapeDtypeStruct((total, FINE), bf16),
            jax.ShapeDtypeStruct((total, LANES), f32),
        ],
        compiler_params=pltpu.CompilerParams(vmem_limit_bytes=VMEM_BYTES),
        cost_estimate=pl.CostEstimate(flops=0, bytes_accessed=8_000_000, transcendentals=0),
        name="lookups",
        interpret=interpret,
    )(corner_rows.reshape(1, total), *lookup_tables())


def image_kernel(
    info_ref, row_ref, col_ref, *refs, pieces, chunks, row_block, per_row, tile_cols
):
    uv_refs, refs = refs[:pieces], refs[pieces:]
    given, (phase_ref, columns_ref, twist_ref), refs = refs[:3], refs[3:6], refs[7:]
    out_ref, tile_ref, uv_wide, uv_rows, left, total, staged, spill = refs[:8]
    list_ref, sem = refs[8:10]
    here, after, shifts = refs[10:] or given
    step = pl.program_id(0)
    lanes = 2 * tile_cols // LANES
    head = pltpu.make_async_copy(
        tile_ref.at[pl.ds(0, SUB * lanes), :], spill.at[pl.ds(SUB * lanes, SUB * lanes), :], sem
    )
    back = pltpu.make_async_copy(
        spill.at[pl.ds(SUB * lanes, SUB * lanes), :], tile_ref.at[pl.ds(0, SUB * lanes), :], sem
    )

    def add_spilled():
        def row_of(s):
            return lax.rem(row_ref[s] - info_ref[1] + SUB + G, G)

        def wanted(s):
            col_at = col_ref[s] - info_ref[2]
            mine = (col_at >= 0) & (col_at < tile_cols) & (row_of(s) < SUB)
            return mine & (s >= step * size) & (s < (step + 1) * size)

        def one(entry, carry):
            s = list_ref[entry]
            packed = uv_wide[pl.ds((s - step * size) * (HALF + 1), HALF), :]
            add_subgrid(packed, row_of(s), col_ref[s] - info_ref[2], spill, lanes)
            return carry

        found = listed(list_ref, info_ref[0] * per_row, per_row, wanted)
        lax.fori_loop(0, found, one, 0)

    size = uv_rows.shape[1]
    image_rows = phase_ref.shape[1]

    def products(pair, h):
        at = pl.ds(2 * image_rows * h, 2 * image_rows)
        spread = lax.dot_general(
            columns_ref[at, :], uv_rows[pair], (((1,), (1,)), ((), ())), preferred_element_type=f32
        ).astype(bf16)
        turned = cmul((spread[:image_rows], spread[image_rows:]), (phase_ref[0], phase_ref[1]))
        left[h, :image_rows] = turned[0]
        left[h, image_rows:] = turned[1]

    def table_of(index):
        late = shifts[...] > index.astype(f32)
        return jnp.concatenate(
            [
                jnp.where(late, after[:, t : t + LANES], here[:, t : t + LANES])
                for t in range(0, FINE, LANES)
            ],
            axis=1,
        )

    def keep_sums(index, real, image, first):
        even_re, odd_re = real[:, :LOW], real[:, LOW:]
        even_im, odd_im = image[:, :LOW], image[:, LOW:]
        edge = lax.broadcasted_iota(jnp.int32, (image_rows, LOW), 1) == 0
        low = (
            even_re - jnp.where(edge, 0.0, odd_im),
            even_im + jnp.where(edge, 0.0, odd_re),
        )
        high = (
            jnp.where(edge, odd_re, even_re + odd_im),
            jnp.where(edge, odd_im, even_im - odd_re),
        )
        twist = twist_ref[pl.ds(index, 1), :]
        for half, got in enumerate((low, high)):
            start = 2 * LOW * half
            done = cmul(
                got, (twist[:, start : start + LOW], twist[:, start + LOW : start + 2 * LOW])
            )
            for part in range(2):
                at = (index, part, slice(None), pl.ds(LOW * half, LOW))
                total[at] = done[part] if first else total[at] + done[part]

    def sums(pair, h, first):
        index = pair + HALF * h
        four = jnp.dot(left[h], table_of(index), preferred_element_type=f32)
        keep_sums(index, four[:image_rows], four[image_rows:], first)

    def chunk(first):
        if first:
            head.start()
        held = 0
        for piece in uv_refs:

            def spread_out(s, carry, piece=piece, held=held):
                block = piece[pl.ds(pl.multiple_of(s * HALF, HALF), HALF), :]
                uv_wide[pl.ds((held + s) * (HALF + 1), HALF), :] = block.astype(f32)
                return carry

            count = piece.shape[0] // HALF
            lax.fori_loop(0, count, spread_out, 0, unroll=math.gcd(count, 8))
            held += count
        for row in range(HALF):
            uv_rows[row] = uv_wide[pl.ds(row, size, stride=HALF + 1), :].astype(bf16)
        if first:
            head.wait()
        add_spilled()
        pl.when(step == chunks - 1)(back.start)
        if refs[10:]:
            fill_lookups(given[0][...], given[1][...], given[2][...], here, after, shifts)

        def one_pair(pair, carry):
            for h in range(2):
                products(pair, h)
            for h in range(2):
                sums(pair, h, first)
            return carry

        lax.fori_loop(0, HALF, one_pair, 0)
        pl.when(step == chunks - 1)(back.wait)

    @pl.when(step == 0)
    def _():
        chunk(True)

    if chunks > 1:

        @pl.when((step > 0) & (step < chunks))
        def _():
            chunk(False)

    @pl.when(step >= chunks)
    def _():
        first = (step - chunks) * row_block
        wide = 2 * G // LANES
        backward = lax.rem(LOW - lax.broadcasted_iota(jnp.int32, (8, LOW), 1), LOW)

        def eight_rows(group, carry):
            at = pl.ds(pl.multiple_of(first + 8 * group, 8), 8)
            for tile in range(FINE // LANES):
                lanes = pl.ds(tile * LANES, LANES)
                values = [(total[n, 0, at, lanes], total[n, 1, at, lanes]) for n in range(SUB)]
                for k, value in enumerate(short_transform(values)):
                    for part in range(2):
                        ordered = value[part]
                        if tile > 0:
                            ordered = jnp.take_along_axis(
                                ordered, backward, axis=1, mode="promise_in_bounds"
                            )
                        column = 2 * (k * (FINE // LANES) + tile) + part
                        staged[pl.ds(column, 8, stride=wide + 1), :] = ordered
            for row in range(8):
                at = pl.ds(pl.multiple_of((8 * group + row) * wide, wide), wide)
                out_ref[at, :] = staged[row * (wide + 1) : row * (wide + 1) + wide, :]
            return carry

        lax.fori_loop(0, row_block // 8, eight_rows, 0)


def phase_table(corner_cols, first_row, image_rows):
    rows = first_row + jnp.arange(image_rows, dtype=jnp.int32)
    angle = 2.0 * math.pi / G * (rows[:, None] * corner_cols[None, :] % G).astype(f32)
    return jnp.stack([jnp.cos(angle), jnp.sin(angle)]).astype(bf16)


def column_table(first_row, image_rows):
    lane, line = np.arange(PACK)[None, None, :], np.arange(4)[:, None, None]
    angle = 2.0 * math.pi / G * (np.arange(image_rows)[None, :, None] * (lane % SUB))
    angle = angle + 0.5 * math.pi * (lane // SUB % 2 - line % 2)
    same = lane // (2 * SUB) == line // 2
    re, im = [
        jnp.asarray(np.where(same, f(angle), 0.0).reshape(-1, PACK), f32) for f in (np.cos, np.sin)
    ]
    turn = first_row * (jnp.arange(PACK, dtype=jnp.int32) % SUB) % G
    turn = 2.0 * math.pi / G * turn.astype(f32)
    return (re * jnp.cos(turn) - im * jnp.sin(turn)).astype(bf16)


def image_rows_of(
    uv, corners_all, tables, given, tile, info, per_row, tile_rows, tile_cols, interpret=False
):
    phase, columns = tables
    image_rows = phase.shape[1]
    lanes = 2 * tile_cols // LANES
    uv = [piece.reshape(-1, PACK) for piece in uv]
    total = corners_all[0].shape[0]
    size = math.gcd(total, CHUNK) if len(uv) == 1 else total
    chunks = total // size
    row_block = math.gcd(image_rows, 32)
    outs = image_rows // row_block
    wide = 2 * G // LANES
    fine, low = np.arange(FINE), np.arange(LOW)
    scale = 1.0 / (SUB * math.sqrt(total))
    high = np.where(low == 0, LOW, FINE - low)
    angles = [2.0 * math.pi / G * (np.arange(SUB)[:, None] * k[None, :]) for k in (low, high)]
    twist = [f(angle) * scale for angle in angles for f in (np.cos, np.sin)]
    twist = jnp.asarray(np.concatenate(twist, axis=1), f32)
    last = chunks - 1

    def chunk_of(i):
        return jnp.minimum(i, last)

    if len(uv) == 1:
        uv_specs = [pl.BlockSpec((size * HALF, PACK), lambda i, *_: (chunk_of(i), 0))]
    else:
        uv_specs = [pl.BlockSpec(piece.shape, lambda i, *_: (0, 0)) for piece in uv]

    def fixed(operand):
        return pl.BlockSpec(operand.shape, lambda i, *_: (0, 0))

    given_specs = [fixed(operand) for operand in given or ()]
    scratch = []
    if not given:
        given = [corners_all[0].reshape(1, total), *lookup_tables()]
        given_specs = [pl.BlockSpec((1, size), lambda i, *_: (0, chunk_of(i))), *map(fixed, given[1:])]
        scratch = [
            pltpu.VMEM((size, FINE), bf16),
            pltpu.VMEM((size, FINE), bf16),
            pltpu.VMEM((size, LANES), f32),
        ]

    image, tile = pl.pallas_call(
        functools.partial(
            image_kernel, pieces=len(uv), chunks=chunks, row_block=row_block, per_row=per_row,
            tile_cols=tile_cols,
        ),
        grid_spec=pltpu.PrefetchScalarGridSpec(
            num_scalar_prefetch=3,
            grid=(chunks + outs,),
            in_specs=[
                *uv_specs,
                *given_specs,
                pl.BlockSpec((2, image_rows, size), lambda i, *_: (0, 0, chunk_of(i))),
                fixed(columns),
                fixed(twist),
                pl.BlockSpec(memory_space=pl.ANY),
            ],
            out_specs=[
                pl.BlockSpec(
                    (row_block * wide, LANES), lambda i, *_: (jnp.maximum(i - chunks, 0), 0)
                ),
                pl.BlockSpec(memory_space=pl.ANY),
            ],
            scratch_shapes=[
                pltpu.VMEM((size * (HALF + 1) + HALF, PACK), f32),
                pltpu.VMEM((HALF, size, PACK), bf16),
                pltpu.VMEM((2, 2 * image_rows, size), bf16),
                pltpu.VMEM((SUB, 2, image_rows, FINE), f32),
                pltpu.VMEM((8 * (wide + 1) + wide, LANES), f32),
                pltpu.VMEM((3 * SUB * lanes, LANES), f32),
                pltpu.SMEM((per_row + 1,), jnp.int32),
                pltpu.SemaphoreType.DMA(()),
                *scratch,
            ],
        ),
        out_shape=[
            jax.ShapeDtypeStruct((image_rows * wide, LANES), f32),
            jax.ShapeDtypeStruct(tile.shape, f32),
        ],
        input_output_aliases={9 + len(uv): 1},
        compiler_params=pltpu.CompilerParams(vmem_limit_bytes=VMEM_BYTES),
        name="image",
        interpret=interpret,
    )(
        info, *corners_all, *uv,
        *given, phase, columns, twist, tile,
    )
    image = image.reshape(image_rows, G // LANES, 2, LANES)
    tile = tile.reshape(tile_rows, tile_cols // LANES, 2, LANES)
    return (
        jnp.transpose(tile, (0, 2, 1, 3)).reshape(tile_rows, 2, tile_cols),
        jnp.transpose(image, (0, 2, 1, 3)).reshape(image_rows, 2, G),
    )


def packed_beams(beam_terms):
    count = beam_terms.shape[0]
    parts = beam_terms.reshape(count, 2, 2, HALF, SUB)
    return jnp.transpose(parts, (0, 3, 2, 1, 4)).reshape(count, HALF, PACK)


def pixel_factor(screen_depth, shift, vis_count):
    lane = jnp.arange(PACK, dtype=jnp.int32)
    col = lane % SUB
    imag = (lane // SUB) % 2
    row = jnp.arange(HALF, dtype=jnp.int32)[:, None] + (lane // (2 * SUB) * HALF)[None, :]

    def taper(x):
        return 1.0 - ((2.0 * x.astype(f32) + 1.0 - SUB) / SUB) ** 2

    def angle_sq(x):
        return ((x - HALF).astype(f32) * (field_view / SUB)) ** 2

    weight = taper(row) * taper(col) / math.sqrt(vis_count)
    turns = shift[:, None, None] * (row - HALF) % SUB
    angle = (
        -math.pi * screen_depth[:, None, None] * (angle_sq(row) + angle_sq(col))
        + 2.0 * math.pi / SUB * turns.astype(f32)
        - 0.5 * math.pi * imag.astype(f32)
    )
    return jnp.cos(angle) * weight


def from_partner(value, axis, mask):
    count = lax.axis_size(axis)
    return lax.ppermute(value, axis, [(i, i ^ mask) for i in range(count)])


def z_line(own):
    vert_count = lax.axis_size("vert")
    line = [own] + [from_partner(own, "vert", 2 * mask) for mask in range(1, vert_count // 2)]
    return jnp.concatenate(line, axis=0)


def au_lines(line):
    return [line] + [from_partner(line, "au", mask) for mask in range(1, lax.axis_size("au"))]


def with_core(lines):
    return [piece for line in lines for piece in (line, from_partner(line, "vert", 1))]


def whole_gather(own):
    return [lax.all_gather(own, ("au", "vert"), axis=0, tiled=True)]


def gathered_place(owner, by_mask):
    if not by_mask:
        return owner
    vert_count = lax.axis_size("vert")
    au_mask = (owner // vert_count) ^ lax.axis_index("au")
    vert_mask = (owner % vert_count) ^ lax.axis_index("vert")
    return au_mask * vert_count + vert_mask % 2 * (vert_count // 2) + vert_mask // 2


def coded_corners(corners):
    digits = jnp.stack([corners[:, 0] // 128, corners[:, 0] % 128, corners[:, 1] // 128, corners[:, 1] % 128])
    flat = digits.astype(f32).astype(bf16).reshape(-1)
    return jnp.pad(flat, (0, HALF * PACK - flat.shape[0])).reshape(1, HALF, PACK)


def decoded_corners(blocks, count):
    digits = blocks.reshape(blocks.shape[0], HALF * PACK).astype(jnp.int32)
    high_row, low_row, high_col, low_col = [
        digits[:, i * count : (i + 1) * count].reshape(-1) for i in range(4)
    ]
    return (high_row * 128 + low_row, high_col * 128 + low_col)


def on_device(
    visibilities, baseline_offsets, channel_scale, screen_depth, stations, corners, beam_terms
):
    au_count = lax.axis_size("au")
    vert_count = lax.axis_size("vert")
    au_index, vert_index = lax.axis_index("au"), lax.axis_index("vert")
    image_rows = G // (au_count * vert_count)
    count, _, vis_count = visibilities.shape
    own_stations = beam_terms.shape[0]
    held = au_count * vert_count * count * HALF * PACK
    by_mask = held <= MASK_VALUES

    sent = jnp.concatenate([packed_beams(beam_terms), coded_corners(corners)], axis=0)
    offsets = baseline_offsets.reshape(2 * count, -1)
    scale_row = channel_scale.reshape(1, -1)
    part = math.gcd(count, 8)
    skies = [sky_sums(visibilities, offsets, scale_row, 0, part)]
    if by_mask:
        line = z_line(sent)
        line, offsets, skies[0], corners, stations, screen_depth = lax.optimization_barrier(
            (line, offsets, skies[0], corners, stations, screen_depth)
        )
    for s in range(part, count, part):
        skies.append(sky_sums(visibilities, offsets, scale_row, s, part))
    factor = pixel_factor(screen_depth, corners[:, 0] % SUB, vis_count)
    if by_mask:
        lines = au_lines(line)
        lines, skies = lax.optimization_barrier((lines, skies))
        tables = with_core(lines)
    else:
        tables = whole_gather(sent)
    coded = [
        piece.reshape(-1, own_stations + 1, HALF, PACK)[:, own_stations] for piece in tables
    ]
    corners_all = decoded_corners(jnp.concatenate(coded, axis=0), count)
    owners = stations // own_stations
    station_rows = gathered_place(owners, by_mask) * (own_stations + 1) + stations % own_stations
    uv_own = corrected_subgrids(station_rows, tables, skies, factor)

    per_row = vert_count * count
    tile_rows, tile_cols = G // au_count, G // vert_count

    def tile_info(row):
        place = gathered_place(row * vert_count + vert_index, by_mask) // vert_count
        return jnp.stack([place, au_index * tile_rows, vert_index * tile_cols])

    own_info = tile_info(au_index)
    before_info = tile_info(lax.rem(au_index + au_count - 1, au_count))
    first_row = (au_index * vert_count + vert_index) * image_rows
    phase = phase_table(corners_all[1], first_row, image_rows)
    if by_mask:
        line = z_line(uv_own)
        line, phase, corners_all, own_info, before_info, first_row = lax.optimization_barrier(
            (line, phase, corners_all, own_info, before_info, first_row)
        )
        lines = au_lines(line)
        own_row = with_core(lines[:1])
        tile = uv_tile_own(own_row, own_info, corners_all, per_row, tile_rows, tile_cols)
        given = lookups(corners_all[0])
        columns = column_table(first_row, image_rows)
        lines, own_row, tile, given, columns = lax.optimization_barrier(
            (lines, own_row, tile, given, columns)
        )
        uv = own_row + with_core(lines[1:])
    else:
        uv, given = whole_gather(uv_own), None
        columns = column_table(first_row, image_rows)
        tile = uv_tile_own(uv, own_info, corners_all, per_row, tile_rows, tile_cols)
    return image_rows_of(
        uv, corners_all, (phase, columns), given, tile, before_info, per_row, tile_rows, tile_cols
    )


def solution(mesh):
    return jax.shard_map(
        on_device,
        mesh=mesh,
        in_specs=(
            P(("au", "vert"), None, None),
            P(("au", "vert"), None, None),
            P(),
            P(("au", "vert")),
            P(("au", "vert"), None),
            P(("au", "vert"), None),
            P(("au", "vert"), None, None),
        ),
        out_specs=(P("au", None, "vert"), P(("au", "vert"), None, None)),
        check_vma=False,
    )
```
